32 devices in a mesh: tm: 16 (over z, y, x), panel: 2 (over core).
Axes of the slice: x: 2, y: 2, z: 4, core: 2. Of those that a mesh axis runs over, the one named last changes fastest.
Arguments:
- factor_inverse: float32 [16, 768, 768], P('tm', None, 'panel'), may hold values from -1 to 1, as said below
- coupling: float32 [16, 768, 768], P('tm', None, 'panel'), may hold values from -1 to 1
- sigma_after: float32 [768, 768], replicated, may hold values from -1 to 3, as said below
Outputs:
- marginal_cov: float32 [16, 768, 768], P('tm', None, 'panel')
- propagator: bfloat16 [16, 768, 768], P('tm', None, 'panel')
The draws below stay inside these ranges and needn't reach their ends.
Inputs may be any that keep to these rules, and one draw needn't show every extreme that they name: `factor_inverse`: factor_inverse_t is lower triangular with a positive diagonal. sigma_after is symmetric.
All inputs are finite; a program needn't handle non-finite values.
Results may differ from the reference program's by a relative error of at most 0.007.
The reference program's roundings to bfloat16 on the way count: a program that leaves them out, or rounds other values in their place, can miss the bound.
Values may be sent and summed in bfloat16 or wider, within the bound.
No kernel may reach another device: no remote copies, remote signals or barrier semaphores. Data moves between devices by JAX's collectives and lax.ppermute only.
A program may use at most 64 MiB of HBM per device.

```python
import math
import jax
import jax.numpy as jnp
from jax import lax

NB = 768
TIME_BLOCKS = 16


def draw_factor_inverse(key, part):
    key = jax.random.fold_in(key, 11)
    random_key_list = jax.random.split(key, 2)
    diagonal = jnp.exp(jax.random.uniform(random_key_list[0], (TIME_BLOCKS, NB), jnp.float32, math.log(0.1), math.log(0.3)))
    spread = jax.random.normal(random_key_list[1], (TIME_BLOCKS, NB, NB), jnp.float32)
    lower_mask = jnp.tril(jnp.ones((NB, NB), jnp.float32), -1)
    identity = jnp.eye(NB, dtype=jnp.float32)
    body_part = spread * (0.1 / math.sqrt(NB)) * lower_mask + identity * diagonal[:, None, :]
    return body_part


def draw_coupling(key, part):
    key = jax.random.fold_in(key, 23)
    random_key_list = jax.random.split(key, 6)
    slow_flag = jax.random.randint(random_key_list[0], (NB,), 0, 2) == 1
    noise = jax.random.normal(random_key_list[1], (TIME_BLOCKS, NB, NB), jnp.float32)
    slow_rate = jnp.exp(jax.random.uniform(random_key_list[2], (NB,), jnp.float32, math.log(0.5), math.log(1.2))) / TIME_BLOCKS
    fast_rate = jnp.exp(jax.random.uniform(random_key_list[3], (NB,), jnp.float32, math.log(0.1), math.log(0.6)))
    rate = jnp.where(slow_flag, slow_rate, fast_rate)
    block_factor = jnp.exp(jax.random.uniform(random_key_list[4], (TIME_BLOCKS, 1), jnp.float32, math.log(0.7), math.log(1.4)))
    damping_factor = 1.0 - rate[None, :] * block_factor
    spike_block_count = jax.random.randint(random_key_list[5], (3,), 0, TIME_BLOCKS)
    spike_triggered = jnp.any(jnp.arange(TIME_BLOCKS)[:, None] == spike_block_count[None, :], axis=1)
    damping_factor = damping_factor * jnp.where(spike_triggered, 0.75, 1.0)[:, None]
    identity = jnp.eye(NB, dtype=jnp.float32)
    return noise * (0.2 / math.sqrt(NB)) * (1.0 - identity) + identity * damping_factor[:, None, :]


def draw_sigma_after(key, part):
    key = jax.random.fold_in(key, 37)
    random_key_list = jax.random.split(key, 2)
    diagonal = jax.random.uniform(random_key_list[0], (NB,), jnp.float32, 0.5, 1.5)
    noise = jax.random.normal(random_key_list[1], (NB, NB), jnp.float32)
    symmetrized_matrix = (noise + noise.T) * (0.2 / math.sqrt(NB))
    identity = jnp.eye(NB, dtype=jnp.float32)
    return symmetrized_matrix * (1.0 - identity) + identity * diagonal[None, :]


def setup_inputs(seed: int = 0) -> dict:
    arg_keys = jax.random.split(jax.random.key(seed), 4)
    return {
        "factor_inverse": draw_factor_inverse(jax.random.fold_in(arg_keys[3], 71), 0),
        "coupling": draw_coupling(jax.random.fold_in(arg_keys[3], 71), 0),
        "sigma_after": draw_sigma_after(jax.random.fold_in(arg_keys[3], 71), 0),
    }


def reference(factor_inverse, coupling, sigma_after):
    highest = lax.Precision.HIGHEST
    rounded = coupling.astype(jnp.bfloat16)
    covariance = jnp.einsum("tki,tkj->tij", factor_inverse, factor_inverse, precision=highest)
    last_block = rounded[-1].astype(jnp.float32)
    folded = jnp.dot(last_block.T, jnp.dot(sigma_after, last_block, precision=highest), precision=highest)
    covariance = covariance.at[-1].add(folded)
    composite = rounded
    distance = 1
    while distance < TIME_BLOCKS:
        partner_bf = lax.optimization_barrier(covariance[distance:].astype(jnp.bfloat16))
        partner_cov = partner_bf.astype(jnp.float32)
        own_comp = composite[:-distance].astype(jnp.float32)
        middle_bf = jnp.einsum("tij,tjk->tik", partner_cov, own_comp, precision=highest).astype(jnp.bfloat16)
        middle = lax.optimization_barrier(middle_bf).astype(jnp.float32)
        update = jnp.einsum("tji,tjk->tik", own_comp, middle, precision=highest)
        covariance = jnp.concatenate([covariance[:-distance] + update, covariance[-distance:]], axis=0)
        partner_comp = composite[distance:].astype(jnp.float32)
        extended_complement = jnp.einsum("tij,tjk->tik", partner_comp, own_comp, precision=highest).astype(jnp.bfloat16)
        composite = jnp.concatenate([extended_complement, composite[-distance:]], axis=0)
        distance = distance * 2
    return covariance, composite
```

```python
import functools

import jax
import jax.numpy as jnp
from jax import lax
from jax.experimental import pallas as pl
from jax.experimental.pallas import tpu as pltpu
from jax.sharding import PartitionSpec as P

BF = jnp.bfloat16
F32 = jnp.float32
GROUP = 4
ANY = pl.BlockSpec(memory_space=pl.ANY)
VMEM = pl.BlockSpec(memory_space=pltpu.VMEM)
MIB = 1 << 20


def mm(a, b):
    return jnp.dot(a, b, preferred_element_type=F32)


def mm_t(a, b):
    return lax.dot_general(a, b, (((0,), (0,)), ((), ())), preferred_element_type=F32)


def whole(ref):
    return jnp.concatenate([ref[p] for p in range(ref.shape[0])], axis=1)


def put(ref, value):
    width = ref.shape[2]
    for p in range(ref.shape[0]):
        ref[p] = value[:, p * width : (p + 1) * width].astype(ref.dtype)


def where_am_i():
    t = lax.axis_index("tm")
    return t // GROUP, lax.rem(t, GROUP), lax.axis_index("panel")


def run(copies):
    for c in copies:
        c.start()
    for c in copies:
        c.wait()


def copy_all(pairs, sems):
    return [pltpu.make_async_copy(s, d, sems.at[i]) for i, (s, d) in enumerate(pairs)]


def panel_pairs(pieces, dst, q):
    n = len(pieces)
    return [(piece, dst.at[lax.rem(q + r, n)]) for r, piece in enumerate(pieces)]


def group_pairs(own, first, second, diag, dst, lo, q):
    n = len(own)
    pairs = []
    for r in range(n):
        p = lax.rem(q + r, n)
        even = 1 - lax.rem(p, 2)
        near, far = 1 + even, 2 - even
        for mask, piece in ((0, own[r]), (near, first[r]), (far, second[r]), (3, diag[r])):
            slot = jnp.bitwise_xor(lo, mask)
            pairs.append((piece, dst.at[slot, p]))
    return pairs


def split(refs, *counts):
    out, at = [], 0
    for c in counts:
        out.append(refs[at : at + c])
        at += c
    return out


def call(kernel, ins, in_specs, outs, scratch, flops):
    size = sum(a.size * a.dtype.itemsize for a in ins) + sum(
        o.size * o.dtype.itemsize for o in outs
    )
    return pl.pallas_call(
        kernel,
        in_specs=in_specs,
        out_specs=[VMEM] * len(outs),
        out_shape=outs,
        scratch_shapes=scratch,
        compiler_params=pltpu.CompilerParams(vmem_limit_bytes=36 * MIB),
        cost_estimate=pl.CostEstimate(flops=flops, bytes_accessed=size, transcendentals=0),
    )(*ins)


def base_kernel(n, *refs):
    factor, sigma, f_parts, c_parts, (base, base_bf), (f_all, c_all, sig, sems) = split(
        refs, 1, 1, n, n, 2, 4
    )
    factor, sigma = factor[0], sigma[0]
    hi, lo, q = where_am_i()
    width = factor.shape[1]
    run(copy_all(panel_pairs(f_parts, f_all, q), sems))
    own = factor[...]
    high = own.astype(BF)
    low = (own - high.astype(F32)).astype(BF)
    for p in range(n):
        part = f_all[p]
        base[p * width : (p + 1) * width, :] = mm_t(part, high) + mm_t(part, low)

    @pl.when(lax.axis_index("tm") == lax.axis_size("tm") - 1)
    def _():
        run(copy_all(panel_pairs(c_parts, c_all, q) + [(sigma, sig)], sems))
        s = sig[...]
        s_high = s.astype(BF)
        s_low = (s - s_high.astype(F32)).astype(BF)
        c_own = c_all[q]
        mid = mm(s_high, c_own) + mm(s_low, c_own)
        mid_high = mid.astype(BF)
        mid_low = (mid - mid_high.astype(F32)).astype(BF)
        c_full = whole(c_all)
        base[...] += mm_t(c_full, mid_high) + mm_t(c_full, mid_low)

    base_bf[...] = base[...].astype(BF)


def group_comp_kernel(n, *refs):
    own, first, second, diag, outs, (sems,) = split(refs, n, n, n, n, 5, 1)
    c, c01_ref, mine, agg, agg_panel = outs
    hi, lo, q = where_am_i()
    run(copy_all(group_pairs(own, first, second, diag, c, lo, q), sems))
    c01 = mm(whole(c.at[1]), whole(c.at[0])).astype(BF)
    put(c01_ref, c01)
    c23 = mm(whole(c.at[3]), whole(c.at[2])).astype(BF)
    put(agg, mm(c23, c01).astype(BF))
    agg_panel[...] = agg[q]

    @pl.when(lo == 0)
    def _():
        mine[...] = agg[...]

    @pl.when(lo == 1)
    def _():
        put(mine, mm(c23, whole(c.at[1])))

    @pl.when(lo == 2)
    def _():
        put(mine, c23)

    @pl.when(lo == 3)
    def _():
        mine[...] = c[3]


def sandwich(cov, comp_ref, q):
    mid = mm(cov, comp_ref[q]).astype(BF)
    return mm_t(whole(comp_ref), mid)


def group_cov_kernel(n, *refs):
    base, c, c01, own, first, second, diag, outs, scratch = split(
        refs, 1, 1, 1, n, n, n, n, 3, 3
    )
    base, c, c01 = base[0], c[0], c01[0]
    mine, agg, agg_bf = outs
    s, s23, sems = scratch
    hi, lo, q = where_am_i()
    run(copy_all(group_pairs(own, first, second, diag, s, lo, q), sems))
    c2 = whole(c.at[2])
    mid = mm(whole(s.at[3]), c2).astype(BF)
    put(s23, whole(s.at[2]).astype(F32) + mm_t(c2, mid))
    v23 = whole(s23)
    agg[...] = s[0, q].astype(F32)

    @pl.when(lo == 0)
    def _():
        agg[...] = base[...]

    agg[...] += sandwich(whole(s.at[1]), c.at[0], q)
    agg[...] += sandwich(v23, c01, q)
    agg_bf[...] = agg[...].astype(BF)

    @pl.when(lo == 0)
    def _():
        mine[...] = agg[...]

    @pl.when(lo == 1)
    def _():
        mine[...] = base[...] + sandwich(v23, c.at[1], q)

    @pl.when(lo == 2)
    def _():
        mine[...] = base[...] + sandwich(whole(s.at[3]), c.at[2], q)

    @pl.when(lo == 3)
    def _():
        mine[...] = base[...]


def receives(bit):
    hi, lo, q = where_am_i()
    return lax.rem(hi // (1 << bit), 2) == 0


def level_comp_kernel(n, bit, *refs):
    mine, agg, parts, outs, (got, sems) = split(refs, 1, 1, n, 3, 2)
    mine, agg = mine[0], agg[0]
    new_mine, new_agg, new_agg_panel = outs
    hi, lo, q = where_am_i()
    active = receives(bit)

    @pl.when(active)
    def _():
        run(copy_all(panel_pairs(parts, got, q), sems))
        c = whole(got)
        put(new_mine, mm(c, whole(mine)))
        put(new_agg, mm(c, whole(agg)))

    @pl.when(jnp.logical_not(active))
    def _():
        new_mine[...] = mine[...]
        new_agg[...] = agg[...]

    new_agg_panel[...] = new_agg[q]


def last_comp_kernel(n, bit, *refs):
    mine, parts, (out,), (got, sems) = split(refs, 1, n, 1, 2)
    mine = mine[0]
    hi, lo, q = where_am_i()
    active = receives(bit)

    @pl.when(active)
    def _():
        run(copy_all(panel_pairs(parts, got, q), sems))
        out[0] = mm(whole(got), mine[q]).astype(BF)

    @pl.when(jnp.logical_not(active))
    def _():
        out[0] = mine[q]


def level_cov_kernel(n, bit, *refs):
    cov, agg, mine_c, agg_c, parts, outs, (got, sems) = split(refs, 1, 1, 1, 1, n, 3, 2)
    cov, agg, mine_c, agg_c = cov[0], agg[0], mine_c[0], agg_c[0]
    new_cov, new_agg, new_agg_bf = outs
    hi, lo, q = where_am_i()
    active = receives(bit)
    new_cov[...] = cov[...]
    new_agg[...] = agg[...]

    @pl.when(active)
    def _():
        run(copy_all(panel_pairs(parts, got, q), sems))
        s = whole(got)
        new_cov[...] += sandwich(s, mine_c, q)
        new_agg[...] += sandwich(s, agg_c, q)

    new_agg_bf[...] = new_agg[...].astype(BF)


def last_cov_kernel(n, bit, *refs):
    cov, mine_c, parts, (out,), (got, sems) = split(refs, 1, 1, n, 1, 2)
    cov, mine_c = cov[0], mine_c[0]
    hi, lo, q = where_am_i()
    out[0] = cov[...]

    @pl.when(receives(bit))
    def _():
        run(copy_all(panel_pairs(parts, got, q), sems))
        out[0] += sandwich(whole(got), mine_c, q)


def over_panels(x):
    n = lax.axis_size("panel")
    return [x] + [
        lax.ppermute(x, "panel", [((i + r) % n, i) for i in range(n)]) for r in range(1, n)
    ]


def over_group(x):
    steps, n = lax.axis_size("tm"), lax.axis_size("panel")

    def swap(value, odd_mask, even_mask):
        pairs = []
        for t in range(steps):
            for q in range(n):
                mask = odd_mask if q % 2 else even_mask
                pairs.append((t * n + q, (t ^ mask) * n + q))
        return lax.ppermute(value, ("tm", "panel"), pairs)

    first = swap(x, 1, 2)
    second = swap(x, 2, 1)
    diag = swap(first, 2, 1)
    return [over_panels(v) for v in (x, first, second, diag)]


def to_receivers(x, bit):
    steps = lax.axis_size("tm")
    d = 1 << bit
    got = None
    t = lax.axis_index("tm") // GROUP
    for back in range(1, d + 1):
        pairs = [
            (g * GROUP + k, (g - back) * GROUP + k)
            for g in range(d, steps // GROUP, 2 * d)
            for k in range(GROUP)
        ]
        here = lax.ppermute(x, "tm", pairs)
        got = here if got is None else jnp.where(lax.rem(t, d) == d - back, here, got)
    return over_panels(got)


def shards(factor_inverse, coupling, sigma_after):
    steps = lax.axis_size("tm")
    n = lax.axis_size("panel")
    nb, w = factor_inverse.shape[1:]
    levels = (steps // GROUP - 1).bit_length()
    panel_bf = jax.ShapeDtypeStruct((nb, w), BF)
    panel_f32 = jax.ShapeDtypeStruct((nb, w), F32)
    full_bf = jax.ShapeDtypeStruct((n, nb, w), BF)
    group_bf = jax.ShapeDtypeStruct((GROUP, n, nb, w), BF)
    one = 2 * nb * nb * w
    sems = pltpu.SemaphoreType.DMA

    comp = coupling[0].astype(BF)
    c_group = over_group(comp)
    factor = factor_inverse[0]
    f_parts = over_panels(factor.astype(BF))
    base, base_bf = call(
        functools.partial(base_kernel, n),
        [factor, sigma_after, *f_parts, *c_group[0]],
        [VMEM] + [ANY] * (1 + 2 * n),
        [panel_f32, panel_bf],
        [
            pltpu.VMEM((n, nb, w), BF),
            pltpu.VMEM((n, nb, w), BF),
            pltpu.VMEM((nb, n * w), F32),
            sems((n + 1,)),
        ],
        2 * one,
    )
    s_group = over_group(base_bf)
    pieces = [p for block in c_group for p in block]
    c_all, c01, mine_c, agg_c, agg_c_panel = call(
        functools.partial(group_comp_kernel, n),
        pieces,
        [ANY] * len(pieces),
        [group_bf, full_bf, full_bf, full_bf, panel_bf],
        [sems((GROUP * n,))],
        4 * n * one,
    )
    pieces = [p for block in s_group for p in block]
    cov, agg, agg_bf = call(
        functools.partial(group_cov_kernel, n),
        [base, c_all, c01, *pieces],
        [VMEM] * 3 + [ANY] * len(pieces),
        [panel_f32, panel_f32, panel_bf],
        [pltpu.VMEM((GROUP, n, nb, w), BF), pltpu.VMEM((n, nb, w), BF), sems((GROUP * n,))],
        (2 * n + 6) * one,
    )
    out_cov = jax.ShapeDtypeStruct((1, nb, w), F32)
    out_comp = jax.ShapeDtypeStruct((1, nb, w), BF)
    scratch = [pltpu.VMEM((n, nb, w), BF), sems((n,))]
    for bit in range(levels):
        c_parts = to_receivers(agg_c_panel, bit)
        s_parts = to_receivers(agg_bf, bit)
        if bit + 1 < levels:
            new_mine_c, new_agg_c, agg_c_panel = call(
                functools.partial(level_comp_kernel, n, bit),
                [mine_c, agg_c, *c_parts],
                [VMEM] * 2 + [ANY] * n,
                [full_bf, full_bf, panel_bf],
                scratch,
                2 * n * one,
            )
            cov, agg, agg_bf = call(
                functools.partial(level_cov_kernel, n, bit),
                [cov, agg, mine_c, agg_c, *s_parts],
                [VMEM] * 4 + [ANY] * n,
                [panel_f32, panel_f32, panel_bf],
                scratch,
                4 * one,
            )
            mine_c, agg_c = new_mine_c, new_agg_c
        else:
            (prop,) = call(
                functools.partial(last_comp_kernel, n, bit),
                [mine_c, *c_parts],
                [VMEM] + [ANY] * n,
                [out_comp],
                scratch,
                one,
            )
            (cov,) = call(
                functools.partial(last_cov_kernel, n, bit),
                [cov, mine_c, *s_parts],
                [VMEM] * 2 + [ANY] * n,
                [out_cov],
                scratch,
                2 * one,
            )
    return cov, prop


def solution(mesh):
    placed = (P("tm", None, "panel"), P("tm", None, "panel"), P())
    return jax.shard_map(
        shards,
        mesh=mesh,
        in_specs=placed,
        out_specs=(P("tm", None, "panel"), P("tm", None, "panel")),
        check_vma=False,
    )
```

```python
import functools

import jax
import jax.numpy as jnp
from jax import lax
from jax.experimental import pallas as pl
from jax.experimental.pallas import tpu as pltpu
from jax.sharding import PartitionSpec as P

BF = jnp.bfloat16
F32 = jnp.float32
GROUP = 4
ANY = pl.BlockSpec(memory_space=pl.ANY)
VMEM = pl.BlockSpec(memory_space=pltpu.VMEM)
MIB = 1 << 20


def mm(a, b):
    return jnp.dot(a, b, preferred_element_type=F32)


def mm_t(a, b):
    return lax.dot_general(a, b, (((0,), (0,)), ((), ())), preferred_element_type=F32)


def whole(ref):
    return jnp.concatenate([ref[p] for p in range(ref.shape[0])], axis=1)


def put(ref, value):
    width = ref.shape[2]
    for p in range(ref.shape[0]):
        ref[p] = value[:, p * width : (p + 1) * width].astype(ref.dtype)


def where_am_i():
    t = lax.axis_index("tm")
    return t // GROUP, lax.rem(t, GROUP), lax.axis_index("panel")


def run(copies):
    for c in copies:
        c.start()
    for c in copies:
        c.wait()


def copy_all(pairs, sems):
    return [pltpu.make_async_copy(s, d, sems.at[i]) for i, (s, d) in enumerate(pairs)]


def panel_pairs(pieces, dst, q):
    n = len(pieces)
    return [(piece, dst.at[lax.rem(q + r, n)]) for r, piece in enumerate(pieces)]


def group_pairs(own, first, second, diag, dst, lo, q):
    n = len(own)
    pairs = []
    for r in range(n):
        p = lax.rem(q + r, n)
        even = 1 - lax.rem(p, 2)
        near, far = 1 + even, 2 - even
        for mask, piece in ((0, own[r]), (near, first[r]), (far, second[r]), (3, diag[r])):
            slot = jnp.bitwise_xor(lo, mask)
            pairs.append((piece, dst.at[slot, p]))
    return pairs


def split(refs, *counts):
    out, at = [], 0
    for c in counts:
        out.append(refs[at : at + c])
        at += c
    return out


def call(kernel, ins, in_specs, outs, scratch, flops):
    size = sum(a.size * a.dtype.itemsize for a in ins) + sum(
        o.size * o.dtype.itemsize for o in outs
    )
    return pl.pallas_call(
        kernel,
        in_specs=in_specs,
        out_specs=[VMEM] * len(outs),
        out_shape=outs,
        scratch_shapes=scratch,
        compiler_params=pltpu.CompilerParams(vmem_limit_bytes=28 * MIB),
        cost_estimate=pl.CostEstimate(flops=flops, bytes_accessed=size, transcendentals=0),
    )(*ins)


def base_kernel(n, *refs):
    factor, sigma, f_parts, c_parts, (base, base_bf), (f_all, c_all, sig, sems) = split(
        refs, 1, 1, n, n, 2, 4
    )
    factor, sigma = factor[0], sigma[0]
    hi, lo, q = where_am_i()
    width = factor.shape[1]
    run(copy_all(panel_pairs(f_parts, f_all, q), sems))
    own = factor[...]
    high = own.astype(BF)
    low = (own - high.astype(F32)).astype(BF)
    for p in range(n):
        part = f_all[p]
        base[p * width : (p + 1) * width, :] = mm_t(part, high) + mm_t(part, low)

    @pl.when(lax.axis_index("tm") == lax.axis_size("tm") - 1)
    def _():
        run(copy_all(panel_pairs(c_parts, c_all, q) + [(sigma, sig)], sems))
        s = sig[...]
        s_high = s.astype(BF)
        s_low = (s - s_high.astype(F32)).astype(BF)
        c_own = c_all[q]
        mid = mm(s_high, c_own) + mm(s_low, c_own)
        mid_high = mid.astype(BF)
        mid_low = (mid - mid_high.astype(F32)).astype(BF)
        c_full = whole(c_all)
        base[...] += mm_t(c_full, mid_high) + mm_t(c_full, mid_low)

    base_bf[...] = base[...].astype(BF)


def group_comp_kernel(n, *refs):
    own, first, second, diag, outs, (sems,) = split(refs, n, n, n, n, 8, 1)
    c, c_t, c01_ref, c01_t, mine, mine_t, agg, agg_t = outs
    hi, lo, q = where_am_i()
    run(copy_all(group_pairs(own, first, second, diag, c, lo, q), sems))
    c01 = mm(whole(c.at[1]), whole(c.at[0])).astype(BF)
    put(c01_ref, c01)
    c23 = mm(whole(c.at[3]), whole(c.at[2])).astype(BF)
    whole_agg = mm(c23, c01).astype(BF)
    put(agg, whole_agg)
    agg_t[...] = whole_agg.T
    c01_t[...] = c01.T
    for k in range(GROUP - 1):
        c_t[k] = whole(c.at[k]).T

    @pl.when(lo == 0)
    def _():
        mine[...] = agg[...]
        mine_t[...] = agg_t[...]

    @pl.when(lo == 1)
    def _():
        value = mm(c23, whole(c.at[1])).astype(BF)
        put(mine, value)
        mine_t[...] = value.T

    @pl.when(lo == 2)
    def _():
        put(mine, c23)
        mine_t[...] = c23.T

    @pl.when(lo == 3)
    def _():
        mine[...] = c[3]
        mine_t[...] = whole(c.at[3]).T


def sandwich(cov, comp, comp_t):
    return mm(comp_t, mm(cov, comp).astype(BF))


def group_cov_kernel(n, *refs):
    ins, own, first, second, diag, outs, scratch = split(refs, 5, n, n, n, n, 3, 3)
    base, c, c_t, c01, c01_t = ins
    mine, agg, agg_bf = outs
    s, s23, sems = scratch
    hi, lo, q = where_am_i()
    run(copy_all(group_pairs(own, first, second, diag, s, lo, q), sems))
    s23[...] = (
        whole(s.at[2]).astype(F32) + sandwich(whole(s.at[3]), whole(c.at[2]), c_t[2])
    ).astype(BF)
    agg[...] = s[0, q].astype(F32)

    @pl.when(lo == 0)
    def _():
        agg[...] = base[...]

    agg[...] += sandwich(whole(s.at[1]), c[0, q], c_t[0])
    agg[...] += sandwich(s23[...], c01[q], c01_t[...])
    agg_bf[...] = agg[...].astype(BF)

    @pl.when(lo == 0)
    def _():
        mine[...] = agg[...]

    @pl.when(lo == 1)
    def _():
        mine[...] = base[...] + sandwich(s23[...], c[1, q], c_t[1])

    @pl.when(lo == 2)
    def _():
        mine[...] = base[...] + sandwich(whole(s.at[3]), c[2, q], c_t[2])

    @pl.when(lo == 3)
    def _():
        mine[...] = base[...]


def is_lower(bit):
    hi, lo, q = where_am_i()
    return lax.rem(hi // (1 << bit), 2) == 0


def arrived(pieces, dst, lo, q):
    if len(pieces) == dst.shape[0]:
        return panel_pairs(pieces, dst, q)
    n = dst.shape[0]
    rows = dst.shape[1] // GROUP
    pairs = []
    for mask in range(GROUP):
        at = pl.multiple_of(jnp.bitwise_xor(lo, mask) * rows, rows)
        for r in range(n):
            pairs.append(
                (pieces[mask * n + r], dst.at[lax.rem(q + r, n), pl.ds(at, rows), :])
            )
    return pairs


def level_comp_kernel(n, m, bit, *refs):
    ins, parts, outs, (got, sems) = split(refs, 4, m, 7, 2)
    mine, mine_t, agg, agg_t = ins
    new_mine, new_mine_t, left, left_t, new_agg, new_agg_t, share = outs
    hi, lo, q = where_am_i()
    lower = is_lower(bit)
    run(copy_all(arrived(parts, got, lo, q), sems))
    rows = share.shape[0]

    @pl.when(lower)
    def _():
        c = whole(got)
        pair = mm(c, whole(agg)).astype(BF)
        put(new_agg, pair)
        new_agg_t[...] = pair.T
        value = mm(c, whole(mine)).astype(BF)
        put(new_mine, value)
        new_mine_t[...] = value.T
        left[...] = agg[...]
        left_t[...] = agg_t[...]

    @pl.when(jnp.logical_not(lower))
    def _():
        c = whole(got)
        pair = mm(whole(agg), c).astype(BF)
        put(new_agg, pair)
        new_agg_t[...] = pair.T
        new_mine[...] = mine[...]
        new_mine_t[...] = mine_t[...]
        left[...] = got[...]
        left_t[...] = c.T

    share[...] = new_agg[q, pl.ds(pl.multiple_of(lo * rows, rows), rows), :]


def last_comp_kernel(n, m, bit, *refs):
    (mine,), parts, (out,), (got, sems) = split(refs, 1, m, 1, 2)
    hi, lo, q = where_am_i()
    lower = is_lower(bit)

    @pl.when(lower)
    def _():
        run(copy_all(arrived(parts, got, lo, q), sems))
        out[0] = mm(whole(got), mine[q]).astype(BF)

    @pl.when(jnp.logical_not(lower))
    def _():
        out[0] = mine[q]


def level_cov_kernel(n, m, bit, *refs):
    ins, here, parts, outs, (right, left_cols, sems) = split(refs, 6, n, m, 4, 3)
    cov, agg, mine, mine_t, left, left_t = ins
    new_cov, new_agg, new_agg_bf, share = outs
    hi, lo, q = where_am_i()
    lower = is_lower(bit)
    rows = share.shape[0]

    @pl.when(lower)
    def _():
        run(copy_all(arrived(parts, right, lo, q), sems))
        new_agg[...] = agg[...] + sandwich(whole(right), left[q], left_t[...])
        new_cov[...] = cov[...] + sandwich(whole(right), mine[q], mine_t[...])

    @pl.when(jnp.logical_not(lower))
    def _():
        run(copy_all(arrived(parts, left_cols, lo, q), sems))
        run(copy_all(panel_pairs(here, right, q), sems))
        new_agg[...] = left_cols[q].astype(F32) + sandwich(whole(right), left[q], left_t[...])
        new_cov[...] = cov[...]

    new_agg_bf[...] = new_agg[...].astype(BF)
    share[...] = new_agg_bf[pl.ds(pl.multiple_of(lo * rows, rows), rows), :]


def last_cov_kernel(n, m, bit, *refs):
    (cov, mine, mine_t), parts, (out,), (got, sems) = split(refs, 3, m, 1, 2)
    hi, lo, q = where_am_i()
    lower = is_lower(bit)

    @pl.when(lower)
    def _():
        run(copy_all(arrived(parts, got, lo, q), sems))
        out[0] = cov[...] + sandwich(whole(got), mine[q], mine_t[...])

    @pl.when(jnp.logical_not(lower))
    def _():
        out[0] = cov[...]


def over_panels(x):
    n = lax.axis_size("panel")
    return [x] + [
        lax.ppermute(x, "panel", [((i + r) % n, i) for i in range(n)]) for r in range(1, n)
    ]


def swap(value, odd_mask, even_mask):
    steps, n = lax.axis_size("tm"), lax.axis_size("panel")
    pairs = []
    for t in range(steps):
        for q in range(n):
            mask = odd_mask if q % 2 else even_mask
            pairs.append((t * n + q, (t ^ mask) * n + q))
    return lax.ppermute(value, ("tm", "panel"), pairs)


def across(x, bit, last):
    steps = lax.axis_size("tm")
    d = GROUP << bit
    return lax.ppermute(
        x, "tm", [(t, t ^ d) for t in range(steps) if (t ^ d) < steps and (t & d or not last)]
    )


def quarters(x):
    blocks = [x] + [swap(x, mask, mask) for mask in range(1, GROUP)]
    return [p for block in blocks for p in over_panels(block)]


def after(x, *others):
    return lax.optimization_barrier((x, *others))[0]


def shards(factor_inverse, coupling, sigma_after):
    steps = lax.axis_size("tm")
    n = lax.axis_size("panel")
    nb, w = factor_inverse.shape[1:]
    levels = (steps // GROUP - 1).bit_length()
    panel_bf = jax.ShapeDtypeStruct((nb, w), BF)
    panel_f32 = jax.ShapeDtypeStruct((nb, w), F32)
    full_bf = jax.ShapeDtypeStruct((n, nb, w), BF)
    square_bf = jax.ShapeDtypeStruct((nb, nb), BF)
    group_bf = jax.ShapeDtypeStruct((GROUP, n, nb, w), BF)
    turned_bf = jax.ShapeDtypeStruct((GROUP - 1, nb, nb), BF)
    share_bf = jax.ShapeDtypeStruct((nb // GROUP, w), BF)
    full_scratch = pltpu.VMEM((n, nb, w), BF)
    one = 2 * nb * nb * w
    sems = pltpu.SemaphoreType.DMA

    comp = coupling[0].astype(BF)
    c_first = swap(comp, 1, 2)
    c_second = swap(comp, 2, 1)
    c_diag = swap(c_first, 2, 1)
    c_own = over_panels(comp)
    c_pieces = [p for v in (c_first, c_second, c_diag) for p in over_panels(v)]

    factor = after(factor_inverse[0], comp)
    f_parts = over_panels(factor.astype(BF))
    base, base_bf = call(
        functools.partial(base_kernel, n),
        [factor, sigma_after, *f_parts, *c_own],
        [VMEM] + [ANY] * (1 + 2 * n),
        [panel_f32, panel_bf],
        [full_scratch, full_scratch, pltpu.VMEM((nb, n * w), F32), sems((n + 1,))],
        2 * one,
    )
    base_bf = after(base_bf, c_second)
    s_first = swap(base_bf, 1, 2)
    s_second = swap(base_bf, 2, 1)
    c_all, c_t, c01, c01_t, mine, mine_t, agg_c, agg_t = call(
        functools.partial(group_comp_kernel, n),
        c_own + c_pieces,
        [ANY] * (GROUP * n),
        [group_bf, turned_bf, full_bf, square_bf, full_bf, square_bf, full_bf, square_bf],
        [sems((GROUP * n,))],
        4 * n * one,
    )
    agg_panel = lax.dynamic_index_in_dim(agg_c, lax.axis_index("panel"), 0, keepdims=False)
    s_diag = swap(after(s_first, agg_panel), 2, 1)
    s_pieces = [p for v in (base_bf, s_first, s_second, s_diag) for p in over_panels(v)]
    cov, agg, agg_bf = call(
        functools.partial(group_cov_kernel, n),
        [base, c_all, c_t, c01, c01_t, *s_pieces],
        [VMEM] * 5 + [ANY] * (GROUP * n),
        [panel_f32, panel_f32, panel_bf],
        [pltpu.VMEM((GROUP, n, nb, w), BF), pltpu.VMEM((nb, nb), BF), sems((GROUP * n,))],
        (2 * n + 6) * one,
    )
    out_cov = jax.ShapeDtypeStruct((1, nb, w), F32)
    out_comp = jax.ShapeDtypeStruct((1, nb, w), BF)
    c_send, s_send = agg_panel, agg_bf
    for bit in range(levels):
        last = bit + 1 == levels
        spread = quarters if bit else over_panels
        c_parts = spread(across(c_send, bit, last))
        m = len(c_parts)
        if last:
            (prop,) = call(
                functools.partial(last_comp_kernel, n, m, bit),
                [mine, *c_parts],
                [VMEM] + [ANY] * m,
                [out_comp],
                [full_scratch, sems((m,))],
                one,
            )
            s_parts = spread(across(s_send, bit, last))
            (cov,) = call(
                functools.partial(last_cov_kernel, n, m, bit),
                [cov, mine, mine_t, *s_parts],
                [VMEM] * 3 + [ANY] * m,
                [out_cov],
                [full_scratch, sems((m,))],
                2 * one,
            )
            break
        new_mine, new_mine_t, left, left_t, agg_c, agg_t, c_send = call(
            functools.partial(level_comp_kernel, n, m, bit),
            [mine, mine_t, agg_c, agg_t, *c_parts],
            [VMEM] * 4 + [ANY] * m,
            [full_bf, square_bf, full_bf, square_bf, full_bf, square_bf, share_bf],
            [full_scratch, sems((m,))],
            2 * n * one,
        )
        s_parts = spread(across(s_send, bit, last))
        cov, agg, agg_bf, s_send = call(
            functools.partial(level_cov_kernel, n, m, bit),
            [cov, agg, mine, mine_t, left, left_t, *over_panels(agg_bf), *s_parts],
            [VMEM] * 6 + [ANY] * (n + m),
            [panel_f32, panel_f32, panel_bf, share_bf],
            [full_scratch, full_scratch, sems((max(n, m),))],
            4 * one,
        )
        mine, mine_t = new_mine, new_mine_t
    return cov, prop


def solution(mesh):
    placed = (P("tm", None, "panel"), P("tm", None, "panel"), P())
    return jax.shard_map(
        shards,
        mesh=mesh,
        in_specs=placed,
        out_specs=(P("tm", None, "panel"), P("tm", None, "panel")),
        check_vma=False,
    )
```

```python
import functools

import jax
import jax.numpy as jnp
from jax import lax
from jax.experimental import pallas as pl
from jax.experimental.pallas import tpu as pltpu
from jax.sharding import PartitionSpec as P

BF = jnp.bfloat16
F32 = jnp.float32
GROUP = 4
ANY = pl.BlockSpec(memory_space=pl.ANY)
VMEM = pl.BlockSpec(memory_space=pltpu.VMEM)
MIB = 1 << 20


def mm(a, b):
    return jnp.dot(a, b, preferred_element_type=F32)


def mm_t(a, b):
    return lax.dot_general(a, b, (((0,), (0,)), ((), ())), preferred_element_type=F32)


def whole(ref):
    return jnp.concatenate([ref[p] for p in range(ref.shape[0])], axis=1)


def put(ref, value):
    width = ref.shape[2]
    for p in range(ref.shape[0]):
        ref[p] = value[:, p * width : (p + 1) * width].astype(ref.dtype)


def where_am_i():
    t = lax.axis_index("tm")
    return t // GROUP, lax.rem(t, GROUP), lax.axis_index("panel")


def run(copies):
    for c in copies:
        c.start()
    for c in copies:
        c.wait()


def copy_all(pairs, sems):
    return [pltpu.make_async_copy(s, d, sems.at[i]) for i, (s, d) in enumerate(pairs)]


def panel_pairs(pieces, dst, q):
    n = len(pieces)
    return [(piece, dst.at[lax.rem(q + r, n)]) for r, piece in enumerate(pieces)]


def group_pairs(own, first, second, diag, dst, lo, q):
    n = len(own)
    pairs = []
    for r in range(n):
        p = lax.rem(q + r, n)
        even = 1 - lax.rem(p, 2)
        near, far = 1 + even, 2 - even
        for mask, piece in ((0, own[r]), (near, first[r]), (far, second[r]), (3, diag[r])):
            slot = jnp.bitwise_xor(lo, mask)
            pairs.append((piece, dst.at[slot, p]))
    return pairs


def split(refs, *counts):
    out, at = [], 0
    for c in counts:
        out.append(refs[at : at + c])
        at += c
    return out


def call(kernel, ins, in_specs, outs, scratch, flops):
    size = sum(a.size * a.dtype.itemsize for a in ins) + sum(
        o.size * o.dtype.itemsize for o in outs
    )
    return pl.pallas_call(
        kernel,
        in_specs=in_specs,
        out_specs=[VMEM] * len(outs),
        out_shape=outs,
        scratch_shapes=scratch,
        compiler_params=pltpu.CompilerParams(vmem_limit_bytes=28 * MIB),
        cost_estimate=pl.CostEstimate(flops=flops, bytes_accessed=size, transcendentals=0),
    )(*ins)


def base_kernel(n, *refs):
    factor, sigma, f_parts, c_parts, (base, base_bf), (f_all, c_all, sig, sems) = split(
        refs, 1, 1, n, n, 2, 4
    )
    factor, sigma = factor[0], sigma[0]
    hi, lo, q = where_am_i()
    width = factor.shape[1]
    run(copy_all(panel_pairs(f_parts, f_all, q), sems))
    own = factor[...]
    high = own.astype(BF)
    low = (own - high.astype(F32)).astype(BF)
    for p in range(n):
        part = f_all[p]
        base[p * width : (p + 1) * width, :] = mm_t(part, high) + mm_t(part, low)

    @pl.when(lax.axis_index("tm") == lax.axis_size("tm") - 1)
    def _():
        run(copy_all(panel_pairs(c_parts, c_all, q) + [(sigma, sig)], sems))
        s = sig[...]
        s_high = s.astype(BF)
        s_low = (s - s_high.astype(F32)).astype(BF)
        c_own = c_all[q]
        mid = mm(s_high, c_own) + mm(s_low, c_own)
        mid_high = mid.astype(BF)
        mid_low = (mid - mid_high.astype(F32)).astype(BF)
        c_full = whole(c_all)
        base[...] += mm_t(c_full, mid_high) + mm_t(c_full, mid_low)

    base_bf[...] = base[...].astype(BF)


def group_comp_kernel(n, *refs):
    own, first, second, diag, outs, (sems,) = split(refs, n, n, n, n, 4, 1)
    c, c01_ref, c23_ref, agg = outs
    hi, lo, q = where_am_i()
    run(copy_all(group_pairs(own, first, second, diag, c, lo, q), sems))
    c01 = mm(whole(c.at[1]), whole(c.at[0])).astype(BF)
    put(c01_ref, c01)
    c23 = mm(whole(c.at[3]), whole(c.at[2])).astype(BF)
    c23_ref[...] = c23
    put(agg, mm(c23, c01))


def tail_comp_kernel(n, c, c01, c23, agg, *outs):
    c_t, c01_t, mine, mine_t, agg_t = outs
    hi, lo, q = where_am_i()
    agg_t[...] = whole(agg).T
    c01_t[...] = whole(c01).T
    for k in range(GROUP - 1):
        c_t[k] = whole(c.at[k]).T

    @pl.when(lo == 0)
    def _():
        mine[...] = agg[...]
        mine_t[...] = agg_t[...]

    @pl.when(lo == 1)
    def _():
        value = mm(c23[...], whole(c.at[1])).astype(BF)
        put(mine, value)
        mine_t[...] = value.T

    @pl.when(lo == 2)
    def _():
        put(mine, c23[...])
        mine_t[...] = c23[...].T

    @pl.when(lo == 3)
    def _():
        mine[...] = c[3]
        mine_t[...] = whole(c.at[3]).T


def sandwich(cov, comp, comp_t):
    return mm(comp_t, mm(cov, comp).astype(BF))


def group_cov_kernel(n, *refs):
    ins, own, first, second, diag, outs, scratch = split(refs, 5, n, n, n, n, 3, 3)
    base, c, c_t, c01, c01_t = ins
    mine, agg, agg_bf = outs
    s, s23, sems = scratch
    hi, lo, q = where_am_i()
    run(copy_all(group_pairs(own, first, second, diag, s, lo, q), sems))
    s23[...] = (
        whole(s.at[2]).astype(F32) + sandwich(whole(s.at[3]), whole(c.at[2]), c_t[2])
    ).astype(BF)
    agg[...] = s[0, q].astype(F32)

    @pl.when(lo == 0)
    def _():
        agg[...] = base[...]

    agg[...] += sandwich(whole(s.at[1]), c[0, q], c_t[0])
    agg[...] += sandwich(s23[...], c01[q], c01_t[...])
    agg_bf[...] = agg[...].astype(BF)

    @pl.when(lo == 0)
    def _():
        mine[...] = agg[...]

    @pl.when(lo == 1)
    def _():
        mine[...] = base[...] + sandwich(s23[...], c[1, q], c_t[1])

    @pl.when(lo == 2)
    def _():
        mine[...] = base[...] + sandwich(whole(s.at[3]), c[2, q], c_t[2])

    @pl.when(lo == 3)
    def _():
        mine[...] = base[...]


def is_lower(bit):
    hi, lo, q = where_am_i()
    return lax.rem(hi // (1 << bit), 2) == 0


def arrived(pieces, dst, lo, q):
    if len(pieces) == dst.shape[0]:
        return panel_pairs(pieces, dst, q)
    n = dst.shape[0]
    rows = dst.shape[1] // GROUP
    pairs = []
    for mask in range(GROUP):
        at = pl.multiple_of(jnp.bitwise_xor(lo, mask) * rows, rows)
        for r in range(n):
            pairs.append(
                (pieces[mask * n + r], dst.at[lax.rem(q + r, n), pl.ds(at, rows), :])
            )
    return pairs


def level_comp_kernel(n, m, bit, *refs):
    ins, parts, outs, (got, sems) = split(refs, 4, m, 7, 2)
    mine, mine_t, agg, agg_t = ins
    new_mine, new_mine_t, left, left_t, new_agg, new_agg_t, share = outs
    hi, lo, q = where_am_i()
    lower = is_lower(bit)
    run(copy_all(arrived(parts, got, lo, q), sems))
    rows = share.shape[0]

    @pl.when(lower)
    def _():
        c = whole(got)
        pair = mm(c, whole(agg)).astype(BF)
        put(new_agg, pair)
        new_agg_t[...] = pair.T
        value = mm(c, whole(mine)).astype(BF)
        put(new_mine, value)
        new_mine_t[...] = value.T
        left[...] = agg[...]
        left_t[...] = agg_t[...]

    @pl.when(jnp.logical_not(lower))
    def _():
        c = whole(got)
        pair = mm(whole(agg), c).astype(BF)
        put(new_agg, pair)
        new_agg_t[...] = pair.T
        new_mine[...] = mine[...]
        new_mine_t[...] = mine_t[...]
        left[...] = got[...]
        left_t[...] = c.T

    share[...] = new_agg[q, pl.ds(pl.multiple_of(lo * rows, rows), rows), :]


def last_comp_kernel(n, m, bit, *refs):
    (mine,), parts, (out,), (got, sems) = split(refs, 1, m, 1, 2)
    hi, lo, q = where_am_i()
    lower = is_lower(bit)

    @pl.when(lower)
    def _():
        run(copy_all(arrived(parts, got, lo, q), sems))
        out[0] = mm(whole(got), mine[q]).astype(BF)

    @pl.when(jnp.logical_not(lower))
    def _():
        out[0] = mine[q]


def level_cov_kernel(n, m, bit, *refs):
    ins, here, parts, outs, (right, left_cols, sems) = split(refs, 6, n, m, 4, 3)
    cov, agg, mine, mine_t, left, left_t = ins
    new_cov, new_agg, new_agg_bf, share = outs
    hi, lo, q = where_am_i()
    lower = is_lower(bit)
    rows = share.shape[0]

    @pl.when(lower)
    def _():
        run(copy_all(arrived(parts, right, lo, q), sems))
        new_agg[...] = agg[...] + sandwich(whole(right), left[q], left_t[...])
        new_cov[...] = cov[...] + sandwich(whole(right), mine[q], mine_t[...])

    @pl.when(jnp.logical_not(lower))
    def _():
        run(copy_all(arrived(parts, left_cols, lo, q), sems))
        run(copy_all(panel_pairs(here, right, q), sems))
        new_agg[...] = left_cols[q].astype(F32) + sandwich(whole(right), left[q], left_t[...])
        new_cov[...] = cov[...]

    new_agg_bf[...] = new_agg[...].astype(BF)
    share[...] = new_agg_bf[pl.ds(pl.multiple_of(lo * rows, rows), rows), :]


def last_cov_kernel(n, m, bit, *refs):
    (cov, mine, mine_t), parts, (out,), (got, sems) = split(refs, 3, m, 1, 2)
    hi, lo, q = where_am_i()
    lower = is_lower(bit)

    @pl.when(lower)
    def _():
        run(copy_all(arrived(parts, got, lo, q), sems))
        out[0] = cov[...] + sandwich(whole(got), mine[q], mine_t[...])

    @pl.when(jnp.logical_not(lower))
    def _():
        out[0] = cov[...]


def over_panels(x):
    n = lax.axis_size("panel")
    return [x] + [
        lax.ppermute(x, "panel", [((i + r) % n, i) for i in range(n)]) for r in range(1, n)
    ]


def swap(value, odd_mask, even_mask):
    steps, n = lax.axis_size("tm"), lax.axis_size("panel")
    pairs = []
    for t in range(steps):
        for q in range(n):
            mask = odd_mask if q % 2 else even_mask
            pairs.append((t * n + q, (t ^ mask) * n + q))
    return lax.ppermute(value, ("tm", "panel"), pairs)


def across(x, bit, last):
    steps = lax.axis_size("tm")
    d = GROUP << bit
    return lax.ppermute(
        x, "tm", [(t, t ^ d) for t in range(steps) if (t ^ d) < steps and (t & d or not last)]
    )


def in_group(x):
    return [x] + [swap(x, mask, mask) for mask in range(1, GROUP)]


def quarters(x):
    return [p for block in in_group(x) for p in over_panels(block)]


def after(x, *others):
    return lax.optimization_barrier((x, *others))[0]


def shards(factor_inverse, coupling, sigma_after):
    steps = lax.axis_size("tm")
    n = lax.axis_size("panel")
    nb, w = factor_inverse.shape[1:]
    levels = (steps // GROUP - 1).bit_length()
    panel_bf = jax.ShapeDtypeStruct((nb, w), BF)
    panel_f32 = jax.ShapeDtypeStruct((nb, w), F32)
    full_bf = jax.ShapeDtypeStruct((n, nb, w), BF)
    square_bf = jax.ShapeDtypeStruct((nb, nb), BF)
    group_bf = jax.ShapeDtypeStruct((GROUP, n, nb, w), BF)
    turned_bf = jax.ShapeDtypeStruct((GROUP - 1, nb, nb), BF)
    share_bf = jax.ShapeDtypeStruct((nb // GROUP, w), BF)
    full_scratch = pltpu.VMEM((n, nb, w), BF)
    one = 2 * nb * nb * w
    sems = pltpu.SemaphoreType.DMA

    comp = coupling[0].astype(BF)
    c_first = swap(comp, 1, 2)
    c_second = swap(comp, 2, 1)
    factor = after(factor_inverse[0], comp)
    f_parts = over_panels(factor.astype(BF))
    c_own = over_panels(comp)
    base, base_bf = call(
        functools.partial(base_kernel, n),
        [factor, sigma_after, *f_parts, *c_own],
        [VMEM] + [ANY] * (1 + 2 * n),
        [panel_f32, panel_bf],
        [full_scratch, full_scratch, pltpu.VMEM((nb, n * w), F32), sems((n + 1,))],
        2 * one,
    )
    c_diag = swap(after(c_first, base_bf), 2, 1)
    c_pieces = [p for v in (c_first, c_second, c_diag) for p in over_panels(v)]
    base_s = after(base_bf, c_second)
    s_first = swap(base_s, 1, 2)
    s_second = swap(base_s, 2, 1)
    c_all, c01, c23, agg_c = call(
        functools.partial(group_comp_kernel, n),
        c_own + c_pieces,
        [ANY] * (GROUP * n),
        [group_bf, full_bf, square_bf, full_bf],
        [sems((GROUP * n,))],
        3 * n * one,
    )
    agg_panel = lax.dynamic_index_in_dim(agg_c, lax.axis_index("panel"), 0, keepdims=False)
    c_got = across(agg_panel, 0, levels == 1)
    c_t, c01_t, mine, mine_t, agg_t = call(
        functools.partial(tail_comp_kernel, n),
        [c_all, c01, c23, agg_c],
        [VMEM] * 4,
        [turned_bf, square_bf, full_bf, square_bf, square_bf],
        [],
        n * one,
    )
    s_diag = swap(after(s_first, agg_panel), 2, 1)
    s_own = over_panels(after(base_bf, c_got))
    s_pieces = s_own + [p for v in (s_first, s_second, s_diag) for p in over_panels(v)]
    cov, agg, agg_bf = call(
        functools.partial(group_cov_kernel, n),
        [base, c_all, c_t, c01, c01_t, *s_pieces],
        [VMEM] * 5 + [ANY] * (GROUP * n),
        [panel_f32, panel_f32, panel_bf],
        [pltpu.VMEM((GROUP, n, nb, w), BF), pltpu.VMEM((nb, nb), BF), sems((GROUP * n,))],
        (2 * n + 6) * one,
    )
    out_cov = jax.ShapeDtypeStruct((1, nb, w), F32)
    out_comp = jax.ShapeDtypeStruct((1, nb, w), BF)
    c_parts = over_panels(c_got)
    for bit in range(levels):
        last = bit + 1 == levels
        m = len(c_parts)
        if not last:
            new_mine, new_mine_t, left, left_t, agg_c, agg_t, c_send = call(
                functools.partial(level_comp_kernel, n, m, bit),
                [after(mine, agg_bf), mine_t, agg_c, agg_t, *c_parts],
                [VMEM] * 4 + [ANY] * m,
                [full_bf, square_bf, full_bf, square_bf, full_bf, square_bf, share_bf],
                [full_scratch, sems((m,))],
                2 * n * one,
            )
            s_got = across(agg_bf if bit == 0 else s_send, bit, last)
            s_got = after(s_got, c_send)
            s_parts = quarters(s_got) if bit else over_panels(s_got)
            c_blocks = in_group(across(c_send, bit + 1, bit + 2 == levels))
            cov, agg, agg_bf, s_send = call(
                functools.partial(level_cov_kernel, n, m, bit),
                [cov, agg, mine, mine_t, left, left_t, *over_panels(agg_bf), *s_parts],
                [VMEM] * 6 + [ANY] * (n + m),
                [panel_f32, panel_f32, panel_bf, share_bf],
                [full_scratch, full_scratch, sems((max(n, m),))],
                4 * one,
            )
            c_parts = [p for b in c_blocks for p in over_panels(after(b, s_send))]
            mine, mine_t = new_mine, new_mine_t
            continue
        s_got = across(s_send if bit else agg_bf, bit, last)
        s_parts = quarters(s_got) if bit else over_panels(s_got)
        (prop,) = call(
            functools.partial(last_comp_kernel, n, m, bit),
            [mine, *c_parts],
            [VMEM] + [ANY] * m,
            [out_comp],
            [full_scratch, sems((m,))],
            one,
        )
        (cov,) = call(
            functools.partial(last_cov_kernel, n, m, bit),
            [cov, mine, mine_t, *s_parts],
            [VMEM] * 3 + [ANY] * m,
            [out_cov],
            [full_scratch, sems((m,))],
            2 * one,
        )
    return cov, prop


def solution(mesh):
    placed = (P("tm", None, "panel"), P("tm", None, "panel"), P())
    return jax.shard_map(
        shards,
        mesh=mesh,
        in_specs=placed,
        out_specs=(P("tm", None, "panel"), P("tm", None, "panel")),
        check_vma=False,
    )
```

```python
import functools

import jax
import jax.numpy as jnp
from jax import lax
from jax.experimental import pallas as pl
from jax.experimental.pallas import tpu as pltpu
from jax.sharding import PartitionSpec as P

BF = jnp.bfloat16
F32 = jnp.float32
GROUP = 4
ANY = pl.BlockSpec(memory_space=pl.ANY)
VMEM = pl.BlockSpec(memory_space=pltpu.VMEM)
MIB = 1 << 20


def mm(a, b):
    return jnp.dot(a, b, preferred_element_type=F32)


def mm_t(a, b):
    return lax.dot_general(a, b, (((0,), (0,)), ((), ())), preferred_element_type=F32)


def whole(ref):
    return jnp.concatenate([ref[p] for p in range(ref.shape[0])], axis=1)


def put(ref, value):
    width = ref.shape[2]
    for p in range(ref.shape[0]):
        ref[p] = value[:, p * width : (p + 1) * width].astype(ref.dtype)


def where_am_i():
    t = lax.axis_index("tm")
    return t // GROUP, lax.rem(t, GROUP), lax.axis_index("panel")


def run(copies):
    for c in copies:
        c.start()
    for c in copies:
        c.wait()


def copy_all(pairs, sems):
    return [pltpu.make_async_copy(s, d, sems.at[i]) for i, (s, d) in enumerate(pairs)]


def panel_pairs(pieces, dst, q):
    n = len(pieces)
    return [(piece, dst.at[lax.rem(q + r, n)]) for r, piece in enumerate(pieces)]


def group_start(blocks, dst, sems, lo, q, order):
    own, first, second, diag = blocks
    n = len(own)

    def start(slot, r, p, mask, piece):
        @pl.when(jnp.bitwise_xor(lo, mask) == slot)
        def _():
            pltpu.make_async_copy(piece, dst.at[slot, p], sems.at[slot, p]).start()

    for slot in order:
        for r in range(n):
            p = lax.rem(q + r, n)
            even = 1 - lax.rem(p, 2)
            near, far = 1 + even, 2 - even
            for mask, piece in ((0, own[r]), (near, first[r]), (far, second[r]), (3, diag[r])):
                start(slot, r, p, mask, piece)


def group_wait(own, dst, sems, *slots):
    for slot in slots:
        for p in range(len(own)):
            pltpu.make_async_copy(own[p], dst.at[slot, p], sems.at[slot, p]).wait()


def split(refs, *counts):
    out, at = [], 0
    for c in counts:
        out.append(refs[at : at + c])
        at += c
    return out


def call(kernel, ins, in_specs, outs, scratch, flops):
    size = sum(a.size * a.dtype.itemsize for a in ins) + sum(
        o.size * o.dtype.itemsize for o in outs
    )
    return pl.pallas_call(
        kernel,
        in_specs=in_specs,
        out_specs=[VMEM] * len(outs),
        out_shape=outs,
        scratch_shapes=scratch,
        compiler_params=pltpu.CompilerParams(vmem_limit_bytes=28 * MIB),
        cost_estimate=pl.CostEstimate(flops=flops, bytes_accessed=size, transcendentals=0),
    )(*ins)


def base_kernel(n, *refs):
    factor, sigma, f_parts, c_parts, (base, base_bf), (f_all, c_all, sig, sems) = split(
        refs, 1, 1, n, n, 2, 4
    )
    factor, sigma = factor[0], sigma[0]
    hi, lo, q = where_am_i()
    width = factor.shape[1]
    run(copy_all(panel_pairs(f_parts, f_all, q), sems))
    own = factor[...]
    high = own.astype(BF)
    low = (own - high.astype(F32)).astype(BF)
    for p in range(n):
        part = f_all[p]
        base[p * width : (p + 1) * width, :] = mm_t(part, high) + mm_t(part, low)

    @pl.when(lax.axis_index("tm") == lax.axis_size("tm") - 1)
    def _():
        run(copy_all(panel_pairs(c_parts, c_all, q) + [(sigma, sig)], sems))
        s = sig[...]
        s_high = s.astype(BF)
        s_low = (s - s_high.astype(F32)).astype(BF)
        c_own = c_all[q]
        mid = mm(s_high, c_own) + mm(s_low, c_own)
        mid_high = mid.astype(BF)
        mid_low = (mid - mid_high.astype(F32)).astype(BF)
        c_full = whole(c_all)
        base[...] += mm_t(c_full, mid_high) + mm_t(c_full, mid_low)

    base_bf[...] = base[...].astype(BF)


def group_comp_kernel(n, *refs):
    *blocks, outs, (sems,) = split(refs, n, n, n, n, 4, 1)
    c, c01_ref, c23_ref, agg = outs
    hi, lo, q = where_am_i()
    group_start(blocks, c, sems, lo, q, (1, 0, 3, 2))
    group_wait(blocks[0], c, sems, 1, 0)
    c01 = mm(whole(c.at[1]), whole(c.at[0])).astype(BF)
    put(c01_ref, c01)
    group_wait(blocks[0], c, sems, 3, 2)
    c23 = mm(whole(c.at[3]), whole(c.at[2])).astype(BF)
    c23_ref[...] = c23
    put(agg, mm(c23, c01))


def tail_comp_kernel(n, c, c01, c23, agg, *outs):
    c_t, c01_t, mine, mine_t, agg_t = outs
    hi, lo, q = where_am_i()
    agg_t[...] = whole(agg).T
    c01_t[...] = whole(c01).T
    for k in range(GROUP - 1):
        c_t[k] = whole(c.at[k]).T

    @pl.when(lo == 0)
    def _():
        mine[...] = agg[...]
        mine_t[...] = agg_t[...]

    @pl.when(lo == 1)
    def _():
        value = mm(c23[...], whole(c.at[1])).astype(BF)
        put(mine, value)
        mine_t[...] = value.T

    @pl.when(lo == 2)
    def _():
        put(mine, c23[...])
        mine_t[...] = c23[...].T

    @pl.when(lo == 3)
    def _():
        mine[...] = c[3]
        mine_t[...] = whole(c.at[3]).T


def sandwich(cov, comp, comp_t):
    return mm(comp_t, mm(cov, comp).astype(BF))


def group_cov_kernel(n, *refs):
    ins, *blocks, outs, scratch = split(refs, 5, n, n, n, n, 3, 3)
    base, c, c_t, c01, c01_t = ins
    mine, agg, agg_bf = outs
    s, s23, sems = scratch
    hi, lo, q = where_am_i()
    group_start(blocks, s, sems, lo, q, (3, 2, 1, 0))
    group_wait(blocks[0], s, sems, 3)
    mid = mm(whole(s.at[3]), whole(c.at[2])).astype(BF)
    group_wait(blocks[0], s, sems, 2)
    s23[...] = (whole(s.at[2]).astype(F32) + mm(c_t[2], mid)).astype(BF)
    group_wait(blocks[0], s, sems, 1, 0)
    agg[...] = s[0, q].astype(F32)

    @pl.when(lo == 0)
    def _():
        agg[...] = base[...]

    agg[...] += sandwich(whole(s.at[1]), c[0, q], c_t[0])
    agg[...] += sandwich(s23[...], c01[q], c01_t[...])
    agg_bf[...] = agg[...].astype(BF)

    @pl.when(lo == 0)
    def _():
        mine[...] = agg[...]

    @pl.when(lo == 1)
    def _():
        mine[...] = base[...] + sandwich(s23[...], c[1, q], c_t[1])

    @pl.when(lo == 2)
    def _():
        mine[...] = base[...] + sandwich(whole(s.at[3]), c[2, q], c_t[2])

    @pl.when(lo == 3)
    def _():
        mine[...] = base[...]


def is_lower(bit):
    hi, lo, q = where_am_i()
    return lax.rem(hi // (1 << bit), 2) == 0


def panel_rows(q, r, n, w):
    return pl.ds(pl.multiple_of(lax.rem(q + r, n) * w, w), w)


def quarter_rows(place, nb):
    rows = nb // GROUP
    return pl.ds(pl.multiple_of(place * rows, rows), rows)


def times(pieces, right, lo, q, n):
    nb = right.shape[0]
    w = nb // n

    def product(some):
        return sum(mm(x[...], right[panel_rows(q, r, n, w), :]) for r, x in enumerate(some))

    if len(pieces) == n:
        return [(slice(None), product(pieces))]
    return [
        (quarter_rows(jnp.bitwise_xor(lo, k), nb), product(pieces[k * n : k * n + n]))
        for k in range(GROUP)
    ]


def own_columns(pieces, lo, q, n, nb):
    if len(pieces) == n:
        return [(slice(None), pieces[0])]
    return [(quarter_rows(jnp.bitwise_xor(lo, k), nb), pieces[k * n]) for k in range(GROUP)]


def place_whole(pieces, dst, lo, q, n):
    for r in range(n):
        p = lax.rem(q + r, n)
        if len(pieces) == n:
            dst[p] = pieces[r][...]
        else:
            for k in range(GROUP):
                rows = quarter_rows(jnp.bitwise_xor(lo, k), dst.shape[1])
                dst[p, rows, :] = pieces[k * n + r][...]


def share_comp_kernel(n, m, bit, *refs):
    (agg,), parts, (share,), (got, pair) = split(refs, 1, m, 1, 2)
    hi, lo, q = where_am_i()
    lower = is_lower(bit)

    @pl.when(lower)
    def _():
        for rows, value in times(parts, agg.at[q], lo, q, n):
            pair[rows, :] = value.astype(BF)

    @pl.when(jnp.logical_not(lower))
    def _():
        place_whole(parts, got, lo, q, n)
        pair[...] = mm(whole(agg), got[q]).astype(BF)

    share[...] = pair[quarter_rows(lo, pair.shape[0]), :]


def pair_comp_kernel(n, m, bit, *refs):
    (agg,), parts, (new_agg, new_agg_t, share), (got,) = split(refs, 1, m, 3, 1)
    hi, lo, q = where_am_i()
    lower = is_lower(bit)
    place_whole(parts, got, lo, q, n)

    @pl.when(lower)
    def _():
        put(new_agg, mm(whole(got), whole(agg)))

    @pl.when(jnp.logical_not(lower))
    def _():
        put(new_agg, mm(whole(agg), whole(got)))

    new_agg_t[...] = whole(new_agg).T
    share[...] = new_agg[q, quarter_rows(lo, new_agg.shape[1]), :]


def mine_comp_kernel(n, m, bit, *refs):
    (mine, mine_t), parts, (new_mine, new_mine_t) = split(refs, 2, m, 2)
    hi, lo, q = where_am_i()
    lower = is_lower(bit)

    @pl.when(lower)
    def _():
        for p in range(n):
            for rows, value in times(parts, mine.at[p], lo, q, n):
                new_mine[p, rows, :] = value.astype(BF)
        new_mine_t[...] = whole(new_mine).T

    @pl.when(jnp.logical_not(lower))
    def _():
        new_mine[...] = mine[...]
        new_mine_t[...] = mine_t[...]


def last_comp_kernel(n, m, bit, *refs):
    (mine,), parts, (out,) = split(refs, 1, m, 1)
    hi, lo, q = where_am_i()
    lower = is_lower(bit)

    @pl.when(lower)
    def _():
        for rows, value in times(parts, mine.at[q], lo, q, n):
            out[0, rows, :] = value.astype(BF)

    @pl.when(jnp.logical_not(lower))
    def _():
        out[0] = mine[q]


def level_cov_kernel(n, m, bit, to_last, *refs):
    ins, here, c_parts, parts, outs, scratch = split(refs, 6, n, m, m, 2 if to_last else 4, 3)
    cov, agg, mine, mine_t, agg_c, agg_t = ins
    new_cov, share = outs[:2]
    mid, total, got = scratch
    hi, lo, q = where_am_i()
    lower = is_lower(bit)
    nb, w = cov.shape
    mine_rows = quarter_rows(lo, nb)

    def middle(pieces, right):
        for rows, value in times(pieces, right, lo, q, n):
            mid[rows, :] = value.astype(BF)

    @pl.when(lower)
    def _():
        middle(parts, agg_c.at[q])
        if to_last:
            share[...] = (agg[mine_rows, :] + mm(agg_t[mine_rows, :], mid[...])).astype(BF)
        else:
            total[...] = agg[...] + mm(agg_t[...], mid[...])
        middle(parts, mine.at[q])
        new_cov[...] = cov[...] + mm(mine_t[...], mid[...])

    @pl.when(jnp.logical_not(lower))
    def _():
        place_whole(c_parts, got, lo, q, n)
        middle(here, got.at[q])
        for rows, value in own_columns(parts, lo, q, n, nb):
            total[rows, :] = value[...].astype(F32)
        for p in range(n):
            total[p * w : (p + 1) * w, :] += mm_t(got[p], mid[...])
        new_cov[...] = cov[...]
        if to_last:
            share[...] = total[mine_rows, :].astype(BF)

    if not to_last:
        new_agg, new_agg_bf = outs[2:]
        new_agg[...] = total[...]
        new_agg_bf[...] = total[...].astype(BF)
        share[...] = new_agg_bf[mine_rows, :]


def last_cov_kernel(n, m, bit, *refs):
    (cov, mine, mine_t), parts, (out,), (mid,) = split(refs, 3, m, 1, 1)
    hi, lo, q = where_am_i()
    lower = is_lower(bit)

    @pl.when(lower)
    def _():
        for rows, value in times(parts, mine.at[q], lo, q, n):
            mid[rows, :] = value.astype(BF)
        out[0] = cov[...] + mm(mine_t[...], mid[...])

    @pl.when(jnp.logical_not(lower))
    def _():
        out[0] = cov[...]


def over_panels(x):
    n = lax.axis_size("panel")
    return [x] + [
        lax.ppermute(x, "panel", [((i + r) % n, i) for i in range(n)]) for r in range(1, n)
    ]


def swap(value, odd_mask, even_mask):
    steps, n = lax.axis_size("tm"), lax.axis_size("panel")
    pairs = []
    for t in range(steps):
        for q in range(n):
            mask = odd_mask if q % 2 else even_mask
            pairs.append((t * n + q, (t ^ mask) * n + q))
    return lax.ppermute(value, ("tm", "panel"), pairs)


def across(x, bit, last):
    steps = lax.axis_size("tm")
    d = GROUP << bit
    return lax.ppermute(
        x, "tm", [(t, t ^ d) for t in range(steps) if (t ^ d) < steps and (t & d or not last)]
    )


def in_group(x):
    return [x] + [swap(x, mask, mask) for mask in range(1, GROUP)]


def quarters(x):
    return [p for block in in_group(x) for p in over_panels(block)]


def after(x, *others):
    return lax.optimization_barrier((x, *others))[0]


def shards(factor_inverse, coupling, sigma_after):
    steps = lax.axis_size("tm")
    n = lax.axis_size("panel")
    nb, w = factor_inverse.shape[1:]
    levels = (steps // GROUP - 1).bit_length()
    panel_bf = jax.ShapeDtypeStruct((nb, w), BF)
    panel_f32 = jax.ShapeDtypeStruct((nb, w), F32)
    full_bf = jax.ShapeDtypeStruct((n, nb, w), BF)
    square_bf = jax.ShapeDtypeStruct((nb, nb), BF)
    group_bf = jax.ShapeDtypeStruct((GROUP, n, nb, w), BF)
    turned_bf = jax.ShapeDtypeStruct((GROUP - 1, nb, nb), BF)
    share_bf = jax.ShapeDtypeStruct((nb // GROUP, w), BF)
    full_scratch = pltpu.VMEM((n, nb, w), BF)
    one = 2 * nb * nb * w
    sems = pltpu.SemaphoreType.DMA

    comp = coupling[0].astype(BF)
    c_first = swap(comp, 1, 2)
    c_second = swap(comp, 2, 1)
    factor = after(factor_inverse[0], comp)
    f_parts = over_panels(factor.astype(BF))
    c_own = over_panels(comp)
    base, base_bf = call(
        functools.partial(base_kernel, n),
        [factor, sigma_after, *f_parts, *c_own],
        [VMEM] + [ANY] * (1 + 2 * n),
        [panel_f32, panel_bf],
        [full_scratch, full_scratch, pltpu.VMEM((nb, n * w), F32), sems((n + 1,))],
        2 * one,
    )
    c_diag = swap(after(c_first, base_bf), 2, 1)
    s_first = swap(base_bf, 1, 2)
    c_diag = after(c_diag, s_first)
    c_pieces = [p for v in (c_first, c_second, c_diag) for p in over_panels(v)]
    s_second = swap(after(base_bf, c_second), 2, 1)
    c_all, c01, c23, agg_c = call(
        functools.partial(group_comp_kernel, n),
        c_own + c_pieces,
        [ANY] * (GROUP * n),
        [group_bf, full_bf, square_bf, full_bf],
        [sems((GROUP, n))],
        3 * n * one,
    )
    agg_panel = lax.dynamic_index_in_dim(agg_c, lax.axis_index("panel"), 0, keepdims=False)
    c_got = across(agg_panel, 0, levels == 1)
    c_t, c01_t, mine, mine_t, agg_t = call(
        functools.partial(tail_comp_kernel, n),
        [c_all, c01, c23, agg_c],
        [VMEM] * 4,
        [turned_bf, square_bf, full_bf, square_bf, square_bf],
        [],
        n * one,
    )
    s_diag = swap(s_first, 2, 1)
    s_own = over_panels(after(base_bf, c_got))
    s_pieces = s_own + [p for v in (s_first, s_second, s_diag) for p in over_panels(v)]
    cov, agg, agg_bf = call(
        functools.partial(group_cov_kernel, n),
        [base, c_all, c_t, c01, c01_t, *s_pieces],
        [VMEM] * 5 + [ANY] * (GROUP * n),
        [panel_f32, panel_f32, panel_bf],
        [pltpu.VMEM((GROUP, n, nb, w), BF), pltpu.VMEM((nb, nb), BF), sems((GROUP, n))],
        (2 * n + 6) * one,
    )
    out_cov = jax.ShapeDtypeStruct((1, nb, w), F32)
    out_comp = jax.ShapeDtypeStruct((1, nb, w), BF)
    panel_scratch = pltpu.VMEM((nb, w), BF)
    sum_scratch = pltpu.VMEM((nb, w), F32)
    c_parts = over_panels(c_got)
    s_send = agg_bf
    for bit in range(levels):
        last = bit + 1 == levels
        to_last = bit + 2 == levels
        m = len(c_parts)
        s_got = across(s_send, bit, last)
        if last:
            (prop,) = call(
                functools.partial(last_comp_kernel, n, m, bit),
                [mine, *c_parts],
                [VMEM] * (1 + m),
                [out_comp],
                [],
                one,
            )
            s_got = after(s_got, prop)
            s_parts = quarters(s_got) if bit else over_panels(s_got)
            (cov,) = call(
                functools.partial(last_cov_kernel, n, m, bit),
                [cov, mine, mine_t, *s_parts],
                [VMEM] * (3 + m),
                [out_cov],
                [panel_scratch],
                2 * one,
            )
            break
        agg_in = after(agg_c, agg_bf)
        if to_last:
            (c_send,) = call(
                functools.partial(share_comp_kernel, n, m, bit),
                [agg_in, *c_parts],
                [VMEM] * (1 + m),
                [share_bf],
                [full_scratch, panel_scratch],
                one,
            )
        else:
            new_agg_c, new_agg_t, c_send = call(
                functools.partial(pair_comp_kernel, n, m, bit),
                [agg_in, *c_parts],
                [VMEM] * (1 + m),
                [full_bf, square_bf, share_bf],
                [full_scratch],
                n * one,
            )
        c_far = across(c_send, bit + 1, to_last)
        new_mine, new_mine_t = call(
            functools.partial(mine_comp_kernel, n, m, bit),
            [after(mine, c_send), mine_t, *c_parts],
            [VMEM] * (2 + m),
            [full_bf, square_bf],
            [],
            n * one,
        )
        s_got = after(s_got, c_far, new_mine)
        s_parts = quarters(s_got) if bit else over_panels(s_got)
        c_blocks = in_group(c_far)
        outs = call(
            functools.partial(level_cov_kernel, n, m, bit, to_last),
            [cov, agg, mine, mine_t, agg_c, agg_t, *over_panels(agg_bf), *c_parts, *s_parts],
            [VMEM] * (6 + n + 2 * m),
            [panel_f32, share_bf] + ([] if to_last else [panel_f32, panel_bf]),
            [panel_scratch, sum_scratch, full_scratch],
            4 * one,
        )
        cov, s_send = outs[:2]
        if not to_last:
            agg, agg_bf = outs[2:]
            agg_c, agg_t = new_agg_c, new_agg_t
        c_parts = [p for b in c_blocks for p in over_panels(after(b, s_send))]
        mine, mine_t = new_mine, new_mine_t
    return cov, prop


def solution(mesh):
    placed = (P("tm", None, "panel"), P("tm", None, "panel"), P())
    return jax.shard_map(
        shards,
        mesh=mesh,
        in_specs=placed,
        out_specs=(P("tm", None, "panel"), P("tm", None, "panel")),
        check_vma=False,
    )
```

```python
import functools

import jax
import jax.numpy as jnp
from jax import lax
from jax.experimental import pallas as pl
from jax.experimental.pallas import tpu as pltpu
from jax.sharding import PartitionSpec as P

BF = jnp.bfloat16
F32 = jnp.float32
GROUP = 4
ANY = pl.BlockSpec(memory_space=pl.ANY)
VMEM = pl.BlockSpec(memory_space=pltpu.VMEM)
MIB = 1 << 20


def mm(a, b):
    return jnp.dot(a, b, preferred_element_type=F32)


def mm_t(a, b):
    return lax.dot_general(a, b, (((0,), (0,)), ((), ())), preferred_element_type=F32)


def whole(ref):
    return jnp.concatenate([ref[p] for p in range(ref.shape[0])], axis=1)


def put(ref, value):
    width = ref.shape[2]
    for p in range(ref.shape[0]):
        ref[p] = value[:, p * width : (p + 1) * width].astype(ref.dtype)


def where_am_i():
    t = lax.axis_index("tm")
    return t // GROUP, lax.rem(t, GROUP), lax.axis_index("panel")


def run(copies):
    for c in copies:
        c.start()
    for c in copies:
        c.wait()


def copy_all(pairs, sems):
    return [pltpu.make_async_copy(s, d, sems.at[i]) for i, (s, d) in enumerate(pairs)]


def panel_pairs(pieces, dst, q):
    n = len(pieces)
    return [(piece, dst.at[lax.rem(q + r, n)]) for r, piece in enumerate(pieces)]


def group_start(blocks, dst, sems, lo, q, order):
    own, first, second, diag = blocks
    n = len(own)

    def start(slot, r, p, mask, piece):
        @pl.when(jnp.bitwise_xor(lo, mask) == slot)
        def _():
            pltpu.make_async_copy(piece, dst.at[slot, p], sems.at[slot, p]).start()

    for slot in order:
        for r in range(n):
            p = lax.rem(q + r, n)
            even = 1 - lax.rem(p, 2)
            near, far = 1 + even, 2 - even
            for mask, piece in ((0, own[r]), (near, first[r]), (far, second[r]), (3, diag[r])):
                start(slot, r, p, mask, piece)


def group_wait(own, dst, sems, *slots):
    for slot in slots:
        for p in range(len(own)):
            pltpu.make_async_copy(own[p], dst.at[slot, p], sems.at[slot, p]).wait()


def split(refs, *counts):
    out, at = [], 0
    for c in counts:
        out.append(refs[at : at + c])
        at += c
    return out


def call(kernel, ins, in_specs, outs, scratch, flops):
    size = sum(a.size * a.dtype.itemsize for a in ins) + sum(
        o.size * o.dtype.itemsize for o in outs
    )
    return pl.pallas_call(
        kernel,
        in_specs=in_specs,
        out_specs=[VMEM] * len(outs),
        out_shape=outs,
        scratch_shapes=scratch,
        compiler_params=pltpu.CompilerParams(vmem_limit_bytes=28 * MIB),
        cost_estimate=pl.CostEstimate(flops=flops, bytes_accessed=size, transcendentals=0),
    )(*ins)


def base_kernel(n, *refs):
    factor, sigma, f_parts, c_parts, (base, base_bf), (f_all, c_all, sig, sems) = split(
        refs, 1, 1, n, n, 2, 4
    )
    factor, sigma = factor[0], sigma[0]
    hi, lo, q = where_am_i()
    width = factor.shape[1]
    run(copy_all(panel_pairs(f_parts, f_all, q), sems))
    own = factor[...]
    high = own.astype(BF)
    low = (own - high.astype(F32)).astype(BF)
    for p in range(n):
        part = f_all[p]
        base[p * width : (p + 1) * width, :] = mm_t(part, high) + mm_t(part, low)

    @pl.when(lax.axis_index("tm") == lax.axis_size("tm") - 1)
    def _():
        run(copy_all(panel_pairs(c_parts, c_all, q) + [(sigma, sig)], sems))
        s = sig[...]
        s_high = s.astype(BF)
        s_low = (s - s_high.astype(F32)).astype(BF)
        c_own = c_all[q]
        mid = mm(s_high, c_own) + mm(s_low, c_own)
        mid_high = mid.astype(BF)
        mid_low = (mid - mid_high.astype(F32)).astype(BF)
        c_full = whole(c_all)
        base[...] += mm_t(c_full, mid_high) + mm_t(c_full, mid_low)

    base_bf[...] = base[...].astype(BF)


def group_comp_kernel(n, *refs):
    *blocks, outs, (sems,) = split(refs, n, n, n, n, 4, 1)
    c, c01_ref, c23_ref, agg = outs
    hi, lo, q = where_am_i()
    group_start(blocks, c, sems, lo, q, (1, 0, 3, 2))
    group_wait(blocks[0], c, sems, 1, 0)
    c01 = mm(whole(c.at[1]), whole(c.at[0])).astype(BF)
    put(c01_ref, c01)
    group_wait(blocks[0], c, sems, 3, 2)
    c23 = mm(whole(c.at[3]), whole(c.at[2])).astype(BF)
    c23_ref[...] = c23
    put(agg, mm(c23, c01))


def tail_comp_kernel(n, c, c01, c23, agg, *outs):
    c_t, c01_t, mine, mine_t, agg_t = outs
    hi, lo, q = where_am_i()
    agg_t[...] = whole(agg).T
    c01_t[...] = whole(c01).T
    for k in range(GROUP - 1):
        c_t[k] = whole(c.at[k]).T

    @pl.when(lo == 0)
    def _():
        mine[...] = agg[...]
        mine_t[...] = agg_t[...]

    @pl.when(lo == 1)
    def _():
        value = mm(c23[...], whole(c.at[1])).astype(BF)
        put(mine, value)
        mine_t[...] = value.T

    @pl.when(lo == 2)
    def _():
        put(mine, c23[...])
        mine_t[...] = c23[...].T

    @pl.when(lo == 3)
    def _():
        mine[...] = c[3]
        mine_t[...] = whole(c.at[3]).T


def sandwich(cov, comp, comp_t):
    return mm(comp_t, mm(cov, comp).astype(BF))


def group_cov_kernel(n, *refs):
    ins, *blocks, outs, scratch = split(refs, 5, n, n, n, n, 3, 3)
    base, c, c_t, c01, c01_t = ins
    mine, agg, agg_bf = outs
    s, s23, sems = scratch
    hi, lo, q = where_am_i()
    group_start(blocks, s, sems, lo, q, (3, 2, 1, 0))
    group_wait(blocks[0], s, sems, 3)
    mid = mm(whole(s.at[3]), whole(c.at[2])).astype(BF)
    group_wait(blocks[0], s, sems, 2)
    s23[...] = (whole(s.at[2]).astype(F32) + mm(c_t[2], mid)).astype(BF)
    group_wait(blocks[0], s, sems, 1, 0)
    agg[...] = s[0, q].astype(F32)

    @pl.when(lo == 0)
    def _():
        agg[...] = base[...]

    agg[...] += sandwich(whole(s.at[1]), c[0, q], c_t[0])
    agg[...] += sandwich(s23[...], c01[q], c01_t[...])
    agg_bf[...] = agg[...].astype(BF)

    @pl.when(lo == 0)
    def _():
        mine[...] = agg[...]

    @pl.when(lo == 1)
    def _():
        mine[...] = base[...] + sandwich(s23[...], c[1, q], c_t[1])

    @pl.when(lo == 2)
    def _():
        mine[...] = base[...] + sandwich(whole(s.at[3]), c[2, q], c_t[2])

    @pl.when(lo == 3)
    def _():
        mine[...] = base[...]


def is_lower(bit):
    hi, lo, q = where_am_i()
    return lax.rem(hi // (1 << bit), 2) == 0


def panel_rows(q, r, n, w):
    return pl.ds(pl.multiple_of(lax.rem(q + r, n) * w, w), w)


def quarter_rows(place, nb):
    rows = nb // GROUP
    return pl.ds(pl.multiple_of(place * rows, rows), rows)


def times(pieces, right, lo, q, n):
    nb = right.shape[0]
    w = nb // n

    def product(some):
        return sum(mm(x[...], right[panel_rows(q, r, n, w), :]) for r, x in enumerate(some))

    if len(pieces) == n:
        return [(slice(None), product(pieces))]
    return [
        (quarter_rows(jnp.bitwise_xor(lo, k), nb), product(pieces[k * n : k * n + n]))
        for k in range(GROUP)
    ]


def own_columns(pieces, lo, q, n, nb):
    if len(pieces) == n:
        return [(slice(None), pieces[0])]
    return [(quarter_rows(jnp.bitwise_xor(lo, k), nb), pieces[k * n]) for k in range(GROUP)]


def place_whole(pieces, dst, lo, q, n):
    for r in range(n):
        p = lax.rem(q + r, n)
        if len(pieces) == n:
            dst[p] = pieces[r][...]
        else:
            for k in range(GROUP):
                rows = quarter_rows(jnp.bitwise_xor(lo, k), dst.shape[1])
                dst[p, rows, :] = pieces[k * n + r][...]


def share_comp_kernel(n, m, bit, *refs):
    (agg,), parts, (share,), (got, pair) = split(refs, 1, m, 1, 2)
    hi, lo, q = where_am_i()
    lower = is_lower(bit)

    @pl.when(lower)
    def _():
        for rows, value in times(parts, agg.at[q], lo, q, n):
            pair[rows, :] = value.astype(BF)

    @pl.when(jnp.logical_not(lower))
    def _():
        place_whole(parts, got, lo, q, n)
        pair[...] = mm(whole(agg), got[q]).astype(BF)

    share[...] = pair[quarter_rows(lo, pair.shape[0]), :]


def pair_comp_kernel(n, m, bit, *refs):
    (agg,), parts, (new_agg, new_agg_t, share), (got,) = split(refs, 1, m, 3, 1)
    hi, lo, q = where_am_i()
    lower = is_lower(bit)
    place_whole(parts, got, lo, q, n)

    @pl.when(lower)
    def _():
        put(new_agg, mm(whole(got), whole(agg)))

    @pl.when(jnp.logical_not(lower))
    def _():
        put(new_agg, mm(whole(agg), whole(got)))

    new_agg_t[...] = whole(new_agg).T
    share[...] = new_agg[q, quarter_rows(lo, new_agg.shape[1]), :]


def mine_comp_kernel(n, m, bit, *refs):
    (mine, mine_t), parts, (new_mine, new_mine_t) = split(refs, 2, m, 2)
    hi, lo, q = where_am_i()
    lower = is_lower(bit)

    @pl.when(lower)
    def _():
        for p in range(n):
            for rows, value in times(parts, mine.at[p], lo, q, n):
                new_mine[p, rows, :] = value.astype(BF)
        new_mine_t[...] = whole(new_mine).T

    @pl.when(jnp.logical_not(lower))
    def _():
        new_mine[...] = mine[...]
        new_mine_t[...] = mine_t[...]


def last_comp_kernel(n, m, bit, *refs):
    (mine,), parts, (out,) = split(refs, 1, m, 1)
    hi, lo, q = where_am_i()
    lower = is_lower(bit)

    @pl.when(lower)
    def _():
        for rows, value in times(parts, mine.at[q], lo, q, n):
            out[0, rows, :] = value.astype(BF)

    @pl.when(jnp.logical_not(lower))
    def _():
        out[0] = mine[q]


def level_cov_kernel(n, m, bit, to_last, *refs):
    ins, here, c_parts, parts, outs, scratch = split(refs, 6, n, m, m, 2 if to_last else 4, 3)
    cov, agg, mine, mine_t, agg_c, agg_t = ins
    new_cov, share = outs[:2]
    mid, total, got = scratch
    hi, lo, q = where_am_i()
    lower = is_lower(bit)
    nb, w = cov.shape
    mine_rows = quarter_rows(lo, nb)

    def middle(pieces, right):
        for rows, value in times(pieces, right, lo, q, n):
            mid[rows, :] = value.astype(BF)

    @pl.when(lower)
    def _():
        middle(parts, agg_c.at[q])
        if to_last:
            share[...] = (agg[mine_rows, :] + mm(agg_t[mine_rows, :], mid[...])).astype(BF)
        else:
            total[...] = agg[...] + mm(agg_t[...], mid[...])
        middle(parts, mine.at[q])
        new_cov[...] = cov[...] + mm(mine_t[...], mid[...])

    @pl.when(jnp.logical_not(lower))
    def _():
        place_whole(c_parts, got, lo, q, n)
        middle(here, got.at[q])
        for rows, value in own_columns(parts, lo, q, n, nb):
            total[rows, :] = value[...].astype(F32)
        for p in range(n):
            total[p * w : (p + 1) * w, :] += mm_t(got[p], mid[...])
        new_cov[...] = cov[...]
        if to_last:
            share[...] = total[mine_rows, :].astype(BF)

    if not to_last:
        new_agg, new_agg_bf = outs[2:]
        new_agg[...] = total[...]
        new_agg_bf[...] = total[...].astype(BF)
        share[...] = new_agg_bf[mine_rows, :]


def last_cov_kernel(n, m, bit, *refs):
    (cov, mine, mine_t), parts, (out,), (mid,) = split(refs, 3, m, 1, 1)
    hi, lo, q = where_am_i()
    lower = is_lower(bit)

    @pl.when(lower)
    def _():
        for rows, value in times(parts, mine.at[q], lo, q, n):
            mid[rows, :] = value.astype(BF)
        out[0] = cov[...] + mm(mine_t[...], mid[...])

    @pl.when(jnp.logical_not(lower))
    def _():
        out[0] = cov[...]


def over_panels(x):
    n = lax.axis_size("panel")
    return [x] + [
        lax.ppermute(x, "panel", [((i + r) % n, i) for i in range(n)]) for r in range(1, n)
    ]


def swap(value, odd_mask, even_mask):
    steps, n = lax.axis_size("tm"), lax.axis_size("panel")
    pairs = []
    for t in range(steps):
        for q in range(n):
            mask = odd_mask if q % 2 else even_mask
            pairs.append((t * n + q, (t ^ mask) * n + q))
    return lax.ppermute(value, ("tm", "panel"), pairs)


def across(x, bit, last):
    steps = lax.axis_size("tm")
    d = GROUP << bit
    return lax.ppermute(
        x, "tm", [(t, t ^ d) for t in range(steps) if (t ^ d) < steps and (t & d or not last)]
    )


def in_group(x):
    return [x] + [swap(x, mask, mask) for mask in range(1, GROUP)]


def quarters(x):
    return [p for block in in_group(x) for p in over_panels(block)]


def after(x, *others):
    return lax.optimization_barrier((x, *others))[0]


def shards(factor_inverse, coupling, sigma_after):
    steps = lax.axis_size("tm")
    n = lax.axis_size("panel")
    nb, w = factor_inverse.shape[1:]
    levels = (steps // GROUP - 1).bit_length()
    panel_bf = jax.ShapeDtypeStruct((nb, w), BF)
    panel_f32 = jax.ShapeDtypeStruct((nb, w), F32)
    full_bf = jax.ShapeDtypeStruct((n, nb, w), BF)
    square_bf = jax.ShapeDtypeStruct((nb, nb), BF)
    group_bf = jax.ShapeDtypeStruct((GROUP, n, nb, w), BF)
    turned_bf = jax.ShapeDtypeStruct((GROUP - 1, nb, nb), BF)
    share_bf = jax.ShapeDtypeStruct((nb // GROUP, w), BF)
    full_scratch = pltpu.VMEM((n, nb, w), BF)
    one = 2 * nb * nb * w
    sems = pltpu.SemaphoreType.DMA

    comp = coupling[0].astype(BF)
    c_first = swap(comp, 1, 2)
    c_second = swap(comp, 2, 1)
    factor = after(factor_inverse[0], comp)
    f_parts = over_panels(factor.astype(BF))
    c_own = over_panels(comp)
    base, base_bf = call(
        functools.partial(base_kernel, n),
        [factor, sigma_after, *f_parts, *c_own],
        [VMEM] + [ANY] * (1 + 2 * n),
        [panel_f32, panel_bf],
        [full_scratch, full_scratch, pltpu.VMEM((nb, n * w), F32), sems((n + 1,))],
        2 * one,
    )
    c_diag = swap(c_first, 2, 1)
    s_first = swap(base_bf, 1, 2)
    c_pieces = [p for v in (c_first, c_second, c_diag) for p in over_panels(v)]
    s_second = swap(base_bf, 2, 1)
    c_all, c01, c23, agg_c = call(
        functools.partial(group_comp_kernel, n),
        c_own + c_pieces,
        [ANY] * (GROUP * n),
        [group_bf, full_bf, square_bf, full_bf],
        [sems((GROUP, n))],
        3 * n * one,
    )
    agg_panel = lax.dynamic_index_in_dim(agg_c, lax.axis_index("panel"), 0, keepdims=False)
    c_got = across(agg_panel, 0, levels == 1)
    c_t, c01_t, mine, mine_t, agg_t = call(
        functools.partial(tail_comp_kernel, n),
        [c_all, c01, c23, agg_c],
        [VMEM] * 4,
        [turned_bf, square_bf, full_bf, square_bf, square_bf],
        [],
        n * one,
    )
    s_diag = swap(s_first, 2, 1)
    s_own = over_panels(base_bf)
    s_pieces = s_own + [p for v in (s_first, s_second, s_diag) for p in over_panels(v)]
    cov, agg, agg_bf = call(
        functools.partial(group_cov_kernel, n),
        [base, c_all, c_t, c01, c01_t, *s_pieces],
        [VMEM] * 5 + [ANY] * (GROUP * n),
        [panel_f32, panel_f32, panel_bf],
        [pltpu.VMEM((GROUP, n, nb, w), BF), pltpu.VMEM((nb, nb), BF), sems((GROUP, n))],
        (2 * n + 6) * one,
    )
    out_cov = jax.ShapeDtypeStruct((1, nb, w), F32)
    out_comp = jax.ShapeDtypeStruct((1, nb, w), BF)
    panel_scratch = pltpu.VMEM((nb, w), BF)
    sum_scratch = pltpu.VMEM((nb, w), F32)
    c_parts = over_panels(c_got)
    s_send = agg_bf
    for bit in range(levels):
        last = bit + 1 == levels
        to_last = bit + 2 == levels
        m = len(c_parts)
        s_got = s_far if bit else across(after(s_send, c_got), bit, last)
        if last:
            (prop,) = call(
                functools.partial(last_comp_kernel, n, m, bit),
                [mine, *c_parts],
                [VMEM] * (1 + m),
                [out_comp],
                [],
                one,
            )
            s_parts = quarters(s_got) if bit else over_panels(s_got)
            (cov,) = call(
                functools.partial(last_cov_kernel, n, m, bit),
                [cov, mine, mine_t, *s_parts],
                [VMEM] * (3 + m),
                [out_cov],
                [panel_scratch],
                2 * one,
            )
            break
        agg_in = after(agg_c, agg_bf)
        if to_last:
            (c_send,) = call(
                functools.partial(share_comp_kernel, n, m, bit),
                [agg_in, *c_parts],
                [VMEM] * (1 + m),
                [share_bf],
                [full_scratch, panel_scratch],
                one,
            )
        else:
            new_agg_c, new_agg_t, c_send = call(
                functools.partial(pair_comp_kernel, n, m, bit),
                [agg_in, *c_parts],
                [VMEM] * (1 + m),
                [full_bf, square_bf, share_bf],
                [full_scratch],
                n * one,
            )
        c_far = across(c_send, bit + 1, to_last)
        new_mine, new_mine_t = call(
            functools.partial(mine_comp_kernel, n, m, bit),
            [after(mine, c_send), mine_t, *c_parts],
            [VMEM] * (2 + m),
            [full_bf, square_bf],
            [],
            n * one,
        )
        s_got = after(s_got, c_far, new_mine)
        s_parts = quarters(s_got) if bit else over_panels(s_got)
        outs = call(
            functools.partial(level_cov_kernel, n, m, bit, to_last),
            [cov, agg, mine, mine_t, agg_c, agg_t, *over_panels(agg_bf), *c_parts, *s_parts],
            [VMEM] * (6 + n + 2 * m),
            [panel_f32, share_bf] + ([] if to_last else [panel_f32, panel_bf]),
            [panel_scratch, sum_scratch, full_scratch],
            4 * one,
        )
        cov, s_send = outs[:2]
        if not to_last:
            agg, agg_bf = outs[2:]
            agg_c, agg_t = new_agg_c, new_agg_t
        s_far = across(s_send, bit + 1, to_last)
        c_blocks = in_group(after(c_far, s_send))
        c_parts = [p for b in c_blocks for p in over_panels(after(b, s_far))]
        mine, mine_t = new_mine, new_mine_t
    return cov, prop


def solution(mesh):
    placed = (P("tm", None, "panel"), P("tm", None, "panel"), P())
    return jax.shard_map(
        shards,
        mesh=mesh,
        in_specs=placed,
        out_specs=(P("tm", None, "panel"), P("tm", None, "panel")),
        check_vma=False,
    )
```

```python
import functools

import jax
import jax.numpy as jnp
from jax import lax
from jax.experimental import pallas as pl
from jax.experimental.pallas import tpu as pltpu
from jax.sharding import PartitionSpec as P

BF = jnp.bfloat16
F32 = jnp.float32
GROUP = 4
BLOCK = 128
ANY = pl.BlockSpec(memory_space=pl.ANY)
VMEM = pl.BlockSpec(memory_space=pltpu.VMEM)
MIB = 1 << 20


def mm(a, b):
    return jnp.dot(a, b, preferred_element_type=F32)


def mm_t(a, b):
    return lax.dot_general(a, b, (((0,), (0,)), ((), ())), preferred_element_type=F32)


def whole(ref):
    return jnp.concatenate([ref[p] for p in range(ref.shape[0])], axis=1)


def put(ref, value):
    width = ref.shape[2]
    for p in range(ref.shape[0]):
        ref[p] = value[:, p * width : (p + 1) * width].astype(ref.dtype)


def where_am_i():
    t = lax.axis_index("tm")
    return t // GROUP, lax.rem(t, GROUP), lax.axis_index("panel")


def run(copies):
    for c in copies:
        c.start()
    for c in copies:
        c.wait()


def copy_all(pairs, sems):
    return [pltpu.make_async_copy(s, d, sems.at[i]) for i, (s, d) in enumerate(pairs)]


def panel_pairs(pieces, dst, q):
    n = len(pieces)
    return [(piece, dst.at[lax.rem(q + r, n)]) for r, piece in enumerate(pieces)]


def group_start(blocks, dst, sems, lo, q, order):
    own, first, second, diag = blocks
    n = len(own)

    def start(slot, r, p, mask, piece):
        @pl.when(jnp.bitwise_xor(lo, mask) == slot)
        def _():
            pltpu.make_async_copy(piece, dst.at[slot, p], sems.at[slot, p]).start()

    for slot in order:
        for r in range(n):
            p = lax.rem(q + r, n)
            even = 1 - lax.rem(p, 2)
            near, far = 1 + even, 2 - even
            for mask, piece in ((0, own[r]), (near, first[r]), (far, second[r]), (3, diag[r])):
                start(slot, r, p, mask, piece)


def group_wait(own, dst, sems, *slots):
    for slot in slots:
        for p in range(len(own)):
            pltpu.make_async_copy(own[p], dst.at[slot, p], sems.at[slot, p]).wait()


def packs(n, w):
    return n == 2 and w % BLOCK == 0


def packed_shape(n, nb, w):
    if not packs(n, w):
        return nb, w
    k = w // BLOCK
    return (k * (k + 1) // 2 + (k * k + 1) // 2) * BLOCK, BLOCK


def triangle(k):
    return [(i, j) for i in range(k) for j in range(i + 1)]


def halves(k):
    every = [(a, b) for a in range(k) for b in range(k)]
    half = (k * k + 1) // 2
    return every[:half], every[k * k - half :]


def pack(panel, out, q, n):
    nb, w = panel.shape
    if not packs(n, w):
        out[...] = panel[...].astype(BF)
        return
    k = w // BLOCK
    at = 0
    for i, j in triangle(k):
        rows = pl.ds(pl.multiple_of(q * w + i * BLOCK, BLOCK), BLOCK)
        out[at : at + BLOCK, :] = panel[rows, j * BLOCK : (j + 1) * BLOCK].astype(BF)
        at += BLOCK
    for side, blocks in enumerate(halves(k)):

        @pl.when(q == side)
        def _():
            to = at
            for a, b in blocks:
                i, j = (b, a) if side else (w // BLOCK + a, b)
                value = panel[i * BLOCK : (i + 1) * BLOCK, j * BLOCK : (j + 1) * BLOCK]
                out[to : to + BLOCK, :] = value.astype(BF)
                to += BLOCK


def unpack(src, dst, n):
    nb = dst.shape[0]
    w = nb // n
    if not packs(n, w):
        dst[...] = whole(src)
        return
    k = w // BLOCK

    def both(block, i, j):
        dst[i * BLOCK : (i + 1) * BLOCK, j * BLOCK : (j + 1) * BLOCK] = block
        if i != j:
            dst[j * BLOCK : (j + 1) * BLOCK, i * BLOCK : (i + 1) * BLOCK] = block.T

    seen = set()
    for p in range(n):
        at = 0
        for i, j in triangle(k):
            both(src[p, at : at + BLOCK, :], p * k + i, p * k + j)
            at += BLOCK
        for a, b in halves(k)[p]:
            if (a, b) not in seen:
                i, j = (b, k + a) if p else (k + a, b)
                both(src[p, at : at + BLOCK, :], i, j)
            seen.add((a, b))
            at += BLOCK


def panel_of(matrix, q, n, use):
    w = matrix.shape[1] // n
    for p in range(n):

        @pl.when(q == p)
        def _():
            use(matrix[:, p * w : (p + 1) * w])


def split(refs, *counts):
    out, at = [], 0
    for c in counts:
        out.append(refs[at : at + c])
        at += c
    return out


def call(kernel, ins, in_specs, outs, scratch, flops):
    size = sum(a.size * a.dtype.itemsize for a in ins) + sum(
        o.size * o.dtype.itemsize for o in outs
    )
    return pl.pallas_call(
        kernel,
        in_specs=in_specs,
        out_specs=[VMEM] * len(outs),
        out_shape=outs,
        scratch_shapes=scratch,
        compiler_params=pltpu.CompilerParams(vmem_limit_bytes=28 * MIB),
        cost_estimate=pl.CostEstimate(flops=flops, bytes_accessed=size, transcendentals=0),
    )(*ins)


def base_kernel(n, *refs):
    factor, sigma, f_parts, c_parts, (base, base_bf), (f_all, c_all, sig, sems) = split(
        refs, 1, 1, n, n, 2, 4
    )
    factor, sigma = factor[0], sigma[0]
    hi, lo, q = where_am_i()
    width = factor.shape[1]
    run(copy_all(panel_pairs(f_parts, f_all, q), sems))
    own = factor[...]
    high = own.astype(BF)
    low = (own - high.astype(F32)).astype(BF)
    for p in range(n):
        part = f_all[p]
        base[p * width : (p + 1) * width, :] = mm_t(part, high) + mm_t(part, low)

    @pl.when(lax.axis_index("tm") == lax.axis_size("tm") - 1)
    def _():
        run(copy_all(panel_pairs(c_parts, c_all, q) + [(sigma, sig)], sems))
        s = sig[...]
        s_high = s.astype(BF)
        s_low = (s - s_high.astype(F32)).astype(BF)
        c_own = c_all[q]
        mid = mm(s_high, c_own) + mm(s_low, c_own)
        mid_high = mid.astype(BF)
        mid_low = (mid - mid_high.astype(F32)).astype(BF)
        c_full = whole(c_all)
        base[...] += mm_t(c_full, mid_high) + mm_t(c_full, mid_low)

    pack(base, base_bf, q, n)


def group_comp_kernel(n, *refs):
    *blocks, outs, (sems,) = split(refs, n, n, n, n, 4, 1)
    c, c01_ref, c23_ref, agg = outs
    hi, lo, q = where_am_i()
    group_start(blocks, c, sems, lo, q, (1, 0, 3, 2))
    group_wait(blocks[0], c, sems, 1, 0)
    c01 = mm(whole(c.at[1]), whole(c.at[0])).astype(BF)
    put(c01_ref, c01)
    group_wait(blocks[0], c, sems, 3, 2)
    c23 = mm(whole(c.at[3]), whole(c.at[2])).astype(BF)
    c23_ref[...] = c23
    put(agg, mm(c23, c01))


def tail_comp_kernel(n, c, c01, c23, agg, *outs):
    c_t, c01_t, mine, mine_t, agg_t = outs
    hi, lo, q = where_am_i()
    agg_t[...] = whole(agg).T
    c01_t[...] = whole(c01).T
    for k in range(GROUP - 1):
        c_t[k] = whole(c.at[k]).T

    @pl.when(lo == 0)
    def _():
        mine[...] = agg[...]
        mine_t[...] = agg_t[...]

    @pl.when(lo == 1)
    def _():
        value = mm(c23[...], whole(c.at[1])).astype(BF)
        put(mine, value)
        mine_t[...] = value.T

    @pl.when(lo == 2)
    def _():
        put(mine, c23[...])
        mine_t[...] = c23[...].T

    @pl.when(lo == 3)
    def _():
        mine[...] = c[3]
        mine_t[...] = whole(c.at[3]).T


def sandwich(cov, comp, comp_t):
    return mm(comp_t, mm(cov, comp).astype(BF))


def group_cov_kernel(n, *refs):
    ins, *blocks, outs, scratch = split(refs, 5, n, n, n, n, 3, 4)
    base, c, c_t, c01, c01_t = ins
    mine, agg, agg_bf = outs
    sent, s, s23, sems = scratch
    hi, lo, q = where_am_i()
    group_start(blocks, sent, sems, lo, q, (3, 2, 1, 0))
    group_wait(blocks[0], sent, sems, 3)
    unpack(sent.at[3], s.at[3], n)
    mid = mm(s[3], whole(c.at[2])).astype(BF)
    group_wait(blocks[0], sent, sems, 2)
    unpack(sent.at[2], s.at[2], n)
    s23[...] = (s[2].astype(F32) + mm(c_t[2], mid)).astype(BF)
    group_wait(blocks[0], sent, sems, 1, 0)
    unpack(sent.at[1], s.at[1], n)

    @pl.when(lo == 0)
    def _():
        agg[...] = base[...]

    @pl.when(lo != 0)
    def _():
        unpack(sent.at[0], s.at[0], n)

        def use(columns):
            agg[...] = columns.astype(F32)

        panel_of(s.at[0], q, n, use)

    agg[...] += sandwich(s[1], c[0, q], c_t[0])
    agg[...] += sandwich(s23[...], c01[q], c01_t[...])
    pack(agg, agg_bf, q, n)

    @pl.when(lo == 0)
    def _():
        mine[...] = agg[...]

    @pl.when(lo == 1)
    def _():
        mine[...] = base[...] + sandwich(s23[...], c[1, q], c_t[1])

    @pl.when(lo == 2)
    def _():
        mine[...] = base[...] + sandwich(s[3], c[2, q], c_t[2])

    @pl.when(lo == 3)
    def _():
        mine[...] = base[...]


def is_lower(bit):
    hi, lo, q = where_am_i()
    return lax.rem(hi // (1 << bit), 2) == 0


def panel_rows(q, r, n, w):
    return pl.ds(pl.multiple_of(lax.rem(q + r, n) * w, w), w)


def quarter_rows(place, nb):
    rows = nb // GROUP
    return pl.ds(pl.multiple_of(place * rows, rows), rows)


def times(pieces, right, q):
    n = len(pieces)
    w = right.shape[0] // n
    return sum(mm(x[...], right[panel_rows(q, r, n, w), :]) for r, x in enumerate(pieces))


def place_whole(pieces, dst, q):
    for r, piece in enumerate(pieces):
        dst[lax.rem(q + r, len(pieces))] = piece[...]


def join_kernel(*refs):
    *quarters, out = refs
    hi, lo, q = where_am_i()
    for k, piece in enumerate(quarters):
        out[quarter_rows(jnp.bitwise_xor(lo, k), out.shape[0]), :] = piece[...]


def share_comp_kernel(n, bit, *refs):
    (agg,), parts, (share,), (got, pair) = split(refs, 1, n, 1, 2)
    hi, lo, q = where_am_i()
    lower = is_lower(bit)

    @pl.when(lower)
    def _():
        pair[...] = times(parts, agg.at[q], q).astype(BF)

    @pl.when(jnp.logical_not(lower))
    def _():
        place_whole(parts, got, q)
        pair[...] = mm(whole(agg), got[q]).astype(BF)

    share[...] = pair[quarter_rows(lo, pair.shape[0]), :]


def pair_comp_kernel(n, bit, *refs):
    (agg,), parts, (new_agg, new_agg_t, share), (got,) = split(refs, 1, n, 3, 1)
    hi, lo, q = where_am_i()
    lower = is_lower(bit)
    place_whole(parts, got, q)

    @pl.when(lower)
    def _():
        put(new_agg, mm(whole(got), whole(agg)))

    @pl.when(jnp.logical_not(lower))
    def _():
        put(new_agg, mm(whole(agg), whole(got)))

    new_agg_t[...] = whole(new_agg).T
    share[...] = new_agg[q, quarter_rows(lo, new_agg.shape[1]), :]


def mine_comp_kernel(n, bit, *refs):
    (mine, mine_t), parts, (new_mine, new_mine_t) = split(refs, 2, n, 2)
    hi, lo, q = where_am_i()
    lower = is_lower(bit)

    @pl.when(lower)
    def _():
        for p in range(n):
            new_mine[p] = times(parts, mine.at[p], q).astype(BF)
        new_mine_t[...] = whole(new_mine).T

    @pl.when(jnp.logical_not(lower))
    def _():
        new_mine[...] = mine[...]
        new_mine_t[...] = mine_t[...]


def last_comp_kernel(n, bit, *refs):
    (mine,), parts, (out,) = split(refs, 1, n, 1)
    hi, lo, q = where_am_i()
    lower = is_lower(bit)

    @pl.when(lower)
    def _():
        out[0] = times(parts, mine.at[q], q).astype(BF)

    @pl.when(jnp.logical_not(lower))
    def _():
        out[0] = mine[q]


def pair_cov_kernel(n, bit, to_last, *refs):
    ins, here, c_parts, parts, outs, scratch = split(refs, 3, n, n, n, 2 if to_last else 4, 5)
    agg, agg_c, agg_t = ins
    share, right = outs[:2]
    sent, mid, total, got, packed = scratch
    hi, lo, q = where_am_i()
    lower = is_lower(bit)
    nb, w = agg.shape
    place_whole(parts, sent, q)
    unpack(sent, right, n)

    @pl.when(lower)
    def _():
        total[...] = agg[...] + sandwich(right[...], agg_c[q], agg_t[...])

    @pl.when(jnp.logical_not(lower))
    def _():
        def use(columns):
            total[...] = columns.astype(F32)

        panel_of(right, q, n, use)
        place_whole(here, sent, q)
        unpack(sent, right, n)
        place_whole(c_parts, got, q)
        mid[...] = mm(right[...], got[q]).astype(BF)
        for p in range(n):
            total[p * w : (p + 1) * w, :] += mm_t(got[p], mid[...])

    pack(total, packed, q, n)
    share[...] = packed[quarter_rows(lo, packed.shape[0]), :]
    if not to_last:
        new_agg, new_agg_bf = outs[2:]
        new_agg[...] = total[...]
        new_agg_bf[...] = packed[...]


def mine_cov_kernel(n, bit, cov, mine, mine_t, right, out):
    hi, lo, q = where_am_i()
    lower = is_lower(bit)

    @pl.when(lower)
    def _():
        out[...] = cov[...] + sandwich(right[...], mine[q], mine_t[...])

    @pl.when(jnp.logical_not(lower))
    def _():
        out[...] = cov[...]


def last_cov_kernel(n, bit, *refs):
    (cov, mine, mine_t), parts, (out,), (sent, right) = split(refs, 3, n, 1, 2)
    hi, lo, q = where_am_i()
    lower = is_lower(bit)

    @pl.when(lower)
    def _():
        place_whole(parts, sent, q)
        unpack(sent, right, n)
        out[0] = cov[...] + sandwich(right[...], mine[q], mine_t[...])

    @pl.when(jnp.logical_not(lower))
    def _():
        out[0] = cov[...]


def over_panels(x):
    n = lax.axis_size("panel")
    return [x] + [
        lax.ppermute(x, "panel", [((i + r) % n, i) for i in range(n)]) for r in range(1, n)
    ]


def swap(value, odd_mask, even_mask):
    steps, n = lax.axis_size("tm"), lax.axis_size("panel")
    pairs = []
    for t in range(steps):
        for q in range(n):
            mask = odd_mask if q % 2 else even_mask
            pairs.append((t * n + q, (t ^ mask) * n + q))
    return lax.ppermute(value, ("tm", "panel"), pairs)


def across(x, bit, last):
    steps = lax.axis_size("tm")
    d = GROUP << bit
    return lax.ppermute(
        x, "tm", [(t, t ^ d) for t in range(steps) if (t ^ d) < steps and (t & d or not last)]
    )


def in_group(x):
    return [x] + [swap(x, mask, mask) for mask in range(1, GROUP)]


def joined(x):
    quarters = in_group(x)
    rows, lanes = x.shape
    whole_panel = jax.ShapeDtypeStruct((rows * GROUP, lanes), x.dtype)
    return call(join_kernel, quarters, [VMEM] * GROUP, [whole_panel], [], 0)[0]


def after(x, *others):
    return lax.optimization_barrier((x, *others))[0]


def shards(factor_inverse, coupling, sigma_after):
    steps = lax.axis_size("tm")
    n = lax.axis_size("panel")
    nb, w = factor_inverse.shape[1:]
    levels = (steps // GROUP - 1).bit_length()
    panel_bf = jax.ShapeDtypeStruct((nb, w), BF)
    panel_f32 = jax.ShapeDtypeStruct((nb, w), F32)
    full_bf = jax.ShapeDtypeStruct((n, nb, w), BF)
    square_bf = jax.ShapeDtypeStruct((nb, nb), BF)
    group_bf = jax.ShapeDtypeStruct((GROUP, n, nb, w), BF)
    turned_bf = jax.ShapeDtypeStruct((GROUP - 1, nb, nb), BF)
    share_bf = jax.ShapeDtypeStruct((nb // GROUP, w), BF)
    full_scratch = pltpu.VMEM((n, nb, w), BF)
    rows, lanes = packed_shape(n, nb, w)
    packed_bf = jax.ShapeDtypeStruct((rows, lanes), BF)
    packed_share = jax.ShapeDtypeStruct((rows // GROUP, lanes), BF)
    packed_scratch = pltpu.VMEM((n, rows, lanes), BF)
    square_scratch = pltpu.VMEM((nb, nb), BF)
    one = 2 * nb * nb * w
    sems = pltpu.SemaphoreType.DMA

    comp = coupling[0].astype(BF)
    c_first = swap(comp, 1, 2)
    c_second = swap(comp, 2, 1)
    factor = after(factor_inverse[0], comp)
    f_parts = over_panels(factor.astype(BF))
    c_own = over_panels(comp)
    base, base_bf = call(
        functools.partial(base_kernel, n),
        [factor, sigma_after, *f_parts, *c_own],
        [VMEM] + [ANY] * (1 + 2 * n),
        [panel_f32, packed_bf],
        [full_scratch, full_scratch, pltpu.VMEM((nb, n * w), F32), sems((n + 1,))],
        2 * one,
    )
    s_first = swap(base_bf, 1, 2)
    c_diag = swap(after(c_first, s_first), 2, 1)
    c_pieces = [p for v in (c_first, c_second, c_diag) for p in over_panels(v)]
    s_second = swap(base_bf, 2, 1)
    c_all, c01, c23, agg_c = call(
        functools.partial(group_comp_kernel, n),
        c_own + c_pieces,
        [ANY] * (GROUP * n),
        [group_bf, full_bf, square_bf, full_bf],
        [sems((GROUP, n))],
        3 * n * one,
    )
    agg_panel = lax.dynamic_index_in_dim(agg_c, lax.axis_index("panel"), 0, keepdims=False)
    c_got = across(agg_panel, 0, levels == 1)
    c_t, c01_t, mine, mine_t, agg_t = call(
        functools.partial(tail_comp_kernel, n),
        [c_all, c01, c23, agg_c],
        [VMEM] * 4,
        [turned_bf, square_bf, full_bf, square_bf, square_bf],
        [],
        n * one,
    )
    s_diag = after(swap(s_first, 2, 1), agg_panel)
    s_own = over_panels(base_bf)
    s_pieces = s_own + [p for v in (s_first, s_second, s_diag) for p in over_panels(v)]
    cov, agg, agg_bf = call(
        functools.partial(group_cov_kernel, n),
        [base, c_all, c_t, c01, c01_t, *s_pieces],
        [VMEM] * 5 + [ANY] * (GROUP * n),
        [panel_f32, panel_f32, packed_bf],
        [
            pltpu.VMEM((GROUP, n, rows, lanes), BF),
            pltpu.VMEM((GROUP, nb, nb), BF),
            square_scratch,
            sems((GROUP, n)),
        ],
        (2 * n + 6) * one,
    )
    out_cov = jax.ShapeDtypeStruct((1, nb, w), F32)
    out_comp = jax.ShapeDtypeStruct((1, nb, w), BF)
    panel_scratch = pltpu.VMEM((nb, w), BF)
    sum_scratch = pltpu.VMEM((nb, w), F32)
    c_parts = over_panels(after(c_got, agg_bf))
    s_got = across(after(agg_bf, c_got), 0, levels == 1)
    for bit in range(levels):
        last = bit + 1 == levels
        to_last = bit + 2 == levels
        if last:
            (prop,) = call(
                functools.partial(last_comp_kernel, n, bit),
                [mine, *c_parts],
                [VMEM] * (1 + n),
                [out_comp],
                [],
                one,
            )
            s_parts = over_panels(after(s_got, prop))
            (cov,) = call(
                functools.partial(last_cov_kernel, n, bit),
                [cov, mine, mine_t, *s_parts],
                [VMEM] * (3 + n),
                [out_cov],
                [packed_scratch, square_scratch],
                2 * one,
            )
            break
        agg_in = after(agg_c, agg_bf)
        if to_last:
            (c_send,) = call(
                functools.partial(share_comp_kernel, n, bit),
                [agg_in, *c_parts],
                [VMEM] * (1 + n),
                [share_bf],
                [full_scratch, panel_scratch],
                one,
            )
        else:
            new_agg_c, new_agg_t, c_send = call(
                functools.partial(pair_comp_kernel, n, bit),
                [agg_in, *c_parts],
                [VMEM] * (1 + n),
                [full_bf, square_bf, share_bf],
                [full_scratch],
                n * one,
            )
        c_far = across(c_send, bit + 1, to_last)
        new_mine, new_mine_t = call(
            functools.partial(mine_comp_kernel, n, bit),
            [after(mine, c_send), mine_t, *c_parts],
            [VMEM] * (2 + n),
            [full_bf, square_bf],
            [],
            n * one,
        )
        s_parts = over_panels(after(s_got, c_far, new_mine))
        outs = call(
            functools.partial(pair_cov_kernel, n, bit, to_last),
            [agg, agg_c, agg_t, *over_panels(agg_bf), *c_parts, *s_parts],
            [VMEM] * (3 + 3 * n),
            [packed_share, square_bf] + ([] if to_last else [panel_f32, packed_bf]),
            [
                packed_scratch,
                panel_scratch,
                sum_scratch,
                full_scratch,
                pltpu.VMEM((rows, lanes), BF),
            ],
            2 * one,
        )
        s_send, right = outs[:2]
        (cov,) = call(
            functools.partial(mine_cov_kernel, n, bit),
            [cov, mine, mine_t, right],
            [VMEM] * 4,
            [panel_f32],
            [],
            2 * one,
        )
        if not to_last:
            agg, agg_bf = outs[2:]
            agg_c, agg_t = new_agg_c, new_agg_t
        s_far = across(s_send, bit + 1, to_last)
        c_parts = over_panels(after(joined(after(c_far, cov)), s_far))
        s_got = joined(s_far)
        mine, mine_t = new_mine, new_mine_t
    return cov, prop


def solution(mesh):
    placed = (P("tm", None, "panel"), P("tm", None, "panel"), P())
    return jax.shard_map(
        shards,
        mesh=mesh,
        in_specs=placed,
        out_specs=(P("tm", None, "panel"), P("tm", None, "panel")),
        check_vma=False,
    )
```

```python
import functools

import jax
import jax.numpy as jnp
from jax import lax
from jax.experimental import pallas as pl
from jax.experimental.pallas import tpu as pltpu
from jax.sharding import PartitionSpec as P

BF = jnp.bfloat16
F32 = jnp.float32
GROUP = 4
BLOCK = 128
ANY = pl.BlockSpec(memory_space=pl.ANY)
VMEM = pl.BlockSpec(memory_space=pltpu.VMEM)
MIB = 1 << 20


def mm(a, b):
    return jnp.dot(a, b, preferred_element_type=F32)


def mm_t(a, b):
    return lax.dot_general(a, b, (((0,), (0,)), ((), ())), preferred_element_type=F32)


def whole(ref):
    return jnp.concatenate([ref[p] for p in range(ref.shape[0])], axis=1)


def put(ref, value):
    width = ref.shape[2]
    for p in range(ref.shape[0]):
        ref[p] = value[:, p * width : (p + 1) * width].astype(ref.dtype)


def where_am_i():
    t = lax.axis_index("tm")
    return t // GROUP, lax.rem(t, GROUP), lax.axis_index("panel")


def run(copies):
    for c in copies:
        c.start()
    for c in copies:
        c.wait()


def copy_all(pairs, sems):
    return [pltpu.make_async_copy(s, d, sems.at[i]) for i, (s, d) in enumerate(pairs)]


def panel_pairs(pieces, dst, q):
    n = len(pieces)
    return [(piece, dst.at[lax.rem(q + r, n)]) for r, piece in enumerate(pieces)]


def group_start(blocks, dst, sems, lo, q, order):
    own, first, second, diag = blocks
    n = len(own)

    def start(slot, r, p, mask, piece):
        @pl.when(jnp.bitwise_xor(lo, mask) == slot)
        def _():
            pltpu.make_async_copy(piece, dst.at[slot, p], sems.at[slot, p]).start()

    for slot in order:
        for r in range(n):
            p = lax.rem(q + r, n)
            even = 1 - lax.rem(p, 2)
            near, far = 1 + even, 2 - even
            for mask, piece in ((0, own[r]), (near, first[r]), (far, second[r]), (3, diag[r])):
                start(slot, r, p, mask, piece)


def group_wait(own, dst, sems, *slots):
    for slot in slots:
        for p in range(len(own)):
            pltpu.make_async_copy(own[p], dst.at[slot, p], sems.at[slot, p]).wait()


def packs(n, w):
    return n == 2 and w % BLOCK == 0


def packed_shape(n, nb, w):
    if not packs(n, w):
        return nb, w
    k = w // BLOCK
    return (k * (k + 1) // 2 + (k * k + 1) // 2) * BLOCK, BLOCK


def triangle(k):
    return [(i, j) for i in range(k) for j in range(i + 1)]


def halves(k):
    every = [(a, b) for a in range(k) for b in range(k)]
    half = (k * k + 1) // 2
    return every[:half], every[k * k - half :]


def pack(panel, out, q, n):
    nb, w = panel.shape
    if not packs(n, w):
        out[...] = panel[...].astype(BF)
        return
    k = w // BLOCK
    at = 0
    for i, j in triangle(k):
        rows = pl.ds(pl.multiple_of(q * w + i * BLOCK, BLOCK), BLOCK)
        out[at : at + BLOCK, :] = panel[rows, j * BLOCK : (j + 1) * BLOCK].astype(BF)
        at += BLOCK
    for side, blocks in enumerate(halves(k)):

        @pl.when(q == side)
        def _():
            to = at
            for a, b in blocks:
                i, j = (b, a) if side else (w // BLOCK + a, b)
                value = panel[i * BLOCK : (i + 1) * BLOCK, j * BLOCK : (j + 1) * BLOCK]
                out[to : to + BLOCK, :] = value.astype(BF)
                to += BLOCK


def unpack(src, dst, n):
    nb = dst.shape[0]
    w = nb // n
    if not packs(n, w):
        dst[...] = whole(src)
        return
    k = w // BLOCK

    def both(block, i, j):
        dst[i * BLOCK : (i + 1) * BLOCK, j * BLOCK : (j + 1) * BLOCK] = block
        if i != j:
            dst[j * BLOCK : (j + 1) * BLOCK, i * BLOCK : (i + 1) * BLOCK] = block.T

    seen = set()
    for p in range(n):
        at = 0
        for i, j in triangle(k):
            both(src[p, at : at + BLOCK, :], p * k + i, p * k + j)
            at += BLOCK
        for a, b in halves(k)[p]:
            if (a, b) not in seen:
                i, j = (b, k + a) if p else (k + a, b)
                both(src[p, at : at + BLOCK, :], i, j)
            seen.add((a, b))
            at += BLOCK


def panel_of(matrix, q, n, use):
    w = matrix.shape[1] // n
    for p in range(n):

        @pl.when(q == p)
        def _():
            use(matrix[:, p * w : (p + 1) * w])


def split(refs, *counts):
    out, at = [], 0
    for c in counts:
        out.append(refs[at : at + c])
        at += c
    return out


def call(kernel, ins, in_specs, outs, scratch, flops):
    size = sum(a.size * a.dtype.itemsize for a in ins) + sum(
        o.size * o.dtype.itemsize for o in outs
    )
    return pl.pallas_call(
        kernel,
        in_specs=in_specs,
        out_specs=[VMEM] * len(outs),
        out_shape=outs,
        scratch_shapes=scratch,
        compiler_params=pltpu.CompilerParams(vmem_limit_bytes=28 * MIB),
        cost_estimate=pl.CostEstimate(flops=flops, bytes_accessed=size, transcendentals=0),
    )(*ins)


def base_kernel(n, *refs):
    factor, sigma, f_parts, c_parts, (base, base_bf), (f_all, c_all, sig, sems) = split(
        refs, 1, 1, n, n, 2, 4
    )
    factor, sigma = factor[0], sigma[0]
    hi, lo, q = where_am_i()
    width = factor.shape[1]
    run(copy_all(panel_pairs(f_parts, f_all, q), sems))
    own = factor[...]
    high = own.astype(BF)
    low = (own - high.astype(F32)).astype(BF)
    for p in range(n):
        part = f_all[p]
        base[p * width : (p + 1) * width, :] = mm_t(part, high) + mm_t(part, low)

    @pl.when(lax.axis_index("tm") == lax.axis_size("tm") - 1)
    def _():
        run(copy_all(panel_pairs(c_parts, c_all, q) + [(sigma, sig)], sems))
        s = sig[...]
        s_high = s.astype(BF)
        s_low = (s - s_high.astype(F32)).astype(BF)
        c_own = c_all[q]
        mid = mm(s_high, c_own) + mm(s_low, c_own)
        mid_high = mid.astype(BF)
        mid_low = (mid - mid_high.astype(F32)).astype(BF)
        c_full = whole(c_all)
        base[...] += mm_t(c_full, mid_high) + mm_t(c_full, mid_low)

    pack(base, base_bf, q, n)


def group_comp_kernel(n, *refs):
    *blocks, outs, (sems,) = split(refs, n, n, n, n, 4, 1)
    c, c01_ref, c23_ref, agg = outs
    hi, lo, q = where_am_i()
    group_start(blocks, c, sems, lo, q, (1, 0, 3, 2))
    group_wait(blocks[0], c, sems, 1, 0)
    c01 = mm(whole(c.at[1]), whole(c.at[0])).astype(BF)
    put(c01_ref, c01)
    group_wait(blocks[0], c, sems, 3, 2)
    c23 = mm(whole(c.at[3]), whole(c.at[2])).astype(BF)
    c23_ref[...] = c23
    put(agg, mm(c23, c01))


def tail_comp_kernel(n, c, c01, c23, agg, *outs):
    c_t, c01_t, mine, mine_t, agg_t = outs
    hi, lo, q = where_am_i()
    agg_t[...] = whole(agg).T
    c01_t[...] = whole(c01).T
    for k in range(GROUP - 1):
        c_t[k] = whole(c.at[k]).T

    @pl.when(lo == 0)
    def _():
        mine[...] = agg[...]
        mine_t[...] = agg_t[...]

    @pl.when(lo == 1)
    def _():
        value = mm(c23[...], whole(c.at[1])).astype(BF)
        put(mine, value)
        mine_t[...] = value.T

    @pl.when(lo == 2)
    def _():
        put(mine, c23[...])
        mine_t[...] = c23[...].T

    @pl.when(lo == 3)
    def _():
        mine[...] = c[3]
        mine_t[...] = whole(c.at[3]).T


def sandwich(cov, comp, comp_t):
    return mm(comp_t, mm(cov, comp).astype(BF))


def group_cov_kernel(n, *refs):
    ins, *blocks, outs, scratch = split(refs, 5, n, n, n, n, 4, 3)
    base, c, c_t, c01, c01_t = ins
    agg, agg_bf, s3, s23 = outs
    sent, s, sems = scratch
    hi, lo, q = where_am_i()
    group_start(blocks, sent, sems, lo, q, (3, 2, 1, 0))
    group_wait(blocks[0], sent, sems, 3)
    unpack(sent.at[3], s.at[3], n)
    mid = mm(s[3], whole(c.at[2])).astype(BF)
    group_wait(blocks[0], sent, sems, 2)
    unpack(sent.at[2], s.at[2], n)
    s23[...] = (s[2].astype(F32) + mm(c_t[2], mid)).astype(BF)
    group_wait(blocks[0], sent, sems, 1, 0)
    unpack(sent.at[1], s.at[1], n)

    @pl.when(lo == 0)
    def _():
        agg[...] = base[...]

    @pl.when(lo != 0)
    def _():
        unpack(sent.at[0], s.at[0], n)

        def use(columns):
            agg[...] = columns.astype(F32)

        panel_of(s.at[0], q, n, use)

    agg[...] += sandwich(s[1], c[0, q], c_t[0])
    agg[...] += sandwich(s23[...], c01[q], c01_t[...])
    pack(agg, agg_bf, q, n)
    s3[...] = s[3]


def group_mine_kernel(base, agg, s3, s23, c, c_t, mine):
    hi, lo, q = where_am_i()

    @pl.when(lo == 0)
    def _():
        mine[...] = agg[...]

    @pl.when(lo == 1)
    def _():
        mine[...] = base[...] + sandwich(s23[...], c[1, q], c_t[1])

    @pl.when(lo == 2)
    def _():
        mine[...] = base[...] + sandwich(s3[...], c[2, q], c_t[2])

    @pl.when(lo == 3)
    def _():
        mine[...] = base[...]


def is_lower(bit):
    hi, lo, q = where_am_i()
    return lax.rem(hi // (1 << bit), 2) == 0


def panel_rows(q, r, n, w):
    return pl.ds(pl.multiple_of(lax.rem(q + r, n) * w, w), w)


def quarter_rows(place, nb):
    rows = nb // GROUP
    return pl.ds(pl.multiple_of(place * rows, rows), rows)


def times(pieces, right, q):
    n = len(pieces)
    w = right.shape[0] // n
    return sum(mm(x[...], right[panel_rows(q, r, n, w), :]) for r, x in enumerate(pieces))


def place_whole(pieces, dst, q):
    for r, piece in enumerate(pieces):
        dst[lax.rem(q + r, len(pieces))] = piece[...]


def join_kernel(*refs):
    *quarters, out = refs
    hi, lo, q = where_am_i()
    for k, piece in enumerate(quarters):
        out[quarter_rows(jnp.bitwise_xor(lo, k), out.shape[0]), :] = piece[...]


def share_comp_kernel(n, bit, *refs):
    (agg,), parts, (share,), (got, pair) = split(refs, 1, n, 1, 2)
    hi, lo, q = where_am_i()
    lower = is_lower(bit)

    @pl.when(lower)
    def _():
        pair[...] = times(parts, agg.at[q], q).astype(BF)

    @pl.when(jnp.logical_not(lower))
    def _():
        place_whole(parts, got, q)
        pair[...] = mm(whole(agg), got[q]).astype(BF)

    share[...] = pair[quarter_rows(lo, pair.shape[0]), :]


def pair_comp_kernel(n, bit, *refs):
    (agg,), parts, (new_agg, new_agg_t, share), (got,) = split(refs, 1, n, 3, 1)
    hi, lo, q = where_am_i()
    lower = is_lower(bit)
    place_whole(parts, got, q)

    @pl.when(lower)
    def _():
        put(new_agg, mm(whole(got), whole(agg)))

    @pl.when(jnp.logical_not(lower))
    def _():
        put(new_agg, mm(whole(agg), whole(got)))

    new_agg_t[...] = whole(new_agg).T
    share[...] = new_agg[q, quarter_rows(lo, new_agg.shape[1]), :]


def mine_comp_kernel(n, bit, *refs):
    (mine, mine_t), parts, (new_mine, new_mine_t) = split(refs, 2, n, 2)
    hi, lo, q = where_am_i()
    lower = is_lower(bit)

    @pl.when(lower)
    def _():
        for p in range(n):
            new_mine[p] = times(parts, mine.at[p], q).astype(BF)
        new_mine_t[...] = whole(new_mine).T

    @pl.when(jnp.logical_not(lower))
    def _():
        new_mine[...] = mine[...]
        new_mine_t[...] = mine_t[...]


def last_comp_kernel(n, bit, *refs):
    (mine,), parts, (out,) = split(refs, 1, n, 1)
    hi, lo, q = where_am_i()
    lower = is_lower(bit)

    @pl.when(lower)
    def _():
        out[0] = times(parts, mine.at[q], q).astype(BF)

    @pl.when(jnp.logical_not(lower))
    def _():
        out[0] = mine[q]


def pair_cov_kernel(n, bit, to_last, *refs):
    ins, here, c_parts, parts, outs, scratch = split(refs, 3, n, n, n, 2 if to_last else 4, 5)
    agg, agg_c, agg_t = ins
    share, right = outs[:2]
    sent, mid, total, got, packed = scratch
    hi, lo, q = where_am_i()
    lower = is_lower(bit)
    nb, w = agg.shape
    place_whole(parts, sent, q)
    unpack(sent, right, n)

    @pl.when(lower)
    def _():
        total[...] = agg[...] + sandwich(right[...], agg_c[q], agg_t[...])

    @pl.when(jnp.logical_not(lower))
    def _():
        def use(columns):
            total[...] = columns.astype(F32)

        panel_of(right, q, n, use)
        place_whole(here, sent, q)
        unpack(sent, right, n)
        place_whole(c_parts, got, q)
        mid[...] = mm(right[...], got[q]).astype(BF)
        for p in range(n):
            total[p * w : (p + 1) * w, :] += mm_t(got[p], mid[...])

    pack(total, packed, q, n)
    share[...] = packed[quarter_rows(lo, packed.shape[0]), :]
    if not to_last:
        new_agg, new_agg_bf = outs[2:]
        new_agg[...] = total[...]
        new_agg_bf[...] = packed[...]


def mine_cov_kernel(n, bit, cov, mine, mine_t, right, out):
    hi, lo, q = where_am_i()
    lower = is_lower(bit)

    @pl.when(lower)
    def _():
        out[...] = cov[...] + sandwich(right[...], mine[q], mine_t[...])

    @pl.when(jnp.logical_not(lower))
    def _():
        out[...] = cov[...]


def last_cov_kernel(n, bit, *refs):
    (cov, mine, mine_t), parts, (out,), (sent, right) = split(refs, 3, n, 1, 2)
    hi, lo, q = where_am_i()
    lower = is_lower(bit)

    @pl.when(lower)
    def _():
        place_whole(parts, sent, q)
        unpack(sent, right, n)
        out[0] = cov[...] + sandwich(right[...], mine[q], mine_t[...])

    @pl.when(jnp.logical_not(lower))
    def _():
        out[0] = cov[...]


def over_panels(x):
    n = lax.axis_size("panel")
    return [x] + [
        lax.ppermute(x, "panel", [((i + r) % n, i) for i in range(n)]) for r in range(1, n)
    ]


def swap(value, odd_mask, even_mask):
    steps, n = lax.axis_size("tm"), lax.axis_size("panel")
    pairs = []
    for t in range(steps):
        for q in range(n):
            mask = odd_mask if q % 2 else even_mask
            pairs.append((t * n + q, (t ^ mask) * n + q))
    return lax.ppermute(value, ("tm", "panel"), pairs)


def across(x, bit, last):
    steps = lax.axis_size("tm")
    d = GROUP << bit
    return lax.ppermute(
        x, "tm", [(t, t ^ d) for t in range(steps) if (t ^ d) < steps and (t & d or not last)]
    )


def in_group(x):
    return [x] + [swap(x, mask, mask) for mask in range(1, GROUP)]


def joined(x, *earlier):
    quarters = lax.optimization_barrier((*in_group(x), *earlier))[:GROUP]
    rows, lanes = x.shape
    whole_panel = jax.ShapeDtypeStruct((rows * GROUP, lanes), x.dtype)
    return call(join_kernel, quarters, [VMEM] * GROUP, [whole_panel], [], 0)[0]


def after(x, *others):
    return lax.optimization_barrier((x, *others))[0]


def shards(factor_inverse, coupling, sigma_after):
    steps = lax.axis_size("tm")
    n = lax.axis_size("panel")
    nb, w = factor_inverse.shape[1:]
    levels = (steps // GROUP - 1).bit_length()
    panel_bf = jax.ShapeDtypeStruct((nb, w), BF)
    panel_f32 = jax.ShapeDtypeStruct((nb, w), F32)
    full_bf = jax.ShapeDtypeStruct((n, nb, w), BF)
    square_bf = jax.ShapeDtypeStruct((nb, nb), BF)
    group_bf = jax.ShapeDtypeStruct((GROUP, n, nb, w), BF)
    turned_bf = jax.ShapeDtypeStruct((GROUP - 1, nb, nb), BF)
    share_bf = jax.ShapeDtypeStruct((nb // GROUP, w), BF)
    full_scratch = pltpu.VMEM((n, nb, w), BF)
    rows, lanes = packed_shape(n, nb, w)
    packed_bf = jax.ShapeDtypeStruct((rows, lanes), BF)
    packed_share = jax.ShapeDtypeStruct((rows // GROUP, lanes), BF)
    packed_scratch = pltpu.VMEM((n, rows, lanes), BF)
    square_scratch = pltpu.VMEM((nb, nb), BF)
    one = 2 * nb * nb * w
    sems = pltpu.SemaphoreType.DMA

    comp = coupling[0].astype(BF)
    c_first = swap(comp, 1, 2)
    c_second = swap(comp, 2, 1)
    factor = after(factor_inverse[0], comp)
    f_parts = over_panels(factor.astype(BF))
    c_own = over_panels(comp)
    base, base_bf = call(
        functools.partial(base_kernel, n),
        [factor, sigma_after, *f_parts, *c_own],
        [VMEM] + [ANY] * (1 + 2 * n),
        [panel_f32, packed_bf],
        [full_scratch, full_scratch, pltpu.VMEM((nb, n * w), F32), sems((n + 1,))],
        2 * one,
    )
    s_first = swap(base_bf, 1, 2)
    c_diag = swap(after(c_first, s_first), 2, 1)
    s_second = swap(base_bf, 2, 1)
    c_diag = after(c_diag, s_second)
    c_pieces = [p for v in (c_first, c_second, c_diag) for p in over_panels(v)]
    c_all, c01, c23, agg_c = call(
        functools.partial(group_comp_kernel, n),
        c_own + c_pieces,
        [ANY] * (GROUP * n),
        [group_bf, full_bf, square_bf, full_bf],
        [sems((GROUP, n))],
        3 * n * one,
    )
    agg_panel = lax.dynamic_index_in_dim(agg_c, lax.axis_index("panel"), 0, keepdims=False)
    c_got = across(agg_panel, 0, levels == 1)
    c_t, c01_t, mine, mine_t, agg_t = call(
        functools.partial(tail_comp_kernel, n),
        [c_all, c01, c23, agg_c],
        [VMEM] * 4,
        [turned_bf, square_bf, full_bf, square_bf, square_bf],
        [],
        n * one,
    )
    s_diag = after(swap(s_first, 2, 1), agg_panel)
    s_own = over_panels(base_bf)
    s_pieces = s_own + [p for v in (s_first, s_second, s_diag) for p in over_panels(v)]
    agg, agg_bf, s3, s23 = call(
        functools.partial(group_cov_kernel, n),
        [base, c_all, c_t, c01, c01_t, *s_pieces],
        [VMEM] * 5 + [ANY] * (GROUP * n),
        [panel_f32, packed_bf, square_bf, square_bf],
        [
            pltpu.VMEM((GROUP, n, rows, lanes), BF),
            pltpu.VMEM((GROUP, nb, nb), BF),
            sems((GROUP, n)),
        ],
        (2 * n + 4) * one,
    )
    (cov,) = call(
        group_mine_kernel,
        [base, agg, s3, s23, c_all, c_t],
        [VMEM] * 6,
        [panel_f32],
        [],
        2 * one,
    )
    out_cov = jax.ShapeDtypeStruct((1, nb, w), F32)
    out_comp = jax.ShapeDtypeStruct((1, nb, w), BF)
    panel_scratch = pltpu.VMEM((nb, w), BF)
    sum_scratch = pltpu.VMEM((nb, w), F32)
    c_parts = over_panels(after(c_got, agg_bf))
    s_got = across(agg_bf, 0, levels == 1)
    for bit in range(levels):
        last = bit + 1 == levels
        to_last = bit + 2 == levels
        if last:
            (prop,) = call(
                functools.partial(last_comp_kernel, n, bit),
                [mine, *c_parts],
                [VMEM] * (1 + n),
                [out_comp],
                [],
                one,
            )
            s_parts = over_panels(after(s_got, prop))
            (cov,) = call(
                functools.partial(last_cov_kernel, n, bit),
                [cov, mine, mine_t, *s_parts],
                [VMEM] * (3 + n),
                [out_cov],
                [packed_scratch, square_scratch],
                2 * one,
            )
            break
        agg_in = after(agg_c, agg_bf)
        if to_last:
            (c_send,) = call(
                functools.partial(share_comp_kernel, n, bit),
                [agg_in, *c_parts],
                [VMEM] * (1 + n),
                [share_bf],
                [full_scratch, panel_scratch],
                one,
            )
        else:
            new_agg_c, new_agg_t, c_send = call(
                functools.partial(pair_comp_kernel, n, bit),
                [agg_in, *c_parts],
                [VMEM] * (1 + n),
                [full_bf, square_bf, share_bf],
                [full_scratch],
                n * one,
            )
        c_far = across(c_send, bit + 1, to_last)
        new_mine, new_mine_t = call(
            functools.partial(mine_comp_kernel, n, bit),
            [after(mine, c_send), mine_t, *c_parts],
            [VMEM] * (2 + n),
            [full_bf, square_bf],
            [],
            n * one,
        )
        s_parts = over_panels(after(s_got, c_far, new_mine))
        outs = call(
            functools.partial(pair_cov_kernel, n, bit, to_last),
            [agg, agg_c, agg_t, *over_panels(agg_bf), *c_parts, *s_parts],
            [VMEM] * (3 + 3 * n),
            [packed_share, square_bf] + ([] if to_last else [panel_f32, packed_bf]),
            [
                packed_scratch,
                panel_scratch,
                sum_scratch,
                full_scratch,
                pltpu.VMEM((rows, lanes), BF),
            ],
            2 * one,
        )
        s_send, right = outs[:2]
        s_far = across(s_send, bit + 1, to_last)
        (cov,) = call(
            functools.partial(mine_cov_kernel, n, bit),
            [after(cov, s_far), mine, mine_t, right],
            [VMEM] * 4,
            [panel_f32],
            [],
            20 * one,
        )
        if not to_last:
            agg, agg_bf = outs[2:]
            agg_c, agg_t = new_agg_c, new_agg_t
        c_parts = over_panels(joined(after(c_far, s_send), cov))
        s_got = joined(s_far)
        mine, mine_t = new_mine, new_mine_t
    return cov, prop


def solution(mesh):
    placed = (P("tm", None, "panel"), P("tm", None, "panel"), P())
    return jax.shard_map(
        shards,
        mesh=mesh,
        in_specs=placed,
        out_specs=(P("tm", None, "panel"), P("tm", None, "panel")),
        check_vma=False,
    )
```

```python
import functools

import jax
import jax.numpy as jnp
from jax import lax
from jax.experimental import pallas as pl
from jax.experimental.pallas import tpu as pltpu
from jax.sharding import PartitionSpec as P

BF = jnp.bfloat16
F32 = jnp.float32
GROUP = 4
BLOCK = 128
ANY = pl.BlockSpec(memory_space=pl.ANY)
VMEM = pl.BlockSpec(memory_space=pltpu.VMEM)
MIB = 1 << 20


def mm(a, b):
    return jnp.dot(a, b, preferred_element_type=F32)


def mm_t(a, b):
    return lax.dot_general(a, b, (((0,), (0,)), ((), ())), preferred_element_type=F32)


def whole(ref):
    return jnp.concatenate([ref[p] for p in range(ref.shape[0])], axis=1)


def put(ref, value):
    width = ref.shape[2]
    for p in range(ref.shape[0]):
        ref[p] = value[:, p * width : (p + 1) * width].astype(ref.dtype)


def where_am_i():
    t = lax.axis_index("tm")
    return t // GROUP, lax.rem(t, GROUP), lax.axis_index("panel")


def run(copies):
    for c in copies:
        c.start()
    for c in copies:
        c.wait()


def copy_all(pairs, sems):
    return [pltpu.make_async_copy(s, d, sems.at[i]) for i, (s, d) in enumerate(pairs)]


def panel_pairs(pieces, dst, q):
    n = len(pieces)
    return [(piece, dst.at[lax.rem(q + r, n)]) for r, piece in enumerate(pieces)]


def group_start(blocks, dst, sems, lo, q, order):
    own, first, second, diag = blocks
    n = len(own)

    def start(slot, r, p, mask, piece):
        @pl.when(jnp.bitwise_xor(lo, mask) == slot)
        def _():
            pltpu.make_async_copy(piece, dst.at[slot, p], sems.at[slot, p]).start()

    for slot in order:
        for r in range(n):
            p = lax.rem(q + r, n)
            even = 1 - lax.rem(p, 2)
            near, far = 1 + even, 2 - even
            for mask, piece in ((0, own[r]), (near, first[r]), (far, second[r]), (3, diag[r])):
                start(slot, r, p, mask, piece)


def group_wait(own, dst, sems, *slots):
    for slot in slots:
        for p in range(len(own)):
            pltpu.make_async_copy(own[p], dst.at[slot, p], sems.at[slot, p]).wait()


def packs(n, w):
    return n == 2 and w % BLOCK == 0


def packed_shape(n, nb, w):
    if not packs(n, w):
        return nb, w
    k = w // BLOCK
    return (k * (k + 1) // 2 + (k * k + 1) // 2) * BLOCK, BLOCK


def triangle(k):
    return [(i, j) for i in range(k) for j in range(i + 1)]


def halves(k):
    every = [(a, b) for a in range(k) for b in range(k)]
    half = (k * k + 1) // 2
    return every[:half], every[k * k - half :]


def pack(panel, out, q, n):
    nb, w = panel.shape
    if not packs(n, w):
        out[...] = panel[...].astype(BF)
        return
    k = w // BLOCK
    at = 0
    for i, j in triangle(k):
        rows = pl.ds(pl.multiple_of(q * w + i * BLOCK, BLOCK), BLOCK)
        out[at : at + BLOCK, :] = panel[rows, j * BLOCK : (j + 1) * BLOCK].astype(BF)
        at += BLOCK
    for side, blocks in enumerate(halves(k)):

        @pl.when(q == side)
        def _():
            to = at
            for a, b in blocks:
                i, j = (b, a) if side else (w // BLOCK + a, b)
                value = panel[i * BLOCK : (i + 1) * BLOCK, j * BLOCK : (j + 1) * BLOCK]
                out[to : to + BLOCK, :] = value.astype(BF)
                to += BLOCK


def unpack(src, dst, n):
    nb = dst.shape[0]
    w = nb // n
    if not packs(n, w):
        dst[...] = whole(src)
        return
    k = w // BLOCK

    def both(block, i, j):
        dst[i * BLOCK : (i + 1) * BLOCK, j * BLOCK : (j + 1) * BLOCK] = block
        if i != j:
            dst[j * BLOCK : (j + 1) * BLOCK, i * BLOCK : (i + 1) * BLOCK] = block.T

    seen = set()
    for p in range(n):
        at = 0
        for i, j in triangle(k):
            both(src[p, at : at + BLOCK, :], p * k + i, p * k + j)
            at += BLOCK
        for a, b in halves(k)[p]:
            if (a, b) not in seen:
                i, j = (b, k + a) if p else (k + a, b)
                both(src[p, at : at + BLOCK, :], i, j)
            seen.add((a, b))
            at += BLOCK


def panel_of(matrix, q, n, use):
    w = matrix.shape[1] // n
    for p in range(n):

        @pl.when(q == p)
        def _():
            use(matrix[:, p * w : (p + 1) * w])


def split(refs, *counts):
    out, at = [], 0
    for c in counts:
        out.append(refs[at : at + c])
        at += c
    return out


def call(kernel, ins, in_specs, outs, scratch, flops, aliases=None):
    size = sum(a.size * a.dtype.itemsize for a in ins) + sum(
        o.size * o.dtype.itemsize for o in outs
    )
    return pl.pallas_call(
        kernel,
        in_specs=in_specs,
        out_specs=[VMEM] * len(outs),
        out_shape=outs,
        scratch_shapes=scratch,
        input_output_aliases=aliases or {},
        compiler_params=pltpu.CompilerParams(vmem_limit_bytes=28 * MIB),
        cost_estimate=pl.CostEstimate(flops=flops, bytes_accessed=size, transcendentals=0),
    )(*ins)


def base_kernel(n, *refs):
    factor, sigma, f_parts, c_parts, (base, base_bf), (f_all, c_all, sig, sems) = split(
        refs, 1, 1, n, n, 2, 4
    )
    factor, sigma = factor[0], sigma[0]
    hi, lo, q = where_am_i()
    width = factor.shape[1]
    run(copy_all(panel_pairs(f_parts, f_all, q), sems))
    own = factor[...]
    high = own.astype(BF)
    low = (own - high.astype(F32)).astype(BF)
    for p in range(n):
        part = f_all[p]
        base[p * width : (p + 1) * width, :] = mm_t(part, high) + mm_t(part, low)

    @pl.when(lax.axis_index("tm") == lax.axis_size("tm") - 1)
    def _():
        run(copy_all(panel_pairs(c_parts, c_all, q) + [(sigma, sig)], sems))
        s = sig[...]
        s_high = s.astype(BF)
        s_low = (s - s_high.astype(F32)).astype(BF)
        c_own = c_all[q]
        mid = mm(s_high, c_own) + mm(s_low, c_own)
        mid_high = mid.astype(BF)
        mid_low = (mid - mid_high.astype(F32)).astype(BF)
        c_full = whole(c_all)
        base[...] += mm_t(c_full, mid_high) + mm_t(c_full, mid_low)

    pack(base, base_bf, q, n)


def near_comp_kernel(n, *refs):
    own, first, second, (c, c_t, pair), (sems,) = split(refs, n, n, n, 3, 1)
    hi, lo, q = where_am_i()
    pairs = []
    for r in range(n):
        p = lax.rem(q + r, n)
        even = 1 - lax.rem(p, 2)
        for mask, piece in ((0, own[r]), (1 + even, first[r]), (2 - even, second[r])):
            pairs.append((piece, c.at[jnp.bitwise_xor(lo, mask), p]))
    run(copy_all(pairs, sems))
    pair[...] = pair_product(c, lo)
    for mask in range(GROUP - 1):
        slot = jnp.bitwise_xor(lo, mask)
        c_t[slot] = whole(c.at[slot]).T


def pair_product(c, member):
    odd = lax.rem(member, 2)
    return mm(whole(c.at[member - odd + 1]), whole(c.at[member - odd])).astype(BF)


def group_comp_kernel(n, *refs):
    (c, pair), diag, (_, c01, c23, agg), (other, sems) = split(refs, 2, n, 4, 2)
    hi, lo, q = where_am_i()
    slot = jnp.bitwise_xor(lo, 3)
    run(copy_all(panel_pairs(diag, c.at[slot], q), sems))
    other[...] = pair_product(c, slot)

    @pl.when(lo < 2)
    def _():
        put(c01, pair[...])
        c23[...] = other[...]

    @pl.when(lo >= 2)
    def _():
        put(c01, other[...])
        c23[...] = pair[...]

    put(agg, mm(c23[...], whole(c01)))


def turn_comp_kernel(c, c_t, c01, _, c01_t):
    hi, lo, q = where_am_i()
    slot = jnp.bitwise_xor(lo, 3)
    c_t[slot] = whole(c.at[slot]).T
    c01_t[...] = whole(c01).T


def tail_comp_kernel(c, c_t, c23, agg, mine, mine_t, agg_t):
    hi, lo, q = where_am_i()
    agg_t[...] = whole(agg).T

    @pl.when(lo == 0)
    def _():
        mine[...] = agg[...]
        mine_t[...] = agg_t[...]

    @pl.when(lo == 1)
    def _():
        value = mm(c23[...], whole(c.at[1])).astype(BF)
        put(mine, value)
        mine_t[...] = value.T

    @pl.when(lo == 2)
    def _():
        put(mine, c23[...])
        mine_t[...] = c23[...].T

    @pl.when(lo == 3)
    def _():
        mine[...] = c[3]
        mine_t[...] = c_t[3]


def sandwich(cov, comp, comp_t):
    return mm(comp_t, mm(cov, comp).astype(BF))


def group_cov_kernel(n, *refs):
    ins, *blocks, outs, scratch = split(refs, 5, n, n, n, n, 4, 3)
    base, c, c_t, c01, c01_t = ins
    agg, agg_bf, s3, s23 = outs
    sent, s, sems = scratch
    hi, lo, q = where_am_i()
    group_start(blocks, sent, sems, lo, q, (3, 2, 1, 0))
    group_wait(blocks[0], sent, sems, 3)
    unpack(sent.at[3], s.at[3], n)
    mid = mm(s[3], whole(c.at[2])).astype(BF)
    group_wait(blocks[0], sent, sems, 2)
    unpack(sent.at[2], s.at[2], n)
    s23[...] = (s[2].astype(F32) + mm(c_t[2], mid)).astype(BF)
    group_wait(blocks[0], sent, sems, 1, 0)
    unpack(sent.at[1], s.at[1], n)

    @pl.when(lo == 0)
    def _():
        agg[...] = base[...]

    @pl.when(lo != 0)
    def _():
        unpack(sent.at[0], s.at[0], n)

        def use(columns):
            agg[...] = columns.astype(F32)

        panel_of(s.at[0], q, n, use)

    agg[...] += sandwich(s[1], c[0, q], c_t[0])
    agg[...] += sandwich(s23[...], c01[q], c01_t[...])
    pack(agg, agg_bf, q, n)
    s3[...] = s[3]


def group_mine_kernel(base, agg, s3, s23, c, c_t, mine):
    hi, lo, q = where_am_i()

    @pl.when(lo == 0)
    def _():
        mine[...] = agg[...]

    @pl.when(lo == 1)
    def _():
        mine[...] = base[...] + sandwich(s23[...], c[1, q], c_t[1])

    @pl.when(lo == 2)
    def _():
        mine[...] = base[...] + sandwich(s3[...], c[2, q], c_t[2])

    @pl.when(lo == 3)
    def _():
        mine[...] = base[...]


def is_lower(bit):
    hi, lo, q = where_am_i()
    return lax.rem(hi // (1 << bit), 2) == 0


def panel_rows(q, r, n, w):
    return pl.ds(pl.multiple_of(lax.rem(q + r, n) * w, w), w)


def quarter_rows(place, nb):
    rows = nb // GROUP
    return pl.ds(pl.multiple_of(place * rows, rows), rows)


def times(pieces, right, q):
    n = len(pieces)
    w = right.shape[0] // n
    return sum(mm(x[...], right[panel_rows(q, r, n, w), :]) for r, x in enumerate(pieces))


def place_whole(pieces, dst, q):
    for r, piece in enumerate(pieces):
        dst[lax.rem(q + r, len(pieces))] = piece[...]


def join_kernel(*refs):
    *quarters, out = refs
    hi, lo, q = where_am_i()
    for k, piece in enumerate(quarters):
        out[quarter_rows(jnp.bitwise_xor(lo, k), out.shape[0]), :] = piece[...]


def share_comp_kernel(n, bit, agg, got, *refs):
    quarters, (share,) = split(refs, n, 1)
    hi, lo, q = where_am_i()
    lower = is_lower(bit)
    nb, w = got.shape

    @pl.when(lower)
    def _():
        share[...] = times(quarters, agg.at[q], q).astype(BF)

    @pl.when(jnp.logical_not(lower))
    def _():
        rows = quarter_rows(lo, nb)
        share[...] = sum(
            mm(agg[p, rows, :], got[p * w : (p + 1) * w, :]) for p in range(n)
        ).astype(BF)


def pair_comp_kernel(n, bit, *refs):
    (agg,), parts, (new_agg, new_agg_t, share), (got,) = split(refs, 1, n, 3, 1)
    hi, lo, q = where_am_i()
    lower = is_lower(bit)
    place_whole(parts, got, q)

    @pl.when(lower)
    def _():
        put(new_agg, mm(whole(got), whole(agg)))

    @pl.when(jnp.logical_not(lower))
    def _():
        put(new_agg, mm(whole(agg), whole(got)))

    new_agg_t[...] = whole(new_agg).T
    share[...] = new_agg[q, quarter_rows(lo, new_agg.shape[1]), :]


def mine_comp_kernel(n, bit, *refs):
    (mine, mine_t), parts, (new_mine, new_mine_t) = split(refs, 2, n, 2)
    hi, lo, q = where_am_i()
    lower = is_lower(bit)

    @pl.when(lower)
    def _():
        for p in range(n):
            new_mine[p] = times(parts, mine.at[p], q).astype(BF)
        new_mine_t[...] = whole(new_mine).T

    @pl.when(jnp.logical_not(lower))
    def _():
        new_mine[...] = mine[...]
        new_mine_t[...] = mine_t[...]


def last_comp_kernel(n, bit, *refs):
    (mine,), parts, (out,) = split(refs, 1, n, 1)
    hi, lo, q = where_am_i()
    lower = is_lower(bit)

    @pl.when(lower)
    def _():
        out[0] = times(parts, mine.at[q], q).astype(BF)

    @pl.when(jnp.logical_not(lower))
    def _():
        out[0] = mine[q]


def pair_cov_kernel(n, bit, to_last, *refs):
    ins, here, c_parts, parts, outs, scratch = split(refs, 3, n, n, n, 2 if to_last else 4, 5)
    agg, agg_c, agg_t = ins
    share, right = outs[:2]
    sent, mid, total, got, packed = scratch
    hi, lo, q = where_am_i()
    lower = is_lower(bit)
    nb, w = agg.shape
    place_whole(parts, sent, q)
    unpack(sent, right, n)

    @pl.when(lower)
    def _():
        total[...] = agg[...] + sandwich(right[...], agg_c[q], agg_t[...])

    @pl.when(jnp.logical_not(lower))
    def _():
        def use(columns):
            total[...] = columns.astype(F32)

        panel_of(right, q, n, use)
        place_whole(here, sent, q)
        unpack(sent, right, n)
        place_whole(c_parts, got, q)
        mid[...] = mm(right[...], got[q]).astype(BF)
        for p in range(n):
            total[p * w : (p + 1) * w, :] += mm_t(got[p], mid[...])

    pack(total, packed, q, n)
    share[...] = packed[quarter_rows(lo, packed.shape[0]), :]
    if not to_last:
        new_agg, new_agg_bf = outs[2:]
        new_agg[...] = total[...]
        new_agg_bf[...] = packed[...]


def mine_cov_kernel(n, bit, cov, mine, mine_t, right, out):
    hi, lo, q = where_am_i()
    lower = is_lower(bit)

    @pl.when(lower)
    def _():
        out[...] = cov[...] + sandwich(right[...], mine[q], mine_t[...])

    @pl.when(jnp.logical_not(lower))
    def _():
        out[...] = cov[...]


def last_cov_kernel(n, bit, *refs):
    (cov, mine, mine_t), parts, (out,), (sent, right) = split(refs, 3, n, 1, 2)
    hi, lo, q = where_am_i()
    lower = is_lower(bit)

    @pl.when(lower)
    def _():
        place_whole(parts, sent, q)
        unpack(sent, right, n)
        out[0] = cov[...] + sandwich(right[...], mine[q], mine_t[...])

    @pl.when(jnp.logical_not(lower))
    def _():
        out[0] = cov[...]


def over_panels(x):
    n = lax.axis_size("panel")
    return [x] + [
        lax.ppermute(x, "panel", [((i + r) % n, i) for i in range(n)]) for r in range(1, n)
    ]


def swap(value, odd_mask, even_mask):
    steps, n = lax.axis_size("tm"), lax.axis_size("panel")
    pairs = []
    for t in range(steps):
        for q in range(n):
            mask = odd_mask if q % 2 else even_mask
            pairs.append((t * n + q, (t ^ mask) * n + q))
    return lax.ppermute(value, ("tm", "panel"), pairs)


def across(x, bit, last):
    steps = lax.axis_size("tm")
    d = GROUP << bit
    return lax.ppermute(
        x, "tm", [(t, t ^ d) for t in range(steps) if (t ^ d) < steps and (t & d or not last)]
    )


def in_group(x):
    return [x] + [swap(x, mask, mask) for mask in range(1, GROUP)]


def joined(quarters):
    rows, lanes = quarters[0].shape
    whole_panel = jax.ShapeDtypeStruct((rows * GROUP, lanes), BF)
    return call(join_kernel, quarters, [VMEM] * GROUP, [whole_panel], [], 0)[0]


def after(x, *others):
    return lax.optimization_barrier((x, *others))[0]


def shards(factor_inverse, coupling, sigma_after):
    steps = lax.axis_size("tm")
    n = lax.axis_size("panel")
    nb, w = factor_inverse.shape[1:]
    levels = (steps // GROUP - 1).bit_length()
    panel_bf = jax.ShapeDtypeStruct((nb, w), BF)
    panel_f32 = jax.ShapeDtypeStruct((nb, w), F32)
    full_bf = jax.ShapeDtypeStruct((n, nb, w), BF)
    square_bf = jax.ShapeDtypeStruct((nb, nb), BF)
    group_bf = jax.ShapeDtypeStruct((GROUP, n, nb, w), BF)
    turned_bf = jax.ShapeDtypeStruct((GROUP, nb, nb), BF)
    share_bf = jax.ShapeDtypeStruct((nb // GROUP, w), BF)
    full_scratch = pltpu.VMEM((n, nb, w), BF)
    rows, lanes = packed_shape(n, nb, w)
    packed_bf = jax.ShapeDtypeStruct((rows, lanes), BF)
    packed_share = jax.ShapeDtypeStruct((rows // GROUP, lanes), BF)
    packed_scratch = pltpu.VMEM((n, rows, lanes), BF)
    square_scratch = pltpu.VMEM((nb, nb), BF)
    one = 2 * nb * nb * w
    sems = pltpu.SemaphoreType.DMA

    comp = coupling[0].astype(BF)
    c_first = swap(comp, 1, 2)
    c_second = swap(comp, 2, 1)
    factor = after(factor_inverse[0], comp)
    f_parts = over_panels(factor.astype(BF))
    c_own = over_panels(comp)
    base, base_bf = call(
        functools.partial(base_kernel, n),
        [factor, sigma_after, *f_parts, *c_own],
        [VMEM] + [ANY] * (1 + 2 * n),
        [panel_f32, packed_bf],
        [full_scratch, full_scratch, pltpu.VMEM((nb, n * w), F32), sems((n + 1,))],
        2 * one,
    )
    s_first = swap(base_bf, 1, 2)
    c_diag = swap(after(c_first, s_first), 2, 1)
    s_second = swap(base_bf, 2, 1)
    s_diag = swap(s_first, 2, 1)
    c_near = [p for v in (c_first, c_second) for p in over_panels(v)]
    c_all, c_t, pair = call(
        functools.partial(near_comp_kernel, n),
        c_own + c_near,
        [ANY] * (3 * n),
        [group_bf, turned_bf, square_bf],
        [sems((3 * n,))],
        n * one,
    )
    c_all, c01, c23, agg_c = call(
        functools.partial(group_comp_kernel, n),
        [c_all, pair, *over_panels(after(c_diag, s_second, s_diag, pair))],
        [VMEM] * 2 + [ANY] * n,
        [group_bf, full_bf, square_bf, full_bf],
        [square_scratch, sems((n,))],
        2 * n * one,
        {0: 0},
    )
    agg_panel = lax.dynamic_index_in_dim(agg_c, lax.axis_index("panel"), 0, keepdims=False)
    c_got = across(agg_panel, 0, levels == 1)
    c_t, c01_t = call(
        turn_comp_kernel,
        [c_all, c_t, c01],
        [VMEM] * 3,
        [turned_bf, square_bf],
        [],
        0,
        {1: 0},
    )
    s_diag = after(s_diag, agg_panel)
    s_pieces = [p for v in (base_bf, s_first, s_second, s_diag) for p in over_panels(v)]
    agg, agg_bf, s3, s23 = call(
        functools.partial(group_cov_kernel, n),
        [base, c_all, c_t, c01, c01_t, *s_pieces],
        [VMEM] * 5 + [ANY] * (GROUP * n),
        [panel_f32, packed_bf, square_bf, square_bf],
        [
            pltpu.VMEM((GROUP, n, rows, lanes), BF),
            pltpu.VMEM((GROUP, nb, nb), BF),
            sems((GROUP, n)),
        ],
        (2 * n + 4) * one,
    )
    mine, mine_t, agg_t = call(
        tail_comp_kernel,
        [c_all, c_t, c23, after(agg_c, agg_bf)],
        [VMEM] * 4,
        [full_bf, square_bf, square_bf],
        [],
        n * one,
    )
    (cov,) = call(
        group_mine_kernel,
        [base, agg, s3, s23, c_all, c_t],
        [VMEM] * 6,
        [panel_f32],
        [],
        2 * one,
    )
    out_cov = jax.ShapeDtypeStruct((1, nb, w), F32)
    out_comp = jax.ShapeDtypeStruct((1, nb, w), BF)
    panel_scratch = pltpu.VMEM((nb, w), BF)
    sum_scratch = pltpu.VMEM((nb, w), F32)
    c_got = after(c_got, agg_bf)
    c_parts = over_panels(c_got)
    s_got = across(agg_bf, 0, levels == 1)
    for bit in range(levels):
        last = bit + 1 == levels
        to_last = bit + 2 == levels
        if last:
            (prop,) = call(
                functools.partial(last_comp_kernel, n, bit),
                [after(mine, s_got), *c_parts],
                [VMEM] * (1 + n),
                [out_comp],
                [],
                one,
            )
            s_parts = over_panels(s_got)
            (cov,) = call(
                functools.partial(last_cov_kernel, n, bit),
                [cov, mine, mine_t, *s_parts],
                [VMEM] * (3 + n),
                [out_cov],
                [packed_scratch, square_scratch],
                2 * one,
            )
            break
        agg_in = after(agg_c, agg_bf)
        if to_last:
            at = lax.rem(lax.axis_index("tm"), GROUP) * (nb // GROUP)
            quarter = lax.dynamic_slice_in_dim(c_got, at, nb // GROUP, 0)
            (c_send,) = call(
                functools.partial(share_comp_kernel, n, bit),
                [agg_in, c_got, *over_panels(quarter)],
                [VMEM] * (2 + n),
                [share_bf],
                [],
                one // 4,
            )
        else:
            new_agg_c, new_agg_t, c_send = call(
                functools.partial(pair_comp_kernel, n, bit),
                [agg_in, *c_parts],
                [VMEM] * (1 + n),
                [full_bf, square_bf, share_bf],
                [full_scratch],
                n * one,
            )
        c_far = across(c_send, bit + 1, to_last)
        new_mine, new_mine_t = call(
            functools.partial(mine_comp_kernel, n, bit),
            [after(mine, c_send), mine_t, *c_parts],
            [VMEM] * (2 + n),
            [full_bf, square_bf],
            [],
            n * one,
        )
        s_parts = over_panels(after(s_got, c_far, mine, cov))
        outs = call(
            functools.partial(pair_cov_kernel, n, bit, to_last),
            [agg, agg_c, agg_t, *over_panels(agg_bf), *c_parts, *s_parts],
            [VMEM] * (3 + 3 * n),
            [packed_share, square_bf] + ([] if to_last else [panel_f32, packed_bf]),
            [
                packed_scratch,
                panel_scratch,
                sum_scratch,
                full_scratch,
                pltpu.VMEM((rows, lanes), BF),
            ],
            2 * one,
        )
        s_send, right = outs[:2]
        s_far = across(s_send, bit + 1, to_last)
        (cov,) = call(
            functools.partial(mine_cov_kernel, n, bit),
            [cov, mine, mine_t, right],
            [VMEM] * 4,
            [panel_f32],
            [],
            2 * one,
        )
        if not to_last:
            agg, agg_bf = outs[2:]
            agg_c, agg_t = new_agg_c, new_agg_t
        s_blocks = in_group(s_far)
        s_got = joined(s_blocks)
        c_blocks = in_group(after(c_far, s_send))
        c_blocks[0] = after(c_blocks[0], cov, new_mine)
        c_got = after(joined(c_blocks), *s_blocks[1:])
        c_parts = over_panels(c_got)
        mine, mine_t = new_mine, new_mine_t
    return cov, prop


def solution(mesh):
    placed = (P("tm", None, "panel"), P("tm", None, "panel"), P())
    return jax.shard_map(
        shards,
        mesh=mesh,
        in_specs=placed,
        out_specs=(P("tm", None, "panel"), P("tm", None, "panel")),
        check_vma=False,
    )
```

```python
import functools

import jax
import jax.numpy as jnp
from jax import lax
from jax.experimental import pallas as pl
from jax.experimental.pallas import tpu as pltpu
from jax.sharding import PartitionSpec as P

BF = jnp.bfloat16
F32 = jnp.float32
GROUP = 4
BLOCK = 128
ANY = pl.BlockSpec(memory_space=pl.ANY)
VMEM = pl.BlockSpec(memory_space=pltpu.VMEM)
MIB = 1 << 20


def mm(a, b):
    return jnp.dot(a, b, preferred_element_type=F32)


def mm_t(a, b):
    return lax.dot_general(a, b, (((0,), (0,)), ((), ())), preferred_element_type=F32)


def whole(ref):
    return jnp.concatenate([ref[p] for p in range(ref.shape[0])], axis=1)


def put(ref, value):
    width = ref.shape[2]
    for p in range(ref.shape[0]):
        ref[p] = value[:, p * width : (p + 1) * width].astype(ref.dtype)


def where_am_i():
    t = lax.axis_index("tm")
    return t // GROUP, lax.rem(t, GROUP), lax.axis_index("panel")


def run(copies):
    for c in copies:
        c.start()
    for c in copies:
        c.wait()


def copy_all(pairs, sems):
    return [pltpu.make_async_copy(s, d, sems.at[i]) for i, (s, d) in enumerate(pairs)]


def panel_pairs(pieces, dst, q):
    n = len(pieces)
    return [(piece, dst.at[lax.rem(q + r, n)]) for r, piece in enumerate(pieces)]


def group_start(blocks, dst, sems, lo, q):
    own, first, second, diag = blocks
    n = len(own)
    for r in range(n):
        p = lax.rem(q + r, n)
        even = 1 - lax.rem(p, 2)
        for mask, piece in ((3, diag[r]), (1 + even, first[r]), (2 - even, second[r]), (0, own[r])):
            slot = jnp.bitwise_xor(lo, mask)
            pltpu.make_async_copy(piece, dst.at[slot, p], sems.at[slot, p]).start()


def group_wait(own, dst, sems, *slots):
    for slot in slots:
        for p in range(len(own)):
            pltpu.make_async_copy(own[p], dst.at[slot, p], sems.at[slot, p]).wait()


def packs(n, w):
    return n == 2 and w % BLOCK == 0


def packed_shape(n, nb, w):
    if not packs(n, w):
        return nb, w
    k = w // BLOCK
    return (k * (k + 1) // 2 + (k * k + 1) // 2) * BLOCK, BLOCK


def triangle(k):
    return [(i, j) for i in range(k) for j in range(i + 1)]


def halves(k):
    every = [(a, b) for a in range(k) for b in range(k)]
    half = (k * k + 1) // 2
    return every[:half], every[k * k - half :]


def pack(panel, out, q, n):
    nb, w = panel.shape
    if not packs(n, w):
        out[...] = panel[...].astype(BF)
        return
    k = w // BLOCK
    at = 0
    for i, j in triangle(k):
        rows = pl.ds(pl.multiple_of(q * w + i * BLOCK, BLOCK), BLOCK)
        out[at : at + BLOCK, :] = panel[rows, j * BLOCK : (j + 1) * BLOCK].astype(BF)
        at += BLOCK
    for side, blocks in enumerate(halves(k)):

        @pl.when(q == side)
        def _():
            to = at
            for a, b in blocks:
                i, j = (b, a) if side else (w // BLOCK + a, b)
                value = panel[i * BLOCK : (i + 1) * BLOCK, j * BLOCK : (j + 1) * BLOCK]
                out[to : to + BLOCK, :] = value.astype(BF)
                to += BLOCK


def unpack(src, dst, n):
    nb = dst.shape[0]
    w = nb // n
    if not packs(n, w):
        dst[...] = whole(src)
        return
    k = w // BLOCK

    def both(block, i, j):
        dst[i * BLOCK : (i + 1) * BLOCK, j * BLOCK : (j + 1) * BLOCK] = block
        if i != j:
            dst[j * BLOCK : (j + 1) * BLOCK, i * BLOCK : (i + 1) * BLOCK] = block.T

    seen = set()
    for p in range(n):
        at = 0
        for i, j in triangle(k):
            both(src[p, at : at + BLOCK, :], p * k + i, p * k + j)
            at += BLOCK
        for a, b in halves(k)[p]:
            if (a, b) not in seen:
                i, j = (b, k + a) if p else (k + a, b)
                both(src[p, at : at + BLOCK, :], i, j)
            seen.add((a, b))
            at += BLOCK


def panel_of(matrix, q, n, use):
    w = matrix.shape[1] // n
    for p in range(n):

        @pl.when(q == p)
        def _():
            use(matrix[:, p * w : (p + 1) * w])


def split(refs, *counts):
    out, at = [], 0
    for c in counts:
        out.append(refs[at : at + c])
        at += c
    return out


def call(kernel, ins, in_specs, outs, scratch, flops):
    size = sum(a.size * a.dtype.itemsize for a in ins) + sum(
        o.size * o.dtype.itemsize for o in outs
    )
    return pl.pallas_call(
        kernel,
        in_specs=in_specs,
        out_specs=[VMEM] * len(outs),
        out_shape=outs,
        scratch_shapes=scratch,
        compiler_params=pltpu.CompilerParams(vmem_limit_bytes=24 * MIB),
        cost_estimate=pl.CostEstimate(flops=flops, bytes_accessed=size, transcendentals=0),
    )(*ins)


def base_kernel(n, *refs):
    factor, sigma, f_parts, c_parts, (base, base_bf), (f_all, c_all, sig, sems) = split(
        refs, 1, 1, n, n, 2, 4
    )
    factor, sigma = factor[0], sigma[0]
    hi, lo, q = where_am_i()
    width = factor.shape[1]
    run(copy_all(panel_pairs(f_parts, f_all, q), sems))
    own = factor[...]
    high = own.astype(BF)
    low = (own - high.astype(F32)).astype(BF)
    for p in range(n):
        part = f_all[p]
        base[p * width : (p + 1) * width, :] = mm_t(part, high) + mm_t(part, low)

    @pl.when(lax.axis_index("tm") == lax.axis_size("tm") - 1)
    def _():
        run(copy_all(panel_pairs(c_parts, c_all, q) + [(sigma, sig)], sems))
        s = sig[...]
        s_high = s.astype(BF)
        s_low = (s - s_high.astype(F32)).astype(BF)
        c_own = c_all[q]
        mid = mm(s_high, c_own) + mm(s_low, c_own)
        mid_high = mid.astype(BF)
        mid_low = (mid - mid_high.astype(F32)).astype(BF)
        c_full = whole(c_all)
        base[...] += mm_t(c_full, mid_high) + mm_t(c_full, mid_low)

    pack(base, base_bf, q, n)


def pair_product(c, member):
    odd = lax.rem(member, 2)
    return mm(whole(c.at[member - odd + 1]), whole(c.at[member - odd])).astype(BF)


def near_comp_kernel(n, *refs):
    own, first, second, (pair,), (c, sems) = split(refs, n, n, n, 1, 2)
    hi, lo, q = where_am_i()
    pairs = []
    for r in range(n):
        p = lax.rem(q + r, n)
        even = 1 - lax.rem(p, 2)
        for mask, piece in ((0, own[r]), (1 + even, first[r]), (2 - even, second[r])):
            pairs.append((piece, c.at[jnp.bitwise_xor(lo, mask), p]))
    run(copy_all(pairs, sems))
    pair[...] = pair_product(c, lo)


def group_comp_kernel(n, *refs):
    (pair,), *blocks, outs, (other, sems) = split(refs, 1, n, n, n, n, 4, 2)
    c, c01, c23, agg = outs
    hi, lo, q = where_am_i()
    group_start(blocks, c, sems, lo, q)
    far = jnp.bitwise_xor(lo, 3)
    group_wait(blocks[0], c, sems, far, jnp.bitwise_xor(lo, 2))
    other[...] = pair_product(c, far)

    @pl.when(lo < 2)
    def _():
        put(c01, pair[...])
        c23[...] = other[...]

    @pl.when(lo >= 2)
    def _():
        put(c01, other[...])
        c23[...] = pair[...]

    put(agg, mm(c23[...], whole(c01)))
    group_wait(blocks[0], c, sems, lo, jnp.bitwise_xor(lo, 1))


def turn_comp_kernel(c, c01, c0_t, c2_t, c01_t):
    c0_t[...] = whole(c.at[0]).T
    c2_t[...] = whole(c.at[2]).T
    c01_t[...] = whole(c01).T


def tail_comp_kernel(c, c23, agg, mine, mine_t, agg_t):
    hi, lo, q = where_am_i()
    agg_t[...] = whole(agg).T

    @pl.when(lo == 0)
    def _():
        mine[...] = agg[...]

    @pl.when(lo == 1)
    def _():
        put(mine, mm(c23[...], whole(c.at[1])))

    @pl.when(lo == 2)
    def _():
        put(mine, c23[...])

    @pl.when(lo == 3)
    def _():
        mine[...] = c[3]

    mine_t[...] = whole(mine).T


def sandwich(cov, comp, comp_t):
    return mm(comp_t, mm(cov, comp).astype(BF))


def group_cov_kernel(n, *refs):
    ins, *blocks, outs, scratch = split(refs, 6, n, n, n, n, 4, 3)
    base, c, c0_t, c2_t, c01, c01_t = ins
    agg, agg_bf, s3, s23 = outs
    sent, s, sems = scratch
    hi, lo, q = where_am_i()
    group_start(blocks, sent, sems, lo, q)
    group_wait(blocks[0], sent, sems, 3, 2, 1, 0)
    unpack(sent.at[3], s3, n)
    for k in range(GROUP - 1):
        unpack(sent.at[k], s.at[k], n)
    mid = mm(s3[...], whole(c.at[2])).astype(BF)
    s23[...] = (s[2].astype(F32) + mm(c2_t[...], mid)).astype(BF)
    w = agg.shape[1]
    first = s[0, :, :w]
    for p in range(1, n):
        first = jnp.where(q == p, s[0, :, p * w : (p + 1) * w], first)
    total = jnp.where(lo == 0, base[...], first.astype(F32))
    total += sandwich(s[1], c[0, q], c0_t[...])
    agg[...] = total + sandwich(s23[...], c01[q], c01_t[...])
    pack(agg, agg_bf, q, n)


def group_mine_kernel(base, agg, s3, s23, c, mine):
    hi, lo, q = where_am_i()

    @pl.when(lo == 0)
    def _():
        mine[...] = agg[...]

    @pl.when(lo == 1)
    def _():
        mine[...] = base[...] + sandwich(s23[...], c[1, q], whole(c.at[1]).T)

    @pl.when(lo == 2)
    def _():
        mine[...] = base[...] + sandwich(s3[...], c[2, q], whole(c.at[2]).T)

    @pl.when(lo == 3)
    def _():
        mine[...] = base[...]


def is_lower(bit):
    hi, lo, q = where_am_i()
    return lax.rem(hi // (1 << bit), 2) == 0


def panel_rows(q, r, n, w):
    return pl.ds(pl.multiple_of(lax.rem(q + r, n) * w, w), w)


def quarter_rows(place, nb):
    rows = nb // GROUP
    return pl.ds(pl.multiple_of(place * rows, rows), rows)


def times(pieces, right, q):
    n = len(pieces)
    w = right.shape[0] // n
    return sum(mm(x[...], right[panel_rows(q, r, n, w), :]) for r, x in enumerate(pieces))


def place_whole(pieces, dst, q):
    for r, piece in enumerate(pieces):
        dst[lax.rem(q + r, len(pieces))] = piece[...]


def join_kernel(*refs):
    *quarters, out = refs
    hi, lo, q = where_am_i()
    for k, piece in enumerate(quarters):
        out[quarter_rows(jnp.bitwise_xor(lo, k), out.shape[0]), :] = piece[...]


def share_comp_kernel(n, bit, agg, got, *refs):
    quarters, (share,) = split(refs, n, 1)
    hi, lo, q = where_am_i()
    lower = is_lower(bit)
    nb, w = got.shape

    @pl.when(lower)
    def _():
        share[...] = times(quarters, agg.at[q], q).astype(BF)

    @pl.when(jnp.logical_not(lower))
    def _():
        rows = quarter_rows(lo, nb)
        share[...] = sum(
            mm(agg[p, rows, :], got[p * w : (p + 1) * w, :]) for p in range(n)
        ).astype(BF)


def pair_comp_kernel(n, bit, *refs):
    (agg,), parts, (new_agg, new_agg_t, share), (got,) = split(refs, 1, n, 3, 1)
    hi, lo, q = where_am_i()
    lower = is_lower(bit)
    place_whole(parts, got, q)

    @pl.when(lower)
    def _():
        put(new_agg, mm(whole(got), whole(agg)))

    @pl.when(jnp.logical_not(lower))
    def _():
        put(new_agg, mm(whole(agg), whole(got)))

    new_agg_t[...] = whole(new_agg).T
    share[...] = new_agg[q, quarter_rows(lo, new_agg.shape[1]), :]


def mine_comp_kernel(n, bit, *refs):
    (mine, mine_t), parts, (new_mine, new_mine_t) = split(refs, 2, n, 2)
    hi, lo, q = where_am_i()
    lower = is_lower(bit)

    @pl.when(lower)
    def _():
        for p in range(n):
            new_mine[p] = times(parts, mine.at[p], q).astype(BF)
        new_mine_t[...] = whole(new_mine).T

    @pl.when(jnp.logical_not(lower))
    def _():
        new_mine[...] = mine[...]
        new_mine_t[...] = mine_t[...]


def last_comp_kernel(n, bit, *refs):
    (mine,), parts, (out,) = split(refs, 1, n, 1)
    hi, lo, q = where_am_i()
    lower = is_lower(bit)

    @pl.when(lower)
    def _():
        out[0] = times(parts, mine.at[q], q).astype(BF)

    @pl.when(jnp.logical_not(lower))
    def _():
        out[0] = mine[q]


def pair_cov_kernel(n, bit, to_last, *refs):
    ins, here, c_parts, parts, outs, scratch = split(refs, 3, n, n, n, 2 if to_last else 4, 5)
    agg, agg_c, agg_t = ins
    share, right = outs[:2]
    sent, mid, total, got, packed = scratch
    hi, lo, q = where_am_i()
    lower = is_lower(bit)
    nb, w = agg.shape
    place_whole(parts, sent, q)
    unpack(sent, right, n)

    @pl.when(lower)
    def _():
        total[...] = agg[...] + sandwich(right[...], agg_c[q], agg_t[...])

    @pl.when(jnp.logical_not(lower))
    def _():
        def use(columns):
            total[...] = columns.astype(F32)

        panel_of(right, q, n, use)
        place_whole(here, sent, q)
        unpack(sent, right, n)
        place_whole(c_parts, got, q)
        mid[...] = mm(right[...], got[q]).astype(BF)
        for p in range(n):
            total[p * w : (p + 1) * w, :] += mm_t(got[p], mid[...])

    pack(total, packed, q, n)
    share[...] = packed[quarter_rows(lo, packed.shape[0]), :]
    if not to_last:
        new_agg, new_agg_bf = outs[2:]
        new_agg[...] = total[...]
        new_agg_bf[...] = packed[...]


def mine_cov_kernel(n, bit, cov, mine, mine_t, right, out):
    hi, lo, q = where_am_i()
    lower = is_lower(bit)

    @pl.when(lower)
    def _():
        out[...] = cov[...] + sandwich(right[...], mine[q], mine_t[...])

    @pl.when(jnp.logical_not(lower))
    def _():
        out[...] = cov[...]


def last_cov_kernel(n, bit, *refs):
    (cov, mine, mine_t), parts, (out,), (sent, right) = split(refs, 3, n, 1, 2)
    hi, lo, q = where_am_i()
    lower = is_lower(bit)

    @pl.when(lower)
    def _():
        place_whole(parts, sent, q)
        unpack(sent, right, n)
        out[0] = cov[...] + sandwich(right[...], mine[q], mine_t[...])

    @pl.when(jnp.logical_not(lower))
    def _():
        out[0] = cov[...]


def over_panels(x):
    n = lax.axis_size("panel")
    return [x] + [
        lax.ppermute(x, "panel", [((i + r) % n, i) for i in range(n)]) for r in range(1, n)
    ]


def swap(value, odd_mask, even_mask):
    steps, n = lax.axis_size("tm"), lax.axis_size("panel")
    pairs = []
    for t in range(steps):
        for q in range(n):
            mask = odd_mask if q % 2 else even_mask
            pairs.append((t * n + q, (t ^ mask) * n + q))
    return lax.ppermute(value, ("tm", "panel"), pairs)


def across(x, bit, last):
    steps = lax.axis_size("tm")
    d = GROUP << bit
    return lax.ppermute(
        x, "tm", [(t, t ^ d) for t in range(steps) if (t ^ d) < steps and (t & d or not last)]
    )


def in_group(x):
    return [x] + [swap(x, mask, mask) for mask in range(1, GROUP)]


def joined(quarters):
    rows, lanes = quarters[0].shape
    whole_panel = jax.ShapeDtypeStruct((rows * GROUP, lanes), BF)
    return call(join_kernel, quarters, [VMEM] * GROUP, [whole_panel], [], 0)[0]


def after(x, *others):
    return lax.optimization_barrier((x, *others))[0]


def shards(factor_inverse, coupling, sigma_after):
    steps = lax.axis_size("tm")
    n = lax.axis_size("panel")
    nb, w = factor_inverse.shape[1:]
    levels = (steps // GROUP - 1).bit_length()
    panel_bf = jax.ShapeDtypeStruct((nb, w), BF)
    panel_f32 = jax.ShapeDtypeStruct((nb, w), F32)
    full_bf = jax.ShapeDtypeStruct((n, nb, w), BF)
    square_bf = jax.ShapeDtypeStruct((nb, nb), BF)
    group_bf = jax.ShapeDtypeStruct((GROUP, n, nb, w), BF)
    share_bf = jax.ShapeDtypeStruct((nb // GROUP, w), BF)
    full_scratch = pltpu.VMEM((n, nb, w), BF)
    rows, lanes = packed_shape(n, nb, w)
    packed_bf = jax.ShapeDtypeStruct((rows, lanes), BF)
    packed_share = jax.ShapeDtypeStruct((rows // GROUP, lanes), BF)
    packed_scratch = pltpu.VMEM((n, rows, lanes), BF)
    square_scratch = pltpu.VMEM((nb, nb), BF)
    one = 2 * nb * nb * w
    sems = pltpu.SemaphoreType.DMA

    comp = coupling[0].astype(BF)
    c_first = swap(comp, 1, 2)
    c_second = swap(comp, 2, 1)
    factor = after(factor_inverse[0], comp)
    f_parts = over_panels(factor.astype(BF))
    c_own = over_panels(comp)
    base, base_bf = call(
        functools.partial(base_kernel, n),
        [factor, sigma_after, *f_parts, *c_own],
        [VMEM] + [ANY] * (1 + 2 * n),
        [panel_f32, packed_bf],
        [full_scratch, full_scratch, pltpu.VMEM((nb, n * w), F32), sems((n + 1,))],
        2 * one,
    )
    s_first = swap(base_bf, 1, 2)
    c_diag = swap(after(c_first, s_first), 2, 1)
    s_second = swap(base_bf, 2, 1)
    s_diag = swap(s_first, 2, 1)
    c_near = [p for v in (c_first, c_second) for p in over_panels(v)]
    (pair,) = call(
        functools.partial(near_comp_kernel, n),
        c_own + c_near,
        [ANY] * (3 * n),
        [square_bf],
        [pltpu.VMEM((GROUP, n, nb, w), BF), sems((3 * n,))],
        n * one,
    )
    c_all, c01, c23, agg_c = call(
        functools.partial(group_comp_kernel, n),
        [pair, *c_own, *c_near, *over_panels(after(c_diag, s_second, s_diag, pair))],
        [VMEM] + [ANY] * (GROUP * n),
        [group_bf, full_bf, square_bf, full_bf],
        [square_scratch, sems((GROUP, n))],
        2 * n * one,
    )
    agg_panel = lax.dynamic_index_in_dim(agg_c, lax.axis_index("panel"), 0, keepdims=False)
    c_got = across(agg_panel, 0, levels == 1)
    c0_t, c2_t, c01_t = call(
        turn_comp_kernel, [c_all, c01], [VMEM] * 2, [square_bf] * 3, [], 0
    )
    s_diag = after(s_diag, agg_panel)
    s_pieces = [p for v in (base_bf, s_first, s_second, s_diag) for p in over_panels(v)]
    agg, agg_bf, s3, s23 = call(
        functools.partial(group_cov_kernel, n),
        [base, c_all, c0_t, c2_t, c01, c01_t, *s_pieces],
        [VMEM] * 6 + [ANY] * (GROUP * n),
        [panel_f32, packed_bf, square_bf, square_bf],
        [
            pltpu.VMEM((GROUP, n, rows, lanes), BF),
            pltpu.VMEM((GROUP - 1, nb, nb), BF),
            sems((GROUP, n)),
        ],
        (2 * n + 4) * one,
    )
    mine, mine_t, agg_t = call(
        tail_comp_kernel,
        [c_all, c23, after(agg_c, agg_bf)],
        [VMEM] * 3,
        [full_bf, square_bf, square_bf],
        [],
        n * one,
    )
    (cov,) = call(
        group_mine_kernel,
        [base, agg, s3, s23, c_all],
        [VMEM] * 5,
        [panel_f32],
        [],
        2 * one,
    )
    out_cov = jax.ShapeDtypeStruct((1, nb, w), F32)
    out_comp = jax.ShapeDtypeStruct((1, nb, w), BF)
    panel_scratch = pltpu.VMEM((nb, w), BF)
    sum_scratch = pltpu.VMEM((nb, w), F32)
    c_got = after(c_got, agg_bf)
    c_parts = over_panels(c_got)
    s_got = across(agg_bf, 0, levels == 1)
    for bit in range(levels):
        last = bit + 1 == levels
        to_last = bit + 2 == levels
        if last:
            (prop,) = call(
                functools.partial(last_comp_kernel, n, bit),
                [after(mine, s_got), *c_parts],
                [VMEM] * (1 + n),
                [out_comp],
                [],
                one,
            )
            s_parts = over_panels(s_got)
            (cov,) = call(
                functools.partial(last_cov_kernel, n, bit),
                [cov, mine, mine_t, *s_parts],
                [VMEM] * (3 + n),
                [out_cov],
                [packed_scratch, square_scratch],
                2 * one,
            )
            break
        agg_in = after(agg_c, agg_bf)
        if to_last:
            at = lax.rem(lax.axis_index("tm"), GROUP) * (nb // GROUP)
            quarter = lax.dynamic_slice_in_dim(c_got, at, nb // GROUP, 0)
            (c_send,) = call(
                functools.partial(share_comp_kernel, n, bit),
                [agg_in, c_got, *over_panels(quarter)],
                [VMEM] * (2 + n),
                [share_bf],
                [],
                one // 4,
            )
        else:
            new_agg_c, new_agg_t, c_send = call(
                functools.partial(pair_comp_kernel, n, bit),
                [agg_in, *c_parts],
                [VMEM] * (1 + n),
                [full_bf, square_bf, share_bf],
                [full_scratch],
                n * one,
            )
        c_far = across(c_send, bit + 1, to_last)
        new_mine, new_mine_t = call(
            functools.partial(mine_comp_kernel, n, bit),
            [after(mine, c_send), mine_t, *c_parts],
            [VMEM] * (2 + n),
            [full_bf, square_bf],
            [],
            n * one,
        )
        s_parts = over_panels(after(s_got, c_far, mine, cov))
        outs = call(
            functools.partial(pair_cov_kernel, n, bit, to_last),
            [agg, agg_c, agg_t, *over_panels(agg_bf), *c_parts, *s_parts],
            [VMEM] * (3 + 3 * n),
            [packed_share, square_bf] + ([] if to_last else [panel_f32, packed_bf]),
            [
                packed_scratch,
                panel_scratch,
                sum_scratch,
                full_scratch,
                pltpu.VMEM((rows, lanes), BF),
            ],
            2 * one,
        )
        s_send, right = outs[:2]
        s_far = across(s_send, bit + 1, to_last)
        (cov,) = call(
            functools.partial(mine_cov_kernel, n, bit),
            [cov, mine, mine_t, right],
            [VMEM] * 4,
            [panel_f32],
            [],
            2 * one,
        )
        if not to_last:
            agg, agg_bf = outs[2:]
            agg_c, agg_t = new_agg_c, new_agg_t
        s_blocks = in_group(s_far)
        s_got = joined(s_blocks)
        c_blocks = in_group(after(c_far, s_send))
        c_blocks[0] = after(c_blocks[0], cov, new_mine)
        c_got = after(joined(c_blocks), *s_blocks[1:])
        c_parts = over_panels(c_got)
        mine, mine_t = new_mine, new_mine_t
    return cov, prop


def solution(mesh):
    placed = (P("tm", None, "panel"), P("tm", None, "panel"), P())
    return jax.shard_map(
        shards,
        mesh=mesh,
        in_specs=placed,
        out_specs=(P("tm", None, "panel"), P("tm", None, "panel")),
        check_vma=False,
    )
```

```python
import functools

import jax
import jax.numpy as jnp
from jax import lax
from jax.experimental import pallas as pl
from jax.experimental.pallas import tpu as pltpu
from jax.sharding import PartitionSpec as P

BF = jnp.bfloat16
F32 = jnp.float32
GROUP = 4
BLOCK = 128
ANY = pl.BlockSpec(memory_space=pl.ANY)
VMEM = pl.BlockSpec(memory_space=pltpu.VMEM)
MIB = 1 << 20


def mm(a, b):
    return jnp.dot(a, b, preferred_element_type=F32)


def mm_t(a, b):
    return lax.dot_general(a, b, (((0,), (0,)), ((), ())), preferred_element_type=F32)


def whole(ref):
    return jnp.concatenate([ref[p] for p in range(ref.shape[0])], axis=1)


def put(ref, value):
    width = ref.shape[2]
    for p in range(ref.shape[0]):
        ref[p] = value[:, p * width : (p + 1) * width].astype(ref.dtype)


def where_am_i():
    t = lax.axis_index("tm")
    return t // GROUP, lax.rem(t, GROUP), lax.axis_index("panel")


def run(copies):
    for c in copies:
        c.start()
    for c in copies:
        c.wait()


def copy_all(pairs, sems):
    return [pltpu.make_async_copy(s, d, sems.at[i]) for i, (s, d) in enumerate(pairs)]


def panel_pairs(pieces, dst, q):
    n = len(pieces)
    return [(piece, dst.at[lax.rem(q + r, n)]) for r, piece in enumerate(pieces)]


def group_start(blocks, dst, sems, lo, q):
    own, first, second, diag = blocks
    n = len(own)
    for r in range(n):
        p = lax.rem(q + r, n)
        even = 1 - lax.rem(p, 2)
        for mask, piece in ((3, diag[r]), (1 + even, first[r]), (2 - even, second[r]), (0, own[r])):
            slot = jnp.bitwise_xor(lo, mask)
            pltpu.make_async_copy(piece, dst.at[slot, p], sems.at[slot, p]).start()


def group_wait(own, dst, sems, *slots):
    for slot in slots:
        for p in range(len(own)):
            pltpu.make_async_copy(own[p], dst.at[slot, p], sems.at[slot, p]).wait()


def packs(n, w):
    return n == 2 and w % BLOCK == 0


def packed_shape(n, nb, w):
    if not packs(n, w):
        return nb, w
    k = w // BLOCK
    return (k * (k + 1) // 2 + (k * k + 1) // 2) * BLOCK, BLOCK


def triangle(k):
    return [(i, j) for i in range(k) for j in range(i + 1)]


def halves(k):
    every = [(a, b) for a in range(k) for b in range(k)]
    half = (k * k + 1) // 2
    return every[:half], every[k * k - half :]


def pack(panel, out, q, n):
    nb, w = panel.shape
    if not packs(n, w):
        out[...] = panel[...].astype(BF)
        return
    k = w // BLOCK
    at = 0
    for i, j in triangle(k):
        rows = pl.ds(pl.multiple_of(q * w + i * BLOCK, BLOCK), BLOCK)
        out[at : at + BLOCK, :] = panel[rows, j * BLOCK : (j + 1) * BLOCK].astype(BF)
        at += BLOCK
    for side, blocks in enumerate(halves(k)):

        @pl.when(q == side)
        def _():
            to = at
            for a, b in blocks:
                i, j = (b, a) if side else (w // BLOCK + a, b)
                value = panel[i * BLOCK : (i + 1) * BLOCK, j * BLOCK : (j + 1) * BLOCK]
                out[to : to + BLOCK, :] = value.astype(BF)
                to += BLOCK


def unpack(src, dst, n):
    nb = dst.shape[0]
    w = nb // n
    if not packs(n, w):
        dst[...] = whole(src)
        return
    k = w // BLOCK

    def both(block, i, j):
        dst[i * BLOCK : (i + 1) * BLOCK, j * BLOCK : (j + 1) * BLOCK] = block
        if i != j:
            dst[j * BLOCK : (j + 1) * BLOCK, i * BLOCK : (i + 1) * BLOCK] = block.T

    seen = set()
    for p in range(n):
        at = 0
        for i, j in triangle(k):
            both(src[p, at : at + BLOCK, :], p * k + i, p * k + j)
            at += BLOCK
        for a, b in halves(k)[p]:
            if (a, b) not in seen:
                i, j = (b, k + a) if p else (k + a, b)
                both(src[p, at : at + BLOCK, :], i, j)
            seen.add((a, b))
            at += BLOCK


def panel_of(matrix, q, n, use):
    w = matrix.shape[1] // n
    for p in range(n):

        @pl.when(q == p)
        def _():
            use(matrix[:, p * w : (p + 1) * w])


def split(refs, *counts):
    out, at = [], 0
    for c in counts:
        out.append(refs[at : at + c])
        at += c
    return out


def call(kernel, ins, in_specs, outs, scratch, flops):
    size = sum(a.size * a.dtype.itemsize for a in ins) + sum(
        o.size * o.dtype.itemsize for o in outs
    )
    return pl.pallas_call(
        kernel,
        in_specs=in_specs,
        out_specs=[VMEM] * len(outs),
        out_shape=outs,
        scratch_shapes=scratch,
        compiler_params=pltpu.CompilerParams(vmem_limit_bytes=24 * MIB),
        cost_estimate=pl.CostEstimate(flops=flops, bytes_accessed=size, transcendentals=0),
    )(*ins)


def base_kernel(n, *refs):
    factor, sigma, f_parts, c_parts, (base, base_bf), (f_all, c_all, sig, sems) = split(
        refs, 1, 1, n, n, 2, 4
    )
    factor, sigma = factor[0], sigma[0]
    hi, lo, q = where_am_i()
    width = factor.shape[1]
    run(copy_all(panel_pairs(f_parts, f_all, q), sems))
    own = factor[...]
    high = own.astype(BF)
    low = (own - high.astype(F32)).astype(BF)
    for p in range(n):
        part = f_all[p]
        base[p * width : (p + 1) * width, :] = mm_t(part, high) + mm_t(part, low)

    @pl.when(lax.axis_index("tm") == lax.axis_size("tm") - 1)
    def _():
        run(copy_all(panel_pairs(c_parts, c_all, q) + [(sigma, sig)], sems))
        s = sig[...]
        s_high = s.astype(BF)
        s_low = (s - s_high.astype(F32)).astype(BF)
        c_own = c_all[q]
        mid = mm(s_high, c_own) + mm(s_low, c_own)
        mid_high = mid.astype(BF)
        mid_low = (mid - mid_high.astype(F32)).astype(BF)
        c_full = whole(c_all)
        base[...] += mm_t(c_full, mid_high) + mm_t(c_full, mid_low)

    pack(base, base_bf, q, n)


def pair_product(c, member):
    odd = lax.rem(member, 2)
    return mm(whole(c.at[member - odd + 1]), whole(c.at[member - odd])).astype(BF)


def near_comp_kernel(n, *refs):
    own, first, second, (pair,), (c, sems) = split(refs, n, n, n, 1, 2)
    hi, lo, q = where_am_i()
    pairs = []
    for r in range(n):
        p = lax.rem(q + r, n)
        even = 1 - lax.rem(p, 2)
        for mask, piece in ((0, own[r]), (1 + even, first[r]), (2 - even, second[r])):
            pairs.append((piece, c.at[jnp.bitwise_xor(lo, mask), p]))
    run(copy_all(pairs, sems))
    pair[...] = pair_product(c, lo)


def group_comp_kernel(n, *refs):
    (pair,), *blocks, outs, (other, sems) = split(refs, 1, n, n, n, n, 5, 2)
    c, c01, c23, agg, agg_panel = outs
    hi, lo, q = where_am_i()
    group_start(blocks, c, sems, lo, q)
    far = jnp.bitwise_xor(lo, 3)
    group_wait(blocks[0], c, sems, far, jnp.bitwise_xor(lo, 2))
    other[...] = pair_product(c, far)

    @pl.when(lo < 2)
    def _():
        put(c01, pair[...])
        c23[...] = other[...]

    @pl.when(lo >= 2)
    def _():
        put(c01, other[...])
        c23[...] = pair[...]

    put(agg, mm(c23[...], whole(c01)))
    agg_panel[...] = agg[q]
    group_wait(blocks[0], c, sems, lo, jnp.bitwise_xor(lo, 1))


def turn_comp_kernel(c, c01, c0_t, c2_t, c01_t):
    c0_t[...] = whole(c.at[0]).T
    c2_t[...] = whole(c.at[2]).T
    c01_t[...] = whole(c01).T


def tail_comp_kernel(c, c23, agg, mine, mine_t, agg_t):
    hi, lo, q = where_am_i()
    agg_t[...] = whole(agg).T

    @pl.when(lo == 0)
    def _():
        mine[...] = agg[...]

    @pl.when(lo == 1)
    def _():
        put(mine, mm(c23[...], whole(c.at[1])))

    @pl.when(lo == 2)
    def _():
        put(mine, c23[...])

    @pl.when(lo == 3)
    def _():
        mine[...] = c[3]

    mine_t[...] = whole(mine).T


def sandwich(cov, comp, comp_t):
    return mm(comp_t, mm(cov, comp).astype(BF))


def group_cov_kernel(n, *refs):
    ins, *blocks, outs, scratch = split(refs, 6, n, n, n, n, 4, 3)
    base, c, c0_t, c2_t, c01, c01_t = ins
    agg, agg_bf, s3, s23 = outs
    sent, s, sems = scratch
    hi, lo, q = where_am_i()
    group_start(blocks, sent, sems, lo, q)
    group_wait(blocks[0], sent, sems, 3, 2, 1, 0)
    unpack(sent.at[3], s3, n)
    for k in range(GROUP - 1):
        unpack(sent.at[k], s.at[k], n)
    mid = mm(s3[...], whole(c.at[2])).astype(BF)
    s23[...] = (s[2].astype(F32) + mm(c2_t[...], mid)).astype(BF)
    w = agg.shape[1]
    first = s[0, :, :w]
    for p in range(1, n):
        first = jnp.where(q == p, s[0, :, p * w : (p + 1) * w], first)
    total = jnp.where(lo == 0, base[...], first.astype(F32))
    total += sandwich(s[1], c[0, q], c0_t[...])
    agg[...] = total + sandwich(s23[...], c01[q], c01_t[...])
    pack(agg, agg_bf, q, n)


def group_mine_kernel(base, agg, s3, s23, c, mine):
    hi, lo, q = where_am_i()

    @pl.when(lo == 0)
    def _():
        mine[...] = agg[...]

    @pl.when(lo == 1)
    def _():
        mine[...] = base[...] + sandwich(s23[...], c[1, q], whole(c.at[1]).T)

    @pl.when(lo == 2)
    def _():
        mine[...] = base[...] + sandwich(s3[...], c[2, q], whole(c.at[2]).T)

    @pl.when(lo == 3)
    def _():
        mine[...] = base[...]


def is_lower(bit):
    hi, lo, q = where_am_i()
    return lax.rem(hi // (1 << bit), 2) == 0


def panel_rows(q, r, n, w):
    return pl.ds(pl.multiple_of(lax.rem(q + r, n) * w, w), w)


def quarter_rows(place, nb):
    rows = nb // GROUP
    return pl.ds(pl.multiple_of(place * rows, rows), rows)


def times(pieces, right, q):
    n = len(pieces)
    w = right.shape[0] // n
    return sum(mm(x[...], right[panel_rows(q, r, n, w), :]) for r, x in enumerate(pieces))


def place_whole(pieces, dst, q):
    for r, piece in enumerate(pieces):
        dst[lax.rem(q + r, len(pieces))] = piece[...]


def join_kernel(*refs):
    *quarters, out = refs
    hi, lo, q = where_am_i()
    for k, piece in enumerate(quarters):
        out[quarter_rows(jnp.bitwise_xor(lo, k), out.shape[0]), :] = piece[...]


def quarter_kernel(panel, out):
    hi, lo, q = where_am_i()
    out[...] = panel[quarter_rows(lo, panel.shape[0]), :]


def share_comp_kernel(n, bit, agg, got, *refs):
    quarters, (share,) = split(refs, n, 1)
    hi, lo, q = where_am_i()
    lower = is_lower(bit)
    nb, w = got.shape

    @pl.when(lower)
    def _():
        share[...] = times(quarters, agg.at[q], q).astype(BF)

    @pl.when(jnp.logical_not(lower))
    def _():
        rows = quarter_rows(lo, nb)
        share[...] = sum(
            mm(agg[p, rows, :], got[p * w : (p + 1) * w, :]) for p in range(n)
        ).astype(BF)


def pair_comp_kernel(n, bit, *refs):
    (agg,), parts, (new_agg, new_agg_t, share), (got,) = split(refs, 1, n, 3, 1)
    hi, lo, q = where_am_i()
    lower = is_lower(bit)
    place_whole(parts, got, q)

    @pl.when(lower)
    def _():
        put(new_agg, mm(whole(got), whole(agg)))

    @pl.when(jnp.logical_not(lower))
    def _():
        put(new_agg, mm(whole(agg), whole(got)))

    new_agg_t[...] = whole(new_agg).T
    share[...] = new_agg[q, quarter_rows(lo, new_agg.shape[1]), :]


def mine_comp_kernel(n, bit, *refs):
    (mine, mine_t), parts, (new_mine, new_mine_t) = split(refs, 2, n, 2)
    hi, lo, q = where_am_i()
    lower = is_lower(bit)

    @pl.when(lower)
    def _():
        for p in range(n):
            new_mine[p] = times(parts, mine.at[p], q).astype(BF)
        new_mine_t[...] = whole(new_mine).T

    @pl.when(jnp.logical_not(lower))
    def _():
        new_mine[...] = mine[...]
        new_mine_t[...] = mine_t[...]


def last_comp_kernel(n, bit, *refs):
    (mine,), parts, (out,) = split(refs, 1, n, 1)
    hi, lo, q = where_am_i()
    lower = is_lower(bit)

    @pl.when(lower)
    def _():
        out[0] = times(parts, mine.at[q], q).astype(BF)

    @pl.when(jnp.logical_not(lower))
    def _():
        out[0] = mine[q]


def pair_cov_kernel(n, bit, to_last, *refs):
    ins, here, c_parts, parts, outs, scratch = split(refs, 3, n, n, n, 2 if to_last else 4, 5)
    agg, agg_c, agg_t = ins
    share, right = outs[:2]
    sent, mid, total, got, packed = scratch
    hi, lo, q = where_am_i()
    lower = is_lower(bit)
    nb, w = agg.shape
    place_whole(parts, sent, q)
    unpack(sent, right, n)

    @pl.when(lower)
    def _():
        total[...] = agg[...] + sandwich(right[...], agg_c[q], agg_t[...])

    @pl.when(jnp.logical_not(lower))
    def _():
        def use(columns):
            total[...] = columns.astype(F32)

        panel_of(right, q, n, use)
        place_whole(here, sent, q)
        unpack(sent, right, n)
        place_whole(c_parts, got, q)
        mid[...] = mm(right[...], got[q]).astype(BF)
        for p in range(n):
            total[p * w : (p + 1) * w, :] += mm_t(got[p], mid[...])

    pack(total, packed, q, n)
    share[...] = packed[quarter_rows(lo, packed.shape[0]), :]
    if not to_last:
        new_agg, new_agg_bf = outs[2:]
        new_agg[...] = total[...]
        new_agg_bf[...] = packed[...]


def mine_cov_kernel(n, bit, cov, mine, mine_t, right, out):
    hi, lo, q = where_am_i()
    lower = is_lower(bit)

    @pl.when(lower)
    def _():
        out[...] = cov[...] + sandwich(right[...], mine[q], mine_t[...])

    @pl.when(jnp.logical_not(lower))
    def _():
        out[...] = cov[...]


def last_cov_kernel(n, bit, *refs):
    (cov, mine, mine_t), parts, (out,), (sent, right) = split(refs, 3, n, 1, 2)
    hi, lo, q = where_am_i()
    lower = is_lower(bit)

    @pl.when(lower)
    def _():
        place_whole(parts, sent, q)
        unpack(sent, right, n)
        out[0] = cov[...] + sandwich(right[...], mine[q], mine_t[...])

    @pl.when(jnp.logical_not(lower))
    def _():
        out[0] = cov[...]


def over_panels(x):
    n = lax.axis_size("panel")
    return [x] + [
        lax.ppermute(x, "panel", [((i + r) % n, i) for i in range(n)]) for r in range(1, n)
    ]


def swap(value, odd_mask, even_mask):
    steps, n = lax.axis_size("tm"), lax.axis_size("panel")
    pairs = []
    for t in range(steps):
        for q in range(n):
            mask = odd_mask if q % 2 else even_mask
            pairs.append((t * n + q, (t ^ mask) * n + q))
    return lax.ppermute(value, ("tm", "panel"), pairs)


def across(x, bit, last):
    steps = lax.axis_size("tm")
    d = GROUP << bit
    return lax.ppermute(
        x, "tm", [(t, t ^ d) for t in range(steps) if (t ^ d) < steps and (t & d or not last)]
    )


def in_group(x):
    return [x] + [swap(x, mask, mask) for mask in range(1, GROUP)]


def joined(quarters):
    rows, lanes = quarters[0].shape
    whole_panel = jax.ShapeDtypeStruct((rows * GROUP, lanes), BF)
    return call(join_kernel, quarters, [VMEM] * GROUP, [whole_panel], [], 0)[0]


def after(x, *others):
    return lax.optimization_barrier((x, *others))[0]


def shards(factor_inverse, coupling, sigma_after):
    steps = lax.axis_size("tm")
    n = lax.axis_size("panel")
    nb, w = factor_inverse.shape[1:]
    levels = (steps // GROUP - 1).bit_length()
    panel_bf = jax.ShapeDtypeStruct((nb, w), BF)
    panel_f32 = jax.ShapeDtypeStruct((nb, w), F32)
    full_bf = jax.ShapeDtypeStruct((n, nb, w), BF)
    square_bf = jax.ShapeDtypeStruct((nb, nb), BF)
    group_bf = jax.ShapeDtypeStruct((GROUP, n, nb, w), BF)
    share_bf = jax.ShapeDtypeStruct((nb // GROUP, w), BF)
    full_scratch = pltpu.VMEM((n, nb, w), BF)
    rows, lanes = packed_shape(n, nb, w)
    packed_bf = jax.ShapeDtypeStruct((rows, lanes), BF)
    packed_share = jax.ShapeDtypeStruct((rows // GROUP, lanes), BF)
    packed_scratch = pltpu.VMEM((n, rows, lanes), BF)
    square_scratch = pltpu.VMEM((nb, nb), BF)
    one = 2 * nb * nb * w
    sems = pltpu.SemaphoreType.DMA

    comp = coupling[0].astype(BF)
    c_first = swap(comp, 1, 2)
    c_second = swap(comp, 2, 1)
    factor = after(factor_inverse[0], comp)
    f_parts = over_panels(factor.astype(BF))
    c_own = over_panels(comp)
    base, base_bf = call(
        functools.partial(base_kernel, n),
        [factor, sigma_after, *f_parts, *c_own],
        [VMEM] + [ANY] * (1 + 2 * n),
        [panel_f32, packed_bf],
        [full_scratch, full_scratch, pltpu.VMEM((nb, n * w), F32), sems((n + 1,))],
        2 * one,
    )
    s_first = swap(base_bf, 1, 2)
    c_diag = swap(after(c_first, s_first), 2, 1)
    s_second = swap(base_bf, 2, 1)
    s_diag = swap(s_first, 2, 1)
    c_near = [p for v in (c_first, c_second) for p in over_panels(v)]
    (pair,) = call(
        functools.partial(near_comp_kernel, n),
        c_own + c_near,
        [ANY] * (3 * n),
        [square_bf],
        [pltpu.VMEM((GROUP, n, nb, w), BF), sems((3 * n,))],
        n * one,
    )
    c_all, c01, c23, agg_c, agg_panel = call(
        functools.partial(group_comp_kernel, n),
        [pair, *c_own, *c_near, *over_panels(after(c_diag, s_second, s_diag, pair))],
        [VMEM] + [ANY] * (GROUP * n),
        [group_bf, full_bf, square_bf, full_bf, panel_bf],
        [square_scratch, sems((GROUP, n))],
        2 * n * one,
    )
    c_got = across(agg_panel, 0, levels == 1)
    c0_t, c2_t, c01_t = call(
        turn_comp_kernel, [c_all, c01], [VMEM] * 2, [square_bf] * 3, [], 0
    )
    s_diag = after(s_diag, agg_panel)
    s_pieces = [p for v in (base_bf, s_first, s_second, s_diag) for p in over_panels(v)]
    agg, agg_bf, s3, s23 = call(
        functools.partial(group_cov_kernel, n),
        [base, c_all, c0_t, c2_t, c01, c01_t, *s_pieces],
        [VMEM] * 6 + [ANY] * (GROUP * n),
        [panel_f32, packed_bf, square_bf, square_bf],
        [
            pltpu.VMEM((GROUP, n, rows, lanes), BF),
            pltpu.VMEM((GROUP - 1, nb, nb), BF),
            sems((GROUP, n)),
        ],
        (2 * n + 4) * one,
    )
    mine, mine_t, agg_t = call(
        tail_comp_kernel,
        [c_all, c23, after(agg_c, agg_bf)],
        [VMEM] * 3,
        [full_bf, square_bf, square_bf],
        [],
        n * one,
    )
    (cov,) = call(
        group_mine_kernel,
        [base, agg, s3, s23, c_all],
        [VMEM] * 5,
        [panel_f32],
        [],
        2 * one,
    )
    out_cov = jax.ShapeDtypeStruct((1, nb, w), F32)
    out_comp = jax.ShapeDtypeStruct((1, nb, w), BF)
    panel_scratch = pltpu.VMEM((nb, w), BF)
    sum_scratch = pltpu.VMEM((nb, w), F32)
    c_got = after(c_got, agg_bf)
    c_parts = over_panels(c_got)
    s_got = across(agg_bf, 0, levels == 1)
    for bit in range(levels):
        last = bit + 1 == levels
        to_last = bit + 2 == levels
        if last:
            (prop,) = call(
                functools.partial(last_comp_kernel, n, bit),
                [after(mine, s_got), *c_parts],
                [VMEM] * (1 + n),
                [out_comp],
                [],
                one,
            )
            s_parts = over_panels(s_got)
            (cov,) = call(
                functools.partial(last_cov_kernel, n, bit),
                [cov, mine, mine_t, *s_parts],
                [VMEM] * (3 + n),
                [out_cov],
                [packed_scratch, square_scratch],
                2 * one,
            )
            break
        agg_in = after(agg_c, agg_bf)
        if to_last:
            (quarter,) = call(quarter_kernel, [c_got], [VMEM], [share_bf], [], 0)
            (c_send,) = call(
                functools.partial(share_comp_kernel, n, bit),
                [agg_in, c_got, *over_panels(quarter)],
                [VMEM] * (2 + n),
                [share_bf],
                [],
                one // 4,
            )
        else:
            new_agg_c, new_agg_t, c_send = call(
                functools.partial(pair_comp_kernel, n, bit),
                [agg_in, *c_parts],
                [VMEM] * (1 + n),
                [full_bf, square_bf, share_bf],
                [full_scratch],
                n * one,
            )
        c_far = across(c_send, bit + 1, to_last)
        new_mine, new_mine_t = call(
            functools.partial(mine_comp_kernel, n, bit),
            [after(mine, c_send), mine_t, *c_parts],
            [VMEM] * (2 + n),
            [full_bf, square_bf],
            [],
            n * one,
        )
        s_parts = over_panels(after(s_got, c_far, mine, cov))
        outs = call(
            functools.partial(pair_cov_kernel, n, bit, to_last),
            [agg, agg_c, agg_t, *over_panels(agg_bf), *c_parts, *s_parts],
            [VMEM] * (3 + 3 * n),
            [packed_share, square_bf] + ([] if to_last else [panel_f32, packed_bf]),
            [
                packed_scratch,
                panel_scratch,
                sum_scratch,
                full_scratch,
                pltpu.VMEM((rows, lanes), BF),
            ],
            2 * one,
        )
        s_send, right = outs[:2]
        s_far = across(s_send, bit + 1, to_last)
        (cov,) = call(
            functools.partial(mine_cov_kernel, n, bit),
            [cov, mine, mine_t, right],
            [VMEM] * 4,
            [panel_f32],
            [],
            2 * one,
        )
        if not to_last:
            agg, agg_bf = outs[2:]
            agg_c, agg_t = new_agg_c, new_agg_t
        s_blocks = in_group(s_far)
        s_got = joined(s_blocks)
        c_blocks = in_group(after(c_far, s_send))
        c_blocks[0] = after(c_blocks[0], cov, new_mine)
        c_got = after(joined(c_blocks), *s_blocks[1:])
        c_parts = over_panels(c_got)
        mine, mine_t = new_mine, new_mine_t
    return cov, prop


def solution(mesh):
    placed = (P("tm", None, "panel"), P("tm", None, "panel"), P())
    return jax.shard_map(
        shards,
        mesh=mesh,
        in_specs=placed,
        out_specs=(P("tm", None, "panel"), P("tm", None, "panel")),
        check_vma=False,
    )
```

```python
import functools

import jax
import jax.numpy as jnp
from jax import lax
from jax.experimental import pallas as pl
from jax.experimental.pallas import tpu as pltpu
from jax.sharding import PartitionSpec as P

BF = jnp.bfloat16
F32 = jnp.float32
GROUP = 4
BLOCK = 128
ANY = pl.BlockSpec(memory_space=pl.ANY)
VMEM = pl.BlockSpec(memory_space=pltpu.VMEM)
MIB = 1 << 20


def mm(a, b):
    return jnp.dot(a, b, preferred_element_type=F32)


def mm_t(a, b):
    return lax.dot_general(a, b, (((0,), (0,)), ((), ())), preferred_element_type=F32)


def whole(ref):
    return jnp.concatenate([ref[p] for p in range(ref.shape[0])], axis=1)


def put(ref, value):
    width = ref.shape[2]
    for p in range(ref.shape[0]):
        ref[p] = value[:, p * width : (p + 1) * width].astype(ref.dtype)


def where_am_i():
    t = lax.axis_index("tm")
    return t // GROUP, lax.rem(t, GROUP), lax.axis_index("panel")


def run(copies):
    for c in copies:
        c.start()
    for c in copies:
        c.wait()


def copy_all(pairs, sems):
    return [pltpu.make_async_copy(s, d, sems.at[i]) for i, (s, d) in enumerate(pairs)]


def panel_pairs(pieces, dst, q):
    n = len(pieces)
    return [(piece, dst.at[lax.rem(q + r, n)]) for r, piece in enumerate(pieces)]


def group_start(blocks, dst, sems, lo, q):
    own, first, second, diag = blocks
    n = len(own)
    for r in range(n):
        p = lax.rem(q + r, n)
        even = 1 - lax.rem(p, 2)
        for mask, piece in ((3, diag[r]), (1 + even, first[r]), (2 - even, second[r]), (0, own[r])):
            slot = jnp.bitwise_xor(lo, mask)
            pltpu.make_async_copy(piece, dst.at[slot, p], sems.at[slot, p]).start()


def group_wait(own, dst, sems, *slots):
    for slot in slots:
        for p in range(len(own)):
            pltpu.make_async_copy(own[p], dst.at[slot, p], sems.at[slot, p]).wait()


def packs(n, w):
    return n == 2 and w % BLOCK == 0


def packed_shape(n, nb, w):
    if not packs(n, w):
        return nb, w
    k = w // BLOCK
    return (k * (k + 1) // 2 + (k * k + 1) // 2) * BLOCK, BLOCK


def triangle(k):
    return [(i, j) for i in range(k) for j in range(i + 1)]


def halves(k):
    every = [(a, b) for a in range(k) for b in range(k)]
    half = (k * k + 1) // 2
    return every[:half], every[k * k - half :]


def pack(panel, out, q, n):
    nb, w = panel.shape
    if not packs(n, w):
        out[...] = panel[...].astype(BF)
        return
    k = w // BLOCK
    at = 0
    for i, j in triangle(k):
        rows = pl.ds(pl.multiple_of(q * w + i * BLOCK, BLOCK), BLOCK)
        out[at : at + BLOCK, :] = panel[rows, j * BLOCK : (j + 1) * BLOCK].astype(BF)
        at += BLOCK
    for side, blocks in enumerate(halves(k)):

        @pl.when(q == side)
        def _():
            to = at
            for a, b in blocks:
                i, j = (b, a) if side else (w // BLOCK + a, b)
                value = panel[i * BLOCK : (i + 1) * BLOCK, j * BLOCK : (j + 1) * BLOCK]
                out[to : to + BLOCK, :] = value.astype(BF)
                to += BLOCK


def unpack(src, dst, n):
    nb = dst.shape[0]
    w = nb // n
    if not packs(n, w):
        dst[...] = whole(src)
        return
    k = w // BLOCK

    def both(block, i, j):
        dst[i * BLOCK : (i + 1) * BLOCK, j * BLOCK : (j + 1) * BLOCK] = block
        if i != j:
            dst[j * BLOCK : (j + 1) * BLOCK, i * BLOCK : (i + 1) * BLOCK] = block.T

    seen = set()
    for p in range(n):
        at = 0
        for i, j in triangle(k):
            both(src[p, at : at + BLOCK, :], p * k + i, p * k + j)
            at += BLOCK
        for a, b in halves(k)[p]:
            if (a, b) not in seen:
                i, j = (b, k + a) if p else (k + a, b)
                both(src[p, at : at + BLOCK, :], i, j)
            seen.add((a, b))
            at += BLOCK


def panel_of(matrix, q, n, use):
    w = matrix.shape[1] // n
    for p in range(n):

        @pl.when(q == p)
        def _():
            use(matrix[:, p * w : (p + 1) * w])


def split(refs, *counts):
    out, at = [], 0
    for c in counts:
        out.append(refs[at : at + c])
        at += c
    return out


def call(kernel, ins, in_specs, outs, scratch, flops):
    size = sum(a.size * a.dtype.itemsize for a in ins) + sum(
        o.size * o.dtype.itemsize for o in outs
    )
    return pl.pallas_call(
        kernel,
        in_specs=in_specs,
        out_specs=[VMEM] * len(outs),
        out_shape=outs,
        scratch_shapes=scratch,
        compiler_params=pltpu.CompilerParams(vmem_limit_bytes=24 * MIB),
        cost_estimate=pl.CostEstimate(flops=flops, bytes_accessed=size, transcendentals=0),
    )(*ins)


def base_kernel(n, *refs):
    factor, sigma, f_parts, c_parts, (base, base_bf), (f_all, c_all, sig, sems) = split(
        refs, 1, 1, n, n, 2, 4
    )
    factor, sigma = factor[0], sigma[0]
    hi, lo, q = where_am_i()
    width = factor.shape[1]
    run(copy_all(panel_pairs(f_parts, f_all, q), sems))
    own = factor[...]
    high = own.astype(BF)
    low = (own - high.astype(F32)).astype(BF)
    for p in range(n):
        part = f_all[p]
        base[p * width : (p + 1) * width, :] = mm_t(part, high) + mm_t(part, low)

    @pl.when(lax.axis_index("tm") == lax.axis_size("tm") - 1)
    def _():
        run(copy_all(panel_pairs(c_parts, c_all, q) + [(sigma, sig)], sems))
        s = sig[...]
        s_high = s.astype(BF)
        s_low = (s - s_high.astype(F32)).astype(BF)
        c_own = c_all[q]
        mid = mm(s_high, c_own) + mm(s_low, c_own)
        mid_high = mid.astype(BF)
        mid_low = (mid - mid_high.astype(F32)).astype(BF)
        c_full = whole(c_all)
        base[...] += mm_t(c_full, mid_high) + mm_t(c_full, mid_low)

    pack(base, base_bf, q, n)


def pair_product(c, member):
    odd = lax.rem(member, 2)
    return mm(whole(c.at[member - odd + 1]), whole(c.at[member - odd])).astype(BF)


def near_comp_kernel(n, *refs):
    own, first, second, (pair,), (c, sems) = split(refs, n, n, n, 1, 2)
    hi, lo, q = where_am_i()
    pairs = []
    for r in range(n):
        p = lax.rem(q + r, n)
        even = 1 - lax.rem(p, 2)
        for mask, piece in ((0, own[r]), (1 + even, first[r]), (2 - even, second[r])):
            pairs.append((piece, c.at[jnp.bitwise_xor(lo, mask), p]))
    run(copy_all(pairs, sems))
    pair[...] = pair_product(c, lo)


def group_comp_kernel(n, *refs):
    (pair,), *blocks, outs, (other, sems) = split(refs, 1, n, n, n, n, 5, 2)
    c, c01, c23, agg, agg_panel = outs
    hi, lo, q = where_am_i()
    group_start(blocks, c, sems, lo, q)
    far = jnp.bitwise_xor(lo, 3)
    group_wait(blocks[0], c, sems, far, jnp.bitwise_xor(lo, 2))
    other[...] = pair_product(c, far)

    @pl.when(lo < 2)
    def _():
        put(c01, pair[...])
        c23[...] = other[...]

    @pl.when(lo >= 2)
    def _():
        put(c01, other[...])
        c23[...] = pair[...]

    put(agg, mm(c23[...], whole(c01)))
    agg_panel[...] = agg[q]
    group_wait(blocks[0], c, sems, lo, jnp.bitwise_xor(lo, 1))


def turn_comp_kernel(c, c01, c0_t, c2_t, c01_t):
    c0_t[...] = whole(c.at[0]).T
    c2_t[...] = whole(c.at[2]).T
    c01_t[...] = whole(c01).T


def tail_comp_kernel(c, c23, agg, mine, mine_t, agg_t):
    hi, lo, q = where_am_i()
    agg_t[...] = whole(agg).T

    @pl.when(lo == 0)
    def _():
        mine[...] = agg[...]

    @pl.when(lo == 1)
    def _():
        put(mine, mm(c23[...], whole(c.at[1])))

    @pl.when(lo == 2)
    def _():
        put(mine, c23[...])

    @pl.when(lo == 3)
    def _():
        mine[...] = c[3]

    mine_t[...] = whole(mine).T


def sandwich(cov, comp, comp_t):
    return mm(comp_t, mm(cov, comp).astype(BF))


def group_cov_kernel(n, *refs):
    ins, *blocks, outs, scratch = split(refs, 6, n, n, n, n, 4, 3)
    base, c, c0_t, c2_t, c01, c01_t = ins
    agg, agg_bf, s3, s23 = outs
    sent, s, sems = scratch
    hi, lo, q = where_am_i()
    group_start(blocks, sent, sems, lo, q)
    group_wait(blocks[0], sent, sems, 3, 2, 1, 0)
    unpack(sent.at[3], s3, n)
    for k in range(GROUP - 1):
        unpack(sent.at[k], s.at[k], n)
    mid = mm(s3[...], whole(c.at[2])).astype(BF)
    s23[...] = (s[2].astype(F32) + mm(c2_t[...], mid)).astype(BF)
    w = agg.shape[1]
    first = s[0, :, :w]
    for p in range(1, n):
        first = jnp.where(q == p, s[0, :, p * w : (p + 1) * w], first)
    total = jnp.where(lo == 0, base[...], first.astype(F32))
    total += sandwich(s[1], c[0, q], c0_t[...])
    agg[...] = total + sandwich(s23[...], c01[q], c01_t[...])
    pack(agg, agg_bf, q, n)


def group_mine_kernel(base, agg, s3, s23, c, mine):
    hi, lo, q = where_am_i()

    @pl.when(lo == 0)
    def _():
        mine[...] = agg[...]

    @pl.when(lo == 1)
    def _():
        mine[...] = base[...] + sandwich(s23[...], c[1, q], whole(c.at[1]).T)

    @pl.when(lo == 2)
    def _():
        mine[...] = base[...] + sandwich(s3[...], c[2, q], whole(c.at[2]).T)

    @pl.when(lo == 3)
    def _():
        mine[...] = base[...]


def is_lower(bit):
    hi, lo, q = where_am_i()
    return lax.rem(hi // (1 << bit), 2) == 0


def panel_rows(q, r, n, w):
    return pl.ds(pl.multiple_of(lax.rem(q + r, n) * w, w), w)


def quarter_rows(place, nb):
    rows = nb // GROUP
    return pl.ds(pl.multiple_of(place * rows, rows), rows)


def times(pieces, right, q):
    n = len(pieces)
    w = right.shape[0] // n
    return sum(mm(x[...], right[panel_rows(q, r, n, w), :]) for r, x in enumerate(pieces))


def place_whole(pieces, dst, q):
    for r, piece in enumerate(pieces):
        dst[lax.rem(q + r, len(pieces))] = piece[...]


def join_kernel(*refs):
    *quarters, out = refs
    hi, lo, q = where_am_i()
    for k, piece in enumerate(quarters):
        out[quarter_rows(jnp.bitwise_xor(lo, k), out.shape[0]), :] = piece[...]


def quarter_kernel(panel, out):
    hi, lo, q = where_am_i()
    out[...] = panel[quarter_rows(lo, panel.shape[0]), :]


def share_comp_kernel(n, bit, agg, got, *refs):
    quarters, (share,) = split(refs, n, 1)
    hi, lo, q = where_am_i()
    lower = is_lower(bit)
    nb, w = got.shape

    @pl.when(lower)
    def _():
        share[...] = times(quarters, agg.at[q], q).astype(BF)

    @pl.when(jnp.logical_not(lower))
    def _():
        rows = quarter_rows(lo, nb)
        share[...] = sum(
            mm(agg[p, rows, :], got[p * w : (p + 1) * w, :]) for p in range(n)
        ).astype(BF)


def pair_comp_kernel(n, bit, *refs):
    (agg,), parts, (new_agg, new_agg_t, share), (got,) = split(refs, 1, n, 3, 1)
    hi, lo, q = where_am_i()
    lower = is_lower(bit)
    place_whole(parts, got, q)

    @pl.when(lower)
    def _():
        put(new_agg, mm(whole(got), whole(agg)))

    @pl.when(jnp.logical_not(lower))
    def _():
        put(new_agg, mm(whole(agg), whole(got)))

    new_agg_t[...] = whole(new_agg).T
    share[...] = new_agg[q, quarter_rows(lo, new_agg.shape[1]), :]


def mine_comp_kernel(n, bit, *refs):
    (mine, mine_t), parts, (new_mine, new_mine_t) = split(refs, 2, n, 2)
    hi, lo, q = where_am_i()
    lower = is_lower(bit)

    @pl.when(lower)
    def _():
        for p in range(n):
            new_mine[p] = times(parts, mine.at[p], q).astype(BF)
        new_mine_t[...] = whole(new_mine).T

    @pl.when(jnp.logical_not(lower))
    def _():
        new_mine[...] = mine[...]
        new_mine_t[...] = mine_t[...]


def last_comp_kernel(n, bit, *refs):
    (mine,), parts, (out,) = split(refs, 1, n, 1)
    hi, lo, q = where_am_i()
    lower = is_lower(bit)

    @pl.when(lower)
    def _():
        out[0] = times(parts, mine.at[q], q).astype(BF)

    @pl.when(jnp.logical_not(lower))
    def _():
        out[0] = mine[q]


def pair_cov_kernel(n, bit, to_last, *refs):
    ins, here, c_parts, parts, outs, scratch = split(refs, 3, n, n, n, 2 if to_last else 4, 5)
    agg, agg_c, agg_t = ins
    share, right = outs[:2]
    sent, mid, total, got, packed = scratch
    hi, lo, q = where_am_i()
    lower = is_lower(bit)
    nb, w = agg.shape
    place_whole(parts, sent, q)
    unpack(sent, right, n)

    @pl.when(lower)
    def _():
        total[...] = agg[...] + sandwich(right[...], agg_c[q], agg_t[...])

    @pl.when(jnp.logical_not(lower))
    def _():
        def use(columns):
            total[...] = columns.astype(F32)

        panel_of(right, q, n, use)
        place_whole(here, sent, q)
        unpack(sent, right, n)
        place_whole(c_parts, got, q)
        mid[...] = mm(right[...], got[q]).astype(BF)
        for p in range(n):
            total[p * w : (p + 1) * w, :] += mm_t(got[p], mid[...])

    pack(total, packed, q, n)
    share[...] = packed[quarter_rows(lo, packed.shape[0]), :]
    if not to_last:
        new_agg, new_agg_bf = outs[2:]
        new_agg[...] = total[...]
        new_agg_bf[...] = packed[...]


def mine_cov_kernel(n, bit, cov, mine, mine_t, right, out):
    hi, lo, q = where_am_i()
    lower = is_lower(bit)

    @pl.when(lower)
    def _():
        out[...] = cov[...] + sandwich(right[...], mine[q], mine_t[...])

    @pl.when(jnp.logical_not(lower))
    def _():
        out[...] = cov[...]


def last_cov_kernel(n, bit, *refs):
    (cov, mine, mine_t), parts, (out,), (sent, right) = split(refs, 3, n, 1, 2)
    hi, lo, q = where_am_i()
    lower = is_lower(bit)

    @pl.when(lower)
    def _():
        place_whole(parts, sent, q)
        unpack(sent, right, n)
        out[0] = cov[...] + sandwich(right[...], mine[q], mine_t[...])

    @pl.when(jnp.logical_not(lower))
    def _():
        out[0] = cov[...]


def over_panels(x):
    n = lax.axis_size("panel")
    return [x] + [
        lax.ppermute(x, "panel", [((i + r) % n, i) for i in range(n)]) for r in range(1, n)
    ]


def swap(value, odd_mask, even_mask):
    steps, n = lax.axis_size("tm"), lax.axis_size("panel")
    pairs = []
    for t in range(steps):
        for q in range(n):
            mask = odd_mask if q % 2 else even_mask
            pairs.append((t * n + q, (t ^ mask) * n + q))
    return lax.ppermute(value, ("tm", "panel"), pairs)


def across(x, bit, last):
    steps = lax.axis_size("tm")
    d = GROUP << bit
    return lax.ppermute(
        x, "tm", [(t, t ^ d) for t in range(steps) if (t ^ d) < steps and (t & d or not last)]
    )


def in_group(x):
    return [x] + [swap(x, mask, mask) for mask in range(1, GROUP)]


def joined(quarters):
    rows, lanes = quarters[0].shape
    whole_panel = jax.ShapeDtypeStruct((rows * GROUP, lanes), BF)
    return call(join_kernel, quarters, [VMEM] * GROUP, [whole_panel], [], 0)[0]


def after(x, *others):
    return lax.optimization_barrier((x, *others))[0]


def shards(factor_inverse, coupling, sigma_after):
    steps = lax.axis_size("tm")
    n = lax.axis_size("panel")
    nb, w = factor_inverse.shape[1:]
    levels = (steps // GROUP - 1).bit_length()
    panel_bf = jax.ShapeDtypeStruct((nb, w), BF)
    panel_f32 = jax.ShapeDtypeStruct((nb, w), F32)
    full_bf = jax.ShapeDtypeStruct((n, nb, w), BF)
    square_bf = jax.ShapeDtypeStruct((nb, nb), BF)
    group_bf = jax.ShapeDtypeStruct((GROUP, n, nb, w), BF)
    share_bf = jax.ShapeDtypeStruct((nb // GROUP, w), BF)
    full_scratch = pltpu.VMEM((n, nb, w), BF)
    rows, lanes = packed_shape(n, nb, w)
    packed_bf = jax.ShapeDtypeStruct((rows, lanes), BF)
    packed_share = jax.ShapeDtypeStruct((rows // GROUP, lanes), BF)
    packed_scratch = pltpu.VMEM((n, rows, lanes), BF)
    square_scratch = pltpu.VMEM((nb, nb), BF)
    one = 2 * nb * nb * w
    sems = pltpu.SemaphoreType.DMA

    comp = coupling[0].astype(BF)
    c_first = swap(comp, 1, 2)
    c_second = swap(comp, 2, 1)
    factor = after(factor_inverse[0], comp)
    f_parts = over_panels(factor.astype(BF))
    c_own = over_panels(comp)
    base, base_bf = call(
        functools.partial(base_kernel, n),
        [factor, sigma_after, *f_parts, *c_own],
        [VMEM] + [ANY] * (1 + 2 * n),
        [panel_f32, packed_bf],
        [full_scratch, full_scratch, pltpu.VMEM((nb, n * w), F32), sems((n + 1,))],
        2 * one,
    )
    s_first = swap(base_bf, 1, 2)
    c_diag = swap(after(c_first, s_first), 2, 1)
    s_second = swap(base_bf, 2, 1)
    s_diag = swap(s_first, 2, 1)
    c_near = [p for v in (c_first, c_second) for p in over_panels(v)]
    (pair,) = call(
        functools.partial(near_comp_kernel, n),
        c_own + c_near,
        [ANY] * (3 * n),
        [square_bf],
        [pltpu.VMEM((GROUP, n, nb, w), BF), sems((3 * n,))],
        n * one,
    )
    c_all, c01, c23, agg_c, agg_panel = call(
        functools.partial(group_comp_kernel, n),
        [pair, *c_own, *c_near, *over_panels(after(c_diag, s_second, s_diag, pair))],
        [VMEM] + [ANY] * (GROUP * n),
        [group_bf, full_bf, square_bf, full_bf, panel_bf],
        [square_scratch, sems((GROUP, n))],
        2 * n * one,
    )
    c_got = across(agg_panel, 0, levels == 1)
    c0_t, c2_t, c01_t = call(
        turn_comp_kernel, [c_all, c01], [VMEM] * 2, [square_bf] * 3, [], 0
    )
    s_diag = after(s_diag, agg_panel)
    s_pieces = [p for v in (base_bf, s_first, s_second, s_diag) for p in over_panels(v)]
    agg, agg_bf, s3, s23 = call(
        functools.partial(group_cov_kernel, n),
        [base, c_all, c0_t, c2_t, c01, c01_t, *s_pieces],
        [VMEM] * 6 + [ANY] * (GROUP * n),
        [panel_f32, packed_bf, square_bf, square_bf],
        [
            pltpu.VMEM((GROUP, n, rows, lanes), BF),
            pltpu.VMEM((GROUP - 1, nb, nb), BF),
            sems((GROUP, n)),
        ],
        (2 * n + 4) * one,
    )
    mine, mine_t, agg_t = call(
        tail_comp_kernel,
        [c_all, c23, after(agg_c, agg_bf)],
        [VMEM] * 3,
        [full_bf, square_bf, square_bf],
        [],
        n * one,
    )
    (cov,) = call(
        group_mine_kernel,
        [base, agg, s3, s23, c_all],
        [VMEM] * 5,
        [panel_f32],
        [],
        2 * one,
    )
    out_cov = jax.ShapeDtypeStruct((1, nb, w), F32)
    out_comp = jax.ShapeDtypeStruct((1, nb, w), BF)
    panel_scratch = pltpu.VMEM((nb, w), BF)
    sum_scratch = pltpu.VMEM((nb, w), F32)
    c_got = after(c_got, agg_bf)
    c_parts = over_panels(c_got)
    s_got = across(agg_bf, 0, levels == 1)
    for bit in range(levels):
        last = bit + 1 == levels
        to_last = bit + 2 == levels
        if last:
            (prop,) = call(
                functools.partial(last_comp_kernel, n, bit),
                [after(mine, s_got), *c_parts],
                [VMEM] * (1 + n),
                [out_comp],
                [],
                one,
            )
            s_parts = over_panels(s_got)
            (cov,) = call(
                functools.partial(last_cov_kernel, n, bit),
                [cov, mine, mine_t, *s_parts],
                [VMEM] * (3 + n),
                [out_cov],
                [packed_scratch, square_scratch],
                2 * one,
            )
            break
        agg_in = after(agg_c, agg_bf)
        if to_last:
            (quarter,) = call(quarter_kernel, [c_got], [VMEM], [share_bf], [], 0)
            (c_send,) = call(
                functools.partial(share_comp_kernel, n, bit),
                [agg_in, c_got, *over_panels(quarter)],
                [VMEM] * (2 + n),
                [share_bf],
                [],
                one // 4,
            )
        else:
            new_agg_c, new_agg_t, c_send = call(
                functools.partial(pair_comp_kernel, n, bit),
                [agg_in, *c_parts],
                [VMEM] * (1 + n),
                [full_bf, square_bf, share_bf],
                [full_scratch],
                n * one,
            )
        c_far = across(c_send, bit + 1, to_last)
        new_mine, new_mine_t = call(
            functools.partial(mine_comp_kernel, n, bit),
            [after(mine, c_send), mine_t, *c_parts],
            [VMEM] * (2 + n),
            [full_bf, square_bf],
            [],
            n * one,
        )
        s_parts = over_panels(after(s_got, mine, cov, c_send))
        outs = call(
            functools.partial(pair_cov_kernel, n, bit, to_last),
            [agg, agg_c, agg_t, *over_panels(agg_bf), *c_parts, *s_parts],
            [VMEM] * (3 + 3 * n),
            [packed_share, square_bf] + ([] if to_last else [panel_f32, packed_bf]),
            [
                packed_scratch,
                panel_scratch,
                sum_scratch,
                full_scratch,
                pltpu.VMEM((rows, lanes), BF),
            ],
            2 * one,
        )
        s_send, right = outs[:2]
        s_far = across(s_send, bit + 1, to_last)
        (cov,) = call(
            functools.partial(mine_cov_kernel, n, bit),
            [cov, mine, mine_t, right],
            [VMEM] * 4,
            [panel_f32],
            [],
            2 * one,
        )
        if not to_last:
            agg, agg_bf = outs[2:]
            agg_c, agg_t = new_agg_c, new_agg_t
        s_blocks = in_group(after(s_far, cov, new_mine))
        s_got = joined(s_blocks)
        c_blocks = in_group(after(c_far, s_send))
        c_got = after(joined(c_blocks), *s_blocks[1:])
        c_parts = over_panels(c_got)
        mine, mine_t = new_mine, new_mine_t
    return cov, prop


def solution(mesh):
    placed = (P("tm", None, "panel"), P("tm", None, "panel"), P())
    return jax.shard_map(
        shards,
        mesh=mesh,
        in_specs=placed,
        out_specs=(P("tm", None, "panel"), P("tm", None, "panel")),
        check_vma=False,
    )
```

```python
import functools

import jax
import jax.numpy as jnp
from jax import lax
from jax.experimental import pallas as pl
from jax.experimental.pallas import tpu as pltpu
from jax.sharding import PartitionSpec as P

BF = jnp.bfloat16
F32 = jnp.float32
GROUP = 4
BLOCK = 128
ANY = pl.BlockSpec(memory_space=pl.ANY)
VMEM = pl.BlockSpec(memory_space=pltpu.VMEM)
MIB = 1 << 20


def mm(a, b):
    return jnp.dot(a, b, preferred_element_type=F32)


def mm_t(a, b):
    return lax.dot_general(a, b, (((0,), (0,)), ((), ())), preferred_element_type=F32)


def whole(ref):
    return jnp.concatenate([ref[p] for p in range(ref.shape[0])], axis=1)


def put(ref, value):
    width = ref.shape[2]
    for p in range(ref.shape[0]):
        ref[p] = value[:, p * width : (p + 1) * width].astype(ref.dtype)


def where_am_i():
    t = lax.axis_index("tm")
    return t // GROUP, lax.rem(t, GROUP), lax.axis_index("panel")


def run(copies):
    for c in copies:
        c.start()
    for c in copies:
        c.wait()


def copy_all(pairs, sems):
    return [pltpu.make_async_copy(s, d, sems.at[i]) for i, (s, d) in enumerate(pairs)]


def panel_pairs(pieces, dst, q):
    n = len(pieces)
    return [(piece, dst.at[lax.rem(q + r, n)]) for r, piece in enumerate(pieces)]


def group_start(blocks, dst, sems, lo, q):
    own, first, second, diag = blocks
    n = len(own)
    for r in range(n):
        p = lax.rem(q + r, n)
        even = 1 - lax.rem(p, 2)
        for mask, piece in ((3, diag[r]), (1 + even, first[r]), (2 - even, second[r]), (0, own[r])):
            slot = jnp.bitwise_xor(lo, mask)
            pltpu.make_async_copy(piece, dst.at[slot, p], sems.at[slot, p]).start()


def group_wait(own, dst, sems, *slots):
    for slot in slots:
        for p in range(len(own)):
            pltpu.make_async_copy(own[p], dst.at[slot, p], sems.at[slot, p]).wait()


def packs(n, w):
    return n == 2 and w % BLOCK == 0


def packed_shape(n, nb, w):
    if not packs(n, w):
        return nb, w
    k = w // BLOCK
    return (k * (k + 1) // 2 + (k * k + 1) // 2) * BLOCK, BLOCK


def triangle(k):
    return [(i, j) for i in range(k) for j in range(i + 1)]


def halves(k):
    every = [(a, b) for a in range(k) for b in range(k)]
    half = (k * k + 1) // 2
    return every[:half], every[k * k - half :]


def pack(panel, out, q, n):
    nb, w = panel.shape
    if not packs(n, w):
        out[...] = panel[...].astype(BF)
        return
    k = w // BLOCK
    at = 0
    for i, j in triangle(k):
        rows = pl.ds(pl.multiple_of(q * w + i * BLOCK, BLOCK), BLOCK)
        out[at : at + BLOCK, :] = panel[rows, j * BLOCK : (j + 1) * BLOCK].astype(BF)
        at += BLOCK
    for side, blocks in enumerate(halves(k)):

        @pl.when(q == side)
        def _():
            to = at
            for a, b in blocks:
                i, j = (b, a) if side else (w // BLOCK + a, b)
                value = panel[i * BLOCK : (i + 1) * BLOCK, j * BLOCK : (j + 1) * BLOCK]
                out[to : to + BLOCK, :] = value.astype(BF)
                to += BLOCK


def unpack(src, dst, n):
    nb = dst.shape[0]
    w = nb // n
    if not packs(n, w):
        dst[...] = whole(src)
        return
    k = w // BLOCK

    def both(block, i, j):
        dst[i * BLOCK : (i + 1) * BLOCK, j * BLOCK : (j + 1) * BLOCK] = block
        if i != j:
            dst[j * BLOCK : (j + 1) * BLOCK, i * BLOCK : (i + 1) * BLOCK] = block.T

    seen = set()
    for p in range(n):
        at = 0
        for i, j in triangle(k):
            both(src[p, at : at + BLOCK, :], p * k + i, p * k + j)
            at += BLOCK
        for a, b in halves(k)[p]:
            if (a, b) not in seen:
                i, j = (b, k + a) if p else (k + a, b)
                both(src[p, at : at + BLOCK, :], i, j)
            seen.add((a, b))
            at += BLOCK


def panel_of(matrix, q, n, use):
    w = matrix.shape[1] // n
    for p in range(n):

        @pl.when(q == p)
        def _():
            use(matrix[:, p * w : (p + 1) * w])


def split(refs, *counts):
    out, at = [], 0
    for c in counts:
        out.append(refs[at : at + c])
        at += c
    return out


def call(kernel, ins, in_specs, outs, scratch, flops):
    size = sum(a.size * a.dtype.itemsize for a in ins) + sum(
        o.size * o.dtype.itemsize for o in outs
    )
    return pl.pallas_call(
        kernel,
        in_specs=in_specs,
        out_specs=[VMEM] * len(outs),
        out_shape=outs,
        scratch_shapes=scratch,
        compiler_params=pltpu.CompilerParams(vmem_limit_bytes=24 * MIB),
        cost_estimate=pl.CostEstimate(flops=flops, bytes_accessed=size, transcendentals=0),
    )(*ins)


def base_kernel(n, *refs):
    factor, sigma, f_parts, c_parts, (base, base_bf), (f_all, c_all, sig, sems) = split(
        refs, 1, 1, n, n, 2, 4
    )
    factor, sigma = factor[0], sigma[0]
    hi, lo, q = where_am_i()
    width = factor.shape[1]
    run(copy_all(panel_pairs(f_parts, f_all, q), sems))
    own = factor[...]
    high = own.astype(BF)
    low = (own - high.astype(F32)).astype(BF)
    for p in range(n):
        part = f_all[p]
        base[p * width : (p + 1) * width, :] = mm_t(part, high) + mm_t(part, low)

    @pl.when(lax.axis_index("tm") == lax.axis_size("tm") - 1)
    def _():
        run(copy_all(panel_pairs(c_parts, c_all, q) + [(sigma, sig)], sems))
        s = sig[...]
        s_high = s.astype(BF)
        s_low = (s - s_high.astype(F32)).astype(BF)
        c_own = c_all[q]
        mid = mm(s_high, c_own) + mm(s_low, c_own)
        mid_high = mid.astype(BF)
        mid_low = (mid - mid_high.astype(F32)).astype(BF)
        c_full = whole(c_all)
        base[...] += mm_t(c_full, mid_high) + mm_t(c_full, mid_low)

    pack(base, base_bf, q, n)


def pair_product(c, member):
    odd = lax.rem(member, 2)
    return mm(whole(c.at[member - odd + 1]), whole(c.at[member - odd])).astype(BF)


def near_comp_kernel(n, *refs):
    own, first, second, (pair,), (c, sems) = split(refs, n, n, n, 1, 2)
    hi, lo, q = where_am_i()
    pairs = []
    for r in range(n):
        p = lax.rem(q + r, n)
        even = 1 - lax.rem(p, 2)
        for mask, piece in ((0, own[r]), (1 + even, first[r]), (2 - even, second[r])):
            pairs.append((piece, c.at[jnp.bitwise_xor(lo, mask), p]))
    run(copy_all(pairs, sems))
    pair[...] = pair_product(c, lo)


def group_comp_kernel(n, *refs):
    (pair,), *blocks, outs, (other, sems) = split(refs, 1, n, n, n, n, 5, 2)
    c, c01, c23, agg_cols, share = outs
    hi, lo, q = where_am_i()
    group_start(blocks, c, sems, lo, q)
    far = jnp.bitwise_xor(lo, 3)
    group_wait(blocks[0], c, sems, far, jnp.bitwise_xor(lo, 2))
    other[...] = pair_product(c, far)

    @pl.when(lo < 2)
    def _():
        put(c01, pair[...])
        c23[...] = other[...]

    @pl.when(lo >= 2)
    def _():
        put(c01, other[...])
        c23[...] = pair[...]

    agg_cols[...] = mm(c23[...], c01[q]).astype(BF)
    share[...] = agg_cols[quarter_rows(lo, agg_cols.shape[0]), :]
    group_wait(blocks[0], c, sems, lo, jnp.bitwise_xor(lo, 1))


def turn_comp_kernel(c, c01, c0_t, c2_t, c01_t):
    c0_t[...] = whole(c.at[0]).T
    c2_t[...] = whole(c.at[2]).T
    c01_t[...] = whole(c01).T


def tail_comp_kernel(c, c01, c23, agg, agg_t, mine, mine_t):
    hi, lo, q = where_am_i()
    put(agg, mm(c23[...], whole(c01)))
    agg_t[...] = whole(agg).T

    @pl.when(lo == 0)
    def _():
        mine[...] = agg[...]

    @pl.when(lo == 1)
    def _():
        put(mine, mm(c23[...], whole(c.at[1])))

    @pl.when(lo == 2)
    def _():
        put(mine, c23[...])

    @pl.when(lo == 3)
    def _():
        mine[...] = c[3]

    mine_t[...] = whole(mine).T


def sandwich(cov, comp, comp_t):
    return mm(comp_t, mm(cov, comp).astype(BF))


def group_cov_kernel(n, *refs):
    ins, *blocks, outs, scratch = split(refs, 6, n, n, n, n, 4, 3)
    base, c, c0_t, c2_t, c01, c01_t = ins
    agg, agg_bf, s3, s23 = outs
    sent, s, sems = scratch
    hi, lo, q = where_am_i()
    group_start(blocks, sent, sems, lo, q)
    group_wait(blocks[0], sent, sems, 3, 2, 1, 0)
    unpack(sent.at[3], s3, n)
    for k in range(GROUP - 1):
        unpack(sent.at[k], s.at[k], n)
    mid = mm(s3[...], whole(c.at[2])).astype(BF)
    s23[...] = (s[2].astype(F32) + mm(c2_t[...], mid)).astype(BF)
    w = agg.shape[1]
    first = s[0, :, :w]
    for p in range(1, n):
        first = jnp.where(q == p, s[0, :, p * w : (p + 1) * w], first)
    total = jnp.where(lo == 0, base[...], first.astype(F32))
    total += sandwich(s[1], c[0, q], c0_t[...])
    agg[...] = total + sandwich(s23[...], c01[q], c01_t[...])
    pack(agg, agg_bf, q, n)


def group_mine_kernel(base, agg, s3, s23, c, mine):
    hi, lo, q = where_am_i()

    @pl.when(lo == 0)
    def _():
        mine[...] = agg[...]

    @pl.when(lo == 1)
    def _():
        mine[...] = base[...] + sandwich(s23[...], c[1, q], whole(c.at[1]).T)

    @pl.when(lo == 2)
    def _():
        mine[...] = base[...] + sandwich(s3[...], c[2, q], whole(c.at[2]).T)

    @pl.when(lo == 3)
    def _():
        mine[...] = base[...]


def is_lower(bit):
    hi, lo, q = where_am_i()
    return lax.rem(hi // (1 << bit), 2) == 0


def panel_rows(q, r, n, w):
    return pl.ds(pl.multiple_of(lax.rem(q + r, n) * w, w), w)


def quarter_rows(place, nb):
    rows = nb // GROUP
    return pl.ds(pl.multiple_of(place * rows, rows), rows)


def times(pieces, right, q):
    n = len(pieces)
    w = right.shape[0] // n
    return sum(mm(x[...], right[panel_rows(q, r, n, w), :]) for r, x in enumerate(pieces))


def place_whole(pieces, dst, q):
    for r, piece in enumerate(pieces):
        dst[lax.rem(q + r, len(pieces))] = piece[...]


def join_kernel(*refs):
    *quarters, out = refs
    hi, lo, q = where_am_i()
    for k, piece in enumerate(quarters):
        out[quarter_rows(jnp.bitwise_xor(lo, k), out.shape[0]), :] = piece[...]


def select_kernel(*refs):
    *got, out = refs
    hi, lo, q = where_am_i()
    d = len(got)
    for k, piece in enumerate(got):

        @pl.when(lax.rem(hi, d) == d - 1 - k)
        def _():
            out[...] = piece[...]


def share_comp_kernel(n, agg_cols, *refs):
    quarters, (share,) = split(refs, n, 1)
    hi, lo, q = where_am_i()
    share[...] = times(quarters, agg_cols, q).astype(BF)


def pair_comp_kernel(n, agg, *refs):
    parts, (new_agg, new_agg_t, new_cols, share) = split(refs, n, 4)
    hi, lo, q = where_am_i()
    for p in range(n):
        new_agg[p] = times(parts, agg.at[p], q).astype(BF)
    new_agg_t[...] = whole(new_agg).T
    new_cols[...] = new_agg[q]
    share[...] = new_cols[quarter_rows(lo, new_cols.shape[0]), :]


def mine_comp_kernel(n, bit, *refs):
    (mine, mine_t), parts, (new_mine, new_mine_t) = split(refs, 2, n, 2)
    hi, lo, q = where_am_i()
    lower = is_lower(bit)

    @pl.when(lower)
    def _():
        for p in range(n):
            new_mine[p] = times(parts, mine.at[p], q).astype(BF)
        new_mine_t[...] = whole(new_mine).T

    @pl.when(jnp.logical_not(lower))
    def _():
        new_mine[...] = mine[...]
        new_mine_t[...] = mine_t[...]


def last_comp_kernel(n, bit, *refs):
    (mine,), parts, (out,) = split(refs, 1, n, 1)
    hi, lo, q = where_am_i()
    lower = is_lower(bit)

    @pl.when(lower)
    def _():
        out[0] = times(parts, mine.at[q], q).astype(BF)

    @pl.when(jnp.logical_not(lower))
    def _():
        out[0] = mine[q]


def pair_cov_kernel(n, to_last, agg, agg_cols, agg_t, *refs):
    parts, outs, (sent, total, packed) = split(refs, n, 2 if to_last else 4, 3)
    share, right = outs[:2]
    hi, lo, q = where_am_i()
    place_whole(parts, sent, q)
    unpack(sent, right, n)
    total[...] = agg[...] + sandwich(right[...], agg_cols[...], agg_t[...])
    pack(total, packed, q, n)
    share[...] = packed[quarter_rows(lo, packed.shape[0]), :]
    if not to_last:
        outs[2][...] = total[...]
        outs[3][...] = packed[...]


def mine_cov_kernel(n, bit, cov, mine, mine_t, right, out):
    hi, lo, q = where_am_i()
    lower = is_lower(bit)

    @pl.when(lower)
    def _():
        out[...] = cov[...] + sandwich(right[...], mine[q], mine_t[...])

    @pl.when(jnp.logical_not(lower))
    def _():
        out[...] = cov[...]


def last_cov_kernel(n, bit, *refs):
    (cov, mine, mine_t), parts, (out,), (sent, right) = split(refs, 3, n, 1, 2)
    hi, lo, q = where_am_i()
    lower = is_lower(bit)

    @pl.when(lower)
    def _():
        place_whole(parts, sent, q)
        unpack(sent, right, n)
        out[0] = cov[...] + sandwich(right[...], mine[q], mine_t[...])

    @pl.when(jnp.logical_not(lower))
    def _():
        out[0] = cov[...]


def over_panels(x):
    n = lax.axis_size("panel")
    return [x] + [
        lax.ppermute(x, "panel", [((i + r) % n, i) for i in range(n)]) for r in range(1, n)
    ]


def swap(value, odd_mask, even_mask):
    steps, n = lax.axis_size("tm"), lax.axis_size("panel")
    pairs = []
    for t in range(steps):
        for q in range(n):
            mask = odd_mask if q % 2 else even_mask
            pairs.append((t * n + q, (t ^ mask) * n + q))
    return lax.ppermute(value, ("tm", "panel"), pairs)


def across(x, bit):
    steps = lax.axis_size("tm")
    d = 1 << bit
    got = []
    for back in range(1, d + 1):
        pairs = [
            (g * GROUP + k, (g - back) * GROUP + k)
            for g in range(d, steps // GROUP, 2 * d)
            for k in range(GROUP)
        ]
        got.append(lax.ppermute(x, "tm", pairs))
    if d == 1:
        return got[0]
    return call(select_kernel, got, [VMEM] * d, [jax.ShapeDtypeStruct(x.shape, x.dtype)], [], 0)[0]


def in_group(x):
    return [x] + [swap(x, mask, mask) for mask in range(1, GROUP)]


def joined(quarters):
    rows, lanes = quarters[0].shape
    whole_panel = jax.ShapeDtypeStruct((rows * GROUP, lanes), BF)
    return call(join_kernel, quarters, [VMEM] * GROUP, [whole_panel], [], 0)[0]


def after(x, *others):
    return lax.optimization_barrier((x, *others))[0]


def shards(factor_inverse, coupling, sigma_after):
    steps = lax.axis_size("tm")
    n = lax.axis_size("panel")
    nb, w = factor_inverse.shape[1:]
    levels = (steps // GROUP - 1).bit_length()
    panel_bf = jax.ShapeDtypeStruct((nb, w), BF)
    panel_f32 = jax.ShapeDtypeStruct((nb, w), F32)
    full_bf = jax.ShapeDtypeStruct((n, nb, w), BF)
    square_bf = jax.ShapeDtypeStruct((nb, nb), BF)
    group_bf = jax.ShapeDtypeStruct((GROUP, n, nb, w), BF)
    share_bf = jax.ShapeDtypeStruct((nb // GROUP, w), BF)
    full_scratch = pltpu.VMEM((n, nb, w), BF)
    rows, lanes = packed_shape(n, nb, w)
    packed_bf = jax.ShapeDtypeStruct((rows, lanes), BF)
    packed_share = jax.ShapeDtypeStruct((rows // GROUP, lanes), BF)
    packed_scratch = pltpu.VMEM((n, rows, lanes), BF)
    square_scratch = pltpu.VMEM((nb, nb), BF)
    one = 2 * nb * nb * w
    sems = pltpu.SemaphoreType.DMA

    comp = coupling[0].astype(BF)
    c_first = swap(comp, 1, 2)
    c_second = swap(comp, 2, 1)
    factor = after(factor_inverse[0], comp)
    f_parts = over_panels(factor.astype(BF))
    c_own = over_panels(comp)
    base, base_bf = call(
        functools.partial(base_kernel, n),
        [factor, sigma_after, *f_parts, *c_own],
        [VMEM] + [ANY] * (1 + 2 * n),
        [panel_f32, packed_bf],
        [full_scratch, full_scratch, pltpu.VMEM((nb, n * w), F32), sems((n + 1,))],
        2 * one,
    )
    s_first = swap(base_bf, 1, 2)
    c_diag = swap(after(c_first, s_first), 2, 1)
    s_second = swap(base_bf, 2, 1)
    s_diag = swap(s_first, 2, 1)
    c_near = [p for v in (c_first, c_second) for p in over_panels(v)]
    (pair,) = call(
        functools.partial(near_comp_kernel, n),
        c_own + c_near,
        [ANY] * (3 * n),
        [square_bf],
        [pltpu.VMEM((GROUP, n, nb, w), BF), sems((3 * n,))],
        n * one,
    )
    c_all, c01, c23, agg_cols, c_share = call(
        functools.partial(group_comp_kernel, n),
        [pair, *c_own, *c_near, *over_panels(after(c_diag, s_second, s_diag, pair))],
        [VMEM] + [ANY] * (GROUP * n),
        [group_bf, full_bf, square_bf, panel_bf, share_bf],
        [square_scratch, sems((GROUP, n))],
        2 * n * one,
    )
    c_far = across(c_share, 0)
    c0_t, c2_t, c01_t = call(
        turn_comp_kernel, [c_all, c01], [VMEM] * 2, [square_bf] * 3, [], 0
    )
    s_diag = after(s_diag, c_share)
    s_pieces = [p for v in (base_bf, s_first, s_second, s_diag) for p in over_panels(v)]
    agg, agg_bf, s3, s23 = call(
        functools.partial(group_cov_kernel, n),
        [base, c_all, c0_t, c2_t, c01, c01_t, *s_pieces],
        [VMEM] * 6 + [ANY] * (GROUP * n),
        [panel_f32, packed_bf, square_bf, square_bf],
        [
            pltpu.VMEM((GROUP, n, rows, lanes), BF),
            pltpu.VMEM((GROUP - 1, nb, nb), BF),
            sems((GROUP, n)),
        ],
        (2 * n + 4) * one,
    )
    agg_c, agg_t, mine, mine_t = call(
        tail_comp_kernel,
        [c_all, c01, after(c23, agg_bf)],
        [VMEM] * 3,
        [full_bf, square_bf, full_bf, square_bf],
        [],
        2 * n * one,
    )
    (cov,) = call(
        group_mine_kernel,
        [base, agg, s3, s23, c_all],
        [VMEM] * 5,
        [panel_f32],
        [],
        2 * one,
    )
    out_cov = jax.ShapeDtypeStruct((1, nb, w), F32)
    out_comp = jax.ShapeDtypeStruct((1, nb, w), BF)
    sum_scratch = pltpu.VMEM((nb, w), F32)
    c_far = after(c_far, agg_bf)
    s_got = across(agg_bf, 0)
    for bit in range(levels):
        to_last = bit + 2 == levels
        if bit + 1 == levels:
            c_blocks = in_group(c_far)
            if bit:
                c_blocks[0] = after(c_blocks[0], cov)
            c_panel = joined(c_blocks)
            if bit:
                c_panel = after(c_panel, *s_blocks[1:])
            c_parts = over_panels(c_panel)
            (prop,) = call(
                functools.partial(last_comp_kernel, n, bit),
                [after(mine, s_got), *c_parts],
                [VMEM] * (1 + n),
                [out_comp],
                [],
                one,
            )
            s_parts = over_panels(s_got)
            (cov,) = call(
                functools.partial(last_cov_kernel, n, bit),
                [cov, mine, mine_t, *s_parts],
                [VMEM] * (3 + n),
                [out_cov],
                [packed_scratch, square_scratch],
                2 * one,
            )
            break
        if to_last:
            (c_send,) = call(
                functools.partial(share_comp_kernel, n),
                [agg_cols, *over_panels(c_far)],
                [VMEM] * (1 + n),
                [share_bf],
                [],
                one // 4,
            )
            c_blocks = in_group(after(c_far, c_send))
            c_parts = over_panels(joined(c_blocks))
        else:
            c_blocks = in_group(c_far)
            c_parts = over_panels(joined(c_blocks))
            new_agg_c, new_agg_t, new_cols, c_send = call(
                functools.partial(pair_comp_kernel, n),
                [agg_c, *c_parts],
                [VMEM] * (1 + n),
                [full_bf, square_bf, panel_bf, share_bf],
                [],
                n * one,
            )
        c_far = across(c_send, bit + 1)
        new_mine, new_mine_t = call(
            functools.partial(mine_comp_kernel, n, bit),
            [after(mine, c_send), mine_t, *c_parts],
            [VMEM] * (2 + n),
            [full_bf, square_bf],
            [],
            n * one,
        )
        s_parts = over_panels(after(s_got, mine, cov, c_far, c_blocks[-1]))
        outs = call(
            functools.partial(pair_cov_kernel, n, to_last),
            [agg, agg_cols, agg_t, *s_parts],
            [VMEM] * (3 + n),
            [packed_share, square_bf] + ([] if to_last else [panel_f32, packed_bf]),
            [packed_scratch, sum_scratch, pltpu.VMEM((rows, lanes), BF)],
            2 * one,
        )
        s_send, right = outs[:2]
        s_far = across(s_send, bit + 1)
        (cov,) = call(
            functools.partial(mine_cov_kernel, n, bit),
            [after(cov, s_far), mine, mine_t, right],
            [VMEM] * 4,
            [panel_f32],
            [],
            2 * one,
        )
        if not to_last:
            agg, agg_bf = outs[2:]
            agg_c, agg_t, agg_cols = new_agg_c, new_agg_t, new_cols
        s_blocks = in_group(s_far)
        s_got = joined(s_blocks)
        c_far = after(c_far, s_send)
        mine, mine_t = new_mine, new_mine_t
    return cov, prop


def solution(mesh):
    placed = (P("tm", None, "panel"), P("tm", None, "panel"), P())
    return jax.shard_map(
        shards,
        mesh=mesh,
        in_specs=placed,
        out_specs=(P("tm", None, "panel"), P("tm", None, "panel")),
        check_vma=False,
    )
```

```python
import functools

import jax
import jax.numpy as jnp
from jax import lax
from jax.experimental import pallas as pl
from jax.experimental.pallas import tpu as pltpu
from jax.sharding import PartitionSpec as P

BF = jnp.bfloat16
F32 = jnp.float32
GROUP = 4
BLOCK = 128
ANY = pl.BlockSpec(memory_space=pl.ANY)
VMEM = pl.BlockSpec(memory_space=pltpu.VMEM)
MIB = 1 << 20


def mm(a, b):
    return jnp.dot(a, b, preferred_element_type=F32)


def mm_t(a, b):
    return lax.dot_general(a, b, (((0,), (0,)), ((), ())), preferred_element_type=F32)


def whole(ref):
    return jnp.concatenate([ref[p] for p in range(ref.shape[0])], axis=1)


def put(ref, value):
    width = ref.shape[2]
    for p in range(ref.shape[0]):
        ref[p] = value[:, p * width : (p + 1) * width].astype(ref.dtype)


def where_am_i():
    t = lax.axis_index("tm")
    return t // GROUP, lax.rem(t, GROUP), lax.axis_index("panel")


def run(copies):
    for c in copies:
        c.start()
    for c in copies:
        c.wait()


def copy_all(pairs, sems):
    return [pltpu.make_async_copy(s, d, sems.at[i]) for i, (s, d) in enumerate(pairs)]


def panel_pairs(pieces, dst, q):
    n = len(pieces)
    return [(piece, dst.at[lax.rem(q + r, n)]) for r, piece in enumerate(pieces)]


def group_start(blocks, dst, sems, lo, q):
    own, first, second, diag = blocks
    n = len(own)
    for r in range(n):
        p = lax.rem(q + r, n)
        even = 1 - lax.rem(p, 2)
        for mask, piece in ((3, diag[r]), (1 + even, first[r]), (2 - even, second[r]), (0, own[r])):
            slot = jnp.bitwise_xor(lo, mask)
            pltpu.make_async_copy(piece, dst.at[slot, p], sems.at[slot, p]).start()


def group_wait(own, dst, sems, *slots):
    for slot in slots:
        for p in range(len(own)):
            pltpu.make_async_copy(own[p], dst.at[slot, p], sems.at[slot, p]).wait()


def packs(n, w):
    return n == 2 and w % BLOCK == 0


def packed_shape(n, nb, w):
    if not packs(n, w):
        return nb, w
    k = w // BLOCK
    return (k * (k + 1) // 2 + (k * k + 1) // 2) * BLOCK, BLOCK


def triangle(k):
    return [(i, j) for i in range(k) for j in range(i + 1)]


def halves(k):
    every = [(a, b) for a in range(k) for b in range(k)]
    half = (k * k + 1) // 2
    return every[:half], every[k * k - half :]


def pack(panel, out, q, n):
    nb, w = panel.shape
    if not packs(n, w):
        out[...] = panel[...].astype(BF)
        return
    k = w // BLOCK
    at = 0
    for i, j in triangle(k):
        rows = pl.ds(pl.multiple_of(q * w + i * BLOCK, BLOCK), BLOCK)
        out[at : at + BLOCK, :] = panel[rows, j * BLOCK : (j + 1) * BLOCK].astype(BF)
        at += BLOCK
    for side, blocks in enumerate(halves(k)):

        @pl.when(q == side)
        def _():
            to = at
            for a, b in blocks:
                i, j = (b, a) if side else (w // BLOCK + a, b)
                value = panel[i * BLOCK : (i + 1) * BLOCK, j * BLOCK : (j + 1) * BLOCK]
                out[to : to + BLOCK, :] = value.astype(BF)
                to += BLOCK


def unpack(src, dst, n):
    nb = dst.shape[0]
    w = nb // n
    if not packs(n, w):
        dst[...] = whole(src)
        return
    k = w // BLOCK

    def both(block, i, j):
        dst[i * BLOCK : (i + 1) * BLOCK, j * BLOCK : (j + 1) * BLOCK] = block
        if i != j:
            dst[j * BLOCK : (j + 1) * BLOCK, i * BLOCK : (i + 1) * BLOCK] = block.T

    seen = set()
    for p in range(n):
        at = 0
        for i, j in triangle(k):
            both(src[p, at : at + BLOCK, :], p * k + i, p * k + j)
            at += BLOCK
        for a, b in halves(k)[p]:
            if (a, b) not in seen:
                i, j = (b, k + a) if p else (k + a, b)
                both(src[p, at : at + BLOCK, :], i, j)
            seen.add((a, b))
            at += BLOCK


def panel_of(matrix, q, n, use):
    w = matrix.shape[1] // n
    for p in range(n):

        @pl.when(q == p)
        def _():
            use(matrix[:, p * w : (p + 1) * w])


def split(refs, *counts):
    out, at = [], 0
    for c in counts:
        out.append(refs[at : at + c])
        at += c
    return out


def call(kernel, ins, in_specs, outs, scratch, flops):
    size = sum(a.size * a.dtype.itemsize for a in ins) + sum(
        o.size * o.dtype.itemsize for o in outs
    )
    return pl.pallas_call(
        kernel,
        in_specs=in_specs,
        out_specs=[VMEM] * len(outs),
        out_shape=outs,
        scratch_shapes=scratch,
        compiler_params=pltpu.CompilerParams(vmem_limit_bytes=24 * MIB),
        cost_estimate=pl.CostEstimate(
            flops=flops, bytes_accessed=size if flops else 0, transcendentals=0
        ),
    )(*ins)


def base_kernel(n, *refs):
    factor, sigma, f_parts, c_parts, (base, base_bf), (f_all, c_all, sig, sems) = split(
        refs, 1, 1, n, n, 2, 4
    )
    factor, sigma = factor[0], sigma[0]
    hi, lo, q = where_am_i()
    width = factor.shape[1]
    run(copy_all(panel_pairs(f_parts, f_all, q), sems))
    own = factor[...]
    high = own.astype(BF)
    low = (own - high.astype(F32)).astype(BF)
    for p in range(n):
        part = f_all[p]
        base[p * width : (p + 1) * width, :] = mm_t(part, high) + mm_t(part, low)

    @pl.when(lax.axis_index("tm") == lax.axis_size("tm") - 1)
    def _():
        run(copy_all(panel_pairs(c_parts, c_all, q) + [(sigma, sig)], sems))
        s = sig[...]
        s_high = s.astype(BF)
        s_low = (s - s_high.astype(F32)).astype(BF)
        c_own = c_all[q]
        mid = mm(s_high, c_own) + mm(s_low, c_own)
        mid_high = mid.astype(BF)
        mid_low = (mid - mid_high.astype(F32)).astype(BF)
        c_full = whole(c_all)
        base[...] += mm_t(c_full, mid_high) + mm_t(c_full, mid_low)

    pack(base, base_bf, q, n)


def pair_product(c, member):
    odd = lax.rem(member, 2)
    return mm(whole(c.at[member - odd + 1]), whole(c.at[member - odd])).astype(BF)


def near_comp_kernel(n, *refs):
    own, first, second, (pair,), (c, sems) = split(refs, n, n, n, 1, 2)
    hi, lo, q = where_am_i()
    pairs = []
    for r in range(n):
        p = lax.rem(q + r, n)
        even = 1 - lax.rem(p, 2)
        for mask, piece in ((0, own[r]), (1 + even, first[r]), (2 - even, second[r])):
            pairs.append((piece, c.at[jnp.bitwise_xor(lo, mask), p]))
    run(copy_all(pairs, sems))
    pair[...] = pair_product(c, lo)


def group_comp_kernel(n, *refs):
    (pair,), *blocks, outs, (other, sems) = split(refs, 1, n, n, n, n, 5, 2)
    c, c01, c23, agg_cols, share = outs
    hi, lo, q = where_am_i()
    group_start(blocks, c, sems, lo, q)
    far = jnp.bitwise_xor(lo, 3)
    group_wait(blocks[0], c, sems, far, jnp.bitwise_xor(lo, 2))
    other[...] = pair_product(c, far)

    @pl.when(lo < 2)
    def _():
        put(c01, pair[...])
        c23[...] = other[...]

    @pl.when(lo >= 2)
    def _():
        put(c01, other[...])
        c23[...] = pair[...]

    agg_cols[...] = mm(c23[...], c01[q]).astype(BF)
    share[...] = agg_cols[quarter_rows(lo, agg_cols.shape[0]), :]
    group_wait(blocks[0], c, sems, lo, jnp.bitwise_xor(lo, 1))


def turn_comp_kernel(c, c01, c0_t, c2_t, c01_t):
    c0_t[...] = whole(c.at[0]).T
    c2_t[...] = whole(c.at[2]).T
    c01_t[...] = whole(c01).T


def tail_comp_kernel(c, c01, c23, agg, agg_t, mine, mine_t):
    hi, lo, q = where_am_i()
    put(agg, mm(c23[...], whole(c01)))
    agg_t[...] = whole(agg).T

    @pl.when(lo == 0)
    def _():
        mine[...] = agg[...]

    @pl.when(lo == 1)
    def _():
        put(mine, mm(c23[...], whole(c.at[1])))

    @pl.when(lo == 2)
    def _():
        put(mine, c23[...])

    @pl.when(lo == 3)
    def _():
        mine[...] = c[3]

    mine_t[...] = whole(mine).T


def sandwich(cov, comp, comp_t):
    return mm(comp_t, mm(cov, comp).astype(BF))


def group_cov_kernel(n, *refs):
    ins, *blocks, outs, scratch = split(refs, 6, n, n, n, n, 4, 3)
    base, c, c0_t, c2_t, c01, c01_t = ins
    agg, agg_bf, s3, s23 = outs
    sent, s, sems = scratch
    hi, lo, q = where_am_i()
    group_start(blocks, sent, sems, lo, q)
    group_wait(blocks[0], sent, sems, 3, 2, 1, 0)
    unpack(sent.at[3], s3, n)
    for k in range(GROUP - 1):
        unpack(sent.at[k], s.at[k], n)
    mid = mm(s3[...], whole(c.at[2])).astype(BF)
    s23[...] = (s[2].astype(F32) + mm(c2_t[...], mid)).astype(BF)
    w = agg.shape[1]
    first = s[0, :, :w]
    for p in range(1, n):
        first = jnp.where(q == p, s[0, :, p * w : (p + 1) * w], first)
    total = jnp.where(lo == 0, base[...], first.astype(F32))
    total += sandwich(s[1], c[0, q], c0_t[...])
    agg[...] = total + sandwich(s23[...], c01[q], c01_t[...])
    pack(agg, agg_bf, q, n)


def group_mine_kernel(base, agg, s3, s23, c, mine):
    hi, lo, q = where_am_i()

    @pl.when(lo == 0)
    def _():
        mine[...] = agg[...]

    @pl.when(lo == 1)
    def _():
        mine[...] = base[...] + sandwich(s23[...], c[1, q], whole(c.at[1]).T)

    @pl.when(lo == 2)
    def _():
        mine[...] = base[...] + sandwich(s3[...], c[2, q], whole(c.at[2]).T)

    @pl.when(lo == 3)
    def _():
        mine[...] = base[...]


def is_lower(bit):
    hi, lo, q = where_am_i()
    return lax.rem(hi // (1 << bit), 2) == 0


def panel_rows(q, r, n, w):
    return pl.ds(pl.multiple_of(lax.rem(q + r, n) * w, w), w)


def quarter_rows(place, nb):
    rows = nb // GROUP
    return pl.ds(pl.multiple_of(place * rows, rows), rows)


def times(pieces, right, q):
    n = len(pieces)
    w = right.shape[0] // n
    return sum(mm(x[...], right[panel_rows(q, r, n, w), :]) for r, x in enumerate(pieces))


def place_whole(pieces, dst, q):
    for r, piece in enumerate(pieces):
        dst[lax.rem(q + r, len(pieces))] = piece[...]


def join_kernel(*refs):
    *quarters, out = refs
    hi, lo, q = where_am_i()
    for k, piece in enumerate(quarters):
        out[quarter_rows(jnp.bitwise_xor(lo, k), out.shape[0]), :] = piece[...]


def select_kernel(*refs):
    *got, out = refs
    hi, lo, q = where_am_i()
    d = len(got)
    for k, piece in enumerate(got):

        @pl.when(lax.rem(hi, d) == d - 1 - k)
        def _():
            out[...] = piece[...]


def share_comp_kernel(n, agg_cols, *refs):
    quarters, (share,) = split(refs, n, 1)
    hi, lo, q = where_am_i()
    share[...] = times(quarters, agg_cols, q).astype(BF)


def pair_comp_kernel(n, agg, *refs):
    parts, (new_agg, new_agg_t, new_cols, share) = split(refs, n, 4)
    hi, lo, q = where_am_i()
    for p in range(n):
        new_agg[p] = times(parts, agg.at[p], q).astype(BF)
    new_agg_t[...] = whole(new_agg).T
    new_cols[...] = new_agg[q]
    share[...] = new_cols[quarter_rows(lo, new_cols.shape[0]), :]


def mine_comp_kernel(n, bit, *refs):
    (mine, mine_t), parts, (new_mine, new_mine_t) = split(refs, 2, n, 2)
    hi, lo, q = where_am_i()
    lower = is_lower(bit)

    @pl.when(lower)
    def _():
        for p in range(n):
            new_mine[p] = times(parts, mine.at[p], q).astype(BF)
        new_mine_t[...] = whole(new_mine).T

    @pl.when(jnp.logical_not(lower))
    def _():
        new_mine[...] = mine[...]
        new_mine_t[...] = mine_t[...]


def last_comp_kernel(n, bit, *refs):
    (mine,), parts, (out,) = split(refs, 1, n, 1)
    hi, lo, q = where_am_i()
    lower = is_lower(bit)

    @pl.when(lower)
    def _():
        out[0] = times(parts, mine.at[q], q).astype(BF)

    @pl.when(jnp.logical_not(lower))
    def _():
        out[0] = mine[q]


def pair_cov_kernel(n, to_last, agg, agg_cols, agg_t, *refs):
    parts, outs, (sent, total, packed) = split(refs, n, 2 if to_last else 4, 3)
    share, right = outs[:2]
    hi, lo, q = where_am_i()
    place_whole(parts, sent, q)
    unpack(sent, right, n)
    total[...] = agg[...] + sandwich(right[...], agg_cols[...], agg_t[...])
    pack(total, packed, q, n)
    share[...] = packed[quarter_rows(lo, packed.shape[0]), :]
    if not to_last:
        outs[2][...] = total[...]
        outs[3][...] = packed[...]


def mine_cov_kernel(n, bit, cov, mine, mine_t, right, out):
    hi, lo, q = where_am_i()
    lower = is_lower(bit)

    @pl.when(lower)
    def _():
        out[...] = cov[...] + sandwich(right[...], mine[q], mine_t[...])

    @pl.when(jnp.logical_not(lower))
    def _():
        out[...] = cov[...]


def last_cov_kernel(n, bit, *refs):
    (cov, mine, mine_t), parts, (out,), (sent, right) = split(refs, 3, n, 1, 2)
    hi, lo, q = where_am_i()
    lower = is_lower(bit)

    @pl.when(lower)
    def _():
        place_whole(parts, sent, q)
        unpack(sent, right, n)
        out[0] = cov[...] + sandwich(right[...], mine[q], mine_t[...])

    @pl.when(jnp.logical_not(lower))
    def _():
        out[0] = cov[...]


def over_panels(x):
    n = lax.axis_size("panel")
    return [x] + [
        lax.ppermute(x, "panel", [((i + r) % n, i) for i in range(n)]) for r in range(1, n)
    ]


def swap(value, odd_mask, even_mask):
    steps, n = lax.axis_size("tm"), lax.axis_size("panel")
    pairs = []
    for t in range(steps):
        for q in range(n):
            mask = odd_mask if q % 2 else even_mask
            pairs.append((t * n + q, (t ^ mask) * n + q))
    return lax.ppermute(value, ("tm", "panel"), pairs)


def across(x, bit, *earlier):
    steps = lax.axis_size("tm")
    d = 1 << bit
    got = []
    for back in range(1, d + 1):
        pairs = [
            (g * GROUP + k, (g - back) * GROUP + k)
            for g in range(d, steps // GROUP, 2 * d)
            for k in range(GROUP)
        ]
        source = after(x, *earlier) if back > 1 else x
        got.append(lax.ppermute(source, "tm", pairs))
    return got


def selected(got):
    if len(got) == 1:
        return got[0]
    whole_shape = jax.ShapeDtypeStruct(got[0].shape, got[0].dtype)
    return call(select_kernel, got, [VMEM] * len(got), [whole_shape], [], 0)[0]


def in_group(x):
    return [x] + [swap(x, mask, mask) for mask in range(1, GROUP)]


def joined(quarters):
    rows, lanes = quarters[0].shape
    whole_panel = jax.ShapeDtypeStruct((rows * GROUP, lanes), BF)
    return call(join_kernel, quarters, [VMEM] * GROUP, [whole_panel], [], 0)[0]


def after(x, *others):
    return lax.optimization_barrier((x, *others))[0]


def shards(factor_inverse, coupling, sigma_after):
    steps = lax.axis_size("tm")
    n = lax.axis_size("panel")
    nb, w = factor_inverse.shape[1:]
    levels = (steps // GROUP - 1).bit_length()
    panel_bf = jax.ShapeDtypeStruct((nb, w), BF)
    panel_f32 = jax.ShapeDtypeStruct((nb, w), F32)
    full_bf = jax.ShapeDtypeStruct((n, nb, w), BF)
    square_bf = jax.ShapeDtypeStruct((nb, nb), BF)
    group_bf = jax.ShapeDtypeStruct((GROUP, n, nb, w), BF)
    share_bf = jax.ShapeDtypeStruct((nb // GROUP, w), BF)
    full_scratch = pltpu.VMEM((n, nb, w), BF)
    rows, lanes = packed_shape(n, nb, w)
    packed_bf = jax.ShapeDtypeStruct((rows, lanes), BF)
    packed_share = jax.ShapeDtypeStruct((rows // GROUP, lanes), BF)
    packed_scratch = pltpu.VMEM((n, rows, lanes), BF)
    square_scratch = pltpu.VMEM((nb, nb), BF)
    one = 2 * nb * nb * w
    sems = pltpu.SemaphoreType.DMA

    comp = coupling[0].astype(BF)
    c_first = swap(comp, 1, 2)
    c_second = swap(comp, 2, 1)
    factor = after(factor_inverse[0], comp)
    f_parts = over_panels(factor.astype(BF))
    c_own = over_panels(comp)
    base, base_bf = call(
        functools.partial(base_kernel, n),
        [factor, sigma_after, *f_parts, *c_own],
        [VMEM] + [ANY] * (1 + 2 * n),
        [panel_f32, packed_bf],
        [full_scratch, full_scratch, pltpu.VMEM((nb, n * w), F32), sems((n + 1,))],
        2 * one,
    )
    s_first = swap(base_bf, 1, 2)
    c_diag = swap(after(c_first, s_first), 2, 1)
    s_second = swap(base_bf, 2, 1)
    s_diag = swap(s_first, 2, 1)
    c_near = [p for v in (c_first, c_second) for p in over_panels(v)]
    (pair,) = call(
        functools.partial(near_comp_kernel, n),
        c_own + c_near,
        [ANY] * (3 * n),
        [square_bf],
        [pltpu.VMEM((GROUP, n, nb, w), BF), sems((3 * n,))],
        n * one,
    )
    c_all, c01, c23, agg_cols, c_share = call(
        functools.partial(group_comp_kernel, n),
        [pair, *c_own, *c_near, *over_panels(after(c_diag, s_second, s_diag, pair))],
        [VMEM] + [ANY] * (GROUP * n),
        [group_bf, full_bf, square_bf, panel_bf, share_bf],
        [square_scratch, sems((GROUP, n))],
        2 * n * one,
    )
    (c_far,) = across(c_share, 0)
    c0_t, c2_t, c01_t = call(
        turn_comp_kernel, [c_all, c01], [VMEM] * 2, [square_bf] * 3, [], 0
    )
    s_diag = after(s_diag, c_share)
    s_pieces = [p for v in (base_bf, s_first, s_second, s_diag) for p in over_panels(v)]
    agg, agg_bf, s3, s23 = call(
        functools.partial(group_cov_kernel, n),
        [base, c_all, c0_t, c2_t, c01, c01_t, *s_pieces],
        [VMEM] * 6 + [ANY] * (GROUP * n),
        [panel_f32, packed_bf, square_bf, square_bf],
        [
            pltpu.VMEM((GROUP, n, rows, lanes), BF),
            pltpu.VMEM((GROUP - 1, nb, nb), BF),
            sems((GROUP, n)),
        ],
        (2 * n + 4) * one,
    )
    agg_c, agg_t, mine, mine_t = call(
        tail_comp_kernel,
        [c_all, c01, after(c23, agg_bf)],
        [VMEM] * 3,
        [full_bf, square_bf, full_bf, square_bf],
        [],
        2 * n * one,
    )
    (cov,) = call(
        group_mine_kernel,
        [base, agg, s3, s23, c_all],
        [VMEM] * 5,
        [panel_f32],
        [],
        2 * one,
    )
    out_cov = jax.ShapeDtypeStruct((1, nb, w), F32)
    out_comp = jax.ShapeDtypeStruct((1, nb, w), BF)
    sum_scratch = pltpu.VMEM((nb, w), F32)
    c_far = after(c_far, agg_bf)
    (s_got,) = across(agg_bf, 0)
    for bit in range(levels):
        to_last = bit + 2 == levels
        if bit + 1 == levels:
            c_blocks = in_group(c_far)
            if bit:
                c_blocks[0] = after(c_blocks[0], cov, mine)
            c_panel = joined(c_blocks)
            if bit:
                c_panel = after(c_panel, s_blocks[2], s_blocks[3])
            c_parts = over_panels(c_panel)
            (prop,) = call(
                functools.partial(last_comp_kernel, n, bit),
                [after(mine, s_got), *c_parts],
                [VMEM] * (1 + n),
                [out_comp],
                [],
                one,
            )
            s_parts = over_panels(s_got)
            (cov,) = call(
                functools.partial(last_cov_kernel, n, bit),
                [cov, mine, mine_t, *s_parts],
                [VMEM] * (3 + n),
                [out_cov],
                [packed_scratch, square_scratch],
                2 * one,
            )
            break
        if to_last:
            (c_send,) = call(
                functools.partial(share_comp_kernel, n),
                [agg_cols, *over_panels(c_far)],
                [VMEM] * (1 + n),
                [share_bf],
                [],
                one // 4,
            )
            c_blocks = in_group(after(c_far, c_send))
            c_parts = over_panels(joined(c_blocks))
        else:
            c_blocks = in_group(c_far)
            c_parts = over_panels(joined(c_blocks))
            new_agg_c, new_agg_t, new_cols, c_send = call(
                functools.partial(pair_comp_kernel, n),
                [agg_c, *c_parts],
                [VMEM] * (1 + n),
                [full_bf, square_bf, panel_bf, share_bf],
                [],
                n * one,
            )
        c_sent = across(c_send, bit + 1, s_got)
        c_far = selected(c_sent)
        new_mine, new_mine_t = call(
            functools.partial(mine_comp_kernel, n, bit),
            [after(mine, c_send), mine_t, *c_parts],
            [VMEM] * (2 + n),
            [full_bf, square_bf],
            [],
            0,
        )
        s_parts = over_panels(after(s_got, mine, cov, c_sent[0], *c_blocks[1:]))
        outs = call(
            functools.partial(pair_cov_kernel, n, to_last),
            [agg, agg_cols, agg_t, *s_parts],
            [VMEM] * (3 + n),
            [packed_share, square_bf] + ([] if to_last else [panel_f32, packed_bf]),
            [packed_scratch, sum_scratch, pltpu.VMEM((rows, lanes), BF)],
            2 * one,
        )
        s_send, right = outs[:2]
        s_far = selected(across(s_send, bit + 1))
        (cov,) = call(
            functools.partial(mine_cov_kernel, n, bit),
            [after(cov, s_far), mine, mine_t, right],
            [VMEM] * 4,
            [panel_f32],
            [],
            0,
        )
        if not to_last:
            agg, agg_bf = outs[2:]
            agg_c, agg_t, agg_cols = new_agg_c, new_agg_t, new_cols
        s_blocks = in_group(s_far)
        s_got = joined(s_blocks)
        c_far = after(c_far, s_send)
        mine, mine_t = new_mine, new_mine_t
    return cov, prop


def solution(mesh):
    placed = (P("tm", None, "panel"), P("tm", None, "panel"), P())
    return jax.shard_map(
        shards,
        mesh=mesh,
        in_specs=placed,
        out_specs=(P("tm", None, "panel"), P("tm", None, "panel")),
        check_vma=False,
    )
```

```python
import functools

import jax
import jax.numpy as jnp
from jax import lax
from jax.experimental import pallas as pl
from jax.experimental.pallas import tpu as pltpu
from jax.sharding import PartitionSpec as P

BF = jnp.bfloat16
F32 = jnp.float32
GROUP = 4
BLOCK = 128
ANY = pl.BlockSpec(memory_space=pl.ANY)
VMEM = pl.BlockSpec(memory_space=pltpu.VMEM)
MIB = 1 << 20


def mm(a, b):
    return jnp.dot(a, b, preferred_element_type=F32)


def mm_t(a, b):
    return lax.dot_general(a, b, (((0,), (0,)), ((), ())), preferred_element_type=F32)


def whole(ref):
    return jnp.concatenate([ref[p] for p in range(ref.shape[0])], axis=1)


def put(ref, value):
    width = ref.shape[2]
    for p in range(ref.shape[0]):
        ref[p] = value[:, p * width : (p + 1) * width].astype(ref.dtype)


def where_am_i():
    t = lax.axis_index("tm")
    return t // GROUP, lax.rem(t, GROUP), lax.axis_index("panel")


def run(copies):
    for c in copies:
        c.start()
    for c in copies:
        c.wait()


def copy_all(pairs, sems):
    return [pltpu.make_async_copy(s, d, sems.at[i]) for i, (s, d) in enumerate(pairs)]


def panel_pairs(pieces, dst, q):
    n = len(pieces)
    return [(piece, dst.at[lax.rem(q + r, n)]) for r, piece in enumerate(pieces)]


def group_start(blocks, dst, sems, lo, q):
    own, first, second, diag = blocks
    n = len(own)
    for r in range(n):
        p = lax.rem(q + r, n)
        even = 1 - lax.rem(p, 2)
        for mask, piece in ((3, diag[r]), (1 + even, first[r]), (2 - even, second[r]), (0, own[r])):
            slot = jnp.bitwise_xor(lo, mask)
            pltpu.make_async_copy(piece, dst.at[slot, p], sems.at[slot, p]).start()


def group_wait(own, dst, sems, *slots):
    for slot in slots:
        for p in range(len(own)):
            pltpu.make_async_copy(own[p], dst.at[slot, p], sems.at[slot, p]).wait()


def packs(n, w):
    return n == 2 and w % BLOCK == 0


def packed_shape(n, nb, w):
    if not packs(n, w):
        return nb, w
    k = w // BLOCK
    return (k * (k + 1) // 2 + (k * k + 1) // 2) * BLOCK, BLOCK


def triangle(k):
    return [(i, j) for i in range(k) for j in range(i + 1)]


def halves(k):
    every = [(a, b) for a in range(k) for b in range(k)]
    half = (k * k + 1) // 2
    return every[:half], every[k * k - half :]


def pack(panel, out, q, n):
    nb, w = panel.shape
    if not packs(n, w):
        out[...] = panel[...].astype(BF)
        return
    k = w // BLOCK
    at = 0
    for i, j in triangle(k):
        rows = pl.ds(pl.multiple_of(q * w + i * BLOCK, BLOCK), BLOCK)
        out[at : at + BLOCK, :] = panel[rows, j * BLOCK : (j + 1) * BLOCK].astype(BF)
        at += BLOCK
    for side, blocks in enumerate(halves(k)):

        @pl.when(q == side)
        def _():
            to = at
            for a, b in blocks:
                i, j = (b, a) if side else (w // BLOCK + a, b)
                value = panel[i * BLOCK : (i + 1) * BLOCK, j * BLOCK : (j + 1) * BLOCK]
                out[to : to + BLOCK, :] = value.astype(BF)
                to += BLOCK


def unpack(src, dst, n):
    nb = dst.shape[0]
    w = nb // n
    if not packs(n, w):
        dst[...] = whole(src)
        return
    k = w // BLOCK

    def both(block, i, j):
        dst[i * BLOCK : (i + 1) * BLOCK, j * BLOCK : (j + 1) * BLOCK] = block
        if i != j:
            dst[j * BLOCK : (j + 1) * BLOCK, i * BLOCK : (i + 1) * BLOCK] = block.T

    seen = set()
    for p in range(n):
        at = 0
        for i, j in triangle(k):
            both(src[p, at : at + BLOCK, :], p * k + i, p * k + j)
            at += BLOCK
        for a, b in halves(k)[p]:
            if (a, b) not in seen:
                i, j = (b, k + a) if p else (k + a, b)
                both(src[p, at : at + BLOCK, :], i, j)
            seen.add((a, b))
            at += BLOCK


def panel_of(matrix, q, n, use):
    w = matrix.shape[1] // n
    for p in range(n):

        @pl.when(q == p)
        def _():
            use(matrix[:, p * w : (p + 1) * w])


def split(refs, *counts):
    out, at = [], 0
    for c in counts:
        out.append(refs[at : at + c])
        at += c
    return out


def call(kernel, ins, in_specs, outs, scratch, flops, aliases=None):
    size = sum(a.size * a.dtype.itemsize for a in ins) + sum(
        o.size * o.dtype.itemsize for o in outs
    )
    return pl.pallas_call(
        kernel,
        in_specs=in_specs,
        out_specs=[VMEM] * len(outs),
        out_shape=outs,
        scratch_shapes=scratch,
        input_output_aliases=aliases or {},
        compiler_params=pltpu.CompilerParams(vmem_limit_bytes=24 * MIB),
        cost_estimate=pl.CostEstimate(flops=flops, bytes_accessed=size, transcendentals=0),
    )(*ins)


def base_kernel(n, *refs):
    factor, sigma, f_parts, c_parts, (base, base_bf), (f_all, c_all, sig, sems) = split(
        refs, 1, 1, n, n, 2, 4
    )
    factor, sigma = factor[0], sigma[0]
    hi, lo, q = where_am_i()
    width = factor.shape[1]
    run(copy_all(panel_pairs(f_parts, f_all, q), sems))
    own = factor[...]
    high = own.astype(BF)
    low = (own - high.astype(F32)).astype(BF)
    for p in range(n):
        part = f_all[p]
        base[p * width : (p + 1) * width, :] = mm_t(part, high) + mm_t(part, low)

    @pl.when(lax.axis_index("tm") == lax.axis_size("tm") - 1)
    def _():
        run(copy_all(panel_pairs(c_parts, c_all, q) + [(sigma, sig)], sems))
        s = sig[...]
        s_high = s.astype(BF)
        s_low = (s - s_high.astype(F32)).astype(BF)
        c_own = c_all[q]
        mid = mm(s_high, c_own) + mm(s_low, c_own)
        mid_high = mid.astype(BF)
        mid_low = (mid - mid_high.astype(F32)).astype(BF)
        c_full = whole(c_all)
        base[...] += mm_t(c_full, mid_high) + mm_t(c_full, mid_low)

    pack(base, base_bf, q, n)


def pair_product(c, member):
    odd = lax.rem(member, 2)
    return mm(whole(c.at[member - odd + 1]), whole(c.at[member - odd])).astype(BF)


def near_comp_kernel(n, *refs):
    own, first, second, (c, c_t, pair), (sems,) = split(refs, n, n, n, 3, 1)
    hi, lo, q = where_am_i()
    pairs = []
    for r in range(n):
        p = lax.rem(q + r, n)
        even = 1 - lax.rem(p, 2)
        for mask, piece in ((0, own[r]), (1 + even, first[r]), (2 - even, second[r])):
            pairs.append((piece, c.at[jnp.bitwise_xor(lo, mask), p]))
    run(copy_all(pairs, sems))
    pair[...] = pair_product(c, lo)
    for mask in range(GROUP - 1):
        slot = jnp.bitwise_xor(lo, mask)
        c_t[slot] = whole(c.at[slot]).T


def group_comp_kernel(n, *refs):
    (c, pair), diag, outs, (other, sems) = split(refs, 2, n, 5, 2)
    c_out, c01, c23, agg_cols, share = outs
    hi, lo, q = where_am_i()
    far = jnp.bitwise_xor(lo, 3)
    run(copy_all(panel_pairs(diag, c_out.at[far], q), sems))
    other[...] = pair_product(c_out, far)

    @pl.when(lo < 2)
    def _():
        put(c01, pair[...])
        c23[...] = other[...]

    @pl.when(lo >= 2)
    def _():
        put(c01, other[...])
        c23[...] = pair[...]

    agg_cols[...] = mm(c23[...], c01[q]).astype(BF)
    share[...] = agg_cols[quarter_rows(lo, agg_cols.shape[0]), :]


def turn_comp_kernel(c, c_t, c01, c_t_out, c01_t):
    hi, lo, q = where_am_i()
    far = jnp.bitwise_xor(lo, 3)
    c_t_out[far] = whole(c.at[far]).T
    c01_t[...] = whole(c01).T


def tail_comp_kernel(c, c01, c23, agg, agg_t, mine, mine_t):
    hi, lo, q = where_am_i()
    put(agg, mm(c23[...], whole(c01)))
    agg_t[...] = whole(agg).T

    @pl.when(lo == 0)
    def _():
        mine[...] = agg[...]

    @pl.when(lo == 1)
    def _():
        put(mine, mm(c23[...], whole(c.at[1])))

    @pl.when(lo == 2)
    def _():
        put(mine, c23[...])

    @pl.when(lo == 3)
    def _():
        mine[...] = c[3]

    mine_t[...] = whole(mine).T


def sandwich(cov, comp, comp_t):
    return mm(comp_t, mm(cov, comp).astype(BF))


def group_cov_kernel(n, *refs):
    ins, *blocks, outs, scratch = split(refs, 5, n, n, n, n, 4, 3)
    base, c, c_t, c01, c01_t = ins
    agg, agg_bf, s3, s23 = outs
    sent, s, sems = scratch
    hi, lo, q = where_am_i()
    group_start(blocks, sent, sems, lo, q)
    group_wait(blocks[0], sent, sems, 3, 2, 1, 0)
    unpack(sent.at[3], s3, n)
    for k in range(GROUP - 1):
        unpack(sent.at[k], s.at[k], n)
    mid = mm(s3[...], whole(c.at[2])).astype(BF)
    s23[...] = (s[2].astype(F32) + mm(c_t[2], mid)).astype(BF)
    w = agg.shape[1]
    first = s[0, :, :w]
    for p in range(1, n):
        first = jnp.where(q == p, s[0, :, p * w : (p + 1) * w], first)
    total = jnp.where(lo == 0, base[...], first.astype(F32))
    total += sandwich(s[1], c[0, q], c_t[0])
    agg[...] = total + sandwich(s23[...], c01[q], c01_t[...])
    pack(agg, agg_bf, q, n)


def group_mine_kernel(base, agg, s3, s23, c, c_t, mine):
    hi, lo, q = where_am_i()

    @pl.when(lo == 0)
    def _():
        mine[...] = agg[...]

    @pl.when(lo == 1)
    def _():
        mine[...] = base[...] + sandwich(s23[...], c[1, q], c_t[1])

    @pl.when(lo == 2)
    def _():
        mine[...] = base[...] + sandwich(s3[...], c[2, q], c_t[2])

    @pl.when(lo == 3)
    def _():
        mine[...] = base[...]


def is_lower(bit):
    hi, lo, q = where_am_i()
    return lax.rem(hi // (1 << bit), 2) == 0


def panel_rows(q, r, n, w):
    return pl.ds(pl.multiple_of(lax.rem(q + r, n) * w, w), w)


def quarter_rows(place, nb):
    rows = nb // GROUP
    return pl.ds(pl.multiple_of(place * rows, rows), rows)


def times(pieces, right, q):
    n = len(pieces)
    w = right.shape[0] // n
    return sum(mm(x[...], right[panel_rows(q, r, n, w), :]) for r, x in enumerate(pieces))


def place_whole(pieces, dst, q):
    for r, piece in enumerate(pieces):
        dst[lax.rem(q + r, len(pieces))] = piece[...]


def join_kernel(*refs):
    *quarters, out = refs
    hi, lo, q = where_am_i()
    for k, piece in enumerate(quarters):
        out[quarter_rows(jnp.bitwise_xor(lo, k), out.shape[0]), :] = piece[...]


def select_kernel(*refs):
    *got, out = refs
    hi, lo, q = where_am_i()
    d = len(got)
    for k, piece in enumerate(got):

        @pl.when(lax.rem(hi, d) == d - 1 - k)
        def _():
            out[...] = piece[...]


def share_comp_kernel(n, agg_cols, *refs):
    quarters, (share,) = split(refs, n, 1)
    hi, lo, q = where_am_i()
    share[...] = times(quarters, agg_cols, q).astype(BF)


def pair_comp_kernel(n, agg, *refs):
    parts, (new_agg, new_agg_t, new_cols, share) = split(refs, n, 4)
    hi, lo, q = where_am_i()
    for p in range(n):
        new_agg[p] = times(parts, agg.at[p], q).astype(BF)
    new_agg_t[...] = whole(new_agg).T
    new_cols[...] = new_agg[q]
    share[...] = new_cols[quarter_rows(lo, new_cols.shape[0]), :]


def mine_comp_kernel(n, bit, *refs):
    (mine, mine_t), parts, (new_mine, new_mine_t) = split(refs, 2, n, 2)
    hi, lo, q = where_am_i()
    lower = is_lower(bit)

    @pl.when(lower)
    def _():
        for p in range(n):
            new_mine[p] = times(parts, mine.at[p], q).astype(BF)
        new_mine_t[...] = whole(new_mine).T

    @pl.when(jnp.logical_not(lower))
    def _():
        new_mine[...] = mine[...]
        new_mine_t[...] = mine_t[...]


def last_comp_kernel(n, bit, *refs):
    (mine,), parts, (out,) = split(refs, 1, n, 1)
    hi, lo, q = where_am_i()
    lower = is_lower(bit)

    @pl.when(lower)
    def _():
        out[0] = times(parts, mine.at[q], q).astype(BF)

    @pl.when(jnp.logical_not(lower))
    def _():
        out[0] = mine[q]


def pair_cov_kernel(n, to_last, agg, agg_cols, agg_t, *refs):
    parts, outs, (sent, total, packed) = split(refs, n, 2 if to_last else 4, 3)
    share, right = outs[:2]
    hi, lo, q = where_am_i()
    place_whole(parts, sent, q)
    unpack(sent, right, n)
    total[...] = agg[...] + sandwich(right[...], agg_cols[...], agg_t[...])
    pack(total, packed, q, n)
    share[...] = packed[quarter_rows(lo, packed.shape[0]), :]
    if not to_last:
        outs[2][...] = total[...]
        outs[3][...] = packed[...]


def mine_cov_kernel(n, bit, cov, mine, mine_t, right, out):
    hi, lo, q = where_am_i()
    lower = is_lower(bit)

    @pl.when(lower)
    def _():
        out[...] = cov[...] + sandwich(right[...], mine[q], mine_t[...])

    @pl.when(jnp.logical_not(lower))
    def _():
        out[...] = cov[...]


def last_cov_kernel(n, bit, *refs):
    (cov, mine, mine_t), parts, (out,), (sent, right) = split(refs, 3, n, 1, 2)
    hi, lo, q = where_am_i()
    lower = is_lower(bit)

    @pl.when(lower)
    def _():
        place_whole(parts, sent, q)
        unpack(sent, right, n)
        out[0] = cov[...] + sandwich(right[...], mine[q], mine_t[...])

    @pl.when(jnp.logical_not(lower))
    def _():
        out[0] = cov[...]


def over_panels(x):
    n = lax.axis_size("panel")
    return [x] + [
        lax.ppermute(x, "panel", [((i + r) % n, i) for i in range(n)]) for r in range(1, n)
    ]


def swap(value, odd_mask, even_mask):
    steps, n = lax.axis_size("tm"), lax.axis_size("panel")
    pairs = []
    for t in range(steps):
        for q in range(n):
            mask = odd_mask if q % 2 else even_mask
            pairs.append((t * n + q, (t ^ mask) * n + q))
    return lax.ppermute(value, ("tm", "panel"), pairs)


def across(x, bit):
    steps = lax.axis_size("tm")
    d = 1 << bit
    got = []
    for back in range(1, d + 1):
        pairs = [
            (g * GROUP + k, (g - back) * GROUP + k)
            for g in range(d, steps // GROUP, 2 * d)
            for k in range(GROUP)
        ]
        got.append(lax.ppermute(x, "tm", pairs))
    if d == 1:
        return got[0]
    return call(select_kernel, got, [VMEM] * d, [jax.ShapeDtypeStruct(x.shape, x.dtype)], [], 0)[0]


def in_group(x):
    return [x] + [swap(x, mask, mask) for mask in range(1, GROUP)]


def joined(quarters):
    rows, lanes = quarters[0].shape
    whole_panel = jax.ShapeDtypeStruct((rows * GROUP, lanes), BF)
    return call(join_kernel, quarters, [VMEM] * GROUP, [whole_panel], [], 0)[0]


def after(x, *others):
    return lax.optimization_barrier((x, *others))[0]


def shards(factor_inverse, coupling, sigma_after):
    steps = lax.axis_size("tm")
    n = lax.axis_size("panel")
    nb, w = factor_inverse.shape[1:]
    levels = (steps // GROUP - 1).bit_length()
    panel_bf = jax.ShapeDtypeStruct((nb, w), BF)
    panel_f32 = jax.ShapeDtypeStruct((nb, w), F32)
    full_bf = jax.ShapeDtypeStruct((n, nb, w), BF)
    square_bf = jax.ShapeDtypeStruct((nb, nb), BF)
    group_bf = jax.ShapeDtypeStruct((GROUP, n, nb, w), BF)
    turned_bf = jax.ShapeDtypeStruct((GROUP, nb, nb), BF)
    share_bf = jax.ShapeDtypeStruct((nb // GROUP, w), BF)
    full_scratch = pltpu.VMEM((n, nb, w), BF)
    rows, lanes = packed_shape(n, nb, w)
    packed_bf = jax.ShapeDtypeStruct((rows, lanes), BF)
    packed_share = jax.ShapeDtypeStruct((rows // GROUP, lanes), BF)
    packed_scratch = pltpu.VMEM((n, rows, lanes), BF)
    square_scratch = pltpu.VMEM((nb, nb), BF)
    one = 2 * nb * nb * w
    sems = pltpu.SemaphoreType.DMA

    comp = coupling[0].astype(BF)
    c_first = swap(comp, 1, 2)
    c_second = swap(comp, 2, 1)
    factor = after(factor_inverse[0], comp)
    f_parts = over_panels(factor.astype(BF))
    c_own = over_panels(comp)
    base, base_bf = call(
        functools.partial(base_kernel, n),
        [factor, sigma_after, *f_parts, *c_own],
        [VMEM] + [ANY] * (1 + 2 * n),
        [panel_f32, packed_bf],
        [full_scratch, full_scratch, pltpu.VMEM((nb, n * w), F32), sems((n + 1,))],
        2 * one,
    )
    s_first = swap(base_bf, 1, 2)
    c_diag = swap(c_first, 2, 1)
    s_second = swap(base_bf, 2, 1)
    s_diag = swap(s_first, 2, 1)
    c_near = [p for v in (c_first, c_second) for p in over_panels(v)]
    c_all, c_t, pair = call(
        functools.partial(near_comp_kernel, n),
        c_own + c_near,
        [ANY] * (3 * n),
        [group_bf, turned_bf, square_bf],
        [sems((3 * n,))],
        n * one,
    )
    c_all, c01, c23, agg_cols, c_share = call(
        functools.partial(group_comp_kernel, n),
        [c_all, pair, *over_panels(after(c_diag, s_first, pair))],
        [VMEM] * 2 + [ANY] * n,
        [group_bf, full_bf, square_bf, panel_bf, share_bf],
        [square_scratch, sems((n,))],
        2 * n * one,
        {0: 0},
    )
    c_far = across(c_share, 0)
    c_t, c01_t = call(
        turn_comp_kernel, [c_all, c_t, c01], [VMEM] * 3, [turned_bf, square_bf], [], 0, {1: 0}
    )
    s_second, s_diag = after(s_second, c_share), after(s_diag, c_far)
    s_pieces = [p for v in (base_bf, s_first, s_second, s_diag) for p in over_panels(v)]
    agg, agg_bf, s3, s23 = call(
        functools.partial(group_cov_kernel, n),
        [base, c_all, c_t, c01, c01_t, *s_pieces],
        [VMEM] * 5 + [ANY] * (GROUP * n),
        [panel_f32, packed_bf, square_bf, square_bf],
        [
            pltpu.VMEM((GROUP, n, rows, lanes), BF),
            pltpu.VMEM((GROUP - 1, nb, nb), BF),
            sems((GROUP, n)),
        ],
        (2 * n + 4) * one,
    )
    agg_c, agg_t, mine, mine_t = call(
        tail_comp_kernel,
        [c_all, c01, after(c23, agg_bf)],
        [VMEM] * 3,
        [full_bf, square_bf, full_bf, square_bf],
        [],
        2 * n * one,
    )
    (cov,) = call(
        group_mine_kernel,
        [base, agg, s3, s23, c_all, c_t],
        [VMEM] * 6,
        [panel_f32],
        [],
        2 * one,
    )
    out_cov = jax.ShapeDtypeStruct((1, nb, w), F32)
    out_comp = jax.ShapeDtypeStruct((1, nb, w), BF)
    sum_scratch = pltpu.VMEM((nb, w), F32)
    s_got = across(agg_bf, 0)
    for bit in range(levels):
        to_last = bit + 2 == levels
        if bit + 1 == levels:
            c_parts = over_panels(joined(in_group(c_far)))
            (prop,) = call(
                functools.partial(last_comp_kernel, n, bit),
                [mine, *c_parts],
                [VMEM] * (1 + n),
                [out_comp],
                [],
                one,
            )
            if bit:
                s_got = joined(in_group(after(s_far, prop, cov)))
            s_parts = over_panels(s_got)
            (cov,) = call(
                functools.partial(last_cov_kernel, n, bit),
                [cov, mine, mine_t, *s_parts],
                [VMEM] * (3 + n),
                [out_cov],
                [packed_scratch, square_scratch],
                2 * one,
            )
            break
        if to_last:
            (c_send,) = call(
                functools.partial(share_comp_kernel, n),
                [agg_cols, *over_panels(c_far)],
                [VMEM] * (1 + n),
                [share_bf],
                [],
                one // 4,
            )
            c_blocks = in_group(after(c_far, agg_bf))
            c_parts = over_panels(joined(c_blocks))
        else:
            c_blocks = in_group(c_far)
            c_parts = over_panels(joined(c_blocks))
            new_agg_c, new_agg_t, new_cols, c_send = call(
                functools.partial(pair_comp_kernel, n),
                [agg_c, *c_parts],
                [VMEM] * (1 + n),
                [full_bf, square_bf, panel_bf, share_bf],
                [],
                n * one,
            )
        c_far = after(across(c_send, bit + 1), mine)
        new_mine, new_mine_t = call(
            functools.partial(mine_comp_kernel, n, bit),
            [after(mine, c_send), mine_t, *c_parts],
            [VMEM] * (2 + n),
            [full_bf, square_bf],
            [],
            n * one,
        )
        s_parts = over_panels(after(s_got, mine, cov, *c_blocks[1:]))
        outs = call(
            functools.partial(pair_cov_kernel, n, to_last),
            [agg, agg_cols, agg_t, *s_parts],
            [VMEM] * (3 + n),
            [packed_share, square_bf] + ([] if to_last else [panel_f32, packed_bf]),
            [packed_scratch, sum_scratch, pltpu.VMEM((rows, lanes), BF)],
            2 * one,
        )
        s_send, right = outs[:2]
        s_far = across(s_send, bit + 1)
        (cov,) = call(
            functools.partial(mine_cov_kernel, n, bit),
            [cov, mine, mine_t, right],
            [VMEM] * 4,
            [panel_f32],
            [],
            2 * one,
        )
        if not to_last:
            agg, agg_bf = outs[2:]
            agg_c, agg_t, agg_cols = new_agg_c, new_agg_t, new_cols
        if not to_last:
            s_got = joined(in_group(s_far))
        mine, mine_t = new_mine, new_mine_t
    return cov, prop


def solution(mesh):
    placed = (P("tm", None, "panel"), P("tm", None, "panel"), P())
    return jax.shard_map(
        shards,
        mesh=mesh,
        in_specs=placed,
        out_specs=(P("tm", None, "panel"), P("tm", None, "panel")),
        check_vma=False,
    )
```

```python
import functools

import jax
import jax.numpy as jnp
from jax import lax
from jax.experimental import pallas as pl
from jax.experimental.pallas import tpu as pltpu
from jax.sharding import PartitionSpec as P

BF = jnp.bfloat16
F32 = jnp.float32
GROUP = 4
BLOCK = 128
ANY = pl.BlockSpec(memory_space=pl.ANY)
VMEM = pl.BlockSpec(memory_space=pltpu.VMEM)
MIB = 1 << 20


def mm(a, b):
    return jnp.dot(a, b, preferred_element_type=F32)


def mm_t(a, b):
    return lax.dot_general(a, b, (((0,), (0,)), ((), ())), preferred_element_type=F32)


def whole(ref):
    return jnp.concatenate([ref[p] for p in range(ref.shape[0])], axis=1)


def put(ref, value):
    width = ref.shape[2]
    for p in range(ref.shape[0]):
        ref[p] = value[:, p * width : (p + 1) * width].astype(ref.dtype)


def where_am_i():
    t = lax.axis_index("tm")
    return t // GROUP, lax.rem(t, GROUP), lax.axis_index("panel")


def run(copies):
    for c in copies:
        c.start()
    for c in copies:
        c.wait()


def copy_all(pairs, sems):
    return [pltpu.make_async_copy(s, d, sems.at[i]) for i, (s, d) in enumerate(pairs)]


def panel_pairs(pieces, dst, q):
    n = len(pieces)
    return [(piece, dst.at[lax.rem(q + r, n)]) for r, piece in enumerate(pieces)]


def group_start(blocks, dst, sems, lo, q):
    own, first, second, diag = blocks
    n = len(own)
    for r in range(n):
        p = lax.rem(q + r, n)
        even = 1 - lax.rem(p, 2)
        for mask, piece in ((3, diag[r]), (1 + even, first[r]), (2 - even, second[r]), (0, own[r])):
            slot = jnp.bitwise_xor(lo, mask)
            pltpu.make_async_copy(piece, dst.at[slot, p], sems.at[slot, p]).start()


def group_wait(own, dst, sems, *slots):
    for slot in slots:
        for p in range(len(own)):
            pltpu.make_async_copy(own[p], dst.at[slot, p], sems.at[slot, p]).wait()


def packs(n, w):
    return n == 2 and w % BLOCK == 0


def packed_shape(n, nb, w):
    if not packs(n, w):
        return nb, w
    k = w // BLOCK
    return (k * (k + 1) // 2 + (k * k + 1) // 2) * BLOCK, BLOCK


def triangle(k):
    return [(i, j) for i in range(k) for j in range(i + 1)]


def halves(k):
    every = [(a, b) for a in range(k) for b in range(k)]
    half = (k * k + 1) // 2
    return every[:half], every[k * k - half :]


def pack(panel, out, q, n):
    nb, w = panel.shape
    if not packs(n, w):
        out[...] = panel[...].astype(BF)
        return
    k = w // BLOCK
    at = 0
    for i, j in triangle(k):
        rows = pl.ds(pl.multiple_of(q * w + i * BLOCK, BLOCK), BLOCK)
        out[at : at + BLOCK, :] = panel[rows, j * BLOCK : (j + 1) * BLOCK].astype(BF)
        at += BLOCK
    for side, blocks in enumerate(halves(k)):

        @pl.when(q == side)
        def _():
            to = at
            for a, b in blocks:
                i, j = (b, a) if side else (w // BLOCK + a, b)
                value = panel[i * BLOCK : (i + 1) * BLOCK, j * BLOCK : (j + 1) * BLOCK]
                out[to : to + BLOCK, :] = value.astype(BF)
                to += BLOCK


def unpack(src, dst, n):
    nb = dst.shape[0]
    w = nb // n
    if not packs(n, w):
        dst[...] = whole(src)
        return
    k = w // BLOCK

    def both(block, i, j):
        dst[i * BLOCK : (i + 1) * BLOCK, j * BLOCK : (j + 1) * BLOCK] = block
        if i != j:
            dst[j * BLOCK : (j + 1) * BLOCK, i * BLOCK : (i + 1) * BLOCK] = block.T

    seen = set()
    for p in range(n):
        at = 0
        for i, j in triangle(k):
            both(src[p, at : at + BLOCK, :], p * k + i, p * k + j)
            at += BLOCK
        for a, b in halves(k)[p]:
            if (a, b) not in seen:
                i, j = (b, k + a) if p else (k + a, b)
                both(src[p, at : at + BLOCK, :], i, j)
            seen.add((a, b))
            at += BLOCK


def panel_of(matrix, q, n, use):
    w = matrix.shape[1] // n
    for p in range(n):

        @pl.when(q == p)
        def _():
            use(matrix[:, p * w : (p + 1) * w])


def split(refs, *counts):
    out, at = [], 0
    for c in counts:
        out.append(refs[at : at + c])
        at += c
    return out


def call(kernel, ins, in_specs, outs, scratch, flops, aliases=None):
    size = sum(a.size * a.dtype.itemsize for a in ins) + sum(
        o.size * o.dtype.itemsize for o in outs
    )
    return pl.pallas_call(
        kernel,
        in_specs=in_specs,
        out_specs=[VMEM] * len(outs),
        out_shape=outs,
        scratch_shapes=scratch,
        input_output_aliases=aliases or {},
        compiler_params=pltpu.CompilerParams(vmem_limit_bytes=24 * MIB),
        cost_estimate=pl.CostEstimate(flops=flops, bytes_accessed=size, transcendentals=0),
    )(*ins)


def base_kernel(n, *refs):
    factor, sigma, f_parts, c_parts, (base, base_bf), (f_all, c_all, sig, sems) = split(
        refs, 1, 1, n, n, 2, 4
    )
    factor, sigma = factor[0], sigma[0]
    hi, lo, q = where_am_i()
    width = factor.shape[1]
    run(copy_all(panel_pairs(f_parts, f_all, q), sems))
    own = factor[...]
    high = own.astype(BF)
    low = (own - high.astype(F32)).astype(BF)
    for p in range(n):
        part = f_all[p]
        base[p * width : (p + 1) * width, :] = mm_t(part, high) + mm_t(part, low)

    @pl.when(lax.axis_index("tm") == lax.axis_size("tm") - 1)
    def _():
        run(copy_all(panel_pairs(c_parts, c_all, q) + [(sigma, sig)], sems))
        s = sig[...]
        s_high = s.astype(BF)
        s_low = (s - s_high.astype(F32)).astype(BF)
        c_own = c_all[q]
        mid = mm(s_high, c_own) + mm(s_low, c_own)
        mid_high = mid.astype(BF)
        mid_low = (mid - mid_high.astype(F32)).astype(BF)
        c_full = whole(c_all)
        base[...] += mm_t(c_full, mid_high) + mm_t(c_full, mid_low)

    pack(base, base_bf, q, n)


def pair_product(c, member):
    odd = lax.rem(member, 2)
    return mm(whole(c.at[member - odd + 1]), whole(c.at[member - odd])).astype(BF)


def near_comp_kernel(n, *refs):
    own, first, second, (c, c_t, pair), (sems,) = split(refs, n, n, n, 3, 1)
    hi, lo, q = where_am_i()
    pairs = []
    for r in range(n):
        p = lax.rem(q + r, n)
        even = 1 - lax.rem(p, 2)
        for mask, piece in ((0, own[r]), (1 + even, first[r]), (2 - even, second[r])):
            pairs.append((piece, c.at[jnp.bitwise_xor(lo, mask), p]))
    run(copy_all(pairs, sems))
    pair[...] = pair_product(c, lo)
    for mask in range(GROUP - 1):
        slot = jnp.bitwise_xor(lo, mask)
        c_t[slot] = whole(c.at[slot]).T


def group_comp_kernel(n, *refs):
    (c, pair), diag, outs, (other, sems) = split(refs, 2, n, 5, 2)
    c_out, c01, c23, agg_cols, share = outs
    hi, lo, q = where_am_i()
    far = jnp.bitwise_xor(lo, 3)
    run(copy_all(panel_pairs(diag, c_out.at[far], q), sems))
    other[...] = pair_product(c_out, far)

    @pl.when(lo < 2)
    def _():
        put(c01, pair[...])
        c23[...] = other[...]

    @pl.when(lo >= 2)
    def _():
        put(c01, other[...])
        c23[...] = pair[...]

    agg_cols[...] = mm(c23[...], c01[q]).astype(BF)
    share[...] = agg_cols[quarter_rows(lo, agg_cols.shape[0]), :]


def turn_comp_kernel(c, c_t, c01, c_t_out, c01_t):
    hi, lo, q = where_am_i()
    far = jnp.bitwise_xor(lo, 3)
    c_t_out[far] = whole(c.at[far]).T
    c01_t[...] = whole(c01).T


def tail_comp_kernel(c, c01, c23, agg, agg_t, mine, mine_t):
    hi, lo, q = where_am_i()
    put(agg, mm(c23[...], whole(c01)))
    agg_t[...] = whole(agg).T

    @pl.when(lo == 0)
    def _():
        mine[...] = agg[...]

    @pl.when(lo == 1)
    def _():
        put(mine, mm(c23[...], whole(c.at[1])))

    @pl.when(lo == 2)
    def _():
        put(mine, c23[...])

    @pl.when(lo == 3)
    def _():
        mine[...] = c[3]

    mine_t[...] = whole(mine).T


def sandwich(cov, comp, comp_t):
    return mm(comp_t, mm(cov, comp).astype(BF))


def group_cov_kernel(n, *refs):
    ins, *blocks, outs, scratch = split(refs, 5, n, n, n, n, 4, 3)
    base, c, c_t, c01, c01_t = ins
    agg, agg_bf, s3, s23 = outs
    sent, s, sems = scratch
    hi, lo, q = where_am_i()
    group_start(blocks, sent, sems, lo, q)
    group_wait(blocks[0], sent, sems, 3, 2, 1, 0)
    unpack(sent.at[3], s3, n)
    for k in range(GROUP - 1):
        unpack(sent.at[k], s.at[k], n)
    mid = mm(s3[...], whole(c.at[2])).astype(BF)
    s23[...] = (s[2].astype(F32) + mm(c_t[2], mid)).astype(BF)
    w = agg.shape[1]
    first = s[0, :, :w]
    for p in range(1, n):
        first = jnp.where(q == p, s[0, :, p * w : (p + 1) * w], first)
    total = jnp.where(lo == 0, base[...], first.astype(F32))
    total += sandwich(s[1], c[0, q], c_t[0])
    agg[...] = total + sandwich(s23[...], c01[q], c01_t[...])
    pack(agg, agg_bf, q, n)


def group_mine_kernel(base, agg, s3, s23, c, c_t, mine):
    hi, lo, q = where_am_i()

    @pl.when(lo == 0)
    def _():
        mine[...] = agg[...]

    @pl.when(lo == 1)
    def _():
        mine[...] = base[...] + sandwich(s23[...], c[1, q], c_t[1])

    @pl.when(lo == 2)
    def _():
        mine[...] = base[...] + sandwich(s3[...], c[2, q], c_t[2])

    @pl.when(lo == 3)
    def _():
        mine[...] = base[...]


def is_lower(bit):
    hi, lo, q = where_am_i()
    return lax.rem(hi // (1 << bit), 2) == 0


def panel_rows(q, r, n, w):
    return pl.ds(pl.multiple_of(lax.rem(q + r, n) * w, w), w)


def quarter_rows(place, nb):
    rows = nb // GROUP
    return pl.ds(pl.multiple_of(place * rows, rows), rows)


def times(pieces, right, q):
    n = len(pieces)
    w = right.shape[0] // n
    return sum(mm(x[...], right[panel_rows(q, r, n, w), :]) for r, x in enumerate(pieces))


def place_whole(pieces, dst, q):
    for r, piece in enumerate(pieces):
        dst[lax.rem(q + r, len(pieces))] = piece[...]


def join_kernel(*refs):
    *quarters, out = refs
    hi, lo, q = where_am_i()
    for k, piece in enumerate(quarters):
        out[quarter_rows(jnp.bitwise_xor(lo, k), out.shape[0]), :] = piece[...]


def select_kernel(*refs):
    *got, out = refs
    hi, lo, q = where_am_i()
    d = len(got)
    for k, piece in enumerate(got):

        @pl.when(lax.rem(hi, d) == d - 1 - k)
        def _():
            out[...] = piece[...]


def share_comp_kernel(n, agg_cols, *refs):
    quarters, (share,) = split(refs, n, 1)
    hi, lo, q = where_am_i()
    share[...] = times(quarters, agg_cols, q).astype(BF)


def pair_comp_kernel(n, agg, *refs):
    parts, (new_agg, new_agg_t, new_cols, share) = split(refs, n, 4)
    hi, lo, q = where_am_i()
    for p in range(n):
        new_agg[p] = times(parts, agg.at[p], q).astype(BF)
    new_agg_t[...] = whole(new_agg).T
    new_cols[...] = new_agg[q]
    share[...] = new_cols[quarter_rows(lo, new_cols.shape[0]), :]


def mine_comp_kernel(n, bit, *refs):
    (mine, mine_t), parts, (new_mine, new_mine_t) = split(refs, 2, n, 2)
    hi, lo, q = where_am_i()
    lower = is_lower(bit)

    @pl.when(lower)
    def _():
        for p in range(n):
            new_mine[p] = times(parts, mine.at[p], q).astype(BF)
        new_mine_t[...] = whole(new_mine).T

    @pl.when(jnp.logical_not(lower))
    def _():
        new_mine[...] = mine[...]
        new_mine_t[...] = mine_t[...]


def last_comp_kernel(n, bit, *refs):
    (mine,), parts, (out,) = split(refs, 1, n, 1)
    hi, lo, q = where_am_i()
    lower = is_lower(bit)

    @pl.when(lower)
    def _():
        out[0] = times(parts, mine.at[q], q).astype(BF)

    @pl.when(jnp.logical_not(lower))
    def _():
        out[0] = mine[q]


def pair_cov_kernel(n, to_last, agg, agg_cols, agg_t, *refs):
    parts, outs, (sent, total, packed) = split(refs, n, 2 if to_last else 4, 3)
    share, right = outs[:2]
    hi, lo, q = where_am_i()
    place_whole(parts, sent, q)
    unpack(sent, right, n)
    total[...] = agg[...] + sandwich(right[...], agg_cols[...], agg_t[...])
    pack(total, packed, q, n)
    share[...] = packed[quarter_rows(lo, packed.shape[0]), :]
    if not to_last:
        outs[2][...] = total[...]
        outs[3][...] = packed[...]


def mine_cov_kernel(n, bit, cov, mine, mine_t, right, out):
    hi, lo, q = where_am_i()
    lower = is_lower(bit)

    @pl.when(lower)
    def _():
        out[...] = cov[...] + sandwich(right[...], mine[q], mine_t[...])

    @pl.when(jnp.logical_not(lower))
    def _():
        out[...] = cov[...]


def last_cov_kernel(n, bit, *refs):
    (cov, mine, mine_t), parts, (out,), (sent, right) = split(refs, 3, n, 1, 2)
    hi, lo, q = where_am_i()
    lower = is_lower(bit)

    @pl.when(lower)
    def _():
        place_whole(parts, sent, q)
        unpack(sent, right, n)
        out[0] = cov[...] + sandwich(right[...], mine[q], mine_t[...])

    @pl.when(jnp.logical_not(lower))
    def _():
        out[0] = cov[...]


def over_panels(x):
    n = lax.axis_size("panel")
    return [x] + [
        lax.ppermute(x, "panel", [((i + r) % n, i) for i in range(n)]) for r in range(1, n)
    ]


def swap(value, odd_mask, even_mask):
    steps, n = lax.axis_size("tm"), lax.axis_size("panel")
    pairs = []
    for t in range(steps):
        for q in range(n):
            mask = odd_mask if q % 2 else even_mask
            pairs.append((t * n + q, (t ^ mask) * n + q))
    return lax.ppermute(value, ("tm", "panel"), pairs)


def across(x, bit):
    steps = lax.axis_size("tm")
    d = 1 << bit
    got = []
    for back in range(1, d + 1):
        pairs = [
            (g * GROUP + k, (g - back) * GROUP + k)
            for g in range(d, steps // GROUP, 2 * d)
            for k in range(GROUP)
        ]
        got.append(lax.ppermute(x, "tm", pairs))
    if d == 1:
        return got[0]
    return call(select_kernel, got, [VMEM] * d, [jax.ShapeDtypeStruct(x.shape, x.dtype)], [], 0)[0]


def in_group(x):
    return [x] + [swap(x, mask, mask) for mask in range(1, GROUP)]


def joined(quarters):
    rows, lanes = quarters[0].shape
    whole_panel = jax.ShapeDtypeStruct((rows * GROUP, lanes), BF)
    return call(join_kernel, quarters, [VMEM] * GROUP, [whole_panel], [], 0)[0]


def after(x, *others):
    return lax.optimization_barrier((x, *others))[0]


def shards(factor_inverse, coupling, sigma_after):
    steps = lax.axis_size("tm")
    n = lax.axis_size("panel")
    nb, w = factor_inverse.shape[1:]
    levels = (steps // GROUP - 1).bit_length()
    panel_bf = jax.ShapeDtypeStruct((nb, w), BF)
    panel_f32 = jax.ShapeDtypeStruct((nb, w), F32)
    full_bf = jax.ShapeDtypeStruct((n, nb, w), BF)
    square_bf = jax.ShapeDtypeStruct((nb, nb), BF)
    group_bf = jax.ShapeDtypeStruct((GROUP, n, nb, w), BF)
    turned_bf = jax.ShapeDtypeStruct((GROUP, nb, nb), BF)
    share_bf = jax.ShapeDtypeStruct((nb // GROUP, w), BF)
    full_scratch = pltpu.VMEM((n, nb, w), BF)
    rows, lanes = packed_shape(n, nb, w)
    packed_bf = jax.ShapeDtypeStruct((rows, lanes), BF)
    packed_share = jax.ShapeDtypeStruct((rows // GROUP, lanes), BF)
    packed_scratch = pltpu.VMEM((n, rows, lanes), BF)
    square_scratch = pltpu.VMEM((nb, nb), BF)
    one = 2 * nb * nb * w
    sems = pltpu.SemaphoreType.DMA

    comp = coupling[0].astype(BF)
    c_first = swap(comp, 1, 2)
    c_second = swap(comp, 2, 1)
    factor = after(factor_inverse[0], comp)
    f_parts = over_panels(factor.astype(BF))
    c_own = over_panels(comp)
    base, base_bf = call(
        functools.partial(base_kernel, n),
        [factor, sigma_after, *f_parts, *c_own],
        [VMEM] + [ANY] * (1 + 2 * n),
        [panel_f32, packed_bf],
        [full_scratch, full_scratch, pltpu.VMEM((nb, n * w), F32), sems((n + 1,))],
        2 * one,
    )
    s_first = swap(base_bf, 1, 2)
    c_diag = swap(c_first, 2, 1)
    s_second = swap(base_bf, 2, 1)
    s_diag = swap(s_first, 2, 1)
    c_near = [p for v in (c_first, c_second) for p in over_panels(v)]
    c_all, c_t, pair = call(
        functools.partial(near_comp_kernel, n),
        c_own + c_near,
        [ANY] * (3 * n),
        [group_bf, turned_bf, square_bf],
        [sems((3 * n,))],
        n * one,
    )
    c_all, c01, c23, agg_cols, c_share = call(
        functools.partial(group_comp_kernel, n),
        [c_all, pair, *over_panels(after(c_diag, s_first, pair))],
        [VMEM] * 2 + [ANY] * n,
        [group_bf, full_bf, square_bf, panel_bf, share_bf],
        [square_scratch, sems((n,))],
        2 * n * one,
        {0: 0},
    )
    c_far = across(c_share, 0)
    c_t, c01_t = call(
        turn_comp_kernel, [c_all, c_t, c01], [VMEM] * 3, [turned_bf, square_bf], [], 0, {1: 0}
    )
    first_share = None
    if levels == 2:
        (first_share,) = call(
            functools.partial(share_comp_kernel, n),
            [agg_cols, *over_panels(c_far)],
            [VMEM] * (1 + n),
            [share_bf],
            [],
            one // 4,
        )
    s_second = after(s_second, c_share)
    s_diag = after(s_diag, c_far if first_share is None else first_share)
    s_pieces = [p for v in (base_bf, s_first, s_second, s_diag) for p in over_panels(v)]
    agg, agg_bf, s3, s23 = call(
        functools.partial(group_cov_kernel, n),
        [base, c_all, c_t, c01, c01_t, *s_pieces],
        [VMEM] * 5 + [ANY] * (GROUP * n),
        [panel_f32, packed_bf, square_bf, square_bf],
        [
            pltpu.VMEM((GROUP, n, rows, lanes), BF),
            pltpu.VMEM((GROUP - 1, nb, nb), BF),
            sems((GROUP, n)),
        ],
        (2 * n + 4) * one,
    )
    agg_c, agg_t, mine, mine_t = call(
        tail_comp_kernel,
        [c_all, c01, after(c23, agg_bf)],
        [VMEM] * 3,
        [full_bf, square_bf, full_bf, square_bf],
        [],
        2 * n * one,
    )
    (cov,) = call(
        group_mine_kernel,
        [base, agg, s3, s23, c_all, c_t],
        [VMEM] * 6,
        [panel_f32],
        [],
        2 * one,
    )
    out_cov = jax.ShapeDtypeStruct((1, nb, w), F32)
    out_comp = jax.ShapeDtypeStruct((1, nb, w), BF)
    sum_scratch = pltpu.VMEM((nb, w), F32)
    s_got = across(agg_bf, 0)
    for bit in range(levels):
        to_last = bit + 2 == levels
        if bit + 1 == levels:
            c_blocks = in_group(c_far)
            if bit:
                c_blocks[0] = after(c_blocks[0], cov)
            c_panel = joined(c_blocks)
            if bit:
                c_panel = after(c_panel, *s_blocks[1:])
            c_parts = over_panels(c_panel)
            (prop,) = call(
                functools.partial(last_comp_kernel, n, bit),
                [after(mine, s_got), *c_parts],
                [VMEM] * (1 + n),
                [out_comp],
                [],
                one,
            )
            s_parts = over_panels(s_got)
            (cov,) = call(
                functools.partial(last_cov_kernel, n, bit),
                [cov, mine, mine_t, *s_parts],
                [VMEM] * (3 + n),
                [out_cov],
                [packed_scratch, square_scratch],
                2 * one,
            )
            break
        if to_last:
            c_send = first_share
            if c_send is None:
                (c_send,) = call(
                    functools.partial(share_comp_kernel, n),
                    [agg_cols, *over_panels(c_far)],
                    [VMEM] * (1 + n),
                    [share_bf],
                    [],
                    one // 4,
                )
            c_blocks = in_group(after(c_far, agg_bf))
            c_parts = over_panels(joined(c_blocks))
        else:
            c_blocks = in_group(c_far)
            c_parts = over_panels(joined(c_blocks))
            new_agg_c, new_agg_t, new_cols, c_send = call(
                functools.partial(pair_comp_kernel, n),
                [agg_c, *c_parts],
                [VMEM] * (1 + n),
                [full_bf, square_bf, panel_bf, share_bf],
                [],
                n * one,
            )
        c_far = across(c_send, bit + 1)
        new_mine, new_mine_t = call(
            functools.partial(mine_comp_kernel, n, bit),
            [after(mine, c_send), mine_t, *c_parts],
            [VMEM] * (2 + n),
            [full_bf, square_bf],
            [],
            n * one,
        )
        s_parts = over_panels(after(s_got, mine, cov, c_far, c_blocks[2], c_blocks[3]))
        outs = call(
            functools.partial(pair_cov_kernel, n, to_last),
            [agg, agg_cols, agg_t, *s_parts],
            [VMEM] * (3 + n),
            [packed_share, square_bf] + ([] if to_last else [panel_f32, packed_bf]),
            [packed_scratch, sum_scratch, pltpu.VMEM((rows, lanes), BF)],
            2 * one,
        )
        s_send, right = outs[:2]
        s_far = across(s_send, bit + 1)
        (cov,) = call(
            functools.partial(mine_cov_kernel, n, bit),
            [after(cov, s_far), mine, mine_t, right],
            [VMEM] * 4,
            [panel_f32],
            [],
            2 * one,
        )
        if not to_last:
            agg, agg_bf = outs[2:]
            agg_c, agg_t, agg_cols = new_agg_c, new_agg_t, new_cols
        s_blocks = in_group(s_far)
        s_got = joined(s_blocks)
        c_far = after(c_far, s_send)
        mine, mine_t = new_mine, new_mine_t
    return cov, prop


def solution(mesh):
    placed = (P("tm", None, "panel"), P("tm", None, "panel"), P())
    return jax.shard_map(
        shards,
        mesh=mesh,
        in_specs=placed,
        out_specs=(P("tm", None, "panel"), P("tm", None, "panel")),
        check_vma=False,
    )
```

```python
import functools

import jax
import jax.numpy as jnp
from jax import lax
from jax.experimental import pallas as pl
from jax.experimental.pallas import tpu as pltpu
from jax.sharding import PartitionSpec as P

BF = jnp.bfloat16
F32 = jnp.float32
GROUP = 4
BLOCK = 128
ANY = pl.BlockSpec(memory_space=pl.ANY)
VMEM = pl.BlockSpec(memory_space=pltpu.VMEM)
MIB = 1 << 20


def mm(a, b):
    return jnp.dot(a, b, preferred_element_type=F32)


def mm_t(a, b):
    return lax.dot_general(a, b, (((0,), (0,)), ((), ())), preferred_element_type=F32)


def whole(ref):
    return jnp.concatenate([ref[p] for p in range(ref.shape[0])], axis=1)


def put(ref, value):
    width = ref.shape[2]
    for p in range(ref.shape[0]):
        ref[p] = value[:, p * width : (p + 1) * width].astype(ref.dtype)


def where_am_i():
    t = lax.axis_index("tm")
    return t // GROUP, lax.rem(t, GROUP), lax.axis_index("panel")


def run(copies):
    for c in copies:
        c.start()
    for c in copies:
        c.wait()


def copy_all(pairs, sems):
    return [pltpu.make_async_copy(s, d, sems.at[i]) for i, (s, d) in enumerate(pairs)]


def panel_pairs(pieces, dst, q):
    n = len(pieces)
    return [(piece, dst.at[lax.rem(q + r, n)]) for r, piece in enumerate(pieces)]


def group_start(blocks, dst, sems, lo, q):
    own, first, second, diag = blocks
    n = len(own)
    for r in range(n):
        p = lax.rem(q + r, n)
        even = 1 - lax.rem(p, 2)
        for mask, piece in ((3, diag[r]), (1 + even, first[r]), (2 - even, second[r]), (0, own[r])):
            slot = jnp.bitwise_xor(lo, mask)
            pltpu.make_async_copy(piece, dst.at[slot, p], sems.at[slot, p]).start()


def group_wait(own, dst, sems, *slots):
    for slot in slots:
        for p in range(len(own)):
            pltpu.make_async_copy(own[p], dst.at[slot, p], sems.at[slot, p]).wait()


def packs(n, w):
    return n == 2 and w % BLOCK == 0


def packed_shape(n, nb, w):
    if not packs(n, w):
        return nb, w
    k = w // BLOCK
    return (k * (k + 1) // 2 + (k * k + 1) // 2) * BLOCK, BLOCK


def triangle(k):
    return [(i, j) for i in range(k) for j in range(i + 1)]


def halves(k):
    every = [(a, b) for a in range(k) for b in range(k)]
    half = (k * k + 1) // 2
    return every[:half], every[k * k - half :]


def pack(panel, out, q, n):
    nb, w = panel.shape
    if not packs(n, w):
        out[...] = panel[...].astype(BF)
        return
    k = w // BLOCK
    at = 0
    for i, j in triangle(k):
        rows = pl.ds(pl.multiple_of(q * w + i * BLOCK, BLOCK), BLOCK)
        out[at : at + BLOCK, :] = panel[rows, j * BLOCK : (j + 1) * BLOCK].astype(BF)
        at += BLOCK
    for side, blocks in enumerate(halves(k)):

        @pl.when(q == side)
        def _():
            to = at
            for a, b in blocks:
                i, j = (b, a) if side else (w // BLOCK + a, b)
                value = panel[i * BLOCK : (i + 1) * BLOCK, j * BLOCK : (j + 1) * BLOCK]
                out[to : to + BLOCK, :] = value.astype(BF)
                to += BLOCK


def unpack(src, dst, n):
    nb = dst.shape[0]
    w = nb // n
    if not packs(n, w):
        dst[...] = whole(src)
        return
    k = w // BLOCK

    def both(block, i, j):
        dst[i * BLOCK : (i + 1) * BLOCK, j * BLOCK : (j + 1) * BLOCK] = block
        if i != j:
            dst[j * BLOCK : (j + 1) * BLOCK, i * BLOCK : (i + 1) * BLOCK] = block.T

    seen = set()
    for p in range(n):
        at = 0
        for i, j in triangle(k):
            both(src[p, at : at + BLOCK, :], p * k + i, p * k + j)
            at += BLOCK
        for a, b in halves(k)[p]:
            if (a, b) not in seen:
                i, j = (b, k + a) if p else (k + a, b)
                both(src[p, at : at + BLOCK, :], i, j)
            seen.add((a, b))
            at += BLOCK


def panel_of(matrix, q, n, use):
    w = matrix.shape[1] // n
    for p in range(n):

        @pl.when(q == p)
        def _():
            use(matrix[:, p * w : (p + 1) * w])


def split(refs, *counts):
    out, at = [], 0
    for c in counts:
        out.append(refs[at : at + c])
        at += c
    return out


def call(kernel, ins, in_specs, outs, scratch, flops, aliases=None):
    size = sum(a.size * a.dtype.itemsize for a in ins) + sum(
        o.size * o.dtype.itemsize for o in outs
    )
    return pl.pallas_call(
        kernel,
        in_specs=in_specs,
        out_specs=[VMEM] * len(outs),
        out_shape=outs,
        scratch_shapes=scratch,
        input_output_aliases=aliases or {},
        compiler_params=pltpu.CompilerParams(vmem_limit_bytes=24 * MIB),
        cost_estimate=pl.CostEstimate(flops=flops, bytes_accessed=size, transcendentals=0),
    )(*ins)


def base_kernel(n, *refs):
    factor, sigma, f_parts, c_parts, (base, base_bf), (f_all, c_all, sig, sems) = split(
        refs, 1, 1, n, n, 2, 4
    )
    factor, sigma = factor[0], sigma[0]
    hi, lo, q = where_am_i()
    width = factor.shape[1]
    run(copy_all(panel_pairs(f_parts, f_all, q), sems))
    own = factor[...]
    high = own.astype(BF)
    low = (own - high.astype(F32)).astype(BF)
    for p in range(n):
        part = f_all[p]
        base[p * width : (p + 1) * width, :] = mm_t(part, high) + mm_t(part, low)

    @pl.when(lax.axis_index("tm") == lax.axis_size("tm") - 1)
    def _():
        run(copy_all(panel_pairs(c_parts, c_all, q) + [(sigma, sig)], sems))
        s = sig[...]
        s_high = s.astype(BF)
        s_low = (s - s_high.astype(F32)).astype(BF)
        c_own = c_all[q]
        mid = mm(s_high, c_own) + mm(s_low, c_own)
        mid_high = mid.astype(BF)
        mid_low = (mid - mid_high.astype(F32)).astype(BF)
        c_full = whole(c_all)
        base[...] += mm_t(c_full, mid_high) + mm_t(c_full, mid_low)

    pack(base, base_bf, q, n)


def pair_product(c, member):
    odd = lax.rem(member, 2)
    return mm(whole(c.at[member - odd + 1]), whole(c.at[member - odd])).astype(BF)


def near_comp_kernel(n, *refs):
    own, first, second, (c, c_t, pair), (sems,) = split(refs, n, n, n, 3, 1)
    hi, lo, q = where_am_i()
    pairs = []
    for r in range(n):
        p = lax.rem(q + r, n)
        even = 1 - lax.rem(p, 2)
        for mask, piece in ((0, own[r]), (1 + even, first[r]), (2 - even, second[r])):
            pairs.append((piece, c.at[jnp.bitwise_xor(lo, mask), p]))
    run(copy_all(pairs, sems))
    pair[...] = pair_product(c, lo)
    for mask in range(GROUP - 1):
        slot = jnp.bitwise_xor(lo, mask)
        c_t[slot] = whole(c.at[slot]).T


def group_comp_kernel(n, *refs):
    (c, pair), diag, outs, (other, sems) = split(refs, 2, n, 5, 2)
    c_out, c01, c23, agg_cols, share = outs
    hi, lo, q = where_am_i()
    far = jnp.bitwise_xor(lo, 3)
    run(copy_all(panel_pairs(diag, c_out.at[far], q), sems))
    other[...] = pair_product(c_out, far)

    @pl.when(lo < 2)
    def _():
        put(c01, pair[...])
        c23[...] = other[...]

    @pl.when(lo >= 2)
    def _():
        put(c01, other[...])
        c23[...] = pair[...]

    agg_cols[...] = mm(c23[...], c01[q]).astype(BF)
    share[...] = agg_cols[quarter_rows(lo, agg_cols.shape[0]), :]


def turn_comp_kernel(c, c_t, c01, c_t_out, c01_t):
    hi, lo, q = where_am_i()
    far = jnp.bitwise_xor(lo, 3)
    c_t_out[far] = whole(c.at[far]).T
    c01_t[...] = whole(c01).T


def tail_comp_kernel(c, c01, c23, agg, agg_t, mine, mine_t):
    hi, lo, q = where_am_i()
    put(agg, mm(c23[...], whole(c01)))
    agg_t[...] = whole(agg).T

    @pl.when(lo == 0)
    def _():
        mine[...] = agg[...]

    @pl.when(lo == 1)
    def _():
        put(mine, mm(c23[...], whole(c.at[1])))

    @pl.when(lo == 2)
    def _():
        put(mine, c23[...])

    @pl.when(lo == 3)
    def _():
        mine[...] = c[3]

    mine_t[...] = whole(mine).T


def sandwich(cov, comp, comp_t):
    return mm(comp_t, mm(cov, comp).astype(BF))


def group_cov_kernel(n, *refs):
    ins, *blocks, outs, scratch = split(refs, 5, n, n, n, n, 4, 3)
    base, c, c_t, c01, c01_t = ins
    agg, agg_bf, s3, s23 = outs
    sent, s, sems = scratch
    hi, lo, q = where_am_i()
    group_start(blocks, sent, sems, lo, q)
    group_wait(blocks[0], sent, sems, 3, 2, 1, 0)
    unpack(sent.at[3], s3, n)
    for k in range(GROUP - 1):
        unpack(sent.at[k], s.at[k], n)
    mid = mm(s3[...], whole(c.at[2])).astype(BF)
    s23[...] = (s[2].astype(F32) + mm(c_t[2], mid)).astype(BF)
    w = agg.shape[1]
    first = s[0, :, :w]
    for p in range(1, n):
        first = jnp.where(q == p, s[0, :, p * w : (p + 1) * w], first)
    total = jnp.where(lo == 0, base[...], first.astype(F32))
    total += sandwich(s[1], c[0, q], c_t[0])
    agg[...] = total + sandwich(s23[...], c01[q], c01_t[...])
    pack(agg, agg_bf, q, n)


def group_mine_kernel(base, agg, s3, s23, c, c_t, mine):
    hi, lo, q = where_am_i()

    @pl.when(lo == 0)
    def _():
        mine[...] = agg[...]

    @pl.when(lo == 1)
    def _():
        mine[...] = base[...] + sandwich(s23[...], c[1, q], c_t[1])

    @pl.when(lo == 2)
    def _():
        mine[...] = base[...] + sandwich(s3[...], c[2, q], c_t[2])

    @pl.when(lo == 3)
    def _():
        mine[...] = base[...]


def is_lower(bit):
    hi, lo, q = where_am_i()
    return lax.rem(hi // (1 << bit), 2) == 0


def panel_rows(q, r, n, w):
    return pl.ds(pl.multiple_of(lax.rem(q + r, n) * w, w), w)


def quarter_rows(place, nb):
    rows = nb // GROUP
    return pl.ds(pl.multiple_of(place * rows, rows), rows)


def times(pieces, right, q):
    n = len(pieces)
    w = right.shape[0] // n
    return sum(mm(x[...], right[panel_rows(q, r, n, w), :]) for r, x in enumerate(pieces))


def place_whole(pieces, dst, q):
    for r, piece in enumerate(pieces):
        dst[lax.rem(q + r, len(pieces))] = piece[...]


def join_kernel(*refs):
    *quarters, out = refs
    hi, lo, q = where_am_i()
    for k, piece in enumerate(quarters):
        out[quarter_rows(jnp.bitwise_xor(lo, k), out.shape[0]), :] = piece[...]


def select_kernel(*refs):
    *got, out = refs
    hi, lo, q = where_am_i()
    d = len(got)
    for k, piece in enumerate(got):

        @pl.when(lax.rem(hi, d) == d - 1 - k)
        def _():
            out[...] = piece[...]


def share_comp_kernel(n, agg_cols, *refs):
    quarters, (share,) = split(refs, n, 1)
    hi, lo, q = where_am_i()
    share[...] = times(quarters, agg_cols, q).astype(BF)


def pair_comp_kernel(n, agg, *refs):
    parts, (new_agg, new_agg_t, new_cols, share) = split(refs, n, 4)
    hi, lo, q = where_am_i()
    for p in range(n):
        new_agg[p] = times(parts, agg.at[p], q).astype(BF)
    new_agg_t[...] = whole(new_agg).T
    new_cols[...] = new_agg[q]
    share[...] = new_cols[quarter_rows(lo, new_cols.shape[0]), :]


def mine_comp_kernel(n, bit, *refs):
    (mine, mine_t), parts, (new_mine, new_mine_t) = split(refs, 2, n, 2)
    hi, lo, q = where_am_i()
    lower = is_lower(bit)

    @pl.when(lower)
    def _():
        for p in range(n):
            new_mine[p] = times(parts, mine.at[p], q).astype(BF)
        new_mine_t[...] = whole(new_mine).T

    @pl.when(jnp.logical_not(lower))
    def _():
        new_mine[...] = mine[...]
        new_mine_t[...] = mine_t[...]


def last_comp_kernel(n, bit, *refs):
    (mine,), parts, (out,) = split(refs, 1, n, 1)
    hi, lo, q = where_am_i()
    lower = is_lower(bit)

    @pl.when(lower)
    def _():
        out[0] = times(parts, mine.at[q], q).astype(BF)

    @pl.when(jnp.logical_not(lower))
    def _():
        out[0] = mine[q]


def pair_cov_kernel(n, to_last, agg, agg_cols, agg_t, *refs):
    parts, outs, (sent, total, packed) = split(refs, n, 2 if to_last else 4, 3)
    share, right = outs[:2]
    hi, lo, q = where_am_i()
    place_whole(parts, sent, q)
    unpack(sent, right, n)
    total[...] = agg[...] + sandwich(right[...], agg_cols[...], agg_t[...])
    pack(total, packed, q, n)
    share[...] = packed[quarter_rows(lo, packed.shape[0]), :]
    if not to_last:
        outs[2][...] = total[...]
        outs[3][...] = packed[...]


def mine_cov_kernel(n, bit, cov, mine, mine_t, right, out):
    hi, lo, q = where_am_i()
    lower = is_lower(bit)

    @pl.when(lower)
    def _():
        out[...] = cov[...] + sandwich(right[...], mine[q], mine_t[...])

    @pl.when(jnp.logical_not(lower))
    def _():
        out[...] = cov[...]


def last_cov_kernel(n, bit, *refs):
    (cov, mine, mine_t), parts, (out,), (sent, right) = split(refs, 3, n, 1, 2)
    hi, lo, q = where_am_i()
    lower = is_lower(bit)

    @pl.when(lower)
    def _():
        place_whole(parts, sent, q)
        unpack(sent, right, n)
        out[0] = cov[...] + sandwich(right[...], mine[q], mine_t[...])

    @pl.when(jnp.logical_not(lower))
    def _():
        out[0] = cov[...]


def over_panels(x):
    n = lax.axis_size("panel")
    return [x] + [
        lax.ppermute(x, "panel", [((i + r) % n, i) for i in range(n)]) for r in range(1, n)
    ]


def swap(value, odd_mask, even_mask):
    steps, n = lax.axis_size("tm"), lax.axis_size("panel")
    pairs = []
    for t in range(steps):
        for q in range(n):
            mask = odd_mask if q % 2 else even_mask
            pairs.append((t * n + q, (t ^ mask) * n + q))
    return lax.ppermute(value, ("tm", "panel"), pairs)


def across(x, bit):
    steps = lax.axis_size("tm")
    d = 1 << bit
    got = []
    for back in range(1, d + 1):
        pairs = [
            (g * GROUP + k, (g - back) * GROUP + k)
            for g in range(d, steps // GROUP, 2 * d)
            for k in range(GROUP)
        ]
        got.append(lax.ppermute(x, "tm", pairs))
    if d == 1:
        return got[0]
    return call(select_kernel, got, [VMEM] * d, [jax.ShapeDtypeStruct(x.shape, x.dtype)], [], 0)[0]


def in_group(x):
    return [x] + [swap(x, mask, mask) for mask in range(1, GROUP)]


def joined(quarters):
    rows, lanes = quarters[0].shape
    whole_panel = jax.ShapeDtypeStruct((rows * GROUP, lanes), BF)
    return call(join_kernel, quarters, [VMEM] * GROUP, [whole_panel], [], 0)[0]


def after(x, *others):
    return lax.optimization_barrier((x, *others))[0]


def shards(factor_inverse, coupling, sigma_after):
    steps = lax.axis_size("tm")
    n = lax.axis_size("panel")
    nb, w = factor_inverse.shape[1:]
    levels = (steps // GROUP - 1).bit_length()
    panel_bf = jax.ShapeDtypeStruct((nb, w), BF)
    panel_f32 = jax.ShapeDtypeStruct((nb, w), F32)
    full_bf = jax.ShapeDtypeStruct((n, nb, w), BF)
    square_bf = jax.ShapeDtypeStruct((nb, nb), BF)
    group_bf = jax.ShapeDtypeStruct((GROUP, n, nb, w), BF)
    turned_bf = jax.ShapeDtypeStruct((GROUP, nb, nb), BF)
    share_bf = jax.ShapeDtypeStruct((nb // GROUP, w), BF)
    full_scratch = pltpu.VMEM((n, nb, w), BF)
    rows, lanes = packed_shape(n, nb, w)
    packed_bf = jax.ShapeDtypeStruct((rows, lanes), BF)
    packed_share = jax.ShapeDtypeStruct((rows // GROUP, lanes), BF)
    packed_scratch = pltpu.VMEM((n, rows, lanes), BF)
    square_scratch = pltpu.VMEM((nb, nb), BF)
    one = 2 * nb * nb * w
    sems = pltpu.SemaphoreType.DMA

    comp = coupling[0].astype(BF)
    c_first = swap(comp, 1, 2)
    c_second = swap(comp, 2, 1)
    factor = after(factor_inverse[0], comp)
    f_parts = over_panels(factor.astype(BF))
    c_own = over_panels(comp)
    base, base_bf = call(
        functools.partial(base_kernel, n),
        [factor, sigma_after, *f_parts, *c_own],
        [VMEM] + [ANY] * (1 + 2 * n),
        [panel_f32, packed_bf],
        [full_scratch, full_scratch, pltpu.VMEM((nb, n * w), F32), sems((n + 1,))],
        2 * one,
    )
    s_first = swap(base_bf, 1, 2)
    c_diag = swap(c_first, 2, 1)
    s_second = swap(base_bf, 2, 1)
    s_diag = swap(s_first, 2, 1)
    c_near = [p for v in (c_first, c_second) for p in over_panels(v)]
    c_all, c_t, pair = call(
        functools.partial(near_comp_kernel, n),
        c_own + c_near,
        [ANY] * (3 * n),
        [group_bf, turned_bf, square_bf],
        [sems((3 * n,))],
        n * one,
    )
    c_all, c01, c23, agg_cols, c_share = call(
        functools.partial(group_comp_kernel, n),
        [c_all, pair, *over_panels(after(c_diag, s_first, pair))],
        [VMEM] * 2 + [ANY] * n,
        [group_bf, full_bf, square_bf, panel_bf, share_bf],
        [square_scratch, sems((n,))],
        2 * n * one,
        {0: 0},
    )
    c_far = across(c_share, 0)
    c_t, c01_t = call(
        turn_comp_kernel, [c_all, c_t, c01], [VMEM] * 3, [turned_bf, square_bf], [], 0, {1: 0}
    )
    s_second, s_diag = after(s_second, c_share), after(s_diag, c_t)
    s_pieces = [p for v in (base_bf, s_first, s_second, s_diag) for p in over_panels(v)]
    agg, agg_bf, s3, s23 = call(
        functools.partial(group_cov_kernel, n),
        [base, c_all, c_t, c01, c01_t, *s_pieces],
        [VMEM] * 5 + [ANY] * (GROUP * n),
        [panel_f32, packed_bf, square_bf, square_bf],
        [
            pltpu.VMEM((GROUP, n, rows, lanes), BF),
            pltpu.VMEM((GROUP - 1, nb, nb), BF),
            sems((GROUP, n)),
        ],
        (2 * n + 4) * one,
    )
    agg_c, agg_t, mine, mine_t = call(
        tail_comp_kernel,
        [c_all, c01, after(c23, agg_bf)],
        [VMEM] * 3,
        [full_bf, square_bf, full_bf, square_bf],
        [],
        2 * n * one,
    )
    (cov,) = call(
        group_mine_kernel,
        [base, agg, s3, s23, c_all, c_t],
        [VMEM] * 6,
        [panel_f32],
        [],
        2 * one,
    )
    out_cov = jax.ShapeDtypeStruct((1, nb, w), F32)
    out_comp = jax.ShapeDtypeStruct((1, nb, w), BF)
    sum_scratch = pltpu.VMEM((nb, w), F32)
    c_far = after(c_far, agg_bf)
    s_got = across(agg_bf, 0)
    for bit in range(levels):
        to_last = bit + 2 == levels
        if bit + 1 == levels:
            c_blocks = in_group(c_far)
            if bit:
                c_blocks[0] = after(c_blocks[0], cov)
            c_panel = joined(c_blocks)
            if bit:
                c_panel = after(c_panel, *s_blocks[1:])
            c_parts = over_panels(c_panel)
            (prop,) = call(
                functools.partial(last_comp_kernel, n, bit),
                [after(mine, s_got), *c_parts],
                [VMEM] * (1 + n),
                [out_comp],
                [],
                one,
            )
            s_parts = over_panels(s_got)
            (cov,) = call(
                functools.partial(last_cov_kernel, n, bit),
                [cov, mine, mine_t, *s_parts],
                [VMEM] * (3 + n),
                [out_cov],
                [packed_scratch, square_scratch],
                2 * one,
            )
            break
        if to_last:
            (c_send,) = call(
                functools.partial(share_comp_kernel, n),
                [agg_cols, *over_panels(c_far)],
                [VMEM] * (1 + n),
                [share_bf],
                [],
                one // 4,
            )
            c_blocks = in_group(after(c_far, c_send))
            c_parts = over_panels(joined(c_blocks))
        else:
            c_blocks = in_group(c_far)
            c_parts = over_panels(joined(c_blocks))
            new_agg_c, new_agg_t, new_cols, c_send = call(
                functools.partial(pair_comp_kernel, n),
                [agg_c, *c_parts],
                [VMEM] * (1 + n),
                [full_bf, square_bf, panel_bf, share_bf],
                [],
                n * one,
            )
        c_far = across(c_send, bit + 1)
        new_mine, new_mine_t = call(
            functools.partial(mine_comp_kernel, n, bit),
            [after(mine, c_send), mine_t, *c_parts],
            [VMEM] * (2 + n),
            [full_bf, square_bf],
            [],
            n * one,
        )
        s_parts = over_panels(after(s_got, mine, cov, c_far, c_blocks[2], c_blocks[3]))
        outs = call(
            functools.partial(pair_cov_kernel, n, to_last),
            [agg, agg_cols, agg_t, *s_parts],
            [VMEM] * (3 + n),
            [packed_share, square_bf] + ([] if to_last else [panel_f32, packed_bf]),
            [packed_scratch, sum_scratch, pltpu.VMEM((rows, lanes), BF)],
            2 * one,
        )
        s_send, right = outs[:2]
        s_far = across(s_send, bit + 1)
        (cov,) = call(
            functools.partial(mine_cov_kernel, n, bit),
            [after(cov, s_far), mine, mine_t, right],
            [VMEM] * 4,
            [panel_f32],
            [],
            2 * one,
        )
        if not to_last:
            agg, agg_bf = outs[2:]
            agg_c, agg_t, agg_cols = new_agg_c, new_agg_t, new_cols
        s_blocks = in_group(s_far)
        s_got = joined(s_blocks)
        c_far = after(c_far, s_send)
        mine, mine_t = new_mine, new_mine_t
    return cov, prop


def solution(mesh):
    placed = (P("tm", None, "panel"), P("tm", None, "panel"), P())
    return jax.shard_map(
        shards,
        mesh=mesh,
        in_specs=placed,
        out_specs=(P("tm", None, "panel"), P("tm", None, "panel")),
        check_vma=False,
    )
```

```python
import functools

import jax
import jax.numpy as jnp
from jax import lax
from jax.experimental import pallas as pl
from jax.experimental.pallas import tpu as pltpu
from jax.sharding import PartitionSpec as P

BF = jnp.bfloat16
F32 = jnp.float32
GROUP = 4
BLOCK = 128
ANY = pl.BlockSpec(memory_space=pl.ANY)
VMEM = pl.BlockSpec(memory_space=pltpu.VMEM)
MIB = 1 << 20


def mm(a, b):
    return jnp.dot(a, b, preferred_element_type=F32)


def mm_t(a, b):
    return lax.dot_general(a, b, (((0,), (0,)), ((), ())), preferred_element_type=F32)


def whole(ref):
    return jnp.concatenate([ref[p] for p in range(ref.shape[0])], axis=1)


def put(ref, value):
    width = ref.shape[2]
    for p in range(ref.shape[0]):
        ref[p] = value[:, p * width : (p + 1) * width].astype(ref.dtype)


def where_am_i():
    t = lax.axis_index("tm")
    return t // GROUP, lax.rem(t, GROUP), lax.axis_index("panel")


def run(copies):
    for c in copies:
        c.start()
    for c in copies:
        c.wait()


def copy_all(pairs, sems):
    return [pltpu.make_async_copy(s, d, sems.at[i]) for i, (s, d) in enumerate(pairs)]


def panel_pairs(pieces, dst, q):
    n = len(pieces)
    return [(piece, dst.at[lax.rem(q + r, n)]) for r, piece in enumerate(pieces)]


def group_start(blocks, dst, sems, lo, q):
    own, first, second, diag = blocks
    n = len(own)
    for r in range(n):
        p = lax.rem(q + r, n)
        even = 1 - lax.rem(p, 2)
        for mask, piece in ((3, diag[r]), (1 + even, first[r]), (2 - even, second[r]), (0, own[r])):
            slot = jnp.bitwise_xor(lo, mask)
            pltpu.make_async_copy(piece, dst.at[slot, p], sems.at[slot, p]).start()


def group_wait(own, dst, sems, *slots):
    for slot in slots:
        for p in range(len(own)):
            pltpu.make_async_copy(own[p], dst.at[slot, p], sems.at[slot, p]).wait()


def packs(n, w):
    return n == 2 and w % BLOCK == 0


def packed_shape(n, nb, w):
    if not packs(n, w):
        return nb, w
    k = w // BLOCK
    return (k * (k + 1) // 2 + (k * k + 1) // 2) * BLOCK, BLOCK


def triangle(k):
    return [(i, j) for i in range(k) for j in range(i + 1)]


def halves(k):
    every = [(a, b) for a in range(k) for b in range(k)]
    half = (k * k + 1) // 2
    return every[:half], every[k * k - half :]


def pack(panel, out, q, n):
    nb, w = panel.shape
    if not packs(n, w):
        out[...] = panel[...].astype(BF)
        return
    k = w // BLOCK
    at = 0
    for i, j in triangle(k):
        rows = pl.ds(pl.multiple_of(q * w + i * BLOCK, BLOCK), BLOCK)
        out[at : at + BLOCK, :] = panel[rows, j * BLOCK : (j + 1) * BLOCK].astype(BF)
        at += BLOCK
    for side, blocks in enumerate(halves(k)):

        @pl.when(q == side)
        def _():
            to = at
            for a, b in blocks:
                i, j = (b, a) if side else (w // BLOCK + a, b)
                value = panel[i * BLOCK : (i + 1) * BLOCK, j * BLOCK : (j + 1) * BLOCK]
                out[to : to + BLOCK, :] = value.astype(BF)
                to += BLOCK


def unpack(src, dst, n):
    nb = dst.shape[0]
    w = nb // n
    if not packs(n, w):
        dst[...] = whole(src)
        return
    k = w // BLOCK

    def both(block, i, j):
        dst[i * BLOCK : (i + 1) * BLOCK, j * BLOCK : (j + 1) * BLOCK] = block
        if i != j:
            dst[j * BLOCK : (j + 1) * BLOCK, i * BLOCK : (i + 1) * BLOCK] = block.T

    seen = set()
    for p in range(n):
        at = 0
        for i, j in triangle(k):
            both(src[p, at : at + BLOCK, :], p * k + i, p * k + j)
            at += BLOCK
        for a, b in halves(k)[p]:
            if (a, b) not in seen:
                i, j = (b, k + a) if p else (k + a, b)
                both(src[p, at : at + BLOCK, :], i, j)
            seen.add((a, b))
            at += BLOCK


def panel_of(matrix, q, n, use):
    w = matrix.shape[1] // n
    for p in range(n):

        @pl.when(q == p)
        def _():
            use(matrix[:, p * w : (p + 1) * w])


def split(refs, *counts):
    out, at = [], 0
    for c in counts:
        out.append(refs[at : at + c])
        at += c
    return out


def call(kernel, ins, in_specs, outs, scratch, flops, aliases=None):
    size = sum(a.size * a.dtype.itemsize for a in ins) + sum(
        o.size * o.dtype.itemsize for o in outs
    )
    return pl.pallas_call(
        kernel,
        in_specs=in_specs,
        out_specs=[VMEM] * len(outs),
        out_shape=outs,
        scratch_shapes=scratch,
        input_output_aliases=aliases or {},
        compiler_params=pltpu.CompilerParams(vmem_limit_bytes=24 * MIB),
        cost_estimate=pl.CostEstimate(flops=flops, bytes_accessed=size, transcendentals=0),
    )(*ins)


def base_kernel(n, *refs):
    factor, sigma, f_parts, c_parts, (base, base_bf), (f_all, c_all, sig, sems) = split(
        refs, 1, 1, n, n, 2, 4
    )
    factor, sigma = factor[0], sigma[0]
    hi, lo, q = where_am_i()
    width = factor.shape[1]
    run(copy_all(panel_pairs(f_parts, f_all, q), sems))
    own = factor[...]
    high = own.astype(BF)
    low = (own - high.astype(F32)).astype(BF)
    for p in range(n):
        part = f_all[p]
        base[p * width : (p + 1) * width, :] = mm_t(part, high) + mm_t(part, low)

    @pl.when(lax.axis_index("tm") == lax.axis_size("tm") - 1)
    def _():
        run(copy_all(panel_pairs(c_parts, c_all, q) + [(sigma, sig)], sems))
        s = sig[...]
        s_high = s.astype(BF)
        s_low = (s - s_high.astype(F32)).astype(BF)
        c_own = c_all[q]
        mid = mm(s_high, c_own) + mm(s_low, c_own)
        mid_high = mid.astype(BF)
        mid_low = (mid - mid_high.astype(F32)).astype(BF)
        c_full = whole(c_all)
        base[...] += mm_t(c_full, mid_high) + mm_t(c_full, mid_low)

    pack(base, base_bf, q, n)


def pair_product(c, member):
    odd = lax.rem(member, 2)
    return mm(whole(c.at[member - odd + 1]), whole(c.at[member - odd])).astype(BF)


def near_comp_kernel(n, *refs):
    own, first, second, (c, c_t, pair), (sems,) = split(refs, n, n, n, 3, 1)
    hi, lo, q = where_am_i()
    pairs = []
    for r in range(n):
        p = lax.rem(q + r, n)
        even = 1 - lax.rem(p, 2)
        for mask, piece in ((0, own[r]), (1 + even, first[r]), (2 - even, second[r])):
            pairs.append((piece, c.at[jnp.bitwise_xor(lo, mask), p]))
    run(copy_all(pairs, sems))
    pair[...] = pair_product(c, lo)
    for mask in range(GROUP - 1):
        slot = jnp.bitwise_xor(lo, mask)
        c_t[slot] = whole(c.at[slot]).T


def group_comp_kernel(n, *refs):
    (c, pair), diag, outs, (other, sems) = split(refs, 2, n, 5, 2)
    c_out, c01, c23, agg_cols, share = outs
    hi, lo, q = where_am_i()
    far = jnp.bitwise_xor(lo, 3)
    run(copy_all(panel_pairs(diag, c_out.at[far], q), sems))
    other[...] = pair_product(c_out, far)

    @pl.when(lo < 2)
    def _():
        put(c01, pair[...])
        c23[...] = other[...]

    @pl.when(lo >= 2)
    def _():
        put(c01, other[...])
        c23[...] = pair[...]

    agg_cols[...] = mm(c23[...], c01[q]).astype(BF)
    share[...] = agg_cols[quarter_rows(lo, agg_cols.shape[0]), :]


def turn_comp_kernel(c, c_t, c01, c_t_out, c01_t):
    hi, lo, q = where_am_i()
    far = jnp.bitwise_xor(lo, 3)
    c_t_out[far] = whole(c.at[far]).T
    c01_t[...] = whole(c01).T


def tail_comp_kernel(c, c01, c23, agg, agg_t, mine, mine_t):
    hi, lo, q = where_am_i()
    put(agg, mm(c23[...], whole(c01)))
    agg_t[...] = whole(agg).T

    @pl.when(lo == 0)
    def _():
        mine[...] = agg[...]

    @pl.when(lo == 1)
    def _():
        put(mine, mm(c23[...], whole(c.at[1])))

    @pl.when(lo == 2)
    def _():
        put(mine, c23[...])

    @pl.when(lo == 3)
    def _():
        mine[...] = c[3]

    mine_t[...] = whole(mine).T


def sandwich(cov, comp, comp_t):
    return mm(comp_t, mm(cov, comp).astype(BF))


def group_cov_kernel(n, *refs):
    ins, *blocks, outs, scratch = split(refs, 5, n, n, n, n, 4, 3)
    base, c, c_t, c01, c01_t = ins
    agg, agg_bf, s3, s23 = outs
    sent, s, sems = scratch
    hi, lo, q = where_am_i()
    group_start(blocks, sent, sems, lo, q)
    group_wait(blocks[0], sent, sems, 3, 2, 1, 0)
    unpack(sent.at[3], s3, n)
    for k in range(GROUP - 1):
        unpack(sent.at[k], s.at[k], n)
    mid = mm(s3[...], whole(c.at[2])).astype(BF)
    s23[...] = (s[2].astype(F32) + mm(c_t[2], mid)).astype(BF)
    w = agg.shape[1]
    first = s[0, :, :w]
    for p in range(1, n):
        first = jnp.where(q == p, s[0, :, p * w : (p + 1) * w], first)
    total = jnp.where(lo == 0, base[...], first.astype(F32))
    total += sandwich(s[1], c[0, q], c_t[0])
    agg[...] = total + sandwich(s23[...], c01[q], c01_t[...])
    pack(agg, agg_bf, q, n)


def group_mine_kernel(base, agg, s3, s23, c, c_t, mine):
    hi, lo, q = where_am_i()

    @pl.when(lo == 0)
    def _():
        mine[...] = agg[...]

    @pl.when(lo == 1)
    def _():
        mine[...] = base[...] + sandwich(s23[...], c[1, q], c_t[1])

    @pl.when(lo == 2)
    def _():
        mine[...] = base[...] + sandwich(s3[...], c[2, q], c_t[2])

    @pl.when(lo == 3)
    def _():
        mine[...] = base[...]


def is_lower(bit):
    hi, lo, q = where_am_i()
    return lax.rem(hi // (1 << bit), 2) == 0


def panel_rows(q, r, n, w):
    return pl.ds(pl.multiple_of(lax.rem(q + r, n) * w, w), w)


def quarter_rows(place, nb):
    rows = nb // GROUP
    return pl.ds(pl.multiple_of(place * rows, rows), rows)


def times(pieces, right, q):
    n = len(pieces)
    w = right.shape[0] // n
    return sum(mm(x[...], right[panel_rows(q, r, n, w), :]) for r, x in enumerate(pieces))


def place_whole(pieces, dst, q):
    for r, piece in enumerate(pieces):
        dst[lax.rem(q + r, len(pieces))] = piece[...]


def join_kernel(*refs):
    *quarters, out = refs
    hi, lo, q = where_am_i()
    for k, piece in enumerate(quarters[::-1]):
        out[quarter_rows(jnp.bitwise_xor(lo, k), out.shape[0]), :] = piece[...]


def select_kernel(*refs):
    *got, out = refs
    hi, lo, q = where_am_i()
    d = len(got)
    for k, piece in enumerate(got):

        @pl.when(lax.rem(hi, d) == k)
        def _():
            out[...] = piece[...]


def share_comp_kernel(n, agg_cols, *refs):
    quarters, (share,) = split(refs, n, 1)
    hi, lo, q = where_am_i()
    share[...] = times(quarters, agg_cols, q).astype(BF)


def pair_comp_kernel(n, agg, *refs):
    parts, (new_agg, new_agg_t, new_cols, share) = split(refs, n, 4)
    hi, lo, q = where_am_i()
    for p in range(n):
        new_agg[p] = times(parts, agg.at[p], q).astype(BF)
    new_agg_t[...] = whole(new_agg).T
    new_cols[...] = new_agg[q]
    share[...] = new_cols[quarter_rows(lo, new_cols.shape[0]), :]


def mine_comp_kernel(n, bit, *refs):
    (mine, mine_t), parts, (new_mine, new_mine_t) = split(refs, 2, n, 2)
    hi, lo, q = where_am_i()
    lower = is_lower(bit)

    @pl.when(lower)
    def _():
        for p in range(n):
            new_mine[p] = times(parts, mine.at[p], q).astype(BF)
        new_mine_t[...] = whole(new_mine).T

    @pl.when(jnp.logical_not(lower))
    def _():
        new_mine[...] = mine[...]
        new_mine_t[...] = mine_t[...]


def last_comp_kernel(n, bit, *refs):
    (mine,), parts, (out,) = split(refs, 1, n, 1)
    hi, lo, q = where_am_i()
    lower = is_lower(bit)

    @pl.when(lower)
    def _():
        out[0] = times(parts, mine.at[q], q).astype(BF)

    @pl.when(jnp.logical_not(lower))
    def _():
        out[0] = mine[q]


def pair_cov_kernel(n, to_last, agg, agg_cols, agg_t, *refs):
    parts, outs, (sent, total, packed) = split(refs, n, 2 if to_last else 4, 3)
    share, right = outs[:2]
    hi, lo, q = where_am_i()
    place_whole(parts, sent, q)
    unpack(sent, right, n)
    total[...] = agg[...] + sandwich(right[...], agg_cols[...], agg_t[...])
    pack(total, packed, q, n)
    share[...] = packed[quarter_rows(lo, packed.shape[0]), :]
    if not to_last:
        outs[2][...] = total[...]
        outs[3][...] = packed[...]


def mine_cov_kernel(n, bit, cov, mine, mine_t, right, out):
    hi, lo, q = where_am_i()
    lower = is_lower(bit)

    @pl.when(lower)
    def _():
        out[...] = cov[...] + sandwich(right[...], mine[q], mine_t[...])

    @pl.when(jnp.logical_not(lower))
    def _():
        out[...] = cov[...]


def last_cov_kernel(n, bit, *refs):
    (cov, mine, mine_t), parts, (out,), (sent, right) = split(refs, 3, n, 1, 2)
    hi, lo, q = where_am_i()
    lower = is_lower(bit)

    @pl.when(lower)
    def _():
        place_whole(parts, sent, q)
        unpack(sent, right, n)
        out[0] = cov[...] + sandwich(right[...], mine[q], mine_t[...])

    @pl.when(jnp.logical_not(lower))
    def _():
        out[0] = cov[...]


def over_panels(x):
    n = lax.axis_size("panel")
    return [x] + [
        lax.ppermute(x, "panel", [((i + r) % n, i) for i in range(n)]) for r in range(1, n)
    ]


def swap(value, odd_mask, even_mask):
    steps, n = lax.axis_size("tm"), lax.axis_size("panel")
    pairs = []
    for t in range(steps):
        for q in range(n):
            mask = odd_mask if q % 2 else even_mask
            pairs.append((t * n + q, (t ^ mask) * n + q))
    return lax.ppermute(value, ("tm", "panel"), pairs)


def across(x, bit):
    steps = lax.axis_size("tm")
    d = 1 << bit
    got = []
    for back in range(1, d + 1):
        pairs = [
            (g * GROUP + k, (g - back) * GROUP + k)
            for g in range(d, steps // GROUP, 2 * d)
            for k in range(GROUP)
        ]
        got.append(lax.ppermute(x, "tm", pairs))
    if d == 1:
        return got[0]
    return call(select_kernel, got[::-1], [VMEM] * d, [jax.ShapeDtypeStruct(x.shape, x.dtype)], [], 0)[0]


def in_group(x):
    return [x] + [swap(x, mask, mask) for mask in range(1, GROUP)]


def joined(quarters):
    rows, lanes = quarters[0].shape
    whole_panel = jax.ShapeDtypeStruct((rows * GROUP, lanes), BF)
    return call(join_kernel, quarters[::-1], [VMEM] * GROUP, [whole_panel], [], 0)[0]


def after(x, *others):
    return lax.optimization_barrier((x, *others))[0]


def shards(factor_inverse, coupling, sigma_after):
    steps = lax.axis_size("tm")
    n = lax.axis_size("panel")
    nb, w = factor_inverse.shape[1:]
    levels = (steps // GROUP - 1).bit_length()
    panel_bf = jax.ShapeDtypeStruct((nb, w), BF)
    panel_f32 = jax.ShapeDtypeStruct((nb, w), F32)
    full_bf = jax.ShapeDtypeStruct((n, nb, w), BF)
    square_bf = jax.ShapeDtypeStruct((nb, nb), BF)
    group_bf = jax.ShapeDtypeStruct((GROUP, n, nb, w), BF)
    turned_bf = jax.ShapeDtypeStruct((GROUP, nb, nb), BF)
    share_bf = jax.ShapeDtypeStruct((nb // GROUP, w), BF)
    full_scratch = pltpu.VMEM((n, nb, w), BF)
    rows, lanes = packed_shape(n, nb, w)
    packed_bf = jax.ShapeDtypeStruct((rows, lanes), BF)
    packed_share = jax.ShapeDtypeStruct((rows // GROUP, lanes), BF)
    packed_scratch = pltpu.VMEM((n, rows, lanes), BF)
    square_scratch = pltpu.VMEM((nb, nb), BF)
    one = 2 * nb * nb * w
    sems = pltpu.SemaphoreType.DMA

    comp = coupling[0].astype(BF)
    c_first = swap(comp, 1, 2)
    c_second = swap(comp, 2, 1)
    factor = after(factor_inverse[0], comp)
    f_parts = over_panels(factor.astype(BF))
    c_own = over_panels(comp)
    base, base_bf = call(
        functools.partial(base_kernel, n),
        [factor, sigma_after, *f_parts, *c_own],
        [VMEM] + [ANY] * (1 + 2 * n),
        [panel_f32, packed_bf],
        [full_scratch, full_scratch, pltpu.VMEM((nb, n * w), F32), sems((n + 1,))],
        2 * one,
    )
    s_first = swap(base_bf, 1, 2)
    c_diag = swap(c_first, 2, 1)
    s_second = swap(base_bf, 2, 1)
    s_diag = swap(s_first, 2, 1)
    c_near = [p for v in (c_first, c_second) for p in over_panels(v)]
    c_all, c_t, pair = call(
        functools.partial(near_comp_kernel, n),
        c_own + c_near,
        [ANY] * (3 * n),
        [group_bf, turned_bf, square_bf],
        [sems((3 * n,))],
        n * one,
    )
    c_all, c01, c23, agg_cols, c_share = call(
        functools.partial(group_comp_kernel, n),
        [c_all, pair, *over_panels(after(c_diag, s_first, pair))],
        [VMEM] * 2 + [ANY] * n,
        [group_bf, full_bf, square_bf, panel_bf, share_bf],
        [square_scratch, sems((n,))],
        2 * n * one,
        {0: 0},
    )
    c_far = across(c_share, 0)
    c_t, c01_t = call(
        turn_comp_kernel, [c_all, c_t, c01], [VMEM] * 3, [turned_bf, square_bf], [], 0, {1: 0}
    )
    s_second, s_diag = after(s_second, c_share), after(s_diag, c_t)
    s_pieces = [p for v in (base_bf, s_first, s_second, s_diag) for p in over_panels(v)]
    agg, agg_bf, s3, s23 = call(
        functools.partial(group_cov_kernel, n),
        [base, c_all, c_t, c01, c01_t, *s_pieces],
        [VMEM] * 5 + [ANY] * (GROUP * n),
        [panel_f32, packed_bf, square_bf, square_bf],
        [
            pltpu.VMEM((GROUP, n, rows, lanes), BF),
            pltpu.VMEM((GROUP - 1, nb, nb), BF),
            sems((GROUP, n)),
        ],
        (2 * n + 4) * one,
    )
    agg_c, agg_t, mine, mine_t = call(
        tail_comp_kernel,
        [c_all, c01, after(c23, agg_bf)],
        [VMEM] * 3,
        [full_bf, square_bf, full_bf, square_bf],
        [],
        2 * n * one,
    )
    (cov,) = call(
        group_mine_kernel,
        [base, agg, s3, s23, c_all, c_t],
        [VMEM] * 6,
        [panel_f32],
        [],
        2 * one,
    )
    out_cov = jax.ShapeDtypeStruct((1, nb, w), F32)
    out_comp = jax.ShapeDtypeStruct((1, nb, w), BF)
    sum_scratch = pltpu.VMEM((nb, w), F32)
    c_far = after(c_far, agg_bf)
    s_got = across(agg_bf, 0)
    for bit in range(levels):
        to_last = bit + 2 == levels
        if bit + 1 == levels:
            c_blocks = in_group(c_far)
            if bit:
                c_blocks[0] = after(c_blocks[0], cov)
            c_panel = joined(c_blocks)
            if bit:
                c_panel = after(c_panel, *s_blocks[1:])
            c_parts = over_panels(c_panel)
            (prop,) = call(
                functools.partial(last_comp_kernel, n, bit),
                [after(mine, s_got), *c_parts],
                [VMEM] * (1 + n),
                [out_comp],
                [],
                one,
            )
            s_parts = over_panels(s_got)
            (cov,) = call(
                functools.partial(last_cov_kernel, n, bit),
                [cov, mine, mine_t, *s_parts],
                [VMEM] * (3 + n),
                [out_cov],
                [packed_scratch, square_scratch],
                2 * one,
            )
            break
        if to_last:
            (c_send,) = call(
                functools.partial(share_comp_kernel, n),
                [agg_cols, *over_panels(c_far)],
                [VMEM] * (1 + n),
                [share_bf],
                [],
                one // 4,
            )
            c_blocks = in_group(after(c_far, c_send))
            c_parts = over_panels(joined(c_blocks))
        else:
            c_blocks = in_group(c_far)
            c_parts = over_panels(joined(c_blocks))
            new_agg_c, new_agg_t, new_cols, c_send = call(
                functools.partial(pair_comp_kernel, n),
                [agg_c, *c_parts],
                [VMEM] * (1 + n),
                [full_bf, square_bf, panel_bf, share_bf],
                [],
                n * one,
            )
        c_far = across(c_send, bit + 1)
        new_mine, new_mine_t = call(
            functools.partial(mine_comp_kernel, n, bit),
            [after(mine, c_send), mine_t, *c_parts],
            [VMEM] * (2 + n),
            [full_bf, square_bf],
            [],
            n * one,
        )
        s_parts = over_panels(after(s_got, mine, cov, c_far, c_blocks[2], c_blocks[3]))
        outs = call(
            functools.partial(pair_cov_kernel, n, to_last),
            [agg, agg_cols, agg_t, *s_parts],
            [VMEM] * (3 + n),
            [packed_share, square_bf] + ([] if to_last else [panel_f32, packed_bf]),
            [packed_scratch, sum_scratch, pltpu.VMEM((rows, lanes), BF)],
            2 * one,
        )
        s_send, right = outs[:2]
        s_far = across(s_send, bit + 1)
        (cov,) = call(
            functools.partial(mine_cov_kernel, n, bit),
            [after(cov, s_far), mine, mine_t, right],
            [VMEM] * 4,
            [panel_f32],
            [],
            2 * one,
        )
        if not to_last:
            agg, agg_bf = outs[2:]
            agg_c, agg_t, agg_cols = new_agg_c, new_agg_t, new_cols
        s_blocks = in_group(s_far)
        s_got = joined(s_blocks)
        c_far = after(c_far, s_send)
        mine, mine_t = new_mine, new_mine_t
    return cov, prop


def solution(mesh):
    placed = (P("tm", None, "panel"), P("tm", None, "panel"), P())
    return jax.shard_map(
        shards,
        mesh=mesh,
        in_specs=placed,
        out_specs=(P("tm", None, "panel"), P("tm", None, "panel")),
        check_vma=False,
    )
```

```python
import functools

import jax
import jax.numpy as jnp
from jax import lax
from jax.experimental import pallas as pl
from jax.experimental.pallas import tpu as pltpu
from jax.sharding import PartitionSpec as P

BF = jnp.bfloat16
F32 = jnp.float32
GROUP = 4
BLOCK = 128
ANY = pl.BlockSpec(memory_space=pl.ANY)
VMEM = pl.BlockSpec(memory_space=pltpu.VMEM)
MIB = 1 << 20


def mm(a, b):
    return jnp.dot(a, b, preferred_element_type=F32)


def mm_t(a, b):
    return lax.dot_general(a, b, (((0,), (0,)), ((), ())), preferred_element_type=F32)


def whole(ref):
    return jnp.concatenate([ref[p] for p in range(ref.shape[0])], axis=1)


def put(ref, value):
    width = ref.shape[2]
    for p in range(ref.shape[0]):
        ref[p] = value[:, p * width : (p + 1) * width].astype(ref.dtype)


def where_am_i():
    t = lax.axis_index("tm")
    return t // GROUP, lax.rem(t, GROUP), lax.axis_index("panel")


def run(copies):
    for c in copies:
        c.start()
    for c in copies:
        c.wait()


def copy_all(pairs, sems):
    return [pltpu.make_async_copy(s, d, sems.at[i]) for i, (s, d) in enumerate(pairs)]


def panel_pairs(pieces, dst, q):
    n = len(pieces)
    return [(piece, dst.at[lax.rem(q + r, n)]) for r, piece in enumerate(pieces)]


def group_start(blocks, dst, sems, lo, q):
    own, first, second, diag = blocks
    n = len(own)
    for r in range(n):
        p = lax.rem(q + r, n)
        even = 1 - lax.rem(p, 2)
        for mask, piece in ((3, diag[r]), (1 + even, first[r]), (2 - even, second[r]), (0, own[r])):
            slot = jnp.bitwise_xor(lo, mask)
            pltpu.make_async_copy(piece, dst.at[slot, p], sems.at[slot, p]).start()


def group_wait(own, dst, sems, *slots):
    for slot in slots:
        for p in range(len(own)):
            pltpu.make_async_copy(own[p], dst.at[slot, p], sems.at[slot, p]).wait()


def packs(n, w):
    return n == 2 and w % BLOCK == 0


def packed_shape(n, nb, w):
    if not packs(n, w):
        return nb, w
    k = w // BLOCK
    return (k * (k + 1) // 2 + (k * k + 1) // 2) * BLOCK, BLOCK


def triangle(k):
    return [(i, j) for i in range(k) for j in range(i + 1)]


def halves(k):
    every = [(a, b) for a in range(k) for b in range(k)]
    half = (k * k + 1) // 2
    return every[:half], every[k * k - half :]


def pack(panel, out, q, n):
    nb, w = panel.shape
    if not packs(n, w):
        out[...] = panel[...].astype(BF)
        return
    k = w // BLOCK
    at = 0
    for i, j in triangle(k):
        rows = pl.ds(pl.multiple_of(q * w + i * BLOCK, BLOCK), BLOCK)
        out[at : at + BLOCK, :] = panel[rows, j * BLOCK : (j + 1) * BLOCK].astype(BF)
        at += BLOCK
    for side, blocks in enumerate(halves(k)):

        @pl.when(q == side)
        def _():
            to = at
            for a, b in blocks:
                i, j = (b, a) if side else (w // BLOCK + a, b)
                value = panel[i * BLOCK : (i + 1) * BLOCK, j * BLOCK : (j + 1) * BLOCK]
                out[to : to + BLOCK, :] = value.astype(BF)
                to += BLOCK


def unpack(src, dst, n):
    nb = dst.shape[0]
    w = nb // n
    if not packs(n, w):
        dst[...] = whole(src)
        return
    k = w // BLOCK

    def both(block, i, j):
        dst[i * BLOCK : (i + 1) * BLOCK, j * BLOCK : (j + 1) * BLOCK] = block
        if i != j:
            dst[j * BLOCK : (j + 1) * BLOCK, i * BLOCK : (i + 1) * BLOCK] = block.T

    seen = set()
    for p in range(n):
        at = 0
        for i, j in triangle(k):
            both(src[p, at : at + BLOCK, :], p * k + i, p * k + j)
            at += BLOCK
        for a, b in halves(k)[p]:
            if (a, b) not in seen:
                i, j = (b, k + a) if p else (k + a, b)
                both(src[p, at : at + BLOCK, :], i, j)
            seen.add((a, b))
            at += BLOCK


def panel_of(matrix, q, n, use):
    w = matrix.shape[1] // n
    for p in range(n):

        @pl.when(q == p)
        def _():
            use(matrix[:, p * w : (p + 1) * w])


def split(refs, *counts):
    out, at = [], 0
    for c in counts:
        out.append(refs[at : at + c])
        at += c
    return out


def call(kernel, ins, in_specs, outs, scratch, flops, aliases=None):
    size = sum(a.size * a.dtype.itemsize for a in ins) + sum(
        o.size * o.dtype.itemsize for o in outs
    )
    return pl.pallas_call(
        kernel,
        in_specs=in_specs,
        out_specs=[VMEM] * len(outs),
        out_shape=outs,
        scratch_shapes=scratch,
        input_output_aliases=aliases or {},
        compiler_params=pltpu.CompilerParams(vmem_limit_bytes=24 * MIB),
        cost_estimate=pl.CostEstimate(flops=flops, bytes_accessed=size, transcendentals=0),
    )(*ins)


def base_kernel(n, *refs):
    factor, sigma, f_parts, c_parts, (base, base_bf), (f_all, c_all, sig, sems) = split(
        refs, 1, 1, n, n, 2, 4
    )
    factor, sigma = factor[0], sigma[0]
    hi, lo, q = where_am_i()
    width = factor.shape[1]
    run(copy_all(panel_pairs(f_parts, f_all, q), sems))
    own = factor[...]
    high = own.astype(BF)
    low = (own - high.astype(F32)).astype(BF)
    for p in range(n):
        part = f_all[p]
        base[p * width : (p + 1) * width, :] = mm_t(part, high) + mm_t(part, low)

    @pl.when(lax.axis_index("tm") == lax.axis_size("tm") - 1)
    def _():
        run(copy_all(panel_pairs(c_parts, c_all, q) + [(sigma, sig)], sems))
        s = sig[...]
        s_high = s.astype(BF)
        s_low = (s - s_high.astype(F32)).astype(BF)
        c_own = c_all[q]
        mid = mm(s_high, c_own) + mm(s_low, c_own)
        mid_high = mid.astype(BF)
        mid_low = (mid - mid_high.astype(F32)).astype(BF)
        c_full = whole(c_all)
        base[...] += mm_t(c_full, mid_high) + mm_t(c_full, mid_low)

    pack(base, base_bf, q, n)


def pair_product(c, member):
    odd = lax.rem(member, 2)
    return mm(whole(c.at[member - odd + 1]), whole(c.at[member - odd])).astype(BF)


def near_comp_kernel(n, *refs):
    own, first, second, (c, c_t, pair), (sems,) = split(refs, n, n, n, 3, 1)
    hi, lo, q = where_am_i()
    pairs = []
    for r in range(n):
        p = lax.rem(q + r, n)
        even = 1 - lax.rem(p, 2)
        for mask, piece in ((0, own[r]), (1 + even, first[r]), (2 - even, second[r])):
            pairs.append((piece, c.at[jnp.bitwise_xor(lo, mask), p]))
    run(copy_all(pairs, sems))
    pair[...] = pair_product(c, lo)
    for mask in range(GROUP - 1):
        slot = jnp.bitwise_xor(lo, mask)
        c_t[slot] = whole(c.at[slot]).T


def group_comp_kernel(n, *refs):
    (c, pair), diag, outs, (other, sems) = split(refs, 2, n, 5, 2)
    c_out, c01, c23, agg_cols, share = outs
    hi, lo, q = where_am_i()
    far = jnp.bitwise_xor(lo, 3)
    run(copy_all(panel_pairs(diag, c_out.at[far], q), sems))
    other[...] = pair_product(c_out, far)

    @pl.when(lo < 2)
    def _():
        put(c01, pair[...])
        c23[...] = other[...]

    @pl.when(lo >= 2)
    def _():
        put(c01, other[...])
        c23[...] = pair[...]

    agg_cols[...] = mm(c23[...], c01[q]).astype(BF)
    share[...] = agg_cols[quarter_rows(lo, agg_cols.shape[0]), :]


def turn_comp_kernel(c, c_t, c01, c_t_out, c01_t):
    hi, lo, q = where_am_i()
    far = jnp.bitwise_xor(lo, 3)
    c_t_out[far] = whole(c.at[far]).T
    c01_t[...] = whole(c01).T


def tail_comp_kernel(c, c01, c23, agg, agg_t, mine, mine_t):
    hi, lo, q = where_am_i()
    put(agg, mm(c23[...], whole(c01)))
    agg_t[...] = whole(agg).T

    @pl.when(lo == 0)
    def _():
        mine[...] = agg[...]

    @pl.when(lo == 1)
    def _():
        put(mine, mm(c23[...], whole(c.at[1])))

    @pl.when(lo == 2)
    def _():
        put(mine, c23[...])

    @pl.when(lo == 3)
    def _():
        mine[...] = c[3]

    mine_t[...] = whole(mine).T


def sandwich(cov, comp, comp_t):
    return mm(comp_t, mm(cov, comp).astype(BF))


def group_cov_kernel(n, *refs):
    ins, *blocks, outs, scratch = split(refs, 5, n, n, n, n, 4, 3)
    base, c, c_t, c01, c01_t = ins
    agg, agg_bf, s3, s23 = outs
    sent, s, sems = scratch
    hi, lo, q = where_am_i()
    group_start(blocks, sent, sems, lo, q)
    group_wait(blocks[0], sent, sems, 3, 2, 1, 0)
    unpack(sent.at[3], s3, n)
    for k in range(GROUP - 1):
        unpack(sent.at[k], s.at[k], n)
    mid = mm(s3[...], whole(c.at[2])).astype(BF)
    s23[...] = (s[2].astype(F32) + mm(c_t[2], mid)).astype(BF)
    w = agg.shape[1]
    first = s[0, :, :w]
    for p in range(1, n):
        first = jnp.where(q == p, s[0, :, p * w : (p + 1) * w], first)
    total = jnp.where(lo == 0, base[...], first.astype(F32))
    total += sandwich(s[1], c[0, q], c_t[0])
    agg[...] = total + sandwich(s23[...], c01[q], c01_t[...])
    pack(agg, agg_bf, q, n)


def group_mine_kernel(base, agg, s3, s23, c, c_t, mine):
    hi, lo, q = where_am_i()

    @pl.when(lo == 0)
    def _():
        mine[...] = agg[...]

    @pl.when(lo == 1)
    def _():
        mine[...] = base[...] + sandwich(s23[...], c[1, q], c_t[1])

    @pl.when(lo == 2)
    def _():
        mine[...] = base[...] + sandwich(s3[...], c[2, q], c_t[2])

    @pl.when(lo == 3)
    def _():
        mine[...] = base[...]


def is_lower(bit):
    hi, lo, q = where_am_i()
    return lax.rem(hi // (1 << bit), 2) == 0


def panel_rows(q, r, n, w):
    return pl.ds(pl.multiple_of(lax.rem(q + r, n) * w, w), w)


def quarter_rows(place, nb):
    rows = nb // GROUP
    return pl.ds(pl.multiple_of(place * rows, rows), rows)


def times(pieces, right, q):
    n = len(pieces)
    w = right.shape[0] // n
    return sum(mm(x[...], right[panel_rows(q, r, n, w), :]) for r, x in enumerate(pieces))


def place_whole(pieces, dst, q):
    for r, piece in enumerate(pieces):
        dst[lax.rem(q + r, len(pieces))] = piece[...]


def join_kernel(*refs):
    *quarters, out = refs
    hi, lo, q = where_am_i()
    for k, piece in enumerate(quarters):
        out[quarter_rows(jnp.bitwise_xor(lo, k), out.shape[0]), :] = piece[...]


def select_kernel(*refs):
    *got, out = refs
    hi, lo, q = where_am_i()
    d = len(got)
    for k, piece in enumerate(got):

        @pl.when(lax.rem(hi, d) == k)
        def _():
            out[...] = piece[...]


def share_comp_kernel(n, agg_cols, *refs):
    quarters, (share,) = split(refs, n, 1)
    hi, lo, q = where_am_i()
    share[...] = times(quarters, agg_cols, q).astype(BF)


def pair_comp_kernel(n, agg, *refs):
    parts, (new_agg, new_agg_t, new_cols, share) = split(refs, n, 4)
    hi, lo, q = where_am_i()
    for p in range(n):
        new_agg[p] = times(parts, agg.at[p], q).astype(BF)
    new_agg_t[...] = whole(new_agg).T
    new_cols[...] = new_agg[q]
    share[...] = new_cols[quarter_rows(lo, new_cols.shape[0]), :]


def mine_comp_kernel(n, bit, *refs):
    (mine, mine_t), parts, (new_mine, new_mine_t) = split(refs, 2, n, 2)
    hi, lo, q = where_am_i()
    lower = is_lower(bit)

    @pl.when(lower)
    def _():
        for p in range(n):
            new_mine[p] = times(parts, mine.at[p], q).astype(BF)
        new_mine_t[...] = whole(new_mine).T

    @pl.when(jnp.logical_not(lower))
    def _():
        new_mine[...] = mine[...]
        new_mine_t[...] = mine_t[...]


def pair_cov_kernel(n, to_last, agg, agg_cols, agg_t, *refs):
    parts, outs, (sent, total, packed) = split(refs, n, 2 if to_last else 4, 3)
    share, right = outs[:2]
    hi, lo, q = where_am_i()
    place_whole(parts, sent, q)
    unpack(sent, right, n)
    total[...] = agg[...] + sandwich(right[...], agg_cols[...], agg_t[...])
    pack(total, packed, q, n)
    share[...] = packed[quarter_rows(lo, packed.shape[0]), :]
    if not to_last:
        outs[2][...] = total[...]
        outs[3][...] = packed[...]


def mine_cov_kernel(n, bit, cov, mine, mine_t, right, out):
    hi, lo, q = where_am_i()
    lower = is_lower(bit)

    @pl.when(lower)
    def _():
        out[...] = cov[...] + sandwich(right[...], mine[q], mine_t[...])

    @pl.when(jnp.logical_not(lower))
    def _():
        out[...] = cov[...]


def last_kernel(n, bit, *refs):
    (cov, mine, mine_t), c_parts, s_parts, (out, prop), scratch = split(refs, 3, n, n, 2, 2)
    sent, right = scratch
    hi, lo, q = where_am_i()
    lower = is_lower(bit)

    @pl.when(lower)
    def _():
        place_whole(s_parts, sent, q)
        unpack(sent, right, n)
        out[0] = cov[...] + sandwich(right[...], mine[q], mine_t[...])
        prop[0] = times(c_parts, mine.at[q], q).astype(BF)

    @pl.when(jnp.logical_not(lower))
    def _():
        out[0] = cov[...]
        prop[0] = mine[q]


def over_panels(x):
    n = lax.axis_size("panel")
    return [x] + [
        lax.ppermute(x, "panel", [((i + r) % n, i) for i in range(n)]) for r in range(1, n)
    ]


def swap(value, odd_mask, even_mask):
    steps, n = lax.axis_size("tm"), lax.axis_size("panel")
    pairs = []
    for t in range(steps):
        for q in range(n):
            mask = odd_mask if q % 2 else even_mask
            pairs.append((t * n + q, (t ^ mask) * n + q))
    return lax.ppermute(value, ("tm", "panel"), pairs)


def across(x, bit):
    steps = lax.axis_size("tm")
    d = 1 << bit
    got = []
    for back in range(1, d + 1):
        pairs = [
            (g * GROUP + k, (g - back) * GROUP + k)
            for g in range(d, steps // GROUP, 2 * d)
            for k in range(GROUP)
        ]
        got.append(lax.ppermute(x, "tm", pairs))
    if d == 1:
        return got[0]
    return call(select_kernel, got[::-1], [VMEM] * d, [jax.ShapeDtypeStruct(x.shape, x.dtype)], [], 0)[0]


def in_group(x):
    return [x] + [swap(x, mask, mask) for mask in range(1, GROUP)]


def joined(quarters):
    rows, lanes = quarters[0].shape
    whole_panel = jax.ShapeDtypeStruct((rows * GROUP, lanes), BF)
    return call(join_kernel, quarters, [VMEM] * GROUP, [whole_panel], [], 0)[0]


def after(x, *others):
    return lax.optimization_barrier((x, *others))[0]


def shards(factor_inverse, coupling, sigma_after):
    steps = lax.axis_size("tm")
    n = lax.axis_size("panel")
    nb, w = factor_inverse.shape[1:]
    levels = (steps // GROUP - 1).bit_length()
    panel_bf = jax.ShapeDtypeStruct((nb, w), BF)
    panel_f32 = jax.ShapeDtypeStruct((nb, w), F32)
    full_bf = jax.ShapeDtypeStruct((n, nb, w), BF)
    square_bf = jax.ShapeDtypeStruct((nb, nb), BF)
    group_bf = jax.ShapeDtypeStruct((GROUP, n, nb, w), BF)
    turned_bf = jax.ShapeDtypeStruct((GROUP, nb, nb), BF)
    share_bf = jax.ShapeDtypeStruct((nb // GROUP, w), BF)
    full_scratch = pltpu.VMEM((n, nb, w), BF)
    rows, lanes = packed_shape(n, nb, w)
    packed_bf = jax.ShapeDtypeStruct((rows, lanes), BF)
    packed_share = jax.ShapeDtypeStruct((rows // GROUP, lanes), BF)
    packed_scratch = pltpu.VMEM((n, rows, lanes), BF)
    square_scratch = pltpu.VMEM((nb, nb), BF)
    one = 2 * nb * nb * w
    sems = pltpu.SemaphoreType.DMA

    comp = coupling[0].astype(BF)
    c_first = swap(comp, 1, 2)
    c_second = swap(comp, 2, 1)
    factor = after(factor_inverse[0], comp)
    f_parts = over_panels(factor.astype(BF))
    c_own = over_panels(comp)
    base, base_bf = call(
        functools.partial(base_kernel, n),
        [factor, sigma_after, *f_parts, *c_own],
        [VMEM] + [ANY] * (1 + 2 * n),
        [panel_f32, packed_bf],
        [full_scratch, full_scratch, pltpu.VMEM((nb, n * w), F32), sems((n + 1,))],
        2 * one,
    )
    s_first = swap(base_bf, 1, 2)
    c_diag = swap(c_first, 2, 1)
    s_second = swap(base_bf, 2, 1)
    s_diag = swap(s_first, 2, 1)
    c_near = [p for v in (c_first, c_second) for p in over_panels(v)]
    c_all, c_t, pair = call(
        functools.partial(near_comp_kernel, n),
        c_own + c_near,
        [ANY] * (3 * n),
        [group_bf, turned_bf, square_bf],
        [sems((3 * n,))],
        n * one,
    )
    c_all, c01, c23, agg_cols, c_share = call(
        functools.partial(group_comp_kernel, n),
        [c_all, pair, *over_panels(after(c_diag, s_first, pair))],
        [VMEM] * 2 + [ANY] * n,
        [group_bf, full_bf, square_bf, panel_bf, share_bf],
        [square_scratch, sems((n,))],
        2 * n * one,
        {0: 0},
    )
    c_far = across(c_share, 0)
    c_t, c01_t = call(
        turn_comp_kernel, [c_all, c_t, c01], [VMEM] * 3, [turned_bf, square_bf], [], 0, {1: 0}
    )
    s_second, s_diag = after(s_second, c_share), after(s_diag, c_t)
    s_pieces = [p for v in (base_bf, s_first, s_second, s_diag) for p in over_panels(v)]
    agg, agg_bf, s3, s23 = call(
        functools.partial(group_cov_kernel, n),
        [base, c_all, c_t, c01, c01_t, *s_pieces],
        [VMEM] * 5 + [ANY] * (GROUP * n),
        [panel_f32, packed_bf, square_bf, square_bf],
        [
            pltpu.VMEM((GROUP, n, rows, lanes), BF),
            pltpu.VMEM((GROUP - 1, nb, nb), BF),
            sems((GROUP, n)),
        ],
        (2 * n + 4) * one,
    )
    agg_c, agg_t, mine, mine_t = call(
        tail_comp_kernel,
        [c_all, c01, after(c23, agg_bf)],
        [VMEM] * 3,
        [full_bf, square_bf, full_bf, square_bf],
        [],
        2 * n * one,
    )
    (cov,) = call(
        group_mine_kernel,
        [base, agg, s3, s23, c_all, c_t],
        [VMEM] * 6,
        [panel_f32],
        [],
        2 * one,
    )
    out_cov = jax.ShapeDtypeStruct((1, nb, w), F32)
    out_comp = jax.ShapeDtypeStruct((1, nb, w), BF)
    sum_scratch = pltpu.VMEM((nb, w), F32)
    c_far = after(c_far, agg_bf)
    s_got = across(agg_bf, 0)
    for bit in range(levels):
        to_last = bit + 2 == levels
        if bit + 1 == levels:
            c_blocks = in_group(c_far)
            if bit:
                c_blocks[0] = after(c_blocks[0], cov)
            c_panel = joined(c_blocks)
            if bit:
                c_panel = after(c_panel, *s_blocks[1:])
            c_parts = over_panels(c_panel)
            s_parts = over_panels(s_got)
            cov, prop = call(
                functools.partial(last_kernel, n, bit),
                [cov, mine, mine_t, *c_parts, *s_parts],
                [VMEM] * (3 + 2 * n),
                [out_cov, out_comp],
                [packed_scratch, square_scratch],
                3 * one,
            )
            break
        if to_last:
            (c_send,) = call(
                functools.partial(share_comp_kernel, n),
                [agg_cols, *over_panels(c_far)],
                [VMEM] * (1 + n),
                [share_bf],
                [],
                one // 4,
            )
            c_blocks = in_group(after(c_far, c_send))
            c_parts = over_panels(joined(c_blocks))
        else:
            c_blocks = in_group(c_far)
            c_parts = over_panels(joined(c_blocks))
            new_agg_c, new_agg_t, new_cols, c_send = call(
                functools.partial(pair_comp_kernel, n),
                [agg_c, *c_parts],
                [VMEM] * (1 + n),
                [full_bf, square_bf, panel_bf, share_bf],
                [],
                n * one,
            )
        c_far = across(c_send, bit + 1)
        new_mine, new_mine_t = call(
            functools.partial(mine_comp_kernel, n, bit),
            [after(mine, c_send), mine_t, *c_parts],
            [VMEM] * (2 + n),
            [full_bf, square_bf],
            [],
            n * one,
        )
        s_parts = over_panels(after(s_got, mine, cov, c_far, c_blocks[2], c_blocks[3]))
        outs = call(
            functools.partial(pair_cov_kernel, n, to_last),
            [agg, agg_cols, agg_t, *s_parts],
            [VMEM] * (3 + n),
            [packed_share, square_bf] + ([] if to_last else [panel_f32, packed_bf]),
            [packed_scratch, sum_scratch, pltpu.VMEM((rows, lanes), BF)],
            2 * one,
        )
        s_send, right = outs[:2]
        s_far = across(s_send, bit + 1)
        (cov,) = call(
            functools.partial(mine_cov_kernel, n, bit),
            [after(cov, s_far), mine, mine_t, right],
            [VMEM] * 4,
            [panel_f32],
            [],
            2 * one,
        )
        if not to_last:
            agg, agg_bf = outs[2:]
            agg_c, agg_t, agg_cols = new_agg_c, new_agg_t, new_cols
        s_blocks = in_group(s_far)
        s_got = joined(s_blocks)
        c_far = after(c_far, s_send)
        mine, mine_t = new_mine, new_mine_t
    return cov, prop


def solution(mesh):
    placed = (P("tm", None, "panel"), P("tm", None, "panel"), P())
    return jax.shard_map(
        shards,
        mesh=mesh,
        in_specs=placed,
        out_specs=(P("tm", None, "panel"), P("tm", None, "panel")),
        check_vma=False,
    )
```

```python
import functools

import jax
import jax.numpy as jnp
from jax import lax
from jax.experimental import pallas as pl
from jax.experimental.pallas import tpu as pltpu
from jax.sharding import PartitionSpec as P

BF = jnp.bfloat16
F32 = jnp.float32
GROUP = 4
BLOCK = 128
ANY = pl.BlockSpec(memory_space=pl.ANY)
VMEM = pl.BlockSpec(memory_space=pltpu.VMEM)
MIB = 1 << 20


def mm(a, b):
    return jnp.dot(a, b, preferred_element_type=F32)


def mm_t(a, b):
    return lax.dot_general(a, b, (((0,), (0,)), ((), ())), preferred_element_type=F32)


def whole(ref):
    return jnp.concatenate([ref[p] for p in range(ref.shape[0])], axis=1)


def put(ref, value):
    width = ref.shape[2]
    for p in range(ref.shape[0]):
        ref[p] = value[:, p * width : (p + 1) * width].astype(ref.dtype)


def where_am_i():
    t = lax.axis_index("tm")
    return t // GROUP, lax.rem(t, GROUP), lax.axis_index("panel")


def run(copies):
    for c in copies:
        c.start()
    for c in copies:
        c.wait()


def copy_all(pairs, sems):
    return [pltpu.make_async_copy(s, d, sems.at[i]) for i, (s, d) in enumerate(pairs)]


def panel_pairs(pieces, dst, q):
    n = len(pieces)
    return [(piece, dst.at[lax.rem(q + r, n)]) for r, piece in enumerate(pieces)]


def group_start(blocks, dst, sems, lo, q):
    own, first, second, diag = blocks
    n = len(own)
    for r in range(n):
        p = lax.rem(q + r, n)
        even = 1 - lax.rem(p, 2)
        for mask, piece in ((3, diag[r]), (1 + even, first[r]), (2 - even, second[r]), (0, own[r])):
            slot = jnp.bitwise_xor(lo, mask)
            pltpu.make_async_copy(piece, dst.at[slot, p], sems.at[slot, p]).start()


def group_wait(own, dst, sems, *slots):
    for slot in slots:
        for p in range(len(own)):
            pltpu.make_async_copy(own[p], dst.at[slot, p], sems.at[slot, p]).wait()


def packs(n, w):
    return n == 2 and w % BLOCK == 0


def packed_shape(n, nb, w):
    if not packs(n, w):
        return nb, w
    k = w // BLOCK
    return (k * (k + 1) // 2 + (k * k + 1) // 2) * BLOCK, BLOCK


def triangle(k):
    return [(i, j) for i in range(k) for j in range(i + 1)]


def halves(k):
    every = [(a, b) for a in range(k) for b in range(k)]
    half = (k * k + 1) // 2
    return every[:half], every[k * k - half :]


def pack(panel, out, q, n):
    nb, w = panel.shape
    if not packs(n, w):
        out[...] = panel[...].astype(BF)
        return
    k = w // BLOCK
    at = 0
    for i, j in triangle(k):
        rows = pl.ds(pl.multiple_of(q * w + i * BLOCK, BLOCK), BLOCK)
        out[at : at + BLOCK, :] = panel[rows, j * BLOCK : (j + 1) * BLOCK].astype(BF)
        at += BLOCK
    for side, blocks in enumerate(halves(k)):

        @pl.when(q == side)
        def _():
            to = at
            for a, b in blocks:
                i, j = (b, a) if side else (w // BLOCK + a, b)
                value = panel[i * BLOCK : (i + 1) * BLOCK, j * BLOCK : (j + 1) * BLOCK]
                out[to : to + BLOCK, :] = value.astype(BF)
                to += BLOCK


def unpack(src, dst, n):
    nb = dst.shape[0]
    w = nb // n
    if not packs(n, w):
        dst[...] = whole(src)
        return
    k = w // BLOCK

    def both(block, i, j):
        dst[i * BLOCK : (i + 1) * BLOCK, j * BLOCK : (j + 1) * BLOCK] = block
        if i != j:
            dst[j * BLOCK : (j + 1) * BLOCK, i * BLOCK : (i + 1) * BLOCK] = block.T

    seen = set()
    for p in range(n):
        at = 0
        for i, j in triangle(k):
            both(src[p, at : at + BLOCK, :], p * k + i, p * k + j)
            at += BLOCK
        for a, b in halves(k)[p]:
            if (a, b) not in seen:
                i, j = (b, k + a) if p else (k + a, b)
                both(src[p, at : at + BLOCK, :], i, j)
            seen.add((a, b))
            at += BLOCK


def panel_of(matrix, q, n, use):
    w = matrix.shape[1] // n
    for p in range(n):

        @pl.when(q == p)
        def _():
            use(matrix[:, p * w : (p + 1) * w])


def split(refs, *counts):
    out, at = [], 0
    for c in counts:
        out.append(refs[at : at + c])
        at += c
    return out


def call(kernel, ins, in_specs, outs, scratch, flops, aliases=None):
    size = sum(a.size * a.dtype.itemsize for a in ins) + sum(
        o.size * o.dtype.itemsize for o in outs
    )
    return pl.pallas_call(
        kernel,
        in_specs=in_specs,
        out_specs=[VMEM] * len(outs),
        out_shape=outs,
        scratch_shapes=scratch,
        input_output_aliases=aliases or {},
        compiler_params=pltpu.CompilerParams(vmem_limit_bytes=24 * MIB),
        cost_estimate=pl.CostEstimate(flops=flops, bytes_accessed=size, transcendentals=0),
    )(*ins)


def base_kernel(n, *refs):
    factor, sigma, f_parts, c_parts, (base, base_bf), (f_all, c_all, sig, sems) = split(
        refs, 1, 1, n, n, 2, 4
    )
    factor, sigma = factor[0], sigma[0]
    hi, lo, q = where_am_i()
    width = factor.shape[1]
    run(copy_all(panel_pairs(f_parts, f_all, q), sems))
    own = factor[...]
    high = own.astype(BF)
    low = (own - high.astype(F32)).astype(BF)
    for p in range(n):
        part = f_all[p]
        base[p * width : (p + 1) * width, :] = mm_t(part, high) + mm_t(part, low)

    @pl.when(lax.axis_index("tm") == lax.axis_size("tm") - 1)
    def _():
        run(copy_all(panel_pairs(c_parts, c_all, q) + [(sigma, sig)], sems))
        s = sig[...]
        s_high = s.astype(BF)
        s_low = (s - s_high.astype(F32)).astype(BF)
        c_own = c_all[q]
        mid = mm(s_high, c_own) + mm(s_low, c_own)
        mid_high = mid.astype(BF)
        mid_low = (mid - mid_high.astype(F32)).astype(BF)
        c_full = whole(c_all)
        base[...] += mm_t(c_full, mid_high) + mm_t(c_full, mid_low)

    pack(base, base_bf, q, n)


def pair_product(c, member):
    odd = lax.rem(member, 2)
    return mm(whole(c.at[member - odd + 1]), whole(c.at[member - odd])).astype(BF)


def near_comp_kernel(n, *refs):
    own, first, second, (c, c_t, pair), (sems,) = split(refs, n, n, n, 3, 1)
    hi, lo, q = where_am_i()
    pairs = []
    for r in range(n):
        p = lax.rem(q + r, n)
        even = 1 - lax.rem(p, 2)
        for mask, piece in ((0, own[r]), (1 + even, first[r]), (2 - even, second[r])):
            pairs.append((piece, c.at[jnp.bitwise_xor(lo, mask), p]))
    run(copy_all(pairs, sems))
    pair[...] = pair_product(c, lo)
    for mask in range(GROUP - 1):
        slot = jnp.bitwise_xor(lo, mask)
        c_t[slot] = whole(c.at[slot]).T


def group_comp_kernel(n, *refs):
    (c, pair), diag, outs, (other, sems) = split(refs, 2, n, 5, 2)
    c_out, c01, c23, agg_cols, share = outs
    hi, lo, q = where_am_i()
    far = jnp.bitwise_xor(lo, 3)
    run(copy_all(panel_pairs(diag, c_out.at[far], q), sems))
    other[...] = pair_product(c_out, far)

    @pl.when(lo < 2)
    def _():
        put(c01, pair[...])
        c23[...] = other[...]

    @pl.when(lo >= 2)
    def _():
        put(c01, other[...])
        c23[...] = pair[...]

    agg_cols[...] = mm(c23[...], c01[q]).astype(BF)
    share[...] = agg_cols[quarter_rows(lo, agg_cols.shape[0]), :]


def turn_comp_kernel(c, c_t, c01, c_t_out, c01_t):
    hi, lo, q = where_am_i()
    far = jnp.bitwise_xor(lo, 3)
    c_t_out[far] = whole(c.at[far]).T
    c01_t[...] = whole(c01).T


def tail_comp_kernel(c, c01, c23, agg, agg_t, mine, mine_t):
    hi, lo, q = where_am_i()
    put(agg, mm(c23[...], whole(c01)))
    agg_t[...] = whole(agg).T

    @pl.when(lo == 0)
    def _():
        mine[...] = agg[...]

    @pl.when(lo == 1)
    def _():
        put(mine, mm(c23[...], whole(c.at[1])))

    @pl.when(lo == 2)
    def _():
        put(mine, c23[...])

    @pl.when(lo == 3)
    def _():
        mine[...] = c[3]

    mine_t[...] = whole(mine).T


def sandwich(cov, comp, comp_t):
    return mm(comp_t, mm(cov, comp).astype(BF))


def group_cov_kernel(n, *refs):
    ins, *blocks, outs, scratch = split(refs, 5, n, n, n, n, 4, 3)
    base, c, c_t, c01, c01_t = ins
    agg, agg_bf, s3, s23 = outs
    sent, s, sems = scratch
    hi, lo, q = where_am_i()
    group_start(blocks, sent, sems, lo, q)
    group_wait(blocks[0], sent, sems, 3, 2, 1, 0)
    unpack(sent.at[3], s3, n)
    for k in range(GROUP - 1):
        unpack(sent.at[k], s.at[k], n)
    mid = mm(s3[...], whole(c.at[2])).astype(BF)
    s23[...] = (s[2].astype(F32) + mm(c_t[2], mid)).astype(BF)
    w = agg.shape[1]
    first = s[0, :, :w]
    for p in range(1, n):
        first = jnp.where(q == p, s[0, :, p * w : (p + 1) * w], first)
    total = jnp.where(lo == 0, base[...], first.astype(F32))
    total += sandwich(s[1], c[0, q], c_t[0])
    agg[...] = total + sandwich(s23[...], c01[q], c01_t[...])
    pack(agg, agg_bf, q, n)


def group_mine_kernel(base, agg, s3, s23, c, c_t, mine):
    hi, lo, q = where_am_i()

    @pl.when(lo == 0)
    def _():
        mine[...] = agg[...]

    @pl.when(lo == 1)
    def _():
        mine[...] = base[...] + sandwich(s23[...], c[1, q], c_t[1])

    @pl.when(lo == 2)
    def _():
        mine[...] = base[...] + sandwich(s3[...], c[2, q], c_t[2])

    @pl.when(lo == 3)
    def _():
        mine[...] = base[...]


def is_lower(bit):
    hi, lo, q = where_am_i()
    return lax.rem(hi // (1 << bit), 2) == 0


def panel_rows(q, r, n, w):
    return pl.ds(pl.multiple_of(lax.rem(q + r, n) * w, w), w)


def quarter_rows(place, nb):
    rows = nb // GROUP
    return pl.ds(pl.multiple_of(place * rows, rows), rows)


def times(pieces, right, q):
    n = len(pieces)
    w = right.shape[0] // n
    return sum(mm(x[...], right[panel_rows(q, r, n, w), :]) for r, x in enumerate(pieces))


def place_whole(pieces, dst, q):
    for r, piece in enumerate(pieces):
        dst[lax.rem(q + r, len(pieces))] = piece[...]


def join_kernel(*refs):
    *quarters, out = refs
    hi, lo, q = where_am_i()
    for k, piece in enumerate(quarters[::-1]):
        out[quarter_rows(jnp.bitwise_xor(lo, k), out.shape[0]), :] = piece[...]


def select_kernel(*refs):
    *got, out = refs
    hi, lo, q = where_am_i()
    d = len(got)
    for k, piece in enumerate(got):

        @pl.when(lax.rem(hi, d) == k)
        def _():
            out[...] = piece[...]


def share_comp_kernel(n, agg_cols, *refs):
    quarters, (share,) = split(refs, n, 1)
    hi, lo, q = where_am_i()
    share[...] = times(quarters, agg_cols, q).astype(BF)


def pair_comp_kernel(n, agg, *refs):
    parts, (new_agg, new_agg_t, new_cols, share) = split(refs, n, 4)
    hi, lo, q = where_am_i()
    for p in range(n):
        new_agg[p] = times(parts, agg.at[p], q).astype(BF)
    new_agg_t[...] = whole(new_agg).T
    new_cols[...] = new_agg[q]
    share[...] = new_cols[quarter_rows(lo, new_cols.shape[0]), :]


def mine_comp_kernel(n, bit, *refs):
    (mine, mine_t), parts, (new_mine, new_mine_t) = split(refs, 2, n, 2)
    hi, lo, q = where_am_i()
    lower = is_lower(bit)

    @pl.when(lower)
    def _():
        for p in range(n):
            new_mine[p] = times(parts, mine.at[p], q).astype(BF)
        new_mine_t[...] = whole(new_mine).T

    @pl.when(jnp.logical_not(lower))
    def _():
        new_mine[...] = mine[...]
        new_mine_t[...] = mine_t[...]


def last_comp_kernel(n, bit, *refs):
    (mine,), parts, (out,) = split(refs, 1, n, 1)
    hi, lo, q = where_am_i()
    lower = is_lower(bit)

    @pl.when(lower)
    def _():
        out[0] = times(parts, mine.at[q], q).astype(BF)

    @pl.when(jnp.logical_not(lower))
    def _():
        out[0] = mine[q]


def pair_cov_kernel(n, to_last, agg, agg_cols, agg_t, *refs):
    parts, outs, (sent, total, packed) = split(refs, n, 2 if to_last else 4, 3)
    share, right = outs[:2]
    hi, lo, q = where_am_i()
    place_whole(parts, sent, q)
    unpack(sent, right, n)
    total[...] = agg[...] + sandwich(right[...], agg_cols[...], agg_t[...])
    pack(total, packed, q, n)
    share[...] = packed[quarter_rows(lo, packed.shape[0]), :]
    if not to_last:
        outs[2][...] = total[...]
        outs[3][...] = packed[...]


def mine_cov_kernel(n, bit, cov, mine, mine_t, right, out):
    hi, lo, q = where_am_i()
    lower = is_lower(bit)

    @pl.when(lower)
    def _():
        out[...] = cov[...] + sandwich(right[...], mine[q], mine_t[...])

    @pl.when(jnp.logical_not(lower))
    def _():
        out[...] = cov[...]


def last_cov_kernel(n, bit, *refs):
    (cov, mine, mine_t), parts, (out,), (sent, right) = split(refs, 3, n, 1, 2)
    hi, lo, q = where_am_i()
    lower = is_lower(bit)

    @pl.when(lower)
    def _():
        place_whole(parts, sent, q)
        unpack(sent, right, n)
        out[0] = cov[...] + sandwich(right[...], mine[q], mine_t[...])

    @pl.when(jnp.logical_not(lower))
    def _():
        out[0] = cov[...]


def over_panels(x):
    n = lax.axis_size("panel")
    return [x] + [
        lax.ppermute(x, "panel", [((i + r) % n, i) for i in range(n)]) for r in range(1, n)
    ]


def swap(value, odd_mask, even_mask):
    steps, n = lax.axis_size("tm"), lax.axis_size("panel")
    pairs = []
    for t in range(steps):
        for q in range(n):
            mask = odd_mask if q % 2 else even_mask
            pairs.append((t * n + q, (t ^ mask) * n + q))
    return lax.ppermute(value, ("tm", "panel"), pairs)


def across(x, bit):
    steps = lax.axis_size("tm")
    d = 1 << bit
    got = []
    for back in range(1, d + 1):
        pairs = [
            (g * GROUP + k, (g - back) * GROUP + k)
            for g in range(d, steps // GROUP, 2 * d)
            for k in range(GROUP)
        ]
        got.append(lax.ppermute(x, "tm", pairs))
    if d == 1:
        return got[0]
    return call(select_kernel, got[::-1], [VMEM] * d, [jax.ShapeDtypeStruct(x.shape, x.dtype)], [], 0)[0]


def in_group(x):
    return [x] + [swap(x, mask, mask) for mask in range(1, GROUP)]


def joined(quarters):
    rows, lanes = quarters[0].shape
    whole_panel = jax.ShapeDtypeStruct((rows * GROUP, lanes), BF)
    return call(join_kernel, quarters[::-1], [VMEM] * GROUP, [whole_panel], [], 0)[0]


def after(x, *others):
    return lax.optimization_barrier((x, *others))[0]


def shards(factor_inverse, coupling, sigma_after):
    steps = lax.axis_size("tm")
    n = lax.axis_size("panel")
    nb, w = factor_inverse.shape[1:]
    levels = (steps // GROUP - 1).bit_length()
    panel_bf = jax.ShapeDtypeStruct((nb, w), BF)
    panel_f32 = jax.ShapeDtypeStruct((nb, w), F32)
    full_bf = jax.ShapeDtypeStruct((n, nb, w), BF)
    square_bf = jax.ShapeDtypeStruct((nb, nb), BF)
    group_bf = jax.ShapeDtypeStruct((GROUP, n, nb, w), BF)
    turned_bf = jax.ShapeDtypeStruct((GROUP, nb, nb), BF)
    share_bf = jax.ShapeDtypeStruct((nb // GROUP, w), BF)
    full_scratch = pltpu.VMEM((n, nb, w), BF)
    rows, lanes = packed_shape(n, nb, w)
    packed_bf = jax.ShapeDtypeStruct((rows, lanes), BF)
    packed_share = jax.ShapeDtypeStruct((rows // GROUP, lanes), BF)
    packed_scratch = pltpu.VMEM((n, rows, lanes), BF)
    square_scratch = pltpu.VMEM((nb, nb), BF)
    one = 2 * nb * nb * w
    sems = pltpu.SemaphoreType.DMA

    comp = coupling[0].astype(BF)
    c_first = swap(comp, 1, 2)
    c_second = swap(comp, 2, 1)
    factor = after(factor_inverse[0], comp)
    f_parts = over_panels(factor.astype(BF))
    c_own = over_panels(comp)
    base, base_bf = call(
        functools.partial(base_kernel, n),
        [factor, sigma_after, *f_parts, *c_own],
        [VMEM] + [ANY] * (1 + 2 * n),
        [panel_f32, packed_bf],
        [full_scratch, full_scratch, pltpu.VMEM((nb, n * w), F32), sems((n + 1,))],
        2 * one,
    )
    s_first = swap(base_bf, 1, 2)
    c_diag = swap(c_first, 2, 1)
    s_second = swap(base_bf, 2, 1)
    s_diag = swap(s_first, 2, 1)
    c_near = [p for v in (c_first, c_second) for p in over_panels(v)]
    c_all, c_t, pair = call(
        functools.partial(near_comp_kernel, n),
        c_own + c_near,
        [ANY] * (3 * n),
        [group_bf, turned_bf, square_bf],
        [sems((3 * n,))],
        n * one,
    )
    c_all, c01, c23, agg_cols, c_share = call(
        functools.partial(group_comp_kernel, n),
        [c_all, pair, *over_panels(after(c_diag, s_first, pair))],
        [VMEM] * 2 + [ANY] * n,
        [group_bf, full_bf, square_bf, panel_bf, share_bf],
        [square_scratch, sems((n,))],
        2 * n * one,
        {0: 0},
    )
    c_far = across(c_share, 0)
    c_t, c01_t = call(
        turn_comp_kernel, [c_all, c_t, c01], [VMEM] * 3, [turned_bf, square_bf], [], 0, {1: 0}
    )
    s_second, s_diag = after(s_second, c_share), after(s_diag, c_t)
    s_pieces = [p for v in (base_bf, s_first, s_second, s_diag) for p in over_panels(v)]
    agg, agg_bf, s3, s23 = call(
        functools.partial(group_cov_kernel, n),
        [base, c_all, c_t, c01, c01_t, *s_pieces],
        [VMEM] * 5 + [ANY] * (GROUP * n),
        [panel_f32, packed_bf, square_bf, square_bf],
        [
            pltpu.VMEM((GROUP, n, rows, lanes), BF),
            pltpu.VMEM((GROUP - 1, nb, nb), BF),
            sems((GROUP, n)),
        ],
        (2 * n + 4) * one,
    )
    agg_c, agg_t, mine, mine_t = call(
        tail_comp_kernel,
        [c_all, c01, after(c23, agg_bf)],
        [VMEM] * 3,
        [full_bf, square_bf, full_bf, square_bf],
        [],
        2 * n * one,
    )
    (cov,) = call(
        group_mine_kernel,
        [base, agg, s3, s23, c_all, c_t],
        [VMEM] * 6,
        [panel_f32],
        [],
        2 * one,
    )
    out_cov = jax.ShapeDtypeStruct((1, nb, w), F32)
    out_comp = jax.ShapeDtypeStruct((1, nb, w), BF)
    sum_scratch = pltpu.VMEM((nb, w), F32)
    c_far = after(c_far, agg_bf)
    s_got = across(agg_bf, 0)
    for bit in range(levels):
        to_last = bit + 2 == levels
        if bit + 1 == levels:
            c_blocks = in_group(c_far)
            if bit:
                c_blocks[0] = after(c_blocks[0], cov)
            c_panel = joined(c_blocks)
            if bit:
                c_panel = after(c_panel, *s_blocks[1:])
            c_parts = over_panels(c_panel)
            (prop,) = call(
                functools.partial(last_comp_kernel, n, bit),
                [after(mine, s_got), *c_parts],
                [VMEM] * (1 + n),
                [out_comp],
                [],
                one,
            )
            s_parts = over_panels(s_got)
            (cov,) = call(
                functools.partial(last_cov_kernel, n, bit),
                [cov, mine, mine_t, *s_parts],
                [VMEM] * (3 + n),
                [out_cov],
                [packed_scratch, square_scratch],
                2 * one,
            )
            break
        if to_last:
            (c_send,) = call(
                functools.partial(share_comp_kernel, n),
                [agg_cols, *over_panels(c_far)],
                [VMEM] * (1 + n),
                [share_bf],
                [],
                one // 4,
            )
            c_blocks = in_group(after(c_far, c_send))
            c_parts = over_panels(joined(c_blocks))
        else:
            c_blocks = in_group(c_far)
            c_parts = over_panels(joined(c_blocks))
            new_agg_c, new_agg_t, new_cols, c_send = call(
                functools.partial(pair_comp_kernel, n),
                [agg_c, *c_parts],
                [VMEM] * (1 + n),
                [full_bf, square_bf, panel_bf, share_bf],
                [],
                n * one,
            )
        c_far = across(c_send, bit + 1)
        new_mine, new_mine_t = call(
            functools.partial(mine_comp_kernel, n, bit),
            [after(mine, c_send), mine_t, *c_parts],
            [VMEM] * (2 + n),
            [full_bf, square_bf],
            [],
            n * one,
        )
        s_parts = over_panels(after(s_got, mine, cov, c_far, *c_blocks[1:]))
        outs = call(
            functools.partial(pair_cov_kernel, n, to_last),
            [agg, agg_cols, agg_t, *s_parts],
            [VMEM] * (3 + n),
            [packed_share, square_bf] + ([] if to_last else [panel_f32, packed_bf]),
            [packed_scratch, sum_scratch, pltpu.VMEM((rows, lanes), BF)],
            2 * one,
        )
        s_send, right = outs[:2]
        s_far = across(s_send, bit + 1)
        (cov,) = call(
            functools.partial(mine_cov_kernel, n, bit),
            [after(cov, s_far), mine, mine_t, right],
            [VMEM] * 4,
            [panel_f32],
            [],
            2 * one,
        )
        if not to_last:
            agg, agg_bf = outs[2:]
            agg_c, agg_t, agg_cols = new_agg_c, new_agg_t, new_cols
        s_blocks = in_group(s_far)
        s_got = joined(s_blocks)
        c_far = after(c_far, s_send)
        mine, mine_t = new_mine, new_mine_t
    return cov, prop


def solution(mesh):
    placed = (P("tm", None, "panel"), P("tm", None, "panel"), P())
    return jax.shard_map(
        shards,
        mesh=mesh,
        in_specs=placed,
        out_specs=(P("tm", None, "panel"), P("tm", None, "panel")),
        check_vma=False,
    )
```
